32 devices in a mesh: seq: 16 (over z, x, core), head: 2 (over y).
Axes of the slice: x: 2, y: 2, z: 4, core: 2. Of those that a mesh axis runs over, the one named last changes fastest.
Arguments:
- layer_input: bfloat16 [4096, 768], P(('seq', 'head')), may hold values from -6 to 6
- doc_ids: int32 [4096], P(('seq', 'head')), may hold values from -1 to 3, as said below
- cotangent: bfloat16 [4096, 768], P(('seq', 'head')), may hold values from -6 to 6
- ln1_gain: float32 [768], replicated, may hold values from 0.5 to 1.5
- ln1_bias: float32 [768], replicated, may hold values from -1.75 to 1.75
- w_qkv: bfloat16 [768, 3, 768], P(None, None, 'head'), may hold values from -0.21875 to 0.21875
- bias_qv: float32 [2, 768], P(None, 'head'), may hold values from -1.75 to 1.75
- w_out: bfloat16 [768, 768], P('head'), may hold values from -3.5 to 3.5
- b_out: float32 [768], replicated, may hold values from -1.75 to 1.75
- ln2_gain: float32 [768], replicated, may hold values from 0.5 to 1.5
- ln2_bias: float32 [768], replicated, may hold values from -1.75 to 1.75
- w_up: bfloat16 [768, 3072], P('seq', 'head'), may hold values from -0.21875 to 0.21875
- b_up: float32 [3072], replicated, may hold values from -1.75 to 1.75
- w_down: bfloat16 [3072, 768], P('head', 'seq'), may hold values from -0.109375 to 0.109375
- b_down: float32 [768], replicated, may hold values from -1.75 to 1.75
Outputs:
- layer_output: bfloat16 [4096, 768], P(('seq', 'head'))
- grad_input: float32 [4096, 768], P(('seq', 'head'))
- grad_ln1_gain: float32 [768], replicated
- grad_ln1_bias: float32 [768], replicated
- grad_w_qkv: float32 [768, 3, 768], P(None, None, 'head')
- grad_bias_qv: float32 [2, 768], P(None, 'head')
- grad_w_out: float32 [768, 768], P('head')
- grad_b_out: float32 [768], replicated
- grad_ln2_gain: float32 [768], replicated
- grad_ln2_bias: float32 [768], replicated
- grad_w_up: float32 [768, 3072], P('seq', 'head')
- grad_b_up: float32 [3072], replicated
- grad_w_down: float32 [3072, 768], P('head', 'seq')
- grad_b_down: float32 [768], replicated
The draws below stay inside these ranges and needn't reach their ends.
Inputs may be any that keep to these rules, and one draw needn't show every extreme that they name: `doc_ids`: ids do not fall along the row until its last positions, which hold -1 (padding); there are at most four documents, and the one with id 2 begins within the first 128 positions and ends within the last 256 positions.
All inputs are finite; a program needn't handle non-finite values.
Results may differ from the reference program's by a relative error of at most 0.017.
Values may be sent and summed in bfloat16 or wider, within the bound.
A program may use at most 320 MiB of HBM per device.

```python
import math
from functools import partial
import jax
import jax.numpy as jnp
from jax import lax

D = 768
HEADS = 12
HEAD_DIM = 64
FF = 3072
TOK_DEV = 256
SEG = 2048
TOKENS = 4096


def draw_doc_ids(key, part):
    streams = jax.random.split(key, 4)
    long_start = jax.random.randint(streams[0], (), 1, TOK_DEV // 2)
    first_split = jax.random.randint(streams[1], (), 0, long_start + 1)
    padding = jax.random.randint(streams[2], (), 1, TOK_DEV // 4 + 1)
    tail_length = jax.random.randint(streams[3], (), 1, TOK_DEV // 2)
    long_end = TOKENS - padding - tail_length
    position = jnp.arange(TOKENS, dtype=jnp.int32)
    ident = (position >= first_split).astype(jnp.int32) + (position >= long_start).astype(jnp.int32)
    ident = ident + (position >= long_end).astype(jnp.int32)
    return jnp.where(position >= TOKENS - padding, -1, ident).astype(jnp.int32)


def with_spikes(entries, key, source, target, parts, factor):
    owner, partner = [(jnp.arange(entries.shape[dim]) // (entries.shape[dim] // parts)).reshape([-1 if axis == dim else 1 for axis in range(entries.ndim)]) for dim in (source, target)]
    chosen = jax.random.permutation(key, parts)[partner]
    strong = (owner == chosen) | (owner == (partner + parts // 2) % parts)
    return jnp.where(strong, factor * entries, entries)


def steps_of(stream_key, shape, cuts, least, high):
    def one(axis_at, shards_of):
        steps = jax.random.uniform(jax.random.fold_in(jax.random.fold_in(stream_key, 6), axis_at), (shards_of,), jnp.float32, least / len(cuts), high / len(cuts))
        return jnp.repeat(jnp.exp(steps), shape[axis_at] // shards_of).reshape((-1,) + (1,) * (len(shape) - axis_at - 1))

    loudness = one(*cuts[0])
    for cut in cuts[1:]:
        loudness = loudness * one(*cut)
    return loudness


def scatter_about(rng, dims, scale, limit, cuts=(), kind=jnp.bfloat16):
    loudness = steps_of(rng, dims, cuts, -0.22, 0.18) if cuts else 1.0
    values = jax.random.normal(rng, dims, jnp.float32) * scale * loudness
    return jnp.minimum(jnp.maximum(values, -limit), limit).astype(kind)


def heavy_noise(own_key, extent, scale, reach, pieces, heavy, kind=jnp.bfloat16):
    entries = scale * jax.random.normal(own_key, extent, jnp.float32)
    if pieces:
        entries = entries * steps_of(own_key, extent, pieces, -0.22, 0.18)
    return jnp.clip(with_spikes(entries, jax.random.fold_in(own_key, 3), *heavy), -reach, reach).astype(kind)


def setup_inputs(seed: int = 0) -> dict:
    streams_of = jax.random.split(jax.random.key(seed), 16)
    layer_input = heavy_noise(streams_of[0], (TOKENS, D), 1.0, 6.0, ((0, 32),), (0, 1, 32, 2.75))
    doc_ids = draw_doc_ids(jax.random.fold_in(streams_of[15], 71), 0)
    cotangent = heavy_noise(streams_of[2], (TOKENS, D), 1.0, 6.0, ((0, 32),), (0, 1, 32, 2.75))
    ln1_gain = jnp.clip(1.0 + 0.1 * jax.random.normal(streams_of[3], (D,), jnp.float32), 0.5, 1.5)
    ln1_bias = scatter_about(streams_of[4], (D,), 0.3, 1.75, (), jnp.float32)
    w_qkv = scatter_about(streams_of[5], (D, 3, HEADS * HEAD_DIM), D ** -0.5, 0.21875, ((2, 2),))
    bias_qv = scatter_about(streams_of[6], (2, HEADS * HEAD_DIM), 0.3, 1.75, ((1, 2),), jnp.float32)
    w_out = scatter_about(streams_of[7], (HEADS * HEAD_DIM, D), (max(HEADS * HEAD_DIM // 256, 1)) ** -0.5, 3.5, ((0, 2),))
    b_out = scatter_about(streams_of[8], (D,), 0.3, 1.75, (), jnp.float32)
    ln2_gain = jnp.clip(1.0 + 0.1 * jax.random.normal(streams_of[9], (D,), jnp.float32), 0.5, 1.5)
    ln2_bias = scatter_about(streams_of[10], (D,), 0.3, 1.75, (), jnp.float32)
    w_up = scatter_about(streams_of[11], (D, FF), D ** -0.5, 0.21875, ((0, 16), (1, 2)))
    b_up = scatter_about(streams_of[12], (FF,), 0.3, 1.75, (), jnp.float32)
    w_down = scatter_about(streams_of[13], (FF, D), FF ** -0.5, 0.109375, ((0, 2), (1, 16)))
    b_down = scatter_about(streams_of[14], (D,), 0.3, 1.75, (), jnp.float32)
    return {"layer_input": layer_input, "doc_ids": doc_ids, "cotangent": cotangent, "ln1_gain": ln1_gain, "ln1_bias": ln1_bias, "w_qkv": w_qkv, "bias_qv": bias_qv, "w_out": w_out, "b_out": b_out, "ln2_gain": ln2_gain, "ln2_bias": ln2_bias, "w_up": w_up, "b_up": b_up, "w_down": w_down, "b_down": b_down}


LEVELS = ((1, 1), (2, 2), (4, 4), (8, 6), (16, 12))
EPS = 1e-05
NEGATIVE = -1e+30
HIGH = lax.Precision.HIGHEST

@jax.custom_vjp
def low(v):
    return lax.optimization_barrier(v.astype(jnp.bfloat16)).astype(jnp.float32)

@jax.custom_vjp
def low_back(v):
    return v

def low_keep(v):
    return (low(v), None)

def low_pass(kept, grad):
    return (grad,)

def back_keep(v):
    return (v, None)

def back_low(kept, grad):
    return (low(grad),)
low.defvjp(low_keep, low_pass)
low_back.defvjp(back_keep, back_low)

def layer_norm(values, gain, shift):
    mean = lax.optimization_barrier(jnp.mean(values, axis=-1, keepdims=True))
    centred = values - mean
    spread = lax.optimization_barrier(jnp.mean(centred * centred, axis=-1, keepdims=True))
    return centred * lax.rsqrt(spread + EPS) * gain + shift

def pair_counts(query_pos, key_pos, head):
    total = jnp.zeros((query_pos.shape[0], key_pos.shape[0]), jnp.float32)
    for factor, rate in LEVELS:
        width = SEG * factor
        same = query_pos[:, None] // width == key_pos[None, :] // width
        offset = head % rate
        pick_query = query_pos % width % rate == offset
        pick_key = key_pos % width % rate == offset
        total = total + (same & pick_query[:, None] & pick_key[None, :]).astype(jnp.float32)
    return total

def head_attention(query, key, value, doc_ids, head):
    length = query.shape[0]
    block = math.gcd(length, 2048)
    key_pos = jnp.arange(length, dtype=jnp.int32)
    scale = HEAD_DIM ** (-0.5)

    def one_block(item):
        query_blk, doc_blk, begin = item
        query_pos = begin + jnp.arange(block, dtype=jnp.int32)
        scores = low_back(jnp.dot(query_blk, key.T, precision=HIGH) * scale)
        counts = pair_counts(query_pos, key_pos, head)
        allowed = (key_pos[None, :] <= query_pos[:, None]) & (doc_blk[:, None] == doc_ids[None, :])
        counts = counts * allowed.astype(jnp.float32)
        live = counts > 0
        peak = lax.optimization_barrier(jnp.max(jnp.where(live, scores, NEGATIVE), axis=1, keepdims=True))
        weights = jnp.where(live, counts * jnp.exp(scores - peak), 0.0)
        probs = low(weights / lax.optimization_barrier(jnp.sum(weights, axis=1, keepdims=True)))
        return jnp.dot(probs, value, precision=HIGH)
    number = length // block
    items = (query.reshape(number, block, HEAD_DIM), doc_ids.reshape(number, block), jnp.arange(number, dtype=jnp.int32) * block)
    result = lax.map(jax.checkpoint(one_block), items)
    return result.reshape(length, HEAD_DIM)

def forward(x_float, ln1_gain, ln1_bias, w_qkv, bias_qv, w_out, b_out, ln2_gain, ln2_bias, w_up, b_up, w_down, b_down, doc_ids):
    length = x_float.shape[0]
    norm_one = low(layer_norm(x_float, ln1_gain, ln1_bias))
    mixed = jnp.einsum('td,dch->tch', norm_one, w_qkv, precision=HIGH)
    zero_row = jnp.zeros_like(bias_qv[0:1])
    bias_all = jnp.concatenate([bias_qv[0:1], zero_row, bias_qv[1:2]], axis=0)
    qkv = low_back(low(mixed + bias_all[None]))
    split = qkv.reshape(length, 3, HEADS, HEAD_DIM).transpose(1, 2, 0, 3)
    head_ids = jnp.arange(HEADS, dtype=jnp.int32)
    attn = lax.map(lambda item: head_attention(item[0], item[1], item[2], doc_ids, item[3]), (split[0], split[1], split[2], head_ids))
    attn = low_back(low(attn.transpose(1, 0, 2).reshape(length, HEADS * HEAD_DIM)))
    hidden_one = x_float + low_back(jnp.dot(attn, w_out, precision=HIGH)) + b_out
    norm_two = low(layer_norm(hidden_one, ln2_gain, ln2_bias))
    pre = low_back(jnp.dot(norm_two, w_up, precision=HIGH)) + b_up
    act = low(jax.nn.gelu(pre, approximate=True))
    return hidden_one + jnp.dot(act, w_down, precision=HIGH) + b_down

def reference(layer_input, doc_ids, cotangent, ln1_gain, ln1_bias, w_qkv, bias_qv, w_out, b_out, ln2_gain, ln2_bias, w_up, b_up, w_down, b_down):
    func = partial(forward, doc_ids=doc_ids)
    result, backward = jax.vjp(func, layer_input.astype(jnp.float32), ln1_gain, ln1_bias, w_qkv.astype(jnp.float32), bias_qv, w_out.astype(jnp.float32), b_out, ln2_gain, ln2_bias, w_up.astype(jnp.float32), b_up, w_down.astype(jnp.float32), b_down)
    valid = (doc_ids >= 0).astype(jnp.float32)[:, None]
    grads = backward(cotangent.astype(jnp.float32) * valid)
    return (result.astype(jnp.bfloat16), grads[0], grads[1], grads[2], grads[3], grads[4], grads[5], grads[6], grads[7], grads[8], grads[9], grads[10], grads[11], grads[12])
```

```python
import functools

import jax
import jax.numpy as jnp
import ml_dtypes
import numpy as np
from jax import lax
from jax.experimental import pallas as pl
from jax.experimental.pallas import tpu as pltpu
from jax.sharding import PartitionSpec as P

HEADS = 12
HEAD_DIM = 64
SEG = 2048


LEVELS = ((1, 1), (2, 2), (4, 4), (8, 6), (16, 12))
EPS = 1e-05
NEGATIVE = -1e30
block_limit = 2048
TOKENS = 4096


MESH = pl.DeviceIdType.MESH
VMEM = pltpu.VMEM
LIMIT = 58 << 20
F32 = jnp.float32
B16 = jnp.bfloat16


def dot(a, b):
    return jnp.dot(a, b, preferred_element_type=F32)


def dot_nt(a, b):
    return lax.dot_general(a, b, (((1,), (1,)), ((), ())), preferred_element_type=F32)


def sid(z, x, c):
    return z * 4 + x * 2 + c


class Place:
    def __init__(self):
        s = lax.axis_index("seq")
        self.s, self.y = s, lax.axis_index("head")
        self.z, self.x, self.c = s // 4, (s // 2) % 2, s % 2
        self.seg, self.zl = self.z // 2, self.z % 2
        self.u = s % 8
        self.b = self.u * 2 + self.y
        self.unit = jnp.logical_and(self.u != 3, self.u != 5)
        self.hl = self.u - self.u // 4 - self.u // 6
        self.head = self.y * 6 + self.hl
        self.parity = self.head % 2
        z, x, c, y = self.z, self.x, self.c, self.y
        self.zf = z + 1 - 2 * self.zl
        self.nx, self.ny = (sid(z, 1 - x, c), y), (s, 1 - y)
        self.nz, self.nc = (sid(self.zf, x, c), y), (sid(z, x, 1 - c), y)
        self.far = (sid((z + 2) % 4, x, c), y)
        self.fb = {"x": 4 * (1 - 2 * x), "y": 1 - 2 * y, "z": 8 * (1 - 2 * self.zl), "c": 2 * (1 - 2 * c)}

    def cube(self):
        z, x, c, y = self.z, self.x, self.c, self.y
        for k in range(1, 16):
            zz = self.zf if k & 8 else z
            xx = 1 - x if k & 4 else x
            cc = 1 - c if k & 2 else c
            yy = 1 - y if k & 1 else y
            yield (sid(zz, xx, cc), yy)

    def greet(self):
        others = list(self.cube())
        others += [(sid((self.z + 2) % 4, self.x, self.c), self.y), (sid((self.zf + 2) % 4, self.x, self.c), self.y)]
        barrier = pltpu.get_barrier_semaphore()
        for dev in others:
            pl.semaphore_signal(barrier, inc=1, device_id=dev, device_id_type=MESH)
        pl.semaphore_wait(barrier, len(others))


class Mail:
    def __init__(self, sems):
        self.sems, self.used, self.sent = sems, 0, []

    def send(self, src, dst, rsem, dev, cond=None):
        k = self.used
        self.used += 1

        def make():
            return pltpu.make_async_remote_copy(
                src_ref=src, dst_ref=dst, send_sem=self.sems.at[k], recv_sem=rsem, device_id=dev, device_id_type=MESH
            )

        if cond is None:
            make().start()
        else:
            pl.when(cond)(lambda: make().start())
        self.sent.append((cond, make))

    def got(self, dst, rsem, dev):
        pltpu.make_async_remote_copy(
            src_ref=dst, dst_ref=dst, send_sem=self.sems.at[0], recv_sem=rsem, device_id=dev, device_id_type=MESH
        ).wait_recv()

    def close(self):
        for cond, make in self.sent:
            if cond is None:
                make().wait_send()
            else:
                pl.when(cond)(lambda make=make: make().wait_send())


def both(*terms):
    out = terms[0]
    for term in terms[1:]:
        out = jnp.logical_and(out, term)
    return out


def iota(shape, dim):
    return lax.broadcasted_iota(jnp.int32, shape, dim)


def norm_parts(v):
    mean = jnp.mean(v, axis=-1, keepdims=True)
    cen = v - mean
    inv = lax.rsqrt(jnp.mean(cen * cen, axis=-1, keepdims=True) + EPS)
    return cen * inv, inv


def norm_grad(z, inv, e):
    return (e - jnp.mean(e, axis=-1, keepdims=True) - z * jnp.mean(e * z, axis=-1, keepdims=True)) * inv


def pick_type(pos, head, rows):
    v = pos - head + 24.0
    m = v - 12.0 * jnp.floor((v + 0.5) * (1.0 / 12.0))
    out = jnp.where(m == 0.0, rows[4], rows[0])
    out = jnp.where(m == 6.0, rows[3], out)
    out = jnp.where(jnp.logical_or(m == 4.0, m == 8.0), rows[2], out)
    return jnp.where(jnp.logical_or(m == 2.0, m == 10.0), rows[1], out)


def halves(e, o):
    low = iota(e.shape, 1) < 64
    return jnp.where(low, e, pltpu.roll(o, 64, 1)), jnp.where(low, pltpu.roll(e, 64, 1), o)


def tile_mask(st, c, seg, parity, tq, par, start):
    rr = iota((512, 256), 0)
    near = (c - 2) * 512 + seg * SEG + 2 * (rr & 255) + (rr >> 8)
    far = c * 1024 + 2 * rr + parity
    kpos = near + jnp.asarray(c < 2, jnp.int32) * (far - near)
    qpos = seg * SEG + tq * 512 + 2 * iota((512, 256), 1) + par
    return both(kpos <= qpos, kpos.astype(F32) >= start)


def kernel_one(
    x_ref, dy_ref, doc_ref, wq_ref, bq_ref, g1_ref, b1_ref, wo_own, bo_ref, g2_ref, b2_ref, wud_ref, bup_ref, bd_ref, tab_ref,
    qa, ka, va, ns, lse, ot, strow, dpk, grads, dh_out, lout, sums, supg,
    xs, docs, wb, wo, dyp, orecv, osend, kvs, kvf, attn, vt, hid, n2s, dys, acts, dpre, facc, dacc, ys, yr, fs, fr, fo,
    ss, rsx, rsc, rsd, rsw, rso, rsf, rsy,
):
    p = Place()
    mail = Mail(ss)
    seg, y, b, hl = p.seg, p.y, p.b, p.hl
    p.greet()

    dims = ("x", "y", "z")
    nbr = {"x": p.nx, "y": p.ny, "z": p.nz}
    part = [pl.ds(k * 256, 256) for k in range(3)]
    xs[b] = x_ref[...]
    docs[b] = doc_ref[...]
    order = [[dims[(k + j) % 3] for j in range(3)] for k in range(3)]

    def pass_on(k, blk, dev):
        ref = xs.at[blk, :, part[k]]
        mail.send(ref, ref, rsx.at[k, blk], dev)

    def to_core(k, blk):
        ref = xs.at[blk, :, part[k]]
        mail.send(ref, ref, rsc.at[k, blk], p.nc)

    for j in range(3):
        for k in range(3):
            pass_on(k, b, nbr[order[k][j]])
    for k in range(3):
        to_core(k, b)
    for src in (0, 14, 15):
        for dev in p.cube():
            mail.send(docs.at[src], docs.at[src], rsd.at[src], dev, cond=b == src)

    head = p.head.astype(F32)
    for t in range(4):
        rr = iota((512, 128), 0)
        pos = (seg * SEG + t * 512 + 2 * (rr & 255) + (rr >> 8)).astype(F32)
        qa[t] = pick_type(pos, head, [tab_ref[i : i + 1] for i in range(5)]).astype(B16)
        ka[t + 2] = pick_type(pos, head, [tab_ref[8 + i : 9 + i] for i in range(5)]).astype(B16)

    def seen(k, blk):
        mail.got(xs.at[blk, :, part[k]], rsx.at[k, blk], p.nx)
        to_core(k, blk)

    for k in range(3):
        f = [p.fb[d] for d in order[k]]
        seen(k, b + f[0])
        pass_on(k, b + f[0], nbr[order[k][1]])
        pass_on(k, b + f[0], nbr[order[k][2]])
    for k in range(3):
        f = [p.fb[d] for d in order[k]]
        for blk in (b + f[1], b + f[1] + f[0]):
            seen(k, blk)
            pass_on(k, blk, nbr[order[k][2]])

    def rows_of(s):
        return wb.at[pl.ds(pl.multiple_of(s * 48, 16), 48), :]

    wb[pl.ds(pl.multiple_of(p.s * 48, 16), 48), :] = wud_ref[...]

    def give(s, dev, cond=None):
        mail.send(rows_of(s), rows_of(s), rsw.at[s], dev, cond)

    z, x, c = p.z, p.x, p.c
    give(p.s, (sid((z + 1) % 4, x, c), y), z <= 2)
    give(p.s, (sid((z + 3) % 4, x, c), y), z >= 1)
    give(p.s, p.nx)
    give(p.s, p.nc)
    wo[y] = wo_own[...]
    mail.send(wo.at[y], wo.at[y], rsy.at[0], p.ny)
    dyp[y] = dy_ref[...]
    mail.send(dyp.at[y], dyp.at[y], rsy.at[1], p.ny)

    def chain(d):
        up, dn = (z - d + 4) % 4, (z + d) % 4
        has_up, has_dn = z >= d, z <= 3 - d
        su, sd = sid(up, x, c), sid(dn, x, c)
        pl.when(has_up)(lambda: mail.got(rows_of(su), rsw.at[su], p.nx))
        if d < 3:
            give(su, (sid((z + 1) % 4, x, c), y), both(has_up, z <= 2))
        give(su, p.nx, has_up)
        give(su, p.nc, has_up)
        pl.when(has_dn)(lambda: mail.got(rows_of(sd), rsw.at[sd], p.nx))
        if d < 3:
            give(sd, (sid((z + 3) % 4, x, c), y), both(has_dn, z >= 1))
        give(sd, p.nx, has_dn)
        give(sd, p.nc, has_dn)

    for k in range(3):
        f = [p.fb[d] for d in order[k]]
        for blk in (b + f[2], b + f[2] + f[0], b + f[2] + f[1], b + f[2] + f[1] + f[0]):
            seen(k, blk)
    for i in range(8):
        blk = (i // 4) * 8 + ((i // 2) % 2) * 4 + (1 - c) * 2 + i % 2
        for k in range(3):
            mail.got(xs.at[blk, :, part[k]], rsc.at[k, blk], p.nc)
    for src in (0, 14, 15):
        pl.when(b != src)(lambda src=src: mail.got(docs.at[src], rsd.at[src], p.nx))

    def qkv_step(i, _):
        rows = xs[pl.ds(2 * i, 2)].reshape(256, 768).astype(F32)
        zz, _inv = norm_parts(rows)
        n1 = (zz * g1_ref[...] + b1_ref[...]).astype(B16)
        mix = (dot(n1, wq_ref[...]) + bq_ref[...]).astype(B16)
        t = i // 2
        for yy in range(2):
            for par in range(2):
                at = yy * 128 + par * 64
                to = pl.ds(pl.multiple_of(par * 256 + (i % 2) * 128 + yy * 64, 64), 64)
                m = mix[at : at + 64]
                qa[t, to] = m[:, :128] * B16(0.125) + qa[t, to]
                ka[t + 2, to] = m[:, 128:256] + ka[t + 2, to]
                va[t + 2, to] = m[:, 256:]
                ns[t, to] = n1[at : at + 64]
        return 0

    @pl.when(p.unit)
    def _():
        lax.fori_loop(0, 8, qkv_step, 0)

    lowlane = iota((256, 128), 1) < 64
    first = both(p.unit, seg == 0)
    second = both(p.unit, seg == 1)
    farrows = pl.ds(pl.multiple_of(p.parity * 256, 256), 256)

    @pl.when(first)
    def _():
        for t in range(4):
            kk = ka[t + 2, farrows].astype(F32)
            vv = va[t + 2, farrows].astype(F32)
            kvs[t] = jnp.where(lowlane, kk, pltpu.roll(vv, 64, 1)).astype(B16)

    mail.send(kvs, kvf, rsf.at[0], p.far, first)
    mail.send(docs.at[0], docs.at[16], rsf.at[1], p.far, first)
    chain(1)

    lane = iota((1, 128), 1)
    lane64 = lane < 64

    def code(row):
        return jnp.where(row < 0.0, 4.0, row)

    def count(rows, level):
        lim = iota((2, 128), 1) < 64
        hit = jnp.where(both(lim, code(rows) < level), 1.0, 0.0)
        return jnp.sum(jnp.sum(hit, axis=1, keepdims=True), axis=0, keepdims=True)

    @pl.when(second)
    def _():
        mail.got(docs.at[16], rsf.at[1], p.far)

    pl.when(jnp.logical_not(second))(lambda: docs.__setitem__(16, docs[0]))
    d0, da, db = docs[16][0:2], docs[14][0:2], docs[15][0:2]
    n1c, n2c = count(d0, 1.0), count(d0, 2.0)
    tail = float(TOKENS - 256)
    t3 = count(da, 3.0) + count(db, 3.0) + tail
    t4 = count(da, 4.0) + count(db, 4.0) + tail

    def start_of(row):
        k = code(row)
        out = jnp.where(k == 1.0, n1c, 0.0)
        out = jnp.where(k == 2.0, n2c, out)
        out = jnp.where(k == 3.0, t3, out)
        return jnp.where(k == 4.0, t4, out)

    two = jnp.full((1, 128), 2.0, F32)
    segf = seg.astype(F32)
    for j in range(8):
        t, par = j // 2, j % 2
        ra, rb = two, two
        if t == 0:
            ra = jnp.where(lane64, 2.0 + (1.0 - segf) * (d0[par : par + 1] - 2.0), 2.0)
        if t == 3:
            last = jnp.where(lane64, da[par : par + 1], db[par : par + 1])
            rb = 2.0 + segf * (last - 2.0)
        strow[j] = jnp.concatenate([start_of(ra), start_of(rb)], axis=1)

    @pl.when(p.unit)
    def _():
        for t in range(4):
            vt[t + 2] = va[t + 2].astype(F32).T.astype(B16)

    def far_ready():
        mail.got(kvf, rsf.at[0], p.far)
        for t in range(4):
            rows = pl.ds((t % 2) * 256, 256)
            fpos = ((t * 256 + iota((256, 128), 0)) * 2 + p.parity).astype(F32)
            feat = pick_type(fpos, head, [tab_ref[16 + i : 17 + i] for i in range(5)])
            kv = kvf[t].astype(F32)
            ka[t // 2, rows] = jnp.where(lowlane, kv, feat).astype(B16)
            one = jnp.where(iota((256, 128), 1) == 64, 1.0, 0.0)
            vv = jnp.where(lowlane, pltpu.roll(kv, 64, 1), one)
            va[t // 2, rows] = vv.astype(B16)
        for h in range(2):
            vt[h] = va[h].astype(F32).T.astype(B16)

    pl.when(second)(far_ready)

    def attend(t):
        for par in range(2):
            q = qa[t, par * 256 : par * 256 + 256]
            begin = jnp.where(both(seg == 1, p.parity == par), 0, 2)

            def step(cc, carry):
                m, acc = carry
                st = dot_nt(ka[cc], q)
                st = jnp.where(tile_mask(st, cc, seg, p.parity, t, par, strow[2 * t + par]), st, NEGATIVE)
                m_new = jnp.maximum(m, jnp.max(st, axis=0, keepdims=True))
                pr = jnp.exp(st - m_new).astype(B16)
                return m_new, acc * jnp.exp(m - m_new) + dot(vt[cc], pr)

            m, acc = lax.fori_loop(begin, t + 3, step, (jnp.full((1, 256), NEGATIVE, F32), jnp.zeros((128, 256), F32)))
            total = acc[64:65]
            ot[t, par * 64 : par * 64 + 64] = acc[:64] / total
            lse[2 * t + par] = m + jnp.log(total)
        osend[t] = ot[t].T.astype(B16)

    for t in range(4):
        pl.when(p.unit)(functools.partial(attend, t))
        zz, xx = seg * 2 + t // 2, t % 2
        for cc in range(2):
            for yy in range(2):
                own = both(p.u == t * 2 + cc, y == yy)
                src = osend.at[t, cc * 128 : cc * 128 + 128]
                mail.send(src, orecv.at[p.head], rso.at[p.head], (sid(zz, xx, cc), yy), both(p.unit, jnp.logical_not(own)))

                @pl.when(both(p.unit, own))
                def _(t=t, cc=cc):
                    orecv[p.head] = osend[t, cc * 128 : cc * 128 + 128]

        if t == 1:
            chain(2)
    chain(3)
    for zq in range(4):
        s = sid(zq, 1 - x, c)
        mail.got(rows_of(s), rsw.at[s], p.nx)
        give(s, p.nc)

    for hh in range(12):
        mine = both(p.unit, p.head == hh)
        pl.when(jnp.logical_not(mine))(lambda hh=hh: mail.got(orecv.at[hh], rso.at[hh], p.nx))
    for a in range(6):
        e, o = halves(orecv[2 * a].astype(F32), orecv[2 * a + 1].astype(F32))
        attn[0:128, a * 128 : a * 128 + 128] = e.astype(B16)
        attn[128:256, a * 128 : a * 128 + 128] = o.astype(B16)
    mail.got(wo.at[1 - y], rsy.at[0], p.ny)
    mail.got(dyp.at[1 - y], rsy.at[1], p.ny)
    pair = pl.multiple_of(p.u * 2, 2)
    for par in range(2):
        for yy in range(2):
            at = pl.ds(par * 128 + yy * 64, 64)
            hid[at] = xs[pair + yy, par * 64 : par * 64 + 64].astype(F32)
            dys[at] = dyp[yy, par * 64 : par * 64 + 64]
    hid[...] = hid[...] + dot(attn[...], wo[...].reshape(768, 768)) + bo_ref[...]
    z2, _inv = norm_parts(hid[...])
    n2s[...] = (z2 * g2_ref[...] + b2_ref[...]).astype(B16)
    for i in range(8):
        s = sid(i // 2, i % 2, 1 - c)
        mail.got(rows_of(s), rsw.at[s], p.nc)

    facc[...] = jnp.zeros_like(facc)
    dacc[...] = jnp.zeros_like(dacc)
    k0 = 0.7978845608028654

    def ffn_step(i, _):
        cols = pl.ds(pl.multiple_of(i * 256, 256), 256)
        dcols = pl.ds(pl.multiple_of(1536 + i * 256, 256), 256)
        up, dn = wb[:, cols], wb[:, dcols]
        pre = dot(n2s[...], up) + bup_ref[:, cols]
        sq = pre * pre
        th = jnp.tanh(k0 * pre * (1.0 + 0.044715 * sq))
        half = 0.5 * (1.0 + th)
        act = (pre * half).astype(B16)
        slope = half + 0.5 * pre * (1.0 - th * th) * (k0 * (1.0 + 3.0 * 0.044715 * sq))
        dp = dot(dys[...], dn) * slope
        supg[:, cols] = jnp.broadcast_to(jnp.sum(dp, axis=0, keepdims=True), (8, 256))
        dpl = dp.astype(B16)
        acts[:, cols] = act
        dpre[:, cols] = dpl
        facc[...] += dot_nt(act, dn)
        dacc[...] += dot_nt(dpl, up)
        return 0

    lax.fori_loop(0, 6, ffn_step, 0)
    ys[...] = dacc[...].astype(B16)
    mail.send(ys, yr, rsy.at[2], p.ny)
    for par in range(2):
        fo[par * 64 : par * 64 + 64] = facc[pl.ds(pl.multiple_of(par * 128 + y * 64, 64), 64)]
        fs[par * 64 : par * 64 + 64] = facc[pl.ds(pl.multiple_of(par * 128 + (1 - y) * 64, 64), 64)].astype(B16)
    mail.send(fs, fr, rsy.at[3], p.ny)

    n2t = n2s[...].astype(F32).T.astype(B16)
    dyt = dys[...].astype(F32).T.astype(B16)

    def grad_step(i, _):
        cols = pl.ds(pl.multiple_of(i * 256, 256), 256)
        dcols = pl.ds(pl.multiple_of(1536 + i * 256, 256), 256)
        grads[:, cols] = dot(n2t, dpre[:, cols]).astype(B16)
        grads[:, dcols] = dot(dyt, acts[:, cols]).astype(B16)
        return 0

    lax.fori_loop(0, 6, grad_step, 0)
    mail.got(yr, rsy.at[2], p.ny)
    dn2 = ys[...].astype(F32) + yr[...].astype(F32)
    z2, inv2 = norm_parts(hid[...])
    dyf = dys[...].astype(F32)
    dh = dyf + norm_grad(z2, inv2, dn2 * g2_ref[...])
    facc[...] = dh
    dacc[...] = dn2 * z2
    dhl = dh.astype(B16)
    da_ = dot_nt(dhl, wo[y])
    for a in range(3):
        e, o = halves(da_[0:128, a * 128 : a * 128 + 128], da_[128:256, a * 128 : a * 128 + 128])
        dpk[2 * a] = e.astype(B16)
        dpk[2 * a + 1] = o.astype(B16)
    grads[:, 3072:3456] = dot(dh.T.astype(B16), attn[:, pl.ds(pl.multiple_of(y * 384, 128), 384)]).astype(B16)
    mail.got(fr, rsy.at[3], p.ny)
    total = [jnp.zeros((1, 768), F32)] * 4
    for par in range(2):
        at = pl.ds(pl.multiple_of(par * 128 + y * 64, 64), 64)
        to = slice(par * 64, par * 64 + 64)
        dh_out[to] = facc[at]
        own = (ys[at].astype(F32) + yr[at].astype(F32), dys[at].astype(F32))
        total[0] = total[0] + jnp.sum(dacc[at], axis=0, keepdims=True)
        total[1] = total[1] + jnp.sum(own[0], axis=0, keepdims=True)
        total[2] = total[2] + jnp.sum(facc[at], axis=0, keepdims=True)
        total[3] = total[3] + jnp.sum(own[1], axis=0, keepdims=True)
        lout[to] = (hid[at] + fo[to] + fr[to].astype(F32) + bd_ref[...]).astype(B16)
    for i in range(4):
        sums[i : i + 1] = total[i]
    mail.close()


UNITS = (0, 1, 2, 4, 6, 7)


class Spread:
    def __init__(self, p, mail, ref, sems, some):
        self.p, self.mail, self.ref, self.sems, self.some = p, mail, ref, sems, some

    def has(self, zz, xx, cc):
        return jnp.logical_or(cc == 0, zz % 2 == xx) if self.some else None

    def go(self, s, dev, cond):
        self.mail.send(self.ref.at[s], self.ref.at[s], self.sems.at[s], dev, cond)

    def take(self, s, cond):
        def wait():
            self.mail.got(self.ref.at[s], self.sems.at[s], self.p.nx)

        if cond is None:
            wait()
        else:
            pl.when(cond)(wait)

    def first(self):
        p = self.p
        has = self.has(p.z, p.x, p.c)
        for k in range(1, 4):
            self.go(p.s, (sid((p.z + k) % 4, p.x, p.c), p.y), has)
        self.go(p.s, p.nx, has)
        self.go(p.s, p.nc, has)

    def second(self):
        p = self.p
        for k in range(1, 4):
            zz = (p.z + k) % 4
            s, has = sid(zz, p.x, p.c), self.has(zz, p.x, p.c)
            self.take(s, has)
            self.go(s, p.nx, has)
            self.go(s, p.nc, has)

    def third(self):
        p = self.p
        for zz in range(4):
            s, has = sid(zz, 1 - p.x, p.c), self.has(zz, 1 - p.x, p.c)
            self.take(s, has)
            self.go(s, p.nc, has)

    def last(self):
        p = self.p
        for zz in range(4):
            for xx in range(2):
                self.take(sid(zz, xx, 1 - p.c), self.has(zz, xx, 1 - p.c))


def kernel_two(
    qa, ka, va, ns, lse, ot, strow, dpk, grads, dh, sums, supg, xp, g1_ref, wq_ref,
    gin, wud, wag, woag, vec,
    dor, doa, delta, kt, dka, dva, dqt, dtt, dfs, dfr, packs, dqr, wms, wmr, gc, gxs, gxr, gzs, gzr, dall, dn, dns, dnr, vbuf, vrec,
    ss, rdo, rgc, rgx, rgz, rdf, rdq, rwm, rag, rwo, rdn, rvec,
):
    p = Place()
    mail = Mail(ss)
    seg, y, x, z, c = p.seg, p.y, p.x, p.z, p.c
    first, second = both(p.unit, seg == 0), both(p.unit, seg == 1)
    p.greet()
    mine_t = p.zl * 2 + x
    crow = pl.ds(pl.multiple_of(c * 128, 128), 128)

    for h, u in enumerate(UNITS):
        spot = dor.at[mine_t, crow]
        mail.send(dpk.at[h], spot, rdo.at[p.u], (seg * 8 + u, y), p.u != u)

        @pl.when(p.u == u)
        def _(h=h):
            dor[mine_t, crow] = dpk[h]

    def block(s):
        return pl.ds(pl.multiple_of(s * 48, 16), 48)

    for xq in range(2):
        xx = 1 - x if xq == 0 else x
        for zz in range(4):
            mail.send(grads.at[block(sid(zz, xx, 1 - c))], gc.at[xq, zz], rgc.at[xq, zz], p.nc)

    def prepare():
        for i in range(8):
            pl.when(p.u != i)(lambda i=i: mail.got(dor.at[i // 2, (i % 2) * 128 : (i % 2) * 128 + 128], rdo.at[i], p.nx))
        low = iota((256, 128), 1) < 64
        for t in range(4):
            d = dor[t].astype(F32)
            doa[2 * t] = jnp.where(low, d, 0.0).astype(B16)
            doa[2 * t + 1] = jnp.where(low, pltpu.roll(d, 64, 1), 0.0).astype(B16)
            prod = d.T * ot[t]
            delta[2 * t] = jnp.sum(prod[:64], axis=0, keepdims=True)
            delta[2 * t + 1] = jnp.sum(prod[64:], axis=0, keepdims=True)
            kt[t + 2] = ka[t + 2].astype(F32).T.astype(B16)
        dqt[...] = jnp.zeros_like(dqt)

    pl.when(p.unit)(prepare)

    def pair(cc, j):
        t, par = j // 2, j % 2
        q = qa[t, pl.ds(pl.multiple_of(par * 256, 256), 256)]
        st = dot_nt(ka[cc], q)
        st = jnp.where(tile_mask(st, cc, seg, p.parity, t, par, strow[j]), st, NEGATIVE)
        pr = jnp.exp(st - lse[j])
        do = doa[j]
        ds = (pr * (dot_nt(va[cc], do) - delta[j])).astype(B16)
        dva[...] += dot(pr.astype(B16), do)
        dka[...] += dot(ds, q)
        dqt[j] += dot(kt[cc], ds)

    def clear():
        dka[...] = jnp.zeros_like(dka)
        dva[...] = jnp.zeros_like(dva)

    @pl.when(second)
    def _():
        for h in range(2):
            kt[h] = ka[h].astype(F32).T.astype(B16)

        def chunk(cc, _):
            clear()

            def step(t, _):
                pair(cc, 2 * t + p.parity)
                return 0

            lax.fori_loop(0, 4, step, 0)
            low = iota((512, 128), 1) < 64
            both_ = jnp.where(low, dka[...], pltpu.roll(dva[...], 64, 1)).astype(B16)
            dfs[2 * cc] = both_[:256]
            dfs[2 * cc + 1] = both_[256:]
            return 0

        lax.fori_loop(0, 2, chunk, 0)

    mail.send(dfs, dfr, rdf.at[0], p.far, second)

    def near(t):
        clear()

        def step(j, _):
            pair(t + 2, j)
            return 0

        lax.fori_loop(2 * t, 8, step, 0)
        dtt[64:128, t * 512 : t * 512 + 512] = dka[...].T[:64].astype(B16)
        dtt[128:192, t * 512 : t * 512 + 512] = dva[...].T[:64].astype(B16)

    def add_far(t):
        rows = dfr[t].astype(F32).T.astype(F32)
        at = pl.ds(pl.multiple_of(t * 512 + p.parity * 256, 256), 256)
        dtt[64:128, at] = (dtt[64:128, at].astype(F32) + rows[:64]).astype(B16)
        dtt[128:192, at] = (dtt[128:192, at].astype(F32) + rows[64:]).astype(B16)

    for xq in range(2):
        for zz in range(4):
            mail.got(gc.at[xq, zz], rgc.at[xq, zz], p.nc)
    for zz in range(4):
        rows = block(sid(zz, 1 - x, c))
        gxs[zz] = (grads[rows].astype(F32) + gc[0, zz].astype(F32)).astype(B16)
        mail.send(gxs.at[zz], gxr.at[zz], rgx.at[zz], p.nx)
    pl.when(p.unit)(lambda: near(0))

    def column(zz):
        mail.got(gxr.at[zz], rgx.at[zz], p.nx)
        return grads[block(sid(zz, x, c))].astype(F32) + gc[1, zz].astype(F32) + gxr[zz].astype(F32)

    for k in range(1, 4):
        zz = (z + k) % 4
        gzs[k] = column(zz).astype(B16)
        mail.send(gzs.at[k], gzr.at[z], rgz.at[z], (sid(zz, x, c), y))
    pl.when(p.unit)(lambda: near(1))
    pl.when(p.unit)(lambda: near(2))
    pl.when(p.unit)(lambda: near(3))

    @pl.when(first)
    def _():
        mail.got(dfr, rdf.at[0], p.far)
        for t in range(4):
            add_far(t)

    @pl.when(p.unit)
    def _():
        for j in range(8):
            dtt[0:64, j * 256 : j * 256 + 256] = (dqt[j][:64] * 0.125).astype(B16)
        for t in range(4):
            for k in range(3):
                e = dtt[k * 64 : k * 64 + 64, t * 512 : t * 512 + 256].astype(F32)
                o = dtt[k * 64 : k * 64 + 64, t * 512 + 256 : t * 512 + 512].astype(F32)
                packs[t, k] = jnp.concatenate([e, o], axis=0).T.astype(B16)

    for t in range(4):
        for cc in range(2):
            src = packs.at[t, :, cc * 128 : cc * 128 + 128]
            u = t * 2 + cc
            mail.send(src, dqr.at[p.hl], rdq.at[p.hl], (seg * 8 + u, y), both(p.unit, p.u != u))

            @pl.when(both(p.unit, p.u == u))
            def _(t=t, cc=cc):
                dqr[p.hl] = packs[t, :, cc * 128 : cc * 128 + 128]

    spread = Spread(p, mail, wag, rag, True)

    @pl.when(p.unit)
    def _():
        dw = dot(dtt[...], ns[...].reshape(2048, 768))
        bias = dot_nt(jnp.ones((16, 2048), B16), dtt[...])
        for h in range(2):
            wms[h, 0:96] = dw[h * 96 : h * 96 + 96].astype(B16)
            wms[h, 96:112, 0:192] = bias.astype(B16)
            wms[h, 96:112, 192:768] = jnp.zeros((16, 576), B16)

    mail.send(wms.at[1 - seg], wmr, rwm.at[0], p.far, p.unit)

    total = column(z)
    for k in range(1, 4):
        zz = (z + k) % 4
        mail.got(gzr.at[zz], rgz.at[zz], p.nx)
        total = total + gzr[zz].astype(F32)
    wud[...] = total[:, :3072]
    woag[p.s] = total[:, 3072:].astype(B16)
    spread_out = Spread(p, mail, woag, rwo, False)
    spread_out.first()

    @pl.when(p.unit)
    def _():
        mail.got(wmr, rwm.at[0], p.far)
        wag[p.s] = (wms[seg].astype(F32) + wmr[...].astype(F32)).astype(B16)

    spread.first()

    for h, u in enumerate(UNITS):
        pl.when(p.u != u)(lambda h=h: mail.got(dqr.at[h], rdq.at[h], p.nx))
    for k in range(3):
        for a in range(3):
            e, o = halves(dqr[2 * a, k].astype(F32), dqr[2 * a + 1, k].astype(F32))
            col = k * 384 + a * 128
            dall[0:128, col : col + 128] = e.astype(B16)
            dall[128:256, col : col + 128] = o.astype(B16)
    dn[...] = dot_nt(dall[...], wq_ref[...])
    for par in range(2):
        dns[par * 64 : par * 64 + 64] = dn[pl.ds(pl.multiple_of(par * 128 + (1 - y) * 64, 64), 64)].astype(B16)
    mail.send(dns, dnr, rdn.at[0], p.ny)
    spread_out.second()
    spread.second()
    z1, inv1 = norm_parts(xp[...].astype(F32))
    mail.got(dnr, rdn.at[0], p.ny)
    own = [dn[pl.ds(pl.multiple_of(par * 128 + y * 64, 64), 64)] for par in range(2)]
    dn1 = jnp.concatenate(own, axis=0) + dnr[...].astype(F32)
    gin[...] = dh[...] + norm_grad(z1, inv1, dn1 * g1_ref[...])

    vbuf[0] = jnp.zeros((16, 768), F32)
    vbuf[0, 0:1] = jnp.sum(dn1 * z1, axis=0, keepdims=True)
    vbuf[0, 1:2] = jnp.sum(dn1, axis=0, keepdims=True)
    vbuf[0, 2:6] = sums[0:4]
    vbuf[0, 6:7] = supg[0:1, 0:768] * (1.0 - y.astype(F32))
    vbuf[0, 7:8] = supg[0:1, 768:1536] * (1.0 - y.astype(F32))
    vbuf[0, 8:9] = supg[0:1, 0:768] * y.astype(F32)
    vbuf[0, 9:10] = supg[0:1, 768:1536] * y.astype(F32)
    peers = (p.nc, p.nx, p.nz, p.far, p.ny)
    for i, dev in enumerate(peers):
        mail.send(vbuf.at[i], vrec.at[i], rvec.at[i], dev)
        if i == 1:
            spread_out.third()
        if i == 2:
            spread.third()
        mail.got(vrec.at[i], rvec.at[i], dev)
        new = vbuf[i] + vrec[i]
        if i < 4:
            vbuf[i + 1] = new
        else:
            vec[...] = new
    spread_out.last()
    spread.last()
    mail.close()


def count_table():
    kinds = np.array([[0, 0, 0, 0], [1, 0, 0, 0], [1, 1, 0, 0], [1, 0, 1, 0], [1, 1, 1, 1]], np.float64)
    shared = kinds @ kinds.T
    table = np.zeros((24, 128), np.float64)
    low = lambda v: float(np.asarray(v, dtype=ml_dtypes.bfloat16).astype(np.float64))
    for i in range(5):
        for k in range(5):
            for base, count in ((64, 1.0 + shared[i, k]), (80, shared[i, k])):
                rest = float(np.log(count)) if count > 0 else 0.0
                for e in range(3):
                    table[i, base + 3 * k + e] = low(rest)
                    rest -= low(rest)
        table[8 + i, 64 + 3 * i : 67 + 3 * i] = 1.0
        table[16 + i, 80 + 3 * i : 83 + 3 * i] = 1.0
    return table.astype(np.float32)


def split_rows(v):
    return v.reshape(64, 2, -1).transpose(1, 0, 2).reshape(128, -1)


def join_rows(v):
    return v.reshape(2, 64, -1).transpose(1, 0, 2).reshape(128, -1)


def vm(shape, dtype=B16):
    return pltpu.VMEM(shape, dtype)


def dma(*shape):
    return pltpu.SemaphoreType.DMA(shape)


def out(shape, dtype=F32):
    return jax.ShapeDtypeStruct(shape, dtype)


def in_vmem(count):
    return [pl.BlockSpec(memory_space=pltpu.VMEM)] * count


def call_one(*args):
    shapes = (
        out((4, 512, 128), B16), out((6, 512, 128), B16), out((6, 512, 128), B16), out((4, 512, 768), B16),
        out((8, 1, 256)), out((4, 128, 256)), out((8, 1, 256)), out((6, 128, 128), B16), out((768, 3456), B16),
        out((128, 768)), out((128, 768), B16), out((8, 768)), out((8, 1536)),
    )
    scratch = [
        vm((16, 128, 768)), vm((17, 8, 128), F32), vm((768, 3072)), vm((2, 384, 768)), vm((2, 128, 768)),
        vm((12, 128, 128)), vm((4, 256, 128)), vm((4, 256, 128)), vm((4, 256, 128)), vm((256, 768)), vm((6, 128, 512)),
        vm((256, 768), F32), vm((256, 768)), vm((256, 768)), vm((256, 1536)), vm((256, 1536)), vm((256, 768), F32),
        vm((256, 768), F32), vm((256, 768)), vm((256, 768)), vm((128, 768)), vm((128, 768)), vm((128, 768), F32),
        dma(160), dma(3, 16), dma(3, 16), dma(16), dma(16), dma(12), dma(2), dma(4),
    ]
    return pl.pallas_call(
        kernel_one, out_shape=shapes, in_specs=in_vmem(len(args)), out_specs=tuple(in_vmem(len(shapes))), scratch_shapes=scratch,
        compiler_params=pltpu.CompilerParams(collective_id=0, has_side_effects=True, vmem_limit_bytes=LIMIT),
    )(*args)


def front(layer_input, doc_ids, cotangent, ln1_gain, ln1_bias, w_qkv, bias_qv, w_out, b_out, ln2_gain, ln2_bias, w_up, b_up, w_down, b_down):
    s, y = lax.axis_index("seq"), lax.axis_index("head")
    u = s % 8
    hl = u - u // 4 - u // 6
    row = lambda v: v.reshape(1, -1)
    xp = split_rows(layer_input)
    dyp = split_rows(jnp.where((doc_ids >= 0)[:, None], cotangent, jnp.zeros_like(cotangent)))
    doc = doc_ids.astype(F32).reshape(64, 2).T
    doc = jnp.pad(jnp.concatenate([doc, doc], axis=1), ((0, 6), (0, 0)))
    wide = ((0, 0), (0, 0), (0, 64))
    wq = jnp.pad(lax.dynamic_slice(w_qkv, (0, 0, hl * 64), (768, 3, 64)), wide).reshape(768, 384)
    bq = lax.dynamic_slice(bias_qv, (0, hl * 64), (2, 64))
    zero, one = jnp.zeros((64,), F32), jnp.ones((1,), F32)
    bq = row(jnp.concatenate([bq[0], zero, zero, zero, bq[1], one, zero[:63]]))
    wud = jnp.concatenate([w_up, w_down.T], axis=1)
    bup = row(lax.dynamic_slice(b_up, (y * 1536,), (1536,)))
    return call_one(
        xp, dyp, doc, wq, bq, row(ln1_gain), row(ln1_bias), w_out, row(b_out), row(ln2_gain), row(ln2_bias), wud, bup, row(b_down),
        jnp.asarray(count_table()),
    ), (xp,)


def call_two(*args):
    shapes = (out((128, 768)), out((48, 3072)), out((16, 112, 768), B16), out((16, 48, 384), B16), out((16, 768)))
    scratch = [
        vm((4, 256, 128)), vm((8, 256, 128)), vm((8, 1, 256), F32), vm((6, 128, 512)), vm((512, 128), F32), vm((512, 128), F32),
        vm((8, 128, 256), F32), vm((192, 2048)), vm((4, 256, 128)), vm((4, 256, 128)), vm((4, 3, 256, 128)), vm((6, 3, 128, 128)),
        vm((2, 112, 768)), vm((112, 768)), vm((2, 4, 48, 3456)), vm((4, 48, 3456)), vm((4, 48, 3456)), vm((4, 48, 3456)),
        vm((4, 48, 3456)), vm((256, 1152)), vm((256, 768), F32), vm((128, 768)), vm((128, 768)), vm((5, 16, 768), F32),
        vm((5, 16, 768), F32),
        dma(100), dma(8), dma(2, 4), dma(4), dma(4), dma(1), dma(6), dma(1), dma(16), dma(16), dma(1), dma(5),
    ]
    return pl.pallas_call(
        kernel_two, out_shape=shapes, in_specs=in_vmem(len(args)), out_specs=tuple(in_vmem(len(shapes))), scratch_shapes=scratch,
        compiler_params=pltpu.CompilerParams(collective_id=1, has_side_effects=True, vmem_limit_bytes=LIMIT),
    )(*args)


def fast(*args):
    (qa, ka, va, ns, lse, ot, strow, dpk, grads, dh, lout, sums, supg), (xp,) = front(*args)
    gain, w_qkv = args[3].reshape(1, -1), args[5].reshape(768, 1152)
    gin, wud, wag, woag, vec = call_two(qa, ka, va, ns, lse, ot, strow, dpk, grads, dh, sums, supg, xp, gain, w_qkv)
    heads = jnp.stack([wag[u + 8 * g] for u in UNITS for g in range(2)]).reshape(6, 2, 112, 768)
    w_qkv_grad = heads[:, :, :96].reshape(6, 3, 64, 768).transpose(3, 1, 0, 2).reshape(768, 3, 384).astype(F32)
    bias = heads[:, 0, 96, :192].reshape(6, 3, 64).transpose(1, 0, 2).reshape(3, 384).astype(F32)
    w_out_grad = woag.reshape(768, 384).T.astype(F32)
    return (
        join_rows(lout), join_rows(gin), vec[0], vec[1], w_qkv_grad, jnp.stack([bias[0], bias[2]]), w_out_grad, vec[4], vec[2], vec[3],
        wud[:, :1536], vec[6:10].reshape(3072), wud[:, 1536:].T, vec[5],
    )


def from_behind(value, axis, by):
    length = lax.axis_size(axis)
    pairs = [(i, i + by) for i in range(length) if 0 <= i + by < length]
    return lax.ppermute(value, axis, pairs)


def layer_norm(values, gain, shift):
    mean = jnp.mean(values, axis=-1, keepdims=True)
    centred = values - mean
    spread = jnp.mean(centred * centred, axis=-1, keepdims=True)
    return centred * lax.rsqrt(spread + EPS) * gain + shift


def gelu_tanh(values):
    return jax.nn.gelu(values, approximate=True)


def pick_block(length, limit):
    chosen = 1
    for candidate in range(1, min(length, limit) + 1):
        if length % candidate == 0:
            chosen = candidate
    return chosen


def pair_counts(query_pos, key_pos, head_ids):
    total = None
    for factor, rate in LEVELS:
        width = SEG * factor
        same = query_pos[:, :, None] // width == key_pos[:, None, :] // width
        offset = (head_ids % rate)[:, None]
        pick_query = query_pos % width % rate == offset
        pick_key = key_pos % width % rate == offset
        joint = (same & pick_query[:, :, None] & pick_key[:, None, :]).astype(jnp.float32)
        total = joint if total is None else total + joint
    return total


def block_terms(
    query_blk, query_pos, query_doc, key_blk, key_pos, key_doc, head_ids, nearby, scale
):
    scores = (
        jnp.einsum("qhe,khe->hqk", query_blk, key_blk, preferred_element_type=jnp.float32) * scale
    )
    counts = pair_counts(query_pos, key_pos, head_ids)
    same_segment = query_pos[:, :, None] // SEG == key_pos[:, None, :] // SEG
    keep = same_segment if nearby else jnp.logical_not(same_segment)
    allowed = (
        keep
        & (key_pos[:, None, :] <= query_pos[:, :, None])
        & (query_doc[:, :, None] == key_doc[:, None, :])
    )
    return (scores, counts * allowed.astype(jnp.float32))


def per_device(
    layer_input,
    doc_ids,
    cotangent,
    ln1_gain,
    ln1_bias,
    w_qkv,
    bias_qv,
    w_out,
    b_out,
    ln2_gain,
    ln2_bias,
    w_up,
    b_up,
    w_down,
    b_down,
):
    seq_count = lax.axis_size("seq")
    local_heads = HEADS // lax.axis_size("head")
    local_width = local_heads * HEAD_DIM
    scale = HEAD_DIM ** (-0.5)
    f32 = jnp.float32
    b16 = jnp.bfloat16
    x_float = layer_input.astype(f32)
    norm_one = layer_norm(x_float, ln1_gain, ln1_bias)
    norm_rows, row_doc = (
        lax.all_gather(norm_one.astype(b16), "head", axis=0, tiled=True),
        lax.all_gather(doc_ids, "head", axis=0, tiled=True),
    )
    seq_tokens = norm_rows.shape[0]
    half = seq_tokens // 2
    total_tokens = seq_tokens * seq_count
    total_half = total_tokens // 2
    first_pos = lax.axis_index("seq") * seq_tokens
    last_pos = first_pos + seq_tokens - 1
    local_offsets = jnp.arange(seq_tokens, dtype=jnp.int32)
    query_pos = (first_pos + local_offsets)[None, :]
    query_doc = row_doc[None, :]
    head_ids = lax.axis_index("head") * local_heads + jnp.arange(local_heads, dtype=jnp.int32)
    parity = head_ids % 2
    pick_even = parity == 0

    def compact(rows):
        paired = rows.reshape((half, 2) + rows.shape[1:])
        mask = pick_even.reshape((1, local_heads) + (1,) * (rows.ndim - 2))
        return jnp.where(mask, paired[:, 0], paired[:, 1])

    def expand(rows):
        mask = pick_even.reshape((1, local_heads) + (1,) * (rows.ndim - 2))
        zeros = jnp.zeros_like(rows)
        paired = jnp.stack([jnp.where(mask, rows, zeros), jnp.where(mask, zeros, rows)], axis=1)
        return paired.reshape((seq_tokens,) + rows.shape[1:])

    mixed = jnp.einsum("td,dch->tch", norm_rows, w_qkv, preferred_element_type=f32)
    zero_row = jnp.zeros((1, local_width), f32)
    bias_all = jnp.concatenate([bias_qv[0:1], zero_row, bias_qv[1:2]], axis=0)
    qkv = (mixed + bias_all[None]).astype(b16)
    queries = qkv[:, 0]
    query_heads = queries.reshape(seq_tokens, local_heads, HEAD_DIM)
    key_heads = qkv[:, 1].reshape(seq_tokens, local_heads, HEAD_DIM)
    value_heads = qkv[:, 2].reshape(seq_tokens, local_heads, HEAD_DIM)
    local_keys_c = compact(key_heads)
    local_values_c = compact(value_heads)
    far_keys_all, far_values_all, doc_all = (
        lax.all_gather(local_keys_c, "seq", axis=0, tiled=True),
        lax.all_gather(local_values_c, "seq", axis=0, tiled=True),
        lax.all_gather(row_doc, "seq", axis=0, tiled=True),
    )
    segment_count = SEG // seq_tokens
    own_pair = jnp.stack([key_heads, value_heads], axis=1)
    pair_pieces = [own_pair]
    for step in range(1, segment_count):
        pair_pieces.append(from_behind(own_pair, "seq", step))
    near_pairs = jnp.concatenate(pair_pieces, axis=0)
    near_keys = near_pairs[:, 0]
    near_values = near_pairs[:, 1]
    near_flat = jnp.concatenate(
        [first_pos - step * seq_tokens + local_offsets for step in range(segment_count)]
    )
    near_doc = jnp.take(doc_all, jnp.clip(near_flat, 0, total_tokens - 1))[None, :]
    near_pos = near_flat[None, :]
    far_pos = 2 * jnp.arange(total_half, dtype=jnp.int32)[None, :] + parity[:, None]
    doc_pairs = doc_all.reshape(total_half, 2)
    far_doc = jnp.where(pick_even[:, None], doc_pairs[:, 0][None, :], doc_pairs[:, 1][None, :])
    key_block = pick_block(total_half, block_limit)
    blocks = total_half // key_block
    far_key_blocks = far_keys_all.reshape(blocks, key_block, local_heads, HEAD_DIM)
    far_value_blocks = far_values_all.reshape(blocks, key_block, local_heads, HEAD_DIM)
    far_pos_blocks = far_pos.reshape(local_heads, blocks, key_block).transpose(1, 0, 2)
    far_doc_blocks = far_doc.reshape(local_heads, blocks, key_block).transpose(1, 0, 2)
    far_begin = jnp.arange(blocks, dtype=jnp.int32) * (2 * key_block)

    def merge_stats(current, key_blk, key_pos, key_doc, nearby):
        peak, running = current
        scores, counts = block_terms(
            query_heads, query_pos, query_doc, key_blk, key_pos, key_doc, head_ids, nearby, scale
        )
        live = counts > 0
        new_peak = jnp.maximum(peak, jnp.max(jnp.where(live, scores, NEGATIVE), axis=2))
        terms = jnp.where(live, counts * jnp.exp(scores - new_peak[:, :, None]), 0.0)
        return (new_peak, running * jnp.exp(peak - new_peak) + jnp.sum(terms, axis=2))

    start_state = (
        jnp.full((local_heads, seq_tokens), NEGATIVE, f32),
        jnp.zeros((local_heads, seq_tokens), f32),
    )
    near_state = merge_stats(start_state, near_keys, near_pos, near_doc, True)

    def stats_step(state, item):
        key_blk, pos_blk, doc_blk, begin = item
        return (
            lax.cond(
                begin <= last_pos,
                lambda current: merge_stats(current, key_blk, pos_blk, doc_blk, False),
                lambda current: current,
                state,
            ),
            None,
        )

    (peak_all, running_all), _ = lax.scan(
        stats_step, near_state, (far_key_blocks, far_pos_blocks, far_doc_blocks, far_begin)
    )
    lse = peak_all + jnp.log(running_all)

    def add_output(current, key_blk, value_blk, key_pos, key_doc, nearby):
        scores, counts = block_terms(
            query_heads, query_pos, query_doc, key_blk, key_pos, key_doc, head_ids, nearby, scale
        )
        probs = jnp.where(counts > 0, counts * jnp.exp(scores - lse[:, :, None]), 0.0).astype(b16)
        return current + jnp.einsum("hqk,khe->qhe", probs, value_blk, preferred_element_type=f32)

    zero_heads = jnp.zeros((seq_tokens, local_heads, HEAD_DIM), f32)
    near_output = add_output(zero_heads, near_keys, near_values, near_pos, near_doc, True)

    def output_step(accum, item):
        key_blk, value_blk, pos_blk, doc_blk, begin = item
        return (
            lax.cond(
                begin <= last_pos,
                lambda current: add_output(current, key_blk, value_blk, pos_blk, doc_blk, False),
                lambda current: current,
                accum,
            ),
            None,
        )

    attn_exact, _ = lax.scan(
        output_step,
        near_output,
        (far_key_blocks, far_value_blocks, far_pos_blocks, far_doc_blocks, far_begin),
    )
    attn_low = attn_exact.reshape(seq_tokens, local_width).astype(b16)
    branch = lax.psum_scatter(
        jnp.dot(attn_low, w_out, preferred_element_type=f32).astype(jnp.bfloat16),
        "head",
        scatter_dimension=0,
        tiled=True,
    ).astype(jnp.float32)
    hidden_one = x_float + branch + b_out
    norm_two = layer_norm(hidden_one, ln2_gain, ln2_bias)
    norm_low = norm_two.astype(b16)
    dy_low = (cotangent.astype(f32) * (doc_ids >= 0).astype(f32)[:, None]).astype(b16)
    dy_float = dy_low.astype(f32)
    up_rows, down_rows = (
        lax.all_gather(w_up, "seq", axis=0, tiled=True),
        lax.all_gather(w_down, "seq", axis=1, tiled=True),
    )
    up_full, down_full = (
        lax.all_gather(up_rows, "head", axis=1, tiled=True),
        lax.all_gather(down_rows, "head", axis=0, tiled=True),
    )
    pre_act = jnp.dot(norm_low, up_full, preferred_element_type=f32) + b_up
    act_low = gelu_tanh(pre_act).astype(b16)
    ffn_result = jnp.dot(act_low, down_full, preferred_element_type=f32)
    d_act = jnp.einsum("td,fd->tf", dy_low, down_full, preferred_element_type=f32)
    _, gelu_back = jax.vjp(gelu_tanh, pre_act)
    d_pre = gelu_back(d_act)[0]
    d_pre_low = d_pre.astype(b16)
    bias_up_grad = jnp.sum(d_pre, axis=0)
    up_parts = jnp.einsum("td,tf->df", norm_low, d_pre_low, preferred_element_type=f32)
    down_parts = jnp.einsum("tf,td->fd", act_low, dy_low, preferred_element_type=f32)
    up_grad, down_grad = (
        lax.psum_scatter(
            up_parts.astype(jnp.bfloat16), "head", scatter_dimension=1, tiled=True
        ).astype(jnp.float32),
        lax.psum_scatter(
            down_parts.astype(jnp.bfloat16), "head", scatter_dimension=0, tiled=True
        ).astype(jnp.float32),
    )
    d_norm_two = jnp.einsum("tf,df->td", d_pre_low, up_full, preferred_element_type=f32)
    layer_output = (hidden_one + ffn_result + b_down).astype(b16)
    w_up_grad, w_down_grad = (
        lax.psum_scatter(up_grad, "seq", scatter_dimension=0, tiled=True),
        lax.psum_scatter(down_grad, "seq", scatter_dimension=1, tiled=True),
    )
    _, norm_two_back = jax.vjp(layer_norm, hidden_one, ln2_gain, ln2_bias)
    d_hidden_norm, gain_two_grad, bias_two_grad = norm_two_back(d_norm_two)
    d_hidden = dy_float + d_hidden_norm
    bias_out_grad = jnp.sum(d_hidden, axis=0)
    bias_down_grad = jnp.sum(dy_float, axis=0)
    hidden_rows = lax.all_gather(d_hidden.astype(b16), "head", axis=0, tiled=True)
    w_out_part = jnp.einsum("tc,td->cd", attn_low, hidden_rows, preferred_element_type=f32)
    d_attn = jnp.einsum("td,cd->tc", hidden_rows, w_out, preferred_element_type=f32).astype(b16)
    d_attn_heads = d_attn.reshape(seq_tokens, local_heads, HEAD_DIM)
    delta_rows = jnp.sum(d_attn_heads.astype(f32) * attn_exact, axis=2)
    delta = delta_rows.T

    def score_grads(key_blk, value_blk, key_pos, key_doc, nearby):
        scores, counts = block_terms(
            query_heads, query_pos, query_doc, key_blk, key_pos, key_doc, head_ids, nearby, scale
        )
        exact = jnp.where(counts > 0, counts * jnp.exp(scores - lse[:, :, None]), 0.0)
        d_prob = jnp.einsum("qhe,khe->hqk", d_attn_heads, value_blk, preferred_element_type=f32)
        d_score = (exact * (d_prob - delta[:, :, None])).astype(b16)
        return (exact, d_score)

    exact_near, d_score_near = score_grads(near_keys, near_values, near_pos, near_doc, True)
    d_query_near = jnp.einsum("hqk,khe->qhe", d_score_near, near_keys, preferred_element_type=f32)
    near_key_grad = jnp.einsum(
        "hqk,qhe->khe", d_score_near, query_heads, preferred_element_type=f32
    )
    near_value_grad = jnp.einsum(
        "hqk,qhe->khe", exact_near.astype(b16), d_attn_heads, preferred_element_type=f32
    )
    near_pair_grads = jnp.stack([near_key_grad, near_value_grad], axis=1)
    pair_grad = near_pair_grads[:seq_tokens]
    for step in range(1, segment_count):
        piece = near_pair_grads[step * seq_tokens : (step + 1) * seq_tokens]
        pair_grad = pair_grad + from_behind(piece.astype(jnp.bfloat16), "seq", -step).astype(
            piece.dtype
        )

    def query_grad_step(accum, item):
        key_blk, value_blk, pos_blk, doc_blk, begin = item

        def query_compute(current):
            _, d_score = score_grads(key_blk, value_blk, pos_blk, doc_blk, False)
            return current + jnp.einsum(
                "hqk,khe->qhe", d_score, key_blk, preferred_element_type=f32
            )

        return (lax.cond(begin <= last_pos, query_compute, lambda current: current, accum), None)

    d_query, _ = lax.scan(
        query_grad_step,
        d_query_near,
        (far_key_blocks, far_value_blocks, far_pos_blocks, far_doc_blocks, far_begin),
    )
    d_query = d_query * scale
    stats_rows = jnp.stack([compact(lse.T), compact(delta_rows)], axis=1)
    stats_all = lax.all_gather(stats_rows, "seq", axis=0, tiled=True)
    local_key_pos = first_pos + 2 * jnp.arange(half, dtype=jnp.int32)[None, :] + parity[:, None]
    local_key_doc = compact(jnp.broadcast_to(row_doc[:, None], (seq_tokens, local_heads))).T
    zero_compact = jnp.zeros((half, local_heads, HEAD_DIM), f32)
    query_piece = lax.all_gather(compact(query_heads), "seq", axis=0, tiled=True)
    grad_piece = lax.all_gather(compact(d_attn_heads), "seq", axis=0, tiled=True)
    length = query_piece.shape[0]
    size = pick_block(length, block_limit)
    number = length // size
    pos_piece = 2 * jnp.arange(length, dtype=jnp.int32)[None, :] + parity[:, None]
    items = (
        query_piece.reshape(number, size, local_heads, HEAD_DIM),
        grad_piece.reshape(number, size, local_heads, HEAD_DIM),
        stats_all.reshape(number, size, 2, local_heads),
        pos_piece.reshape(local_heads, number, size).transpose(1, 0, 2),
        far_doc.reshape(local_heads, number, size).transpose(1, 0, 2),
    )

    def one_step(current, item):
        query_blk, grad_blk, stats_blk, pos_blk, doc_blk = item

        def one_compute(pair):
            key_grad, value_grad = pair
            scores, counts = block_terms(
                query_blk,
                pos_blk,
                doc_blk,
                local_keys_c,
                local_key_pos,
                local_key_doc,
                head_ids,
                False,
                scale,
            )
            exact = jnp.where(
                counts > 0, counts * jnp.exp(scores - stats_blk[:, 0].T[:, :, None]), 0.0
            )
            d_prob = jnp.einsum(
                "qhe,khe->hqk", grad_blk, local_values_c, preferred_element_type=f32
            )
            d_score = (exact * (d_prob - stats_blk[:, 1].T[:, :, None])).astype(b16)
            key_grad = key_grad + jnp.einsum(
                "hqk,qhe->khe", d_score, query_blk, preferred_element_type=f32
            )
            value_grad = value_grad + jnp.einsum(
                "hqk,qhe->khe", exact.astype(b16), grad_blk, preferred_element_type=f32
            )
            return (key_grad, value_grad)

        return (
            lax.cond(jnp.max(pos_blk) >= first_pos, one_compute, lambda pair: pair, current),
            None,
        )

    result, _ = lax.scan(one_step, (zero_compact, zero_compact), items)
    far_key_grad, far_value_grad = result
    d_key = (pair_grad[:, 0] + expand(far_key_grad)) * scale
    d_value = pair_grad[:, 1] + expand(far_value_grad)
    d_qkv = jnp.stack(
        [
            d_query.reshape(seq_tokens, local_width),
            d_key.reshape(seq_tokens, local_width),
            d_value.reshape(seq_tokens, local_width),
        ],
        axis=1,
    ).astype(b16)
    d_qkv_float = d_qkv.astype(f32)
    bias_qv_part = jnp.stack(
        [jnp.sum(d_qkv_float[:, 0], axis=0), jnp.sum(d_qkv_float[:, 2], axis=0)], axis=0
    )
    w_qkv_part = jnp.einsum("td,tch->dch", norm_rows, d_qkv, preferred_element_type=f32)
    d_norm_one = lax.psum_scatter(
        jnp.einsum("tch,dch->td", d_qkv, w_qkv, preferred_element_type=f32).astype(jnp.bfloat16),
        "head",
        scatter_dimension=0,
        tiled=True,
    ).astype(jnp.float32)
    _, norm_one_back = jax.vjp(layer_norm, x_float, ln1_gain, ln1_bias)
    d_x_norm, gain_one_grad, bias_one_grad = norm_one_back(d_norm_one)
    grad_input = d_hidden + d_x_norm
    w_qkv_grad, bias_qv_grad, w_out_grad = lax.psum((w_qkv_part, bias_qv_part, w_out_part), "seq")
    summed = lax.psum(
        (
            gain_one_grad,
            bias_one_grad,
            gain_two_grad,
            bias_two_grad,
            bias_out_grad,
            bias_up_grad,
            bias_down_grad,
        ),
        ("seq", "head"),
    )
    return (
        layer_output,
        grad_input,
        summed[0],
        summed[1],
        w_qkv_grad,
        bias_qv_grad,
        w_out_grad,
        summed[4],
        summed[2],
        summed[3],
        w_up_grad,
        summed[5],
        w_down_grad,
        summed[6],
    )


def solution(mesh):
    in_specs = (
        P(("seq", "head"), None),
        P(("seq", "head")),
        P(("seq", "head"), None),
        P(),
        P(),
        P(None, None, "head"),
        P(None, "head"),
        P("head", None),
        P(),
        P(),
        P(),
        P("seq", "head"),
        P(),
        P("head", "seq"),
        P(),
    )
    out_specs = (
        P(("seq", "head"), None),
        P(("seq", "head"), None),
        P(),
        P(),
        P(None, None, "head"),
        P(None, "head"),
        P("head", None),
        P(),
        P(),
        P(),
        P("seq", "head"),
        P(),
        P("head", "seq"),
        P(),
    )
    small = mesh.shape["seq"] == 16 and mesh.shape["head"] == 2
    return jax.shard_map(
        fast if small else per_device, mesh=mesh, in_specs=in_specs, out_specs=out_specs, check_vma=False
    )
```

```python
import functools

import jax
import jax.numpy as jnp
import ml_dtypes
import numpy as np
from jax import lax
from jax.experimental import pallas as pl
from jax.experimental.pallas import tpu as pltpu
from jax.sharding import PartitionSpec as P

HEADS = 12
HEAD_DIM = 64
SEG = 2048


LEVELS = ((1, 1), (2, 2), (4, 4), (8, 6), (16, 12))
EPS = 1e-05
NEGATIVE = -1e30
block_limit = 2048


MESH = pl.DeviceIdType.MESH
VMEM = pltpu.VMEM
LIMIT = 60 << 20
F32 = jnp.float32
B16 = jnp.bfloat16


def dot(a, b):
    return jnp.dot(a, b, preferred_element_type=F32)


def dot_nt(a, b):
    return lax.dot_general(a, b, (((1,), (1,)), ((), ())), preferred_element_type=F32)


def sid(z, x, c):
    return z * 4 + x * 2 + c


class Place:
    def __init__(self):
        s = lax.axis_index("seq")
        self.s, self.y = s, lax.axis_index("head")
        self.z, self.x, self.c = s // 4, (s // 2) % 2, s % 2
        self.seg, self.zl = self.z // 2, self.z % 2
        self.u = s % 8
        self.b = self.u * 2 + self.y
        self.unit = jnp.logical_and(self.u != 3, self.u != 5)
        self.hl = self.u - self.u // 4 - self.u // 6
        self.head = self.y * 6 + self.hl
        self.parity = self.head % 2
        z, x, c, y = self.z, self.x, self.c, self.y
        self.zf = z + 1 - 2 * self.zl
        self.nx, self.ny = (sid(z, 1 - x, c), y), (s, 1 - y)
        self.nz, self.nc = (sid(self.zf, x, c), y), (sid(z, x, 1 - c), y)
        self.far = (sid((z + 2) % 4, x, c), y)
        self.fb = {"x": 4 * (1 - 2 * x), "y": 1 - 2 * y, "z": 8 * (1 - 2 * self.zl), "c": 2 * (1 - 2 * c)}

    def cube(self):
        z, x, c, y = self.z, self.x, self.c, self.y
        for k in range(1, 16):
            zz = self.zf if k & 8 else z
            xx = 1 - x if k & 4 else x
            cc = 1 - c if k & 2 else c
            yy = 1 - y if k & 1 else y
            yield (sid(zz, xx, cc), yy)

    def greet(self):
        others = list(self.cube())
        others += [(sid((self.z + 2) % 4, self.x, self.c), self.y), (sid((self.zf + 2) % 4, self.x, self.c), self.y)]
        barrier = pltpu.get_barrier_semaphore()
        for dev in others:
            pl.semaphore_signal(barrier, inc=1, device_id=dev, device_id_type=MESH)
        self.greeted = len(others)

    def meet(self):
        pl.semaphore_wait(pltpu.get_barrier_semaphore(), self.greeted)


class Mail:
    def __init__(self, sems):
        self.sems, self.used, self.sent = sems, 0, []

    def send(self, src, dst, rsem, dev, cond=None):
        k = self.used
        self.used += 1

        def make():
            return pltpu.make_async_remote_copy(
                src_ref=src, dst_ref=dst, send_sem=self.sems.at[k], recv_sem=rsem, device_id=dev, device_id_type=MESH
            )

        if cond is None:
            make().start()
        else:
            pl.when(cond)(lambda: make().start())
        self.sent.append((cond, make))

    def got(self, dst, rsem, dev):
        pltpu.make_async_remote_copy(
            src_ref=dst, dst_ref=dst, send_sem=self.sems.at[0], recv_sem=rsem, device_id=dev, device_id_type=MESH
        ).wait_recv()

    def close(self):
        for cond, make in self.sent:
            if cond is None:
                make().wait_send()
            else:
                pl.when(cond)(lambda make=make: make().wait_send())
        self.sent = []


def both(*terms):
    out = terms[0]
    for term in terms[1:]:
        out = jnp.logical_and(out, term)
    return out


def iota(shape, dim):
    return lax.broadcasted_iota(jnp.int32, shape, dim)


def norm_parts(v):
    mean = jnp.mean(v, axis=-1, keepdims=True)
    cen = v - mean
    inv = lax.rsqrt(jnp.mean(cen * cen, axis=-1, keepdims=True) + EPS)
    return cen * inv, inv


def norm_grad(z, inv, e):
    return (e - jnp.mean(e, axis=-1, keepdims=True) - z * jnp.mean(e * z, axis=-1, keepdims=True)) * inv


def pick_type(pos, head, rows):
    v = pos - head + 24.0
    m = v - 12.0 * jnp.floor((v + 0.5) * (1.0 / 12.0))
    out = jnp.where(m == 0.0, rows[4], rows[0])
    out = jnp.where(m == 6.0, rows[3], out)
    out = jnp.where(jnp.logical_or(m == 4.0, m == 8.0), rows[2], out)
    return jnp.where(jnp.logical_or(m == 2.0, m == 10.0), rows[1], out)


def halves(e, o):
    low = iota(e.shape, 1) < 64
    return jnp.where(low, e, pltpu.roll(o, 64, 1)), jnp.where(low, pltpu.roll(e, 64, 1), o)


UNITS = (0, 1, 2, 4, 6, 7)


class Spread:
    def __init__(self, p, mail, ref, sems, some):
        self.p, self.mail, self.ref, self.sems, self.some = p, mail, ref, sems, some

    def has(self, zz, xx, cc):
        return jnp.logical_or(cc == 0, zz % 2 == xx) if self.some else None

    def go(self, s, dev, cond):
        self.mail.send(self.ref.at[s], self.ref.at[s], self.sems.at[s], dev, cond)

    def take(self, s, cond):
        def wait():
            self.mail.got(self.ref.at[s], self.sems.at[s], self.p.nx)

        if cond is None:
            wait()
        else:
            pl.when(cond)(wait)

    def first(self):
        p = self.p
        has = self.has(p.z, p.x, p.c)
        for k in range(1, 4):
            self.go(p.s, (sid((p.z + k) % 4, p.x, p.c), p.y), has)
        self.go(p.s, p.nx, has)
        self.go(p.s, p.nc, has)

    def second(self):
        p = self.p
        for k in range(1, 4):
            zz = (p.z + k) % 4
            s, has = sid(zz, p.x, p.c), self.has(zz, p.x, p.c)
            self.take(s, has)
            self.go(s, p.nx, has)
            self.go(s, p.nc, has)

    def third(self):
        p = self.p
        for zz in range(4):
            s, has = sid(zz, 1 - p.x, p.c), self.has(zz, 1 - p.x, p.c)
            self.take(s, has)
            self.go(s, p.nc, has)

    def last(self):
        p = self.p
        for zz in range(4):
            for xx in range(2):
                self.take(sid(zz, xx, 1 - p.c), self.has(zz, xx, 1 - p.c))


class Reduce:
    def __init__(self, p, mail, src, gc, gxs, gxr, gzs, gzr, rc, rx, rz):
        self.__dict__.update(locals())

    def rows(self, zz, xx, cc):
        return pl.ds(pl.multiple_of(sid(zz, xx, cc) * 48, 16), 48)

    def cores(self):
        p = self.p
        for xq in range(2):
            xx = 1 - p.x if xq == 0 else p.x
            for k in (1, 2, 3, 0):
                zz = (p.z + k) % 4
                self.mail.send(self.src.at[self.rows(zz, xx, 1 - p.c)], self.gc.at[xq, zz], self.rc.at[xq, zz], p.nc)

    def over_x(self):
        p = self.p
        for k in (1, 2, 3, 0):
            zz = (p.z + k) % 4
            self.mail.got(self.gc.at[0, zz], self.rc.at[0, zz], p.nc)
            own = self.src[self.rows(zz, 1 - p.x, p.c)].astype(F32)
            self.gxs[zz] = (own + self.gc[0, zz].astype(F32)).astype(B16)
            self.mail.send(self.gxs.at[zz], self.gxr.at[zz], self.rx.at[zz], p.nx)

    def column(self, zz):
        p = self.p
        self.mail.got(self.gc.at[1, zz], self.rc.at[1, zz], p.nc)
        self.mail.got(self.gxr.at[zz], self.rx.at[zz], p.nx)
        return self.src[self.rows(zz, p.x, p.c)].astype(F32) + self.gc[1, zz].astype(F32) + self.gxr[zz].astype(F32)

    def over_z(self, k):
        p = self.p
        zz = (p.z + k) % 4
        self.gzs[k] = self.column(zz).astype(B16)
        self.mail.send(self.gzs.at[k], self.gzr.at[p.z], self.rz.at[p.z], (sid(zz, p.x, p.c), p.y))

    def result(self):
        p = self.p
        total = self.column(p.z)
        for k in range(1, 4):
            zz = (p.z + k) % 4
            self.mail.got(self.gzr.at[zz], self.rz.at[zz], p.nx)
            total = total + self.gzr[zz].astype(F32)
        return total


class Slots:
    def __init__(self, ref, base):
        self.ref, self.base = ref, base

    def span(self, i):
        return pl.ds(pl.multiple_of(self.base + i * 48, 16), 48)

    @property
    def at(self):
        return self

    def __getitem__(self, i):
        return self.ref.at[self.span(i)]

    def __setitem__(self, i, value):
        self.ref[self.span(i)] = value


class Total:
    def __init__(self, p, mail, buf, rec, sems):
        self.mail, self.buf, self.rec, self.sems = mail, buf, rec, sems
        self.peers = (p.nc, p.nx, p.nz, p.far, p.ny)

    def start(self, i):
        self.mail.send(self.buf.at[i], self.rec.at[i], self.sems.at[i], self.peers[i])

    def finish(self, i):
        self.mail.got(self.rec.at[i], self.sems.at[i], self.peers[i])
        new = self.buf[i] + self.rec[i]
        if i < 4:
            self.buf[i + 1] = new
        return new


def mixed(shape, dim_to, dim_from):
    r, i = iota(shape, dim_to), iota(shape, dim_from)
    return jnp.where(i == 2 * (r & 63) + (r >> 6), 1.0, 0.0).astype(B16)


def kernel(
    x_ref, doc_ref, cot_ref, g1_ref, b1_ref, wq_ref, bqv_ref, wo_own, bo_ref, g2_ref, b2_ref, wup_ref, bup_ref, wdn_ref, bd_ref, tab_ref,
    lout, gin, o_g1, o_b1, o_wq, o_bqv, o_wo, o_bo, o_g2, o_b2, o_up, o_bup, o_dn, o_bd,
    qa, ka, va, ns, lse, ot, dpk, grads, gwo, dh_s, wqh, bqh, buph, msc, asc,
    xs, docs, wb, wo, dyp, orecv, osend, kvs, kvf, attn, vt, hid, n2s, dys, acts, dpre, facc, dacc, ys, yr, fs, fr, fo,
    dor, doa, delta, kt, dka, dva, dqt, dtt, dfs, dfr, packs, dqr, wms, wmr, gc, gxr, gzr, hc, hxs, hxr, hzs, hzr, dall, dns, dnr,
    vb1, vr1, vb2, vr2, wag, woag,
    ss, rsx, rsc, rsd, rsw, rso, rsf, rsy, rdo, rgc, rgx, rgz, rhc, rhx, rhz, rdf, rdq, rwm, rag, rwo, rdn, rv1, rv2,
):
    p = Place()
    mail = Mail(ss)
    seg, x, y, z, c, b = p.seg, p.x, p.y, p.z, p.c, p.b
    first, second = both(p.unit, seg == 0), both(p.unit, seg == 1)
    row = lambda ref: ref[...].reshape(1, -1)
    p.greet()

    mix = mixed((128, 128), 0, 1)
    xs[b] = dot(mix, x_ref[...]).astype(B16)
    doc_row = doc_ref[...].astype(F32).reshape(1, 128)
    turn = jnp.where(iota((128, 128), 0) == 2 * (iota((128, 128), 1) & 63), 1.0, 0.0).astype(B16)
    turn_odd = jnp.where(iota((128, 128), 0) == 2 * (iota((128, 128), 1) & 63) + 1, 1.0, 0.0).astype(B16)
    doc8 = jnp.broadcast_to(doc_row, (8, 128)).astype(B16)
    docs[b] = jnp.where(iota((8, 128), 0) == 0, dot(doc8, turn), dot(doc8, turn_odd))
    p.meet()

    dims = ("x", "y", "z")
    nbr = {"x": p.nx, "y": p.ny, "z": p.nz}
    part = [pl.ds(k * 256, 256) for k in range(3)]
    order = [[dims[(k + j) % 3] for j in range(3)] for k in range(3)]

    def pass_on(k, blk, dev):
        ref = xs.at[blk, :, part[k]]
        mail.send(ref, ref, rsx.at[k, blk], dev)

    def to_core(k, blk):
        ref = xs.at[blk, :, part[k]]
        mail.send(ref, ref, rsc.at[k, blk], p.nc)

    for j in range(3):
        for k in range(3):
            pass_on(k, b, nbr[order[k][j]])
    for k in range(3):
        to_core(k, b)
    for src in (0, 14, 15):
        for dev in p.cube():
            mail.send(docs.at[src], docs.at[src], rsd.at[src], dev, cond=b == src)

    pair_cols = pl.ds(pl.multiple_of(p.hl // 2 * 128, 128), 128)
    for odd in range(2):

        @pl.when(p.hl % 2 == odd)
        def _(odd=odd):
            for k in range(3):
                w = wq_ref[k, :, pair_cols].astype(F32)
                w = pltpu.roll(w, 64, 1) if odd else w
                wqh[:, k * 128 : k * 128 + 128] = jnp.where(iota((768, 128), 1) < 64, w, 0.0).astype(B16)
            v = jnp.concatenate([bqv_ref[:, pair_cols], jnp.zeros((6, 128), F32)], axis=0)
            v = pltpu.roll(v, 64, 1) if odd else v
            lane = iota((1, 128), 1)
            bqh[:, 0:128] = jnp.where(lane < 64, v[0:1], 0.0)
            bqh[:, 128:256] = jnp.zeros((1, 128), F32)
            bqh[:, 256:384] = jnp.where(lane < 64, v[1:2], jnp.where(lane == 64, 1.0, 0.0))

    head = p.head.astype(F32)
    for t in range(4):
        rr = iota((512, 128), 0)
        pos = (seg * SEG + t * 512 + 2 * (rr & 255) + (rr >> 8)).astype(F32)
        qa[t] = pick_type(pos, head, [tab_ref[i : i + 1] for i in range(5)]).astype(B16)
        ka[t + 2] = pick_type(pos, head, [tab_ref[8 + i : 9 + i] for i in range(5)]).astype(B16)

    real = jnp.broadcast_to(doc_row, (128, 128)).T >= 0.0
    for k in range(6):
        cols = slice(k * 128, k * 128 + 128)
        kept = jnp.where(real, cot_ref[:, cols].astype(F32), 0.0).astype(B16)
        dyp[y, :, cols] = dot(mix, kept).astype(B16)
    for half in range(2):

        @pl.when(y == half)
        def _(half=half):
            buph[...] = bup_ref[half * 1536 : half * 1536 + 1536].reshape(1, 1536)

    wrow = pl.ds(pl.multiple_of(p.s * 48, 16), 48)
    wb[wrow, 0:1536] = wup_ref[...]
    wb[wrow, 1536:3072] = wdn_ref[...]
    wo[y] = wo_own[...]

    def qkv(i):
        rows = xs[pl.ds(2 * i, 2)].reshape(256, 768).astype(F32)
        zz, _inv = norm_parts(rows)
        n1 = (zz * row(g1_ref) + row(b1_ref)).astype(B16)
        m = (dot(n1, wqh[...]) + bqh[...]).astype(B16)
        t = i // 2
        for yy in range(2):
            for par in range(2):
                at = slice(yy * 128 + par * 64, yy * 128 + par * 64 + 64)
                to = pl.ds(pl.multiple_of(par * 256 + (i % 2) * 128 + yy * 64, 64), 64)
                qa[t, to] = m[at, :128] * B16(0.125) + qa[t, to]
                ka[t + 2, to] = m[at, 128:256] + ka[t + 2, to]
                va[t + 2, to] = m[at, 256:]
                ns[t, to] = n1[at]

    def seen(k, blk):
        mail.got(xs.at[blk, :, part[k]], rsx.at[k, blk], p.nx)
        to_core(k, blk)

    def from_core(blk):
        for k in range(3):
            mail.got(xs.at[blk, :, part[k]], rsc.at[k, blk], p.nc)

    fx, fy, fz, fc = p.fb["x"], p.fb["y"], p.fb["z"], p.fb["c"]

    def qkv_of(*flips):
        at = (b + sum(flips)) // 2
        pl.when(p.unit)(lambda: qkv(at))

    for k in range(3):
        f = [p.fb[d] for d in order[k]]
        seen(k, b + f[0])
        pass_on(k, b + f[0], nbr[order[k][1]])
        pass_on(k, b + f[0], nbr[order[k][2]])
    for k in range(3):
        f = [p.fb[d] for d in order[k]]
        for blk in (b + f[1], b + f[1] + f[0]):
            seen(k, blk)
            pass_on(k, blk, nbr[order[k][2]])

    def rows_of(s):
        return wb.at[pl.ds(pl.multiple_of(s * 48, 16), 48), :]

    def give(s, dev, cond=None):
        mail.send(rows_of(s), rows_of(s), rsw.at[s], dev, cond)

    give(p.s, (sid((z + 1) % 4, x, c), y), z <= 2)
    give(p.s, (sid((z + 3) % 4, x, c), y), z >= 1)
    give(p.s, p.nx)
    give(p.s, p.nc)
    mail.send(wo.at[y], wo.at[y], rsy.at[0], p.ny)
    mail.send(dyp.at[y], dyp.at[y], rsy.at[1], p.ny)

    def chain(d):
        up, dn = (z - d + 4) % 4, (z + d) % 4
        has_up, has_dn = z >= d, z <= 3 - d
        su, sd = sid(up, x, c), sid(dn, x, c)
        pl.when(has_up)(lambda: mail.got(rows_of(su), rsw.at[su], p.nx))
        if d < 3:
            give(su, (sid((z + 1) % 4, x, c), y), both(has_up, z <= 2))
        give(su, p.nx, has_up)
        give(su, p.nc, has_up)
        pl.when(has_dn)(lambda: mail.got(rows_of(sd), rsw.at[sd], p.nx))
        if d < 3:
            give(sd, (sid((z + 3) % 4, x, c), y), both(has_dn, z >= 1))
        give(sd, p.nx, has_dn)
        give(sd, p.nc, has_dn)

    for k in range(3):
        f = [p.fb[d] for d in order[k]]
        for blk in (b + f[2], b + f[2] + f[0], b + f[2] + f[1], b + f[2] + f[1] + f[0]):
            seen(k, blk)
    for flips in ((), (fx,), (fz,), (fx, fz)):
        qkv_of(*flips)
    for flips in ((), (fx,), (fz,), (fx, fz)):
        from_core(b + fc + sum(flips))
        from_core(b + fc + sum(flips) + fy)
        qkv_of(fc, *flips)
    for src in (0, 14, 15):
        pl.when(b != src)(lambda src=src: mail.got(docs.at[src], rsd.at[src], p.nx))

    lowlane = iota((256, 128), 1) < 64
    farrows = pl.ds(pl.multiple_of(p.parity * 256, 256), 256)

    @pl.when(first)
    def _():
        for t in range(4):
            kk = ka[t + 2, farrows].astype(F32)
            vv = va[t + 2, farrows].astype(F32)
            kvs[t] = jnp.where(lowlane, kk, pltpu.roll(vv, 64, 1)).astype(B16)

    mail.send(kvs, kvf, rsf.at[0], p.far, first)
    mail.send(docs.at[0], docs.at[16], rsf.at[1], p.far, first)

    def codes(src, par):
        r = docs[src, par : par + 1]
        return jnp.broadcast_to(jnp.where(r < 0.0, 4.0, r), (128, 128)).T[0:64]

    def mark(ref, at, code, query):
        lane = iota((64, 128), 1)
        hit = (lane - 96).astype(F32) == code
        if query:
            feat = jnp.where(hit, 0.0, jnp.where(lane < 101, NEGATIVE, 0.0))
        else:
            feat = jnp.where(hit, 1.0, 0.0)
        ref[at] = jnp.where(lane >= 96, feat, ref[at].astype(F32)).astype(B16)

    @pl.when(first)
    def _():
        for par in range(2):
            code = codes(0, par)
            at = slice(par * 256, par * 256 + 64)
            mark(qa.at[0], at, code, True)
            mark(ka.at[2], at, code, False)

    @pl.when(second)
    def _():
        for par in range(2):
            for yy in range(2):
                code = codes(14 + yy, par)
                at = slice(par * 256 + 128 + yy * 64, par * 256 + 192 + yy * 64)
                mark(qa.at[3], at, code, True)
                mark(ka.at[5], at, code, False)

    @pl.when(p.unit)
    def _():
        for t in range(4):
            vt[t + 2] = va[t + 2].astype(F32).T.astype(B16)

    rr, ll = iota((512, 512), 0), iota((512, 512), 1)
    causal = lambda st: jnp.where(2 * (rr & 255) + (rr >> 8) <= 2 * (ll & 255) + (ll >> 8), st, NEGATIVE)

    def near_attention(t):
        q = qa[t]

        def update(cc, carry, st):
            m, acc = carry
            m_new = jnp.maximum(m, jnp.max(st, axis=0, keepdims=True))
            pr = jnp.exp(st - m_new).astype(B16)
            return m_new, acc * jnp.exp(m - m_new) + dot(vt[cc], pr)

        state = (jnp.full((1, 512), NEGATIVE, F32), jnp.zeros((128, 512), F32))
        if t:
            state = lax.fori_loop(2, t + 2, lambda cc, s: update(cc, s, dot_nt(ka[cc], q)), state)
        msc[t], asc[t] = update(t + 2, state, causal(dot_nt(ka[t + 2], q)))

    def far_ready():
        mail.got(kvf, rsf.at[0], p.far)
        mail.got(docs.at[16], rsf.at[1], p.far)
        for t in range(4):
            rows = pl.ds((t % 2) * 256, 256)
            fpos = ((t * 256 + iota((256, 128), 0)) * 2 + p.parity).astype(F32)
            feat = pick_type(fpos, head, [tab_ref[16 + i : 17 + i] for i in range(5)])
            kv = kvf[t].astype(F32)
            ka[t // 2, rows] = jnp.where(lowlane, kv, feat).astype(B16)
            one = jnp.where(iota((256, 128), 1) == 64, 1.0, 0.0)
            va[t // 2, rows] = jnp.where(lowlane, pltpu.roll(kv, 64, 1), one).astype(B16)
        even, odd = codes(16, 0), codes(16, 1)
        mark(ka.at[0], slice(0, 64), even + p.parity.astype(F32) * (odd - even), False)
        for h in range(2):
            vt[h] = va[h].astype(F32).T.astype(B16)

    farcols = pl.ds(pl.multiple_of(p.parity * 256, 256), 256)

    def far_attention(t):
        q = qa[t, farcols]
        m = msc[t, :, farcols]
        s0, s1 = dot_nt(ka[0], q), dot_nt(ka[1], q)
        m_new = jnp.maximum(m, jnp.maximum(jnp.max(s0, axis=0, keepdims=True), jnp.max(s1, axis=0, keepdims=True)))
        acc = asc[t, :, farcols] * jnp.exp(m - m_new)
        acc = acc + dot(vt[0], jnp.exp(s0 - m_new).astype(B16))
        acc = acc + dot(vt[1], jnp.exp(s1 - m_new).astype(B16))
        msc[t, :, farcols] = m_new
        asc[t, :, farcols] = acc

    def conclude(t):
        acc = asc[t]
        total = acc[64:65]
        o = acc[:64] / total
        lse[t] = msc[t] + jnp.log(total)
        ot[t] = jnp.concatenate([o[:, :256], o[:, 256:]], axis=0)
        osend[t] = ot[t].T.astype(B16)

    def deliver(t, who):
        for cc in range(2):
            for yy in range(2):
                own = both(p.u == t * 2 + cc, y == yy)
                src = osend.at[t, cc * 128 : cc * 128 + 128]
                dev = (sid(seg * 2 + t // 2, t % 2, cc), yy)
                mail.send(src, orecv.at[p.head], rso.at[p.head], dev, both(who, jnp.logical_not(own)))

                @pl.when(both(who, own))
                def _(cc=cc):
                    orecv[p.head] = osend[t, cc * 128 : cc * 128 + 128]

    for t in range(4):
        pl.when(p.unit)(functools.partial(near_attention, t))
        pl.when(first)(functools.partial(conclude, t))
        deliver(t, first)
        if t == 1:
            chain(1)
        if t == 3:
            chain(2)
    pl.when(second)(far_ready)
    for t in range(4):
        pl.when(second)(functools.partial(far_attention, t))
        pl.when(second)(functools.partial(conclude, t))
        deliver(t, second)
    chain(3)
    for zq in range(4):
        s = sid(zq, 1 - x, c)
        mail.got(rows_of(s), rsw.at[s], p.nx)
        give(s, p.nc)

    for hh in range(12):
        mine = both(p.unit, p.head == hh)
        pl.when(jnp.logical_not(mine))(lambda hh=hh: mail.got(orecv.at[hh], rso.at[hh], p.nx))
    for a in range(6):
        e, o = halves(orecv[2 * a].astype(F32), orecv[2 * a + 1].astype(F32))
        attn[0:128, a * 128 : a * 128 + 128] = e.astype(B16)
        attn[128:256, a * 128 : a * 128 + 128] = o.astype(B16)
    mail.got(wo.at[1 - y], rsy.at[0], p.ny)
    mail.got(dyp.at[1 - y], rsy.at[1], p.ny)
    pair = pl.multiple_of(p.u * 2, 2)
    for par in range(2):
        for yy in range(2):
            at = pl.ds(par * 128 + yy * 64, 64)
            hid[at] = xs[pair + yy, par * 64 : par * 64 + 64].astype(F32)
            dys[at] = dyp[yy, par * 64 : par * 64 + 64]
    hid[...] = hid[...] + dot(attn[...], wo[...].reshape(768, 768)) + row(bo_ref)
    z2, _inv = norm_parts(hid[...])
    n2s[...] = (z2 * row(g2_ref) + row(b2_ref)).astype(B16)
    for i in range(8):
        s = sid(i // 2, i % 2, 1 - c)
        mail.got(rows_of(s), rsw.at[s], p.nc)

    facc[...] = jnp.zeros_like(facc)
    dacc[...] = jnp.zeros_like(dacc)
    k0 = 0.7978845608028654
    vb1[0] = jnp.zeros((8, 768), F32)

    def ffn_step(i, _):
        cols = pl.ds(pl.multiple_of(i * 256, 256), 256)
        dcols = pl.ds(pl.multiple_of(1536 + i * 256, 256), 256)
        up, dn = wb[:, cols], wb[:, dcols]
        pre = dot(n2s[...], up) + buph[:, cols]
        sq = pre * pre
        th = jnp.tanh(k0 * pre * (1.0 + 0.044715 * sq))
        half = 0.5 * (1.0 + th)
        act = (pre * half).astype(B16)
        slope = half + 0.5 * pre * (1.0 - th * th) * (k0 * (1.0 + 3.0 * 0.044715 * sq))
        dp = dot(dys[...], dn) * slope
        buph[:, cols] = jnp.sum(dp, axis=0, keepdims=True)
        dpl = dp.astype(B16)
        acts[:, cols] = act
        dpre[:, cols] = dpl
        facc[...] += dot_nt(act, dn)
        dacc[...] += dot_nt(dpl, up)
        return 0

    lax.fori_loop(0, 6, ffn_step, 0)
    ys[...] = dacc[...].astype(B16)
    mail.send(ys, yr, rsy.at[2], p.ny)
    for par in range(2):
        fo[par * 64 : par * 64 + 64] = facc[pl.ds(pl.multiple_of(par * 128 + y * 64, 64), 64)]
        fs[par * 64 : par * 64 + 64] = facc[pl.ds(pl.multiple_of(par * 128 + (1 - y) * 64, 64), 64)].astype(B16)
    mail.send(fs, fr, rsy.at[3], p.ny)

    n2t = n2s[...].astype(F32).T.astype(B16)
    dyt = dys[...].astype(F32).T.astype(B16)

    def grad_step(i, _):
        cols = pl.ds(pl.multiple_of(i * 256, 256), 256)
        dcols = pl.ds(pl.multiple_of(1536 + i * 256, 256), 256)
        grads[:, cols] = dot(n2t, dpre[:, cols]).astype(B16)
        grads[:, dcols] = dot(dyt, acts[:, cols]).astype(B16)
        return 0

    lax.fori_loop(0, 6, grad_step, 0)
    mail.close()
    ffn_sum = Reduce(p, mail, grads, gc, Slots(wb, 0), gxr, Slots(wb, 192), gzr, rgc, rgx, rgz)
    out_sum = Reduce(p, mail, gwo, hc, hxs, hxr, hzs, hzr, rhc, rhx, rhz)
    ffn_sum.cores()
    mail.got(yr, rsy.at[2], p.ny)
    dn2 = ys[...].astype(F32) + yr[...].astype(F32)
    z2, inv2 = norm_parts(hid[...])
    dh = dys[...].astype(F32) + norm_grad(z2, inv2, dn2 * row(g2_ref))
    facc[...] = dh
    dacc[...] = dn2 * z2
    da_ = dot_nt(dh.astype(B16), wo[y])
    for a in range(3):
        e, o = halves(da_[0:128, a * 128 : a * 128 + 128], da_[128:256, a * 128 : a * 128 + 128])
        dpk[2 * a] = e.astype(B16)
        dpk[2 * a + 1] = o.astype(B16)

    mine_t = p.zl * 2 + x
    crow = pl.ds(pl.multiple_of(c * 128, 128), 128)
    for h, u in enumerate(UNITS):
        mail.send(dpk.at[h], dor.at[mine_t, crow], rdo.at[p.u], (seg * 8 + u, y), p.u != u)

        @pl.when(p.u == u)
        def _(h=h):
            dor[mine_t, crow] = dpk[h]

    ffn_sum.over_x()
    gwo[...] = dot(dh.T.astype(B16), attn[:, pl.ds(pl.multiple_of(y * 384, 128), 384)]).astype(B16)
    out_sum.cores()
    mail.got(fr, rsy.at[3], p.ny)
    sums = [jnp.zeros((1, 768), F32)] * 4
    for par in range(2):
        at = pl.ds(pl.multiple_of(par * 128 + y * 64, 64), 64)
        to = slice(par * 64, par * 64 + 64)
        dh_s[to] = facc[at]
        own = (dacc[at], ys[at].astype(F32) + yr[at].astype(F32), facc[at], dys[at].astype(F32))
        sums = [total + jnp.sum(v, axis=0, keepdims=True) for total, v in zip(sums, own)]
        fo[to] = hid[at] + fo[to] + fr[to].astype(F32) + row(bd_ref)
    back = mixed((128, 128), 1, 0)
    lout[...] = dot(back, fo[...].astype(B16)).astype(B16)
    for i in range(4):
        vb1[0, i : i + 1] = sums[i]
    for half in range(2):

        @pl.when(y == half)
        def _(half=half):
            for k in range(2):
                vb1[0, 4 + 2 * half + k : 5 + 2 * half + k] = buph[:, k * 768 : k * 768 + 768]

    early = Total(p, mail, vb1, vr1, rv1)
    late = Total(p, mail, vb2, vr2, rv2)
    early.start(0)

    def prepare():
        for i in range(8):
            pl.when(p.u != i)(lambda i=i: mail.got(dor.at[i // 2, (i % 2) * 128 : (i % 2) * 128 + 128], rdo.at[i], p.nx))
        low = iota((256, 128), 1) < 64
        for t in range(4):
            d = dor[t].astype(F32)
            doa[t, 0:256] = jnp.where(low, d, 0.0).astype(B16)
            doa[t, 256:512] = jnp.where(low, pltpu.roll(d, 64, 1), 0.0).astype(B16)
            prod = d.T * ot[t]
            delta[t, :, 0:256] = jnp.sum(prod[:64], axis=0, keepdims=True)
            delta[t, :, 256:512] = jnp.sum(prod[64:], axis=0, keepdims=True)
            kt[t + 2] = ka[t + 2].astype(F32).T.astype(B16)
        dqt[...] = jnp.zeros_like(dqt)

    pl.when(p.unit)(prepare)

    def score_grads(cc, q, do, st, lse_row, delta_row):
        pr = jnp.exp(st - lse_row)
        ds = (pr * (dot_nt(va[cc], do) - delta_row)).astype(B16)
        dva[...] += dot(pr.astype(B16), do)
        dka[...] += dot(ds, q)
        return dot(kt[cc], ds)

    def clear():
        dka[...] = jnp.zeros_like(dka)
        dva[...] = jnp.zeros_like(dva)

    @pl.when(second)
    def _():
        for h in range(2):
            kt[h] = ka[h].astype(F32).T.astype(B16)

        def chunk(cc, _):
            clear()

            def step(t, _):
                q, do = qa[t, farcols], doa[t, farcols]
                dqt[t, :, farcols] += score_grads(cc, q, do, dot_nt(ka[cc], q), lse[t, :, farcols], delta[t, :, farcols])
                return 0

            lax.fori_loop(0, 4, step, 0)
            low = iota((512, 128), 1) < 64
            pack = jnp.where(low, dka[...], pltpu.roll(dva[...], 64, 1)).astype(B16)
            dfs[2 * cc] = pack[:256]
            dfs[2 * cc + 1] = pack[256:]
            return 0

        lax.fori_loop(0, 2, chunk, 0)

    mail.send(dfs, dfr, rdf.at[0], p.far, second)

    def near(t):
        clear()
        q, do = qa[t], doa[t]
        dqt[t] += score_grads(t + 2, q, do, causal(dot_nt(ka[t + 2], q)), lse[t], delta[t])
        if t < 3:

            def step(tq, _):
                q, do = qa[tq], doa[tq]
                dqt[tq] += score_grads(t + 2, q, do, dot_nt(ka[t + 2], q), lse[tq], delta[tq])
                return 0

            lax.fori_loop(t + 1, 4, step, 0)
        dtt[64:128, t * 512 : t * 512 + 512] = dka[...].T[:64].astype(B16)
        dtt[128:192, t * 512 : t * 512 + 512] = dva[...].T[:64].astype(B16)

    def add_far(t):
        rows = dfr[t].astype(F32).T
        at = pl.ds(pl.multiple_of(t * 512 + p.parity * 256, 256), 256)
        dtt[64:128, at] = (dtt[64:128, at].astype(F32) + rows[:64]).astype(B16)
        dtt[128:192, at] = (dtt[128:192, at].astype(F32) + rows[64:]).astype(B16)

    out_sum.over_x()
    early.finish(0)
    early.start(1)
    pl.when(p.unit)(lambda: near(0))
    ffn_sum.over_z(1)
    early.finish(1)
    early.start(2)
    pl.when(p.unit)(lambda: near(1))
    ffn_sum.over_z(2)
    early.finish(2)
    early.start(3)
    pl.when(p.unit)(lambda: near(2))
    pl.when(p.unit)(lambda: near(3))
    early.finish(3)
    early.start(4)

    @pl.when(first)
    def _():
        mail.got(dfr, rdf.at[0], p.far)
        for t in range(4):
            add_far(t)

    @pl.when(p.unit)
    def _():
        for t in range(4):
            dtt[0:64, t * 512 : t * 512 + 512] = (dqt[t, 0:64] * 0.125).astype(B16)
            for k in range(3):
                e = dtt[k * 64 : k * 64 + 64, t * 512 : t * 512 + 256].astype(F32)
                o = dtt[k * 64 : k * 64 + 64, t * 512 + 256 : t * 512 + 512].astype(F32)
                packs[t, k] = jnp.concatenate([e, o], axis=0).T.astype(B16)

    for t in range(4):
        for cc in range(2):
            u = t * 2 + cc
            mail.send(packs.at[t, :, cc * 128 : cc * 128 + 128], dqr.at[p.hl], rdq.at[p.hl], (seg * 8 + u, y), both(p.unit, p.u != u))

            @pl.when(both(p.unit, p.u == u))
            def _(t=t, cc=cc):
                dqr[p.hl] = packs[t, :, cc * 128 : cc * 128 + 128]

    spread = Spread(p, mail, wag, rag, True)

    @pl.when(p.unit)
    def _():
        dw = dot(dtt[...], ns[...].reshape(2048, 768))
        bias = dot_nt(jnp.ones((16, 2048), B16), dtt[...])
        for h in range(2):
            wms[h, 0:96] = dw[h * 96 : h * 96 + 96].astype(B16)
            wms[h, 96:112, 0:192] = bias.astype(B16)
            wms[h, 96:112, 192:768] = jnp.zeros((16, 576), B16)

    mail.send(wms.at[1 - seg], wmr, rwm.at[0], p.far, p.unit)
    ffn_sum.over_z(3)
    for k in range(1, 4):
        out_sum.over_z(k)

    for h, u in enumerate(UNITS):
        pl.when(p.u != u)(lambda h=h: mail.got(dqr.at[h], rdq.at[h], p.nx))
    for k in range(3):
        for a in range(3):
            e, o = halves(dqr[2 * a, k].astype(F32), dqr[2 * a + 1, k].astype(F32))
            col = slice(a * 128, a * 128 + 128)
            dall[k, 0:128, col] = e.astype(B16)
            dall[k, 128:256, col] = o.astype(B16)
    facc[...] = dot_nt(dall[0], wq_ref[0]) + dot_nt(dall[1], wq_ref[1]) + dot_nt(dall[2], wq_ref[2])
    for par in range(2):
        dns[par * 64 : par * 64 + 64] = facc[pl.ds(pl.multiple_of(par * 128 + (1 - y) * 64, 64), 64)].astype(B16)
    mail.send(dns, dnr, rdn.at[0], p.ny)

    @pl.when(p.unit)
    def _():
        mail.got(wmr, rwm.at[0], p.far)
        wag[p.s] = (wms[seg].astype(F32) + wmr[...].astype(F32)).astype(B16)

    spread.first()
    o_total = out_sum.result()
    woag[p.s] = o_total.astype(B16)
    spread_out = Spread(p, mail, woag, rwo, False)
    spread_out.first()
    z1, inv1 = norm_parts(xs[b].astype(F32))
    mail.got(dnr, rdn.at[0], p.ny)
    own = [facc[pl.ds(pl.multiple_of(par * 128 + y * 64, 64), 64)] for par in range(2)]
    dn1 = jnp.concatenate(own, axis=0) + dnr[...].astype(F32)
    vb2[0] = jnp.zeros((8, 768), F32)
    vb2[0, 0:1] = jnp.sum(dn1 * z1, axis=0, keepdims=True)
    vb2[0, 1:2] = jnp.sum(dn1, axis=0, keepdims=True)
    late.start(0)
    rest = dh_s[...] + norm_grad(z1, inv1, dn1 * row(g1_ref))
    result = jnp.zeros((128, 768), F32)
    for _k in range(3):
        piece = rest.astype(B16)
        result = result + dot(back, piece)
        rest = rest - piece.astype(F32)
    gin[...] = result
    late.finish(0)
    late.start(1)
    total = ffn_sum.result()
    o_up[...] = total[:, :1536]
    o_dn[...] = total[:, 1536:]
    late.finish(1)
    late.start(2)
    spread.second()
    spread_out.second()
    late.finish(2)
    late.start(3)
    e = early.finish(4)
    for i, ref in enumerate((o_g2, o_b2, o_bo, o_bd)):
        ref[...] = e[i : i + 1].reshape(768)
    for i in range(4):
        o_bup[i * 768 : i * 768 + 768] = e[4 + i : 5 + i].reshape(768)
    spread.third()
    spread_out.third()
    late.finish(3)
    late.start(4)
    spread_out.last()
    o_wo[...] = woag[...].reshape(768, 384).astype(F32).T
    e = late.finish(4)
    o_g1[...] = e[0:1].reshape(768)
    o_b1[...] = e[1:2].reshape(768)
    spread.last()
    for a in range(3):
        u0, u1 = UNITS[2 * a], UNITS[2 * a + 1]
        col = slice(a * 128, a * 128 + 128)
        w0 = jnp.concatenate([wag[u0, 0:96], wag[u0 + 8, 0:96]], axis=0).astype(F32)
        w1 = jnp.concatenate([wag[u1, 0:96], wag[u1 + 8, 0:96]], axis=0).astype(F32)
        for k in range(3):
            at = slice(k * 64, k * 64 + 64)
            o_wq[k, :, col] = jnp.concatenate([w0[at], w1[at]], axis=0).T
        r0, r1 = wag[u0, 96:112].astype(F32), wag[u1, 96:112].astype(F32)
        low = iota((16, 128), 1) < 64
        for k in range(2):
            at = slice(k * 128, k * 128 + 128)
            o_bqv[k : k + 1, col] = jnp.where(low, r0[:, at], pltpu.roll(r1[:, at], 64, 1))[0:1]
    mail.close()
    assert mail.used <= SENDS, mail.used


SENDS = 400


def count_table():
    kinds = np.array([[0, 0, 0, 0], [1, 0, 0, 0], [1, 1, 0, 0], [1, 0, 1, 0], [1, 1, 1, 1]], np.float64)
    shared = kinds @ kinds.T
    table = np.zeros((24, 128), np.float64)
    low = lambda v: float(np.asarray(v, dtype=ml_dtypes.bfloat16).astype(np.float64))
    for i in range(5):
        for k in range(5):
            for base, count in ((64, 1.0 + shared[i, k]), (80, shared[i, k])):
                rest = float(np.log(count)) if count > 0 else 0.0
                for e in range(3):
                    table[i, base + 3 * k + e] = low(rest)
                    rest -= low(rest)
        table[i, 96:101] = [NEGATIVE, NEGATIVE, 0.0, NEGATIVE, NEGATIVE]
        table[8 + i, 64 + 3 * i : 67 + 3 * i] = 1.0
        table[16 + i, 80 + 3 * i : 83 + 3 * i] = 1.0
        table[8 + i, 98] = table[16 + i, 98] = 1.0
    return table.astype(np.float32)


def vm(*shape):
    return pltpu.VMEM(shape, B16)


def vf(*shape):
    return pltpu.VMEM(shape, F32)


def dma(*shape):
    return pltpu.SemaphoreType.DMA(shape)


def in_vmem(count):
    return [pl.BlockSpec(memory_space=pltpu.VMEM)] * count


def fast(
    layer_input, doc_ids, cotangent, ln1_gain, ln1_bias, w_qkv, bias_qv, w_out, b_out, ln2_gain, ln2_bias, w_up, b_up, w_down, b_down
):
    out = lambda shape, dtype=F32: jax.ShapeDtypeStruct(shape, dtype)
    shapes = (
        out((128, 768), B16), out((128, 768)), out((768,)), out((768,)), out((3, 768, 384)), out((2, 384)), out((384, 768)), out((768,)),
        out((768,)), out((768,)), out((48, 1536)), out((3072,)), out((48, 1536)), out((768,)),
    )
    scratch = [
        vm(4, 512, 128), vm(6, 512, 128), vm(6, 512, 128), vm(4, 512, 768), vf(4, 1, 512), vf(4, 128, 256), vm(6, 128, 128),
        vm(768, 3072), vm(768, 384), vf(128, 768), vm(768, 384), vf(1, 384), vf(1, 1536), vf(4, 1, 512), vf(4, 128, 512),
        vm(16, 128, 768), vf(17, 8, 128), vm(768, 3072), vm(2, 384, 768), vm(2, 128, 768), vm(12, 128, 128), vm(4, 256, 128),
        vm(4, 256, 128), vm(4, 256, 128), vm(256, 768), vm(6, 128, 512), vf(256, 768), vm(256, 768), vm(256, 768), vm(256, 1536),
        vm(256, 1536), vf(256, 768), vf(256, 768), vm(256, 768), vm(256, 768), vm(128, 768), vm(128, 768), vf(128, 768),
        vm(4, 256, 128), vm(4, 512, 128), vf(4, 1, 512), vm(6, 128, 512), vf(512, 128), vf(512, 128), vf(4, 128, 512), vm(192, 2048),
        vm(4, 256, 128), vm(4, 256, 128), vm(4, 3, 256, 128), vm(6, 3, 128, 128), vm(2, 112, 768), vm(112, 768),
        vm(2, 4, 48, 3072), vm(4, 48, 3072), vm(4, 48, 3072), vm(2, 4, 48, 384), vm(4, 48, 384), vm(4, 48, 384), vm(4, 48, 384),
        vm(4, 48, 384), vm(3, 256, 384), vm(128, 768), vm(128, 768),
        vf(5, 8, 768), vf(5, 8, 768), vf(5, 8, 768), vf(5, 8, 768), vm(16, 112, 768), vm(16, 48, 384),
        dma(SENDS), dma(3, 16), dma(3, 16), dma(16), dma(16), dma(12), dma(2), dma(4), dma(8), dma(2, 4), dma(4), dma(4), dma(2, 4), dma(4),
        dma(4), dma(1), dma(6), dma(1), dma(16), dma(16), dma(1), dma(5), dma(5),
    ]
    args = (
        layer_input, doc_ids, cotangent, ln1_gain, ln1_bias, w_qkv.transpose(1, 0, 2), bias_qv, w_out, b_out, ln2_gain, ln2_bias, w_up,
        b_up, w_down.T, b_down, jnp.asarray(count_table()),
    )
    outs = pl.pallas_call(
        kernel, out_shape=shapes, in_specs=in_vmem(len(args)), out_specs=tuple(in_vmem(len(shapes))), scratch_shapes=scratch,
        compiler_params=pltpu.CompilerParams(collective_id=0, has_side_effects=True, vmem_limit_bytes=LIMIT),
    )(*args)
    outs = list(outs)
    outs[4] = outs[4].transpose(1, 0, 2)
    outs[12] = outs[12].T
    return tuple(outs)


def from_behind(value, axis, by):
    length = lax.axis_size(axis)
    pairs = [(i, i + by) for i in range(length) if 0 <= i + by < length]
    return lax.ppermute(value, axis, pairs)


def layer_norm(values, gain, shift):
    mean = jnp.mean(values, axis=-1, keepdims=True)
    centred = values - mean
    spread = jnp.mean(centred * centred, axis=-1, keepdims=True)
    return centred * lax.rsqrt(spread + EPS) * gain + shift


def gelu_tanh(values):
    return jax.nn.gelu(values, approximate=True)


def pick_block(length, limit):
    chosen = 1
    for candidate in range(1, min(length, limit) + 1):
        if length % candidate == 0:
            chosen = candidate
    return chosen


def pair_counts(query_pos, key_pos, head_ids):
    total = None
    for factor, rate in LEVELS:
        width = SEG * factor
        same = query_pos[:, :, None] // width == key_pos[:, None, :] // width
        offset = (head_ids % rate)[:, None]
        pick_query = query_pos % width % rate == offset
        pick_key = key_pos % width % rate == offset
        joint = (same & pick_query[:, :, None] & pick_key[:, None, :]).astype(jnp.float32)
        total = joint if total is None else total + joint
    return total


def block_terms(
    query_blk, query_pos, query_doc, key_blk, key_pos, key_doc, head_ids, nearby, scale
):
    scores = (
        jnp.einsum("qhe,khe->hqk", query_blk, key_blk, preferred_element_type=jnp.float32) * scale
    )
    counts = pair_counts(query_pos, key_pos, head_ids)
    same_segment = query_pos[:, :, None] // SEG == key_pos[:, None, :] // SEG
    keep = same_segment if nearby else jnp.logical_not(same_segment)
    allowed = (
        keep
        & (key_pos[:, None, :] <= query_pos[:, :, None])
        & (query_doc[:, :, None] == key_doc[:, None, :])
    )
    return (scores, counts * allowed.astype(jnp.float32))


def per_device(
    layer_input,
    doc_ids,
    cotangent,
    ln1_gain,
    ln1_bias,
    w_qkv,
    bias_qv,
    w_out,
    b_out,
    ln2_gain,
    ln2_bias,
    w_up,
    b_up,
    w_down,
    b_down,
):
    seq_count = lax.axis_size("seq")
    local_heads = HEADS // lax.axis_size("head")
    local_width = local_heads * HEAD_DIM
    scale = HEAD_DIM ** (-0.5)
    f32 = jnp.float32
    b16 = jnp.bfloat16
    x_float = layer_input.astype(f32)
    norm_one = layer_norm(x_float, ln1_gain, ln1_bias)
    norm_rows, row_doc = (
        lax.all_gather(norm_one.astype(b16), "head", axis=0, tiled=True),
        lax.all_gather(doc_ids, "head", axis=0, tiled=True),
    )
    seq_tokens = norm_rows.shape[0]
    half = seq_tokens // 2
    total_tokens = seq_tokens * seq_count
    total_half = total_tokens // 2
    first_pos = lax.axis_index("seq") * seq_tokens
    last_pos = first_pos + seq_tokens - 1
    local_offsets = jnp.arange(seq_tokens, dtype=jnp.int32)
    query_pos = (first_pos + local_offsets)[None, :]
    query_doc = row_doc[None, :]
    head_ids = lax.axis_index("head") * local_heads + jnp.arange(local_heads, dtype=jnp.int32)
    parity = head_ids % 2
    pick_even = parity == 0

    def compact(rows):
        paired = rows.reshape((half, 2) + rows.shape[1:])
        mask = pick_even.reshape((1, local_heads) + (1,) * (rows.ndim - 2))
        return jnp.where(mask, paired[:, 0], paired[:, 1])

    def expand(rows):
        mask = pick_even.reshape((1, local_heads) + (1,) * (rows.ndim - 2))
        zeros = jnp.zeros_like(rows)
        paired = jnp.stack([jnp.where(mask, rows, zeros), jnp.where(mask, zeros, rows)], axis=1)
        return paired.reshape((seq_tokens,) + rows.shape[1:])

    mixed = jnp.einsum("td,dch->tch", norm_rows, w_qkv, preferred_element_type=f32)
    zero_row = jnp.zeros((1, local_width), f32)
    bias_all = jnp.concatenate([bias_qv[0:1], zero_row, bias_qv[1:2]], axis=0)
    qkv = (mixed + bias_all[None]).astype(b16)
    queries = qkv[:, 0]
    query_heads = queries.reshape(seq_tokens, local_heads, HEAD_DIM)
    key_heads = qkv[:, 1].reshape(seq_tokens, local_heads, HEAD_DIM)
    value_heads = qkv[:, 2].reshape(seq_tokens, local_heads, HEAD_DIM)
    local_keys_c = compact(key_heads)
    local_values_c = compact(value_heads)
    far_keys_all, far_values_all, doc_all = (
        lax.all_gather(local_keys_c, "seq", axis=0, tiled=True),
        lax.all_gather(local_values_c, "seq", axis=0, tiled=True),
        lax.all_gather(row_doc, "seq", axis=0, tiled=True),
    )
    segment_count = SEG // seq_tokens
    own_pair = jnp.stack([key_heads, value_heads], axis=1)
    pair_pieces = [own_pair]
    for step in range(1, segment_count):
        pair_pieces.append(from_behind(own_pair, "seq", step))
    near_pairs = jnp.concatenate(pair_pieces, axis=0)
    near_keys = near_pairs[:, 0]
    near_values = near_pairs[:, 1]
    near_flat = jnp.concatenate(
        [first_pos - step * seq_tokens + local_offsets for step in range(segment_count)]
    )
    near_doc = jnp.take(doc_all, jnp.clip(near_flat, 0, total_tokens - 1))[None, :]
    near_pos = near_flat[None, :]
    far_pos = 2 * jnp.arange(total_half, dtype=jnp.int32)[None, :] + parity[:, None]
    doc_pairs = doc_all.reshape(total_half, 2)
    far_doc = jnp.where(pick_even[:, None], doc_pairs[:, 0][None, :], doc_pairs[:, 1][None, :])
    key_block = pick_block(total_half, block_limit)
    blocks = total_half // key_block
    far_key_blocks = far_keys_all.reshape(blocks, key_block, local_heads, HEAD_DIM)
    far_value_blocks = far_values_all.reshape(blocks, key_block, local_heads, HEAD_DIM)
    far_pos_blocks = far_pos.reshape(local_heads, blocks, key_block).transpose(1, 0, 2)
    far_doc_blocks = far_doc.reshape(local_heads, blocks, key_block).transpose(1, 0, 2)
    far_begin = jnp.arange(blocks, dtype=jnp.int32) * (2 * key_block)

    def merge_stats(current, key_blk, key_pos, key_doc, nearby):
        peak, running = current
        scores, counts = block_terms(
            query_heads, query_pos, query_doc, key_blk, key_pos, key_doc, head_ids, nearby, scale
        )
        live = counts > 0
        new_peak = jnp.maximum(peak, jnp.max(jnp.where(live, scores, NEGATIVE), axis=2))
        terms = jnp.where(live, counts * jnp.exp(scores - new_peak[:, :, None]), 0.0)
        return (new_peak, running * jnp.exp(peak - new_peak) + jnp.sum(terms, axis=2))

    start_state = (
        jnp.full((local_heads, seq_tokens), NEGATIVE, f32),
        jnp.zeros((local_heads, seq_tokens), f32),
    )
    near_state = merge_stats(start_state, near_keys, near_pos, near_doc, True)

    def stats_step(state, item):
        key_blk, pos_blk, doc_blk, begin = item
        return (
            lax.cond(
                begin <= last_pos,
                lambda current: merge_stats(current, key_blk, pos_blk, doc_blk, False),
                lambda current: current,
                state,
            ),
            None,
        )

    (peak_all, running_all), _ = lax.scan(
        stats_step, near_state, (far_key_blocks, far_pos_blocks, far_doc_blocks, far_begin)
    )
    lse = peak_all + jnp.log(running_all)

    def add_output(current, key_blk, value_blk, key_pos, key_doc, nearby):
        scores, counts = block_terms(
            query_heads, query_pos, query_doc, key_blk, key_pos, key_doc, head_ids, nearby, scale
        )
        probs = jnp.where(counts > 0, counts * jnp.exp(scores - lse[:, :, None]), 0.0).astype(b16)
        return current + jnp.einsum("hqk,khe->qhe", probs, value_blk, preferred_element_type=f32)

    zero_heads = jnp.zeros((seq_tokens, local_heads, HEAD_DIM), f32)
    near_output = add_output(zero_heads, near_keys, near_values, near_pos, near_doc, True)

    def output_step(accum, item):
        key_blk, value_blk, pos_blk, doc_blk, begin = item
        return (
            lax.cond(
                begin <= last_pos,
                lambda current: add_output(current, key_blk, value_blk, pos_blk, doc_blk, False),
                lambda current: current,
                accum,
            ),
            None,
        )

    attn_exact, _ = lax.scan(
        output_step,
        near_output,
        (far_key_blocks, far_value_blocks, far_pos_blocks, far_doc_blocks, far_begin),
    )
    attn_low = attn_exact.reshape(seq_tokens, local_width).astype(b16)
    branch = lax.psum_scatter(
        jnp.dot(attn_low, w_out, preferred_element_type=f32).astype(jnp.bfloat16),
        "head",
        scatter_dimension=0,
        tiled=True,
    ).astype(jnp.float32)
    hidden_one = x_float + branch + b_out
    norm_two = layer_norm(hidden_one, ln2_gain, ln2_bias)
    norm_low = norm_two.astype(b16)
    dy_low = (cotangent.astype(f32) * (doc_ids >= 0).astype(f32)[:, None]).astype(b16)
    dy_float = dy_low.astype(f32)
    up_rows, down_rows = (
        lax.all_gather(w_up, "seq", axis=0, tiled=True),
        lax.all_gather(w_down, "seq", axis=1, tiled=True),
    )
    up_full, down_full = (
        lax.all_gather(up_rows, "head", axis=1, tiled=True),
        lax.all_gather(down_rows, "head", axis=0, tiled=True),
    )
    pre_act = jnp.dot(norm_low, up_full, preferred_element_type=f32) + b_up
    act_low = gelu_tanh(pre_act).astype(b16)
    ffn_result = jnp.dot(act_low, down_full, preferred_element_type=f32)
    d_act = jnp.einsum("td,fd->tf", dy_low, down_full, preferred_element_type=f32)
    _, gelu_back = jax.vjp(gelu_tanh, pre_act)
    d_pre = gelu_back(d_act)[0]
    d_pre_low = d_pre.astype(b16)
    bias_up_grad = jnp.sum(d_pre, axis=0)
    up_parts = jnp.einsum("td,tf->df", norm_low, d_pre_low, preferred_element_type=f32)
    down_parts = jnp.einsum("tf,td->fd", act_low, dy_low, preferred_element_type=f32)
    up_grad, down_grad = (
        lax.psum_scatter(
            up_parts.astype(jnp.bfloat16), "head", scatter_dimension=1, tiled=True
        ).astype(jnp.float32),
        lax.psum_scatter(
            down_parts.astype(jnp.bfloat16), "head", scatter_dimension=0, tiled=True
        ).astype(jnp.float32),
    )
    d_norm_two = jnp.einsum("tf,df->td", d_pre_low, up_full, preferred_element_type=f32)
    layer_output = (hidden_one + ffn_result + b_down).astype(b16)
    w_up_grad, w_down_grad = (
        lax.psum_scatter(up_grad, "seq", scatter_dimension=0, tiled=True),
        lax.psum_scatter(down_grad, "seq", scatter_dimension=1, tiled=True),
    )
    _, norm_two_back = jax.vjp(layer_norm, hidden_one, ln2_gain, ln2_bias)
    d_hidden_norm, gain_two_grad, bias_two_grad = norm_two_back(d_norm_two)
    d_hidden = dy_float + d_hidden_norm
    bias_out_grad = jnp.sum(d_hidden, axis=0)
    bias_down_grad = jnp.sum(dy_float, axis=0)
    hidden_rows = lax.all_gather(d_hidden.astype(b16), "head", axis=0, tiled=True)
    w_out_part = jnp.einsum("tc,td->cd", attn_low, hidden_rows, preferred_element_type=f32)
    d_attn = jnp.einsum("td,cd->tc", hidden_rows, w_out, preferred_element_type=f32).astype(b16)
    d_attn_heads = d_attn.reshape(seq_tokens, local_heads, HEAD_DIM)
    delta_rows = jnp.sum(d_attn_heads.astype(f32) * attn_exact, axis=2)
    delta = delta_rows.T

    def score_grads(key_blk, value_blk, key_pos, key_doc, nearby):
        scores, counts = block_terms(
            query_heads, query_pos, query_doc, key_blk, key_pos, key_doc, head_ids, nearby, scale
        )
        exact = jnp.where(counts > 0, counts * jnp.exp(scores - lse[:, :, None]), 0.0)
        d_prob = jnp.einsum("qhe,khe->hqk", d_attn_heads, value_blk, preferred_element_type=f32)
        d_score = (exact * (d_prob - delta[:, :, None])).astype(b16)
        return (exact, d_score)

    exact_near, d_score_near = score_grads(near_keys, near_values, near_pos, near_doc, True)
    d_query_near = jnp.einsum("hqk,khe->qhe", d_score_near, near_keys, preferred_element_type=f32)
    near_key_grad = jnp.einsum(
        "hqk,qhe->khe", d_score_near, query_heads, preferred_element_type=f32
    )
    near_value_grad = jnp.einsum(
        "hqk,qhe->khe", exact_near.astype(b16), d_attn_heads, preferred_element_type=f32
    )
    near_pair_grads = jnp.stack([near_key_grad, near_value_grad], axis=1)
    pair_grad = near_pair_grads[:seq_tokens]
    for step in range(1, segment_count):
        piece = near_pair_grads[step * seq_tokens : (step + 1) * seq_tokens]
        pair_grad = pair_grad + from_behind(piece.astype(jnp.bfloat16), "seq", -step).astype(
            piece.dtype
        )

    def query_grad_step(accum, item):
        key_blk, value_blk, pos_blk, doc_blk, begin = item

        def query_compute(current):
            _, d_score = score_grads(key_blk, value_blk, pos_blk, doc_blk, False)
            return current + jnp.einsum(
                "hqk,khe->qhe", d_score, key_blk, preferred_element_type=f32
            )

        return (lax.cond(begin <= last_pos, query_compute, lambda current: current, accum), None)

    d_query, _ = lax.scan(
        query_grad_step,
        d_query_near,
        (far_key_blocks, far_value_blocks, far_pos_blocks, far_doc_blocks, far_begin),
    )
    d_query = d_query * scale
    stats_rows = jnp.stack([compact(lse.T), compact(delta_rows)], axis=1)
    stats_all = lax.all_gather(stats_rows, "seq", axis=0, tiled=True)
    local_key_pos = first_pos + 2 * jnp.arange(half, dtype=jnp.int32)[None, :] + parity[:, None]
    local_key_doc = compact(jnp.broadcast_to(row_doc[:, None], (seq_tokens, local_heads))).T
    zero_compact = jnp.zeros((half, local_heads, HEAD_DIM), f32)
    query_piece = lax.all_gather(compact(query_heads), "seq", axis=0, tiled=True)
    grad_piece = lax.all_gather(compact(d_attn_heads), "seq", axis=0, tiled=True)
    length = query_piece.shape[0]
    size = pick_block(length, block_limit)
    number = length // size
    pos_piece = 2 * jnp.arange(length, dtype=jnp.int32)[None, :] + parity[:, None]
    items = (
        query_piece.reshape(number, size, local_heads, HEAD_DIM),
        grad_piece.reshape(number, size, local_heads, HEAD_DIM),
        stats_all.reshape(number, size, 2, local_heads),
        pos_piece.reshape(local_heads, number, size).transpose(1, 0, 2),
        far_doc.reshape(local_heads, number, size).transpose(1, 0, 2),
    )

    def one_step(current, item):
        query_blk, grad_blk, stats_blk, pos_blk, doc_blk = item

        def one_compute(pair):
            key_grad, value_grad = pair
            scores, counts = block_terms(
                query_blk,
                pos_blk,
                doc_blk,
                local_keys_c,
                local_key_pos,
                local_key_doc,
                head_ids,
                False,
                scale,
            )
            exact = jnp.where(
                counts > 0, counts * jnp.exp(scores - stats_blk[:, 0].T[:, :, None]), 0.0
            )
            d_prob = jnp.einsum(
                "qhe,khe->hqk", grad_blk, local_values_c, preferred_element_type=f32
            )
            d_score = (exact * (d_prob - stats_blk[:, 1].T[:, :, None])).astype(b16)
            key_grad = key_grad + jnp.einsum(
                "hqk,qhe->khe", d_score, query_blk, preferred_element_type=f32
            )
            value_grad = value_grad + jnp.einsum(
                "hqk,qhe->khe", exact.astype(b16), grad_blk, preferred_element_type=f32
            )
            return (key_grad, value_grad)

        return (
            lax.cond(jnp.max(pos_blk) >= first_pos, one_compute, lambda pair: pair, current),
            None,
        )

    result, _ = lax.scan(one_step, (zero_compact, zero_compact), items)
    far_key_grad, far_value_grad = result
    d_key = (pair_grad[:, 0] + expand(far_key_grad)) * scale
    d_value = pair_grad[:, 1] + expand(far_value_grad)
    d_qkv = jnp.stack(
        [
            d_query.reshape(seq_tokens, local_width),
            d_key.reshape(seq_tokens, local_width),
            d_value.reshape(seq_tokens, local_width),
        ],
        axis=1,
    ).astype(b16)
    d_qkv_float = d_qkv.astype(f32)
    bias_qv_part = jnp.stack(
        [jnp.sum(d_qkv_float[:, 0], axis=0), jnp.sum(d_qkv_float[:, 2], axis=0)], axis=0
    )
    w_qkv_part = jnp.einsum("td,tch->dch", norm_rows, d_qkv, preferred_element_type=f32)
    d_norm_one = lax.psum_scatter(
        jnp.einsum("tch,dch->td", d_qkv, w_qkv, preferred_element_type=f32).astype(jnp.bfloat16),
        "head",
        scatter_dimension=0,
        tiled=True,
    ).astype(jnp.float32)
    _, norm_one_back = jax.vjp(layer_norm, x_float, ln1_gain, ln1_bias)
    d_x_norm, gain_one_grad, bias_one_grad = norm_one_back(d_norm_one)
    grad_input = d_hidden + d_x_norm
    w_qkv_grad, bias_qv_grad, w_out_grad = lax.psum((w_qkv_part, bias_qv_part, w_out_part), "seq")
    summed = lax.psum(
        (
            gain_one_grad,
            bias_one_grad,
            gain_two_grad,
            bias_two_grad,
            bias_out_grad,
            bias_up_grad,
            bias_down_grad,
        ),
        ("seq", "head"),
    )
    return (
        layer_output,
        grad_input,
        summed[0],
        summed[1],
        w_qkv_grad,
        bias_qv_grad,
        w_out_grad,
        summed[4],
        summed[2],
        summed[3],
        w_up_grad,
        summed[5],
        w_down_grad,
        summed[6],
    )


def solution(mesh):
    in_specs = (
        P(("seq", "head"), None),
        P(("seq", "head")),
        P(("seq", "head"), None),
        P(),
        P(),
        P(None, None, "head"),
        P(None, "head"),
        P("head", None),
        P(),
        P(),
        P(),
        P("seq", "head"),
        P(),
        P("head", "seq"),
        P(),
    )
    out_specs = (
        P(("seq", "head"), None),
        P(("seq", "head"), None),
        P(),
        P(),
        P(None, None, "head"),
        P(None, "head"),
        P("head", None),
        P(),
        P(),
        P(),
        P("seq", "head"),
        P(),
        P("head", "seq"),
        P(),
    )
    small = mesh.shape["seq"] == 16 and mesh.shape["head"] == 2
    return jax.shard_map(
        fast if small else per_device, mesh=mesh, in_specs=in_specs, out_specs=out_specs, check_vma=False
    )
```

```python
import functools

import jax
import jax.numpy as jnp
import ml_dtypes
import numpy as np
from jax import lax
from jax.experimental import pallas as pl
from jax.experimental.pallas import tpu as pltpu
from jax.sharding import PartitionSpec as P

HEADS = 12
HEAD_DIM = 64
SEG = 2048


LEVELS = ((1, 1), (2, 2), (4, 4), (8, 6), (16, 12))
EPS = 1e-05
NEGATIVE = -1e30
block_limit = 2048


MESH = pl.DeviceIdType.MESH
VMEM = pltpu.VMEM
LIMIT = 60 << 20
F32 = jnp.float32
B16 = jnp.bfloat16


def dot(a, b):
    return jnp.dot(a, b, preferred_element_type=F32)


def dot_nt(a, b):
    return lax.dot_general(a, b, (((1,), (1,)), ((), ())), preferred_element_type=F32)


def sid(z, x, c):
    return z * 4 + x * 2 + c


class Place:
    def __init__(self):
        s = lax.axis_index("seq")
        self.s, self.y = s, lax.axis_index("head")
        self.z, self.x, self.c = s // 4, (s // 2) % 2, s % 2
        self.seg, self.zl = self.z // 2, self.z % 2
        self.u = s % 8
        self.b = self.u * 2 + self.y
        self.unit = jnp.logical_and(self.u != 3, self.u != 5)
        self.hl = self.u - self.u // 4 - self.u // 6
        self.head = self.y * 6 + self.hl
        self.parity = self.head % 2
        z, x, c, y = self.z, self.x, self.c, self.y
        self.zf = z + 1 - 2 * self.zl
        self.nx, self.ny = (sid(z, 1 - x, c), y), (s, 1 - y)
        self.nz, self.nc = (sid(self.zf, x, c), y), (sid(z, x, 1 - c), y)
        self.far = (sid((z + 2) % 4, x, c), y)
        self.fb = {"x": 4 * (1 - 2 * x), "y": 1 - 2 * y, "z": 8 * (1 - 2 * self.zl), "c": 2 * (1 - 2 * c)}

    def cube(self):
        z, x, c, y = self.z, self.x, self.c, self.y
        for k in range(1, 16):
            zz = self.zf if k & 8 else z
            xx = 1 - x if k & 4 else x
            cc = 1 - c if k & 2 else c
            yy = 1 - y if k & 1 else y
            yield (sid(zz, xx, cc), yy)

    def greet(self):
        others = list(self.cube())
        others += [(sid((self.z + 2) % 4, self.x, self.c), self.y), (sid((self.zf + 2) % 4, self.x, self.c), self.y)]
        barrier = pltpu.get_barrier_semaphore()
        for dev in others:
            pl.semaphore_signal(barrier, inc=1, device_id=dev, device_id_type=MESH)
        self.greeted = len(others)

    def meet(self):
        pl.semaphore_wait(pltpu.get_barrier_semaphore(), self.greeted)


class Mail:
    def __init__(self, sems):
        self.sems, self.used, self.sent = sems, 0, []

    def send(self, src, dst, rsem, dev, cond=None):
        k = self.used
        self.used += 1

        def make():
            return pltpu.make_async_remote_copy(
                src_ref=src, dst_ref=dst, send_sem=self.sems.at[k], recv_sem=rsem, device_id=dev, device_id_type=MESH
            )

        if cond is None:
            make().start()
        else:
            pl.when(cond)(lambda: make().start())
        self.sent.append((cond, make))

    def got(self, dst, rsem, dev):
        pltpu.make_async_remote_copy(
            src_ref=dst, dst_ref=dst, send_sem=self.sems.at[0], recv_sem=rsem, device_id=dev, device_id_type=MESH
        ).wait_recv()

    def close(self):
        for cond, make in self.sent:
            if cond is None:
                make().wait_send()
            else:
                pl.when(cond)(lambda make=make: make().wait_send())
        self.sent = []


def both(*terms):
    out = terms[0]
    for term in terms[1:]:
        out = jnp.logical_and(out, term)
    return out


def iota(shape, dim):
    return lax.broadcasted_iota(jnp.int32, shape, dim)


def norm_parts(v):
    mean = jnp.mean(v, axis=-1, keepdims=True)
    cen = v - mean
    inv = lax.rsqrt(jnp.mean(cen * cen, axis=-1, keepdims=True) + EPS)
    return cen * inv, inv


def norm_grad(z, inv, e):
    return (e - jnp.mean(e, axis=-1, keepdims=True) - z * jnp.mean(e * z, axis=-1, keepdims=True)) * inv


def pick_type(pos, head, rows):
    v = pos - head + 24.0
    m = v - 12.0 * jnp.floor((v + 0.5) * (1.0 / 12.0))
    out = jnp.where(m == 0.0, rows[4], rows[0])
    out = jnp.where(m == 6.0, rows[3], out)
    out = jnp.where(jnp.logical_or(m == 4.0, m == 8.0), rows[2], out)
    return jnp.where(jnp.logical_or(m == 2.0, m == 10.0), rows[1], out)


def halves(e, o):
    low = iota(e.shape, 1) < 64
    return jnp.where(low, e, pltpu.roll(o, 64, 1)), jnp.where(low, pltpu.roll(e, 64, 1), o)


UNITS = (0, 1, 2, 4, 6, 7)


class Spread:
    def __init__(self, p, mail, ref, sems, some):
        self.p, self.mail, self.ref, self.sems, self.some = p, mail, ref, sems, some

    def has(self, zz, xx, cc):
        return jnp.logical_or(cc == 0, zz % 2 == xx) if self.some else None

    def go(self, s, dev, cond):
        self.mail.send(self.ref.at[s], self.ref.at[s], self.sems.at[s], dev, cond)

    def take(self, s, cond):
        def wait():
            self.mail.got(self.ref.at[s], self.sems.at[s], self.p.nx)

        if cond is None:
            wait()
        else:
            pl.when(cond)(wait)

    def first(self):
        p = self.p
        has = self.has(p.z, p.x, p.c)
        for k in range(1, 4):
            self.go(p.s, (sid((p.z + k) % 4, p.x, p.c), p.y), has)
        self.go(p.s, p.nx, has)
        self.go(p.s, p.nc, has)

    def second(self):
        p = self.p
        for k in range(1, 4):
            zz = (p.z + k) % 4
            s, has = sid(zz, p.x, p.c), self.has(zz, p.x, p.c)
            self.take(s, has)
            self.go(s, p.nx, has)
            self.go(s, p.nc, has)

    def third(self):
        p = self.p
        for zz in range(4):
            s, has = sid(zz, 1 - p.x, p.c), self.has(zz, 1 - p.x, p.c)
            self.take(s, has)
            self.go(s, p.nc, has)

    def last(self):
        p = self.p
        for zz in range(4):
            for xx in range(2):
                self.take(sid(zz, xx, 1 - p.c), self.has(zz, xx, 1 - p.c))


class Reduce:
    def __init__(self, p, mail, src, gc, gxs, gxr, gzs, gzr, rc, rx, rz):
        self.__dict__.update(locals())

    def rows(self, zz, xx, cc):
        return pl.ds(pl.multiple_of(sid(zz, xx, cc) * 48, 16), 48)

    def cores(self):
        p = self.p
        for xq in range(2):
            xx = 1 - p.x if xq == 0 else p.x
            for k in (1, 2, 3, 0):
                zz = (p.z + k) % 4
                self.mail.send(self.src.at[self.rows(zz, xx, 1 - p.c)], self.gc.at[xq, zz], self.rc.at[xq, zz], p.nc)

    def over_x(self):
        p = self.p
        for k in (1, 2, 3, 0):
            zz = (p.z + k) % 4
            self.mail.got(self.gc.at[0, zz], self.rc.at[0, zz], p.nc)
            own = self.src[self.rows(zz, 1 - p.x, p.c)].astype(F32)
            self.gxs[zz] = (own + self.gc[0, zz].astype(F32)).astype(B16)
            self.mail.send(self.gxs.at[zz], self.gxr.at[zz], self.rx.at[zz], p.nx)

    def column(self, zz):
        p = self.p
        self.mail.got(self.gc.at[1, zz], self.rc.at[1, zz], p.nc)
        self.mail.got(self.gxr.at[zz], self.rx.at[zz], p.nx)
        return self.src[self.rows(zz, p.x, p.c)].astype(F32) + self.gc[1, zz].astype(F32) + self.gxr[zz].astype(F32)

    def over_z(self, k):
        p = self.p
        zz = (p.z + k) % 4
        self.gzs[k] = self.column(zz).astype(B16)
        self.mail.send(self.gzs.at[k], self.gzr.at[p.z], self.rz.at[p.z], (sid(zz, p.x, p.c), p.y))

    def result(self):
        p = self.p
        total = self.column(p.z)
        for k in range(1, 4):
            zz = (p.z + k) % 4
            self.mail.got(self.gzr.at[zz], self.rz.at[zz], p.nx)
            total = total + self.gzr[zz].astype(F32)
        return total


class Total:
    def __init__(self, p, mail, one, two, sem_one, sem_two):
        self.p, self.mail, self.one, self.two, self.sem_one, self.sem_two = p, mail, one, two, sem_one, sem_two
        self.k = (p.x * 2 + p.c) * 2 + p.y

    def start(self):
        p = self.p
        for i in range(1, 4):
            dev = (sid((p.z + i) % 4, p.x, p.c), p.y)
            self.mail.send(self.one.at[p.z], self.one.at[p.z], self.sem_one.at[p.z], dev)

    def middle(self):
        p = self.p
        for i in range(1, 4):
            zz = (p.z + i) % 4
            self.mail.got(self.one.at[zz], self.sem_one.at[zz], p.nx)
        self.two[self.k] = self.one[0] + self.one[1] + self.one[2] + self.one[3]
        for i in range(1, 8):
            xx = 1 - p.x if i & 4 else p.x
            cc = 1 - p.c if i & 2 else p.c
            yy = 1 - p.y if i & 1 else p.y
            self.mail.send(self.two.at[self.k], self.two.at[self.k], self.sem_two.at[self.k], (sid(p.z, xx, cc), yy))

    def finish(self):
        for i in range(8):
            pl.when(self.k != i)(lambda i=i: self.mail.got(self.two.at[i], self.sem_two.at[i], self.p.nx))
        out = self.two[0]
        for i in range(1, 8):
            out = out + self.two[i]
        return out


def mixed(shape, dim_to, dim_from):
    r, i = iota(shape, dim_to), iota(shape, dim_from)
    return jnp.where(i == 2 * (r & 63) + (r >> 6), 1.0, 0.0).astype(B16)


def kernel(
    x_ref, doc_ref, cot_ref, g1_ref, b1_ref, wq_ref, bqv_ref, wo_own, bo_ref, g2_ref, b2_ref, wup_ref, bup_ref, wdn_ref, bd_ref, tab_ref,
    lout, gin, wag, woag, o_ud, o_tot,
    qa, ka, va, ns, lse, ot, dpk, gwo, dh_s, wqh, bqh, buph, msc, asc,
    xs, docs, wb, wo, dyp, orecv, osend, kvs, kvf, attn, vt, hid, n2s, dys, acts, dpre, facc, dacc, ys, yr, fs, fr, fo,
    dor, doa, delta, kt, dka, dva, dqt, dtt, dfs, dfr, packs, dqr, wms, wmr, n2t, dyt, ga, gb, gd, ge, ra, rb, gxr, gzr,
    hc, hxs, hxr, hzs, hzr, dall, dns, dnr, vb1, vr1, vb2, vr2,
    ss, rsx, rsc, rsd, rsw, rso, rsf, rsy, rdo, rga, rgx, rgz, rhc, rhx, rhz, rdf, rdq, rwm, rag, rwo, rdn, rv1, rv2, rv3, rv4,
):
    p = Place()
    mail = Mail(ss)
    seg, x, y, z, c, b = p.seg, p.x, p.y, p.z, p.c, p.b
    first, second = both(p.unit, seg == 0), both(p.unit, seg == 1)
    row = lambda ref: ref[...].reshape(1, -1)
    p.greet()

    mix = mixed((128, 128), 0, 1)
    xs[b] = dot(mix, x_ref[...]).astype(B16)
    doc_row = doc_ref[...].astype(F32).reshape(1, 128)
    turn = jnp.where(iota((128, 128), 0) == 2 * (iota((128, 128), 1) & 63), 1.0, 0.0).astype(B16)
    turn_odd = jnp.where(iota((128, 128), 0) == 2 * (iota((128, 128), 1) & 63) + 1, 1.0, 0.0).astype(B16)
    doc8 = jnp.broadcast_to(doc_row, (8, 128)).astype(B16)
    docs[b] = jnp.where(iota((8, 128), 0) == 0, dot(doc8, turn), dot(doc8, turn_odd))
    wrow = pl.ds(pl.multiple_of(p.s * 48, 16), 48)
    wb[wrow, 0:1536] = wup_ref[...]
    wb[wrow, 1536:3072] = wdn_ref[...]
    p.meet()

    dims = ("x", "y", "z")
    nbr = {"x": p.nx, "y": p.ny, "z": p.nz}
    part = [pl.ds(k * 256, 256) for k in range(3)]
    order = [[dims[(k + j) % 3] for j in range(3)] for k in range(3)]

    def pass_on(k, blk, dev):
        ref = xs.at[blk, :, part[k]]
        mail.send(ref, ref, rsx.at[k, blk], dev)

    def to_core(k, blk):
        ref = xs.at[blk, :, part[k]]
        mail.send(ref, ref, rsc.at[k, blk], p.nc)

    for j in range(3):
        for k in range(3):
            pass_on(k, b, nbr[order[k][j]])
    for k in range(3):
        to_core(k, b)
    for src in (0, 14, 15):
        for dev in p.cube():
            mail.send(docs.at[src], docs.at[src], rsd.at[src], dev, cond=b == src)

    def rows_of(s):
        return wb.at[pl.ds(pl.multiple_of(s * 48, 16), 48), :]

    def give(s, dev, cond=None):
        mail.send(rows_of(s), rows_of(s), rsw.at[s], dev, cond)

    give(p.s, (sid((z + 1) % 4, x, c), y), z <= 2)
    give(p.s, (sid((z + 3) % 4, x, c), y), z >= 1)
    give(p.s, p.nx)
    give(p.s, p.nc)

    pair_cols = pl.ds(pl.multiple_of(p.hl // 2 * 128, 128), 128)
    for odd in range(2):

        @pl.when(p.hl % 2 == odd)
        def _(odd=odd):
            for k in range(3):
                w = wq_ref[k, :, pair_cols].astype(F32)
                w = pltpu.roll(w, 64, 1) if odd else w
                wqh[:, k * 128 : k * 128 + 128] = jnp.where(iota((768, 128), 1) < 64, w, 0.0).astype(B16)
            v = jnp.concatenate([bqv_ref[:, pair_cols], jnp.zeros((6, 128), F32)], axis=0)
            v = pltpu.roll(v, 64, 1) if odd else v
            lane = iota((1, 128), 1)
            bqh[:, 0:128] = jnp.where(lane < 64, v[0:1], 0.0)
            bqh[:, 128:256] = jnp.zeros((1, 128), F32)
            bqh[:, 256:384] = jnp.where(lane < 64, v[1:2], jnp.where(lane == 64, 1.0, 0.0))

    head = p.head.astype(F32)
    for t in range(4):
        rr = iota((512, 128), 0)
        pos = (seg * SEG + t * 512 + 2 * (rr & 255) + (rr >> 8)).astype(F32)
        qa[t] = pick_type(pos, head, [tab_ref[i : i + 1] for i in range(5)]).astype(B16)
        ka[t + 2] = pick_type(pos, head, [tab_ref[8 + i : 9 + i] for i in range(5)]).astype(B16)

    real = jnp.broadcast_to(doc_row, (128, 128)).T >= 0.0
    for k in range(6):
        cols = slice(k * 128, k * 128 + 128)
        kept = jnp.where(real, cot_ref[:, cols].astype(F32), 0.0).astype(B16)
        dyp[y, :, cols] = dot(mix, kept).astype(B16)
    for half in range(2):

        @pl.when(y == half)
        def _(half=half):
            buph[...] = bup_ref[half * 1536 : half * 1536 + 1536].reshape(1, 1536)

    wo[y] = wo_own[...]

    def qkv(i):
        rows = xs[pl.ds(2 * i, 2)].reshape(256, 768).astype(F32)
        zz, _inv = norm_parts(rows)
        n1 = (zz * row(g1_ref) + row(b1_ref)).astype(B16)
        m = (dot(n1, wqh[...]) + bqh[...]).astype(B16)
        t = i // 2
        for yy in range(2):
            for par in range(2):
                at = slice(yy * 128 + par * 64, yy * 128 + par * 64 + 64)
                to = pl.ds(pl.multiple_of(par * 256 + (i % 2) * 128 + yy * 64, 64), 64)
                qa[t, to] = m[at, :128] * B16(0.125) + qa[t, to]
                ka[t + 2, to] = m[at, 128:256] + ka[t + 2, to]
                va[t + 2, to] = m[at, 256:]
                ns[t, to] = n1[at]

    def seen(k, blk):
        mail.got(xs.at[blk, :, part[k]], rsx.at[k, blk], p.nx)
        to_core(k, blk)

    def from_core(blk):
        for k in range(3):
            mail.got(xs.at[blk, :, part[k]], rsc.at[k, blk], p.nc)

    fx, fy, fz, fc = p.fb["x"], p.fb["y"], p.fb["z"], p.fb["c"]

    def qkv_of(*flips):
        at = (b + sum(flips)) // 2
        pl.when(p.unit)(lambda: qkv(at))

    def chain(d):
        up, dn = (z - d + 4) % 4, (z + d) % 4
        has_up, has_dn = z >= d, z <= 3 - d
        su, sd = sid(up, x, c), sid(dn, x, c)
        pl.when(has_up)(lambda: mail.got(rows_of(su), rsw.at[su], p.nx))
        if d < 3:
            give(su, (sid((z + 1) % 4, x, c), y), both(has_up, z <= 2))
        give(su, p.nx, has_up)
        give(su, p.nc, has_up)
        pl.when(has_dn)(lambda: mail.got(rows_of(sd), rsw.at[sd], p.nx))
        if d < 3:
            give(sd, (sid((z + 3) % 4, x, c), y), both(has_dn, z >= 1))
        give(sd, p.nx, has_dn)
        give(sd, p.nc, has_dn)

    flips = [[p.fb[d] for d in order[k]] for k in range(3)]
    for k in range(3):
        f = flips[k]
        seen(k, b + f[0])
        pass_on(k, b + f[0], nbr[order[k][1]])
        pass_on(k, b + f[0], nbr[order[k][2]])
        seen(k, b + f[1])
        pass_on(k, b + f[1], nbr[order[k][2]])
        seen(k, b + f[2])
    mail.send(wo.at[y], wo.at[y], rsy.at[0], p.ny)
    mail.send(dyp.at[y], dyp.at[y], rsy.at[1], p.ny)
    qkv_of()
    for k in range(3):
        f = flips[k]
        seen(k, b + f[1] + f[0])
        pass_on(k, b + f[1] + f[0], nbr[order[k][2]])
    for k in range(3):
        f = flips[k]
        seen(k, b + f[2] + f[0])
        seen(k, b + f[2] + f[1])
    qkv_of(fx)
    qkv_of(fz)
    from_core(b + fc)
    from_core(b + fc + fy)
    qkv_of(fc)
    for k in range(3):
        seen(k, b + fx + fy + fz)
    chain(1)
    qkv_of(fx, fz)
    for more in ((fx,), (fz,), (fx, fz)):
        from_core(b + fc + sum(more))
        from_core(b + fc + sum(more) + fy)
        qkv_of(fc, *more)
    for src in (0, 14, 15):
        pl.when(b != src)(lambda src=src: mail.got(docs.at[src], rsd.at[src], p.nx))

    lowlane = iota((256, 128), 1) < 64
    farrows = pl.ds(pl.multiple_of(p.parity * 256, 256), 256)

    @pl.when(first)
    def _():
        for t in range(4):
            kk = ka[t + 2, farrows].astype(F32)
            vv = va[t + 2, farrows].astype(F32)
            kvs[t] = jnp.where(lowlane, kk, pltpu.roll(vv, 64, 1)).astype(B16)

    mail.send(kvs, kvf, rsf.at[0], p.far, first)
    mail.send(docs.at[0], docs.at[16], rsf.at[1], p.far, first)

    def codes(src, par):
        r = docs[src, par : par + 1]
        return jnp.broadcast_to(jnp.where(r < 0.0, 4.0, r), (128, 128)).T[0:64]

    def mark(ref, at, code, query):
        lane = iota((64, 128), 1)
        hit = (lane - 96).astype(F32) == code
        if query:
            feat = jnp.where(hit, 0.0, jnp.where(lane < 101, NEGATIVE, 0.0))
        else:
            feat = jnp.where(hit, 1.0, 0.0)
        ref[at] = jnp.where(lane >= 96, feat, ref[at].astype(F32)).astype(B16)

    @pl.when(first)
    def _():
        for par in range(2):
            code = codes(0, par)
            at = slice(par * 256, par * 256 + 64)
            mark(qa.at[0], at, code, True)
            mark(ka.at[2], at, code, False)

    @pl.when(second)
    def _():
        for par in range(2):
            for yy in range(2):
                code = codes(14 + yy, par)
                at = slice(par * 256 + 128 + yy * 64, par * 256 + 192 + yy * 64)
                mark(qa.at[3], at, code, True)
                mark(ka.at[5], at, code, False)

    @pl.when(p.unit)
    def _():
        for t in range(4):
            vt[t + 2] = va[t + 2].astype(F32).T.astype(B16)

    rr, ll = iota((512, 512), 0), iota((512, 512), 1)
    causal = lambda st: jnp.where(2 * (rr & 255) + (rr >> 8) <= 2 * (ll & 255) + (ll >> 8), st, NEGATIVE)

    def near_attention(t):
        q = qa[t]

        def update(cc, carry, st):
            m, acc = carry
            m_new = jnp.maximum(m, jnp.max(st, axis=0, keepdims=True))
            pr = jnp.exp(st - m_new).astype(B16)
            return m_new, acc * jnp.exp(m - m_new) + dot(vt[cc], pr)

        state = (jnp.full((1, 512), NEGATIVE, F32), jnp.zeros((128, 512), F32))
        if t:
            state = lax.fori_loop(2, t + 2, lambda cc, s: update(cc, s, dot_nt(ka[cc], q)), state)
        msc[t], asc[t] = update(t + 2, state, causal(dot_nt(ka[t + 2], q)))

    def far_ready():
        mail.got(kvf, rsf.at[0], p.far)
        mail.got(docs.at[16], rsf.at[1], p.far)
        for t in range(4):
            rows = pl.ds((t % 2) * 256, 256)
            fpos = ((t * 256 + iota((256, 128), 0)) * 2 + p.parity).astype(F32)
            feat = pick_type(fpos, head, [tab_ref[16 + i : 17 + i] for i in range(5)])
            kv = kvf[t].astype(F32)
            ka[t // 2, rows] = jnp.where(lowlane, kv, feat).astype(B16)
            one = jnp.where(iota((256, 128), 1) == 64, 1.0, 0.0)
            va[t // 2, rows] = jnp.where(lowlane, pltpu.roll(kv, 64, 1), one).astype(B16)
        even, odd = codes(16, 0), codes(16, 1)
        mark(ka.at[0], slice(0, 64), even + p.parity.astype(F32) * (odd - even), False)
        for h in range(2):
            vt[h] = va[h].astype(F32).T.astype(B16)

    farcols = pl.ds(pl.multiple_of(p.parity * 256, 256), 256)

    def far_attention(t):
        q = qa[t, farcols]
        m = msc[t, :, farcols]
        s0, s1 = dot_nt(ka[0], q), dot_nt(ka[1], q)
        m_new = jnp.maximum(m, jnp.maximum(jnp.max(s0, axis=0, keepdims=True), jnp.max(s1, axis=0, keepdims=True)))
        acc = asc[t, :, farcols] * jnp.exp(m - m_new)
        acc = acc + dot(vt[0], jnp.exp(s0 - m_new).astype(B16))
        acc = acc + dot(vt[1], jnp.exp(s1 - m_new).astype(B16))
        msc[t, :, farcols] = m_new
        asc[t, :, farcols] = acc

    def conclude(t):
        acc = asc[t]
        total = acc[64:65]
        o = acc[:64] / total
        lse[t] = msc[t] + jnp.log(total)
        ot[t] = jnp.concatenate([o[:, :256], o[:, 256:]], axis=0)
        osend[t] = ot[t].T.astype(B16)

    def deliver(t, who):
        for cc in range(2):
            for yy in range(2):
                own = both(p.u == t * 2 + cc, y == yy)
                src = osend.at[t, cc * 128 : cc * 128 + 128]
                dev = (sid(seg * 2 + t // 2, t % 2, cc), yy)
                mail.send(src, orecv.at[p.head], rso.at[p.head], dev, both(who, jnp.logical_not(own)))

                @pl.when(both(who, own))
                def _(cc=cc):
                    orecv[p.head] = osend[t, cc * 128 : cc * 128 + 128]

    for t in range(4):
        pl.when(p.unit)(functools.partial(near_attention, t))
        pl.when(first)(functools.partial(conclude, t))
        deliver(t, first)
        if t == 1:
            chain(2)
    chain(3)
    pl.when(second)(far_ready)
    for t in range(4):
        pl.when(second)(functools.partial(far_attention, t))
        pl.when(second)(functools.partial(conclude, t))
        deliver(t, second)
    for zq in range(4):
        s = sid(zq, 1 - x, c)
        mail.got(rows_of(s), rsw.at[s], p.nx)
        give(s, p.nc)

    for hh in range(12):
        mine = both(p.unit, p.head == hh)
        pl.when(jnp.logical_not(mine))(lambda hh=hh: mail.got(orecv.at[hh], rso.at[hh], p.nx))
    for a in range(6):
        e, o = halves(orecv[2 * a].astype(F32), orecv[2 * a + 1].astype(F32))
        attn[0:128, a * 128 : a * 128 + 128] = e.astype(B16)
        attn[128:256, a * 128 : a * 128 + 128] = o.astype(B16)
    mail.got(wo.at[1 - y], rsy.at[0], p.ny)
    mail.got(dyp.at[1 - y], rsy.at[1], p.ny)
    pair = pl.multiple_of(p.u * 2, 2)
    for par in range(2):
        for yy in range(2):
            at = pl.ds(par * 128 + yy * 64, 64)
            hid[at] = xs[pair + yy, par * 64 : par * 64 + 64].astype(F32)
            dys[at] = dyp[yy, par * 64 : par * 64 + 64]
    hid[...] = hid[...] + dot(attn[...], wo[...].reshape(768, 768)) + row(bo_ref)
    z2, _inv = norm_parts(hid[...])
    n2s[...] = (z2 * row(g2_ref) + row(b2_ref)).astype(B16)
    for i in range(8):
        s = sid(i // 2, i % 2, 1 - c)
        mail.got(rows_of(s), rsw.at[s], p.nc)

    facc[...] = jnp.zeros_like(facc)
    dacc[...] = jnp.zeros_like(dacc)
    k0 = 0.7978845608028654
    vb1[z] = jnp.zeros((8, 768), F32)

    def ffn_step(i, _):
        cols = pl.ds(pl.multiple_of(i * 256, 256), 256)
        dcols = pl.ds(pl.multiple_of(1536 + i * 256, 256), 256)
        up, dn = wb[:, cols], wb[:, dcols]
        pre = dot(n2s[...], up) + buph[:, cols]
        sq = pre * pre
        th = jnp.tanh(k0 * pre * (1.0 + 0.044715 * sq))
        half = 0.5 * (1.0 + th)
        act = (pre * half).astype(B16)
        slope = half + 0.5 * pre * (1.0 - th * th) * (k0 * (1.0 + 3.0 * 0.044715 * sq))
        dp = dot(dys[...], dn) * slope
        buph[:, cols] = jnp.sum(dp, axis=0, keepdims=True)
        dpl = dp.astype(B16)
        acts[:, cols] = act
        dpre[:, cols] = dpl
        facc[...] += dot_nt(act, dn)
        dacc[...] += dot_nt(dpl, up)
        return 0

    lax.fori_loop(0, 6, ffn_step, 0)
    ys[...] = dacc[...].astype(B16)
    mail.send(ys, yr, rsy.at[2], p.ny)
    for par in range(2):
        fo[par * 64 : par * 64 + 64] = facc[pl.ds(pl.multiple_of(par * 128 + y * 64, 64), 64)]
        fs[par * 64 : par * 64 + 64] = facc[pl.ds(pl.multiple_of(par * 128 + (1 - y) * 64, 64), 64)].astype(B16)
    mail.send(fs, fr, rsy.at[3], p.ny)

    n2t[...] = n2s[...].astype(F32).T.astype(B16)
    dyt[...] = dys[...].astype(F32).T.astype(B16)

    def owners(ref, xx, cc):
        at = [pl.ds(pl.multiple_of(sid(zz, xx, cc) * 48, 16), 48) for zz in range(4)]
        up = jnp.concatenate([n2t[i] for i in at], axis=0)
        dn = jnp.concatenate([dyt[i] for i in at], axis=0)

        def step(i, _):
            cols = pl.ds(pl.multiple_of(i * 256, 256), 256)
            dcols = pl.ds(pl.multiple_of(1536 + i * 256, 256), 256)
            u = dot(up, dpre[:, cols]).astype(B16)
            d = dot(dn, acts[:, cols]).astype(B16)
            for zz in range(4):
                ref[zz, :, cols] = u[zz * 48 : zz * 48 + 48]
                ref[zz, :, dcols] = d[zz * 48 : zz * 48 + 48]
            return 0

        lax.fori_loop(0, 6, step, 0)

    out_sum = Reduce(p, mail, gwo, hc, hxs, hxr, hzs, hzr, rhc, rhx, rhz)

    def ffn_over_x(k):
        zz = (z + k) % 4
        gb[zz] = (gb[zz].astype(F32) + ra[zz].astype(F32)).astype(B16)
        mail.send(gb.at[zz], gxr.at[zz], rgx.at[zz], p.nx)

    def ffn_column(zz):
        mail.got(gxr.at[zz], rgx.at[zz], p.nx)
        return ge[zz].astype(F32) + rb[zz].astype(F32) + gxr[zz].astype(F32)

    def ffn_over_z(k):
        zz = (z + k) % 4
        ge[zz] = ffn_column(zz).astype(B16)
        mail.send(ge.at[zz], gzr.at[z], rgz.at[z], (sid(zz, x, c), y))

    owners(ga, 1 - x, 1 - c)
    mail.send(ga, ra, rga.at[0], p.nc)
    owners(gb, 1 - x, c)
    mail.got(ra, rga.at[0], p.nc)
    ffn_over_x(2)
    owners(gd, x, 1 - c)
    mail.send(gd, rb, rga.at[1], p.nc)
    owners(ge, x, c)
    mail.got(yr, rsy.at[2], p.ny)
    dn2 = ys[...].astype(F32) + yr[...].astype(F32)
    z2, inv2 = norm_parts(hid[...])
    dh = dys[...].astype(F32) + norm_grad(z2, inv2, dn2 * row(g2_ref))
    facc[...] = dh
    dacc[...] = dn2 * z2
    da_ = dot_nt(dh.astype(B16), wo[y])
    for a in range(3):
        e, o = halves(da_[0:128, a * 128 : a * 128 + 128], da_[128:256, a * 128 : a * 128 + 128])
        dpk[2 * a] = e.astype(B16)
        dpk[2 * a + 1] = o.astype(B16)

    mine_t = p.zl * 2 + x
    crow = pl.ds(pl.multiple_of(c * 128, 128), 128)
    for h, u in enumerate(UNITS):
        mail.send(dpk.at[h], dor.at[mine_t, crow], rdo.at[p.u], (seg * 8 + u, y), p.u != u)

        @pl.when(p.u == u)
        def _(h=h):
            dor[mine_t, crow] = dpk[h]

    for k in (1, 3, 0):
        ffn_over_x(k)
    mail.got(rb, rga.at[1], p.nc)
    gwo[...] = dot(dh.T.astype(B16), attn[:, pl.ds(pl.multiple_of(y * 384, 128), 384)]).astype(B16)
    out_sum.cores()
    mail.got(fr, rsy.at[3], p.ny)
    sums = [jnp.zeros((1, 768), F32)] * 4
    for par in range(2):
        at = pl.ds(pl.multiple_of(par * 128 + y * 64, 64), 64)
        to = slice(par * 64, par * 64 + 64)
        dh_s[to] = facc[at]
        own = (dacc[at], ys[at].astype(F32) + yr[at].astype(F32), facc[at], dys[at].astype(F32))
        sums = [total + jnp.sum(v, axis=0, keepdims=True) for total, v in zip(sums, own)]
        fo[to] = hid[at] + fo[to] + fr[to].astype(F32) + row(bd_ref)
    back = mixed((128, 128), 1, 0)
    lout[...] = dot(back, fo[...].astype(B16)).astype(B16)
    for i in range(4):
        vb1[z, i : i + 1] = sums[i]
    for half in range(2):

        @pl.when(y == half)
        def _(half=half):
            for k in range(2):
                vb1[z, 4 + 2 * half + k : 5 + 2 * half + k] = buph[:, k * 768 : k * 768 + 768]

    early = Total(p, mail, vb1, vr1, rv1, rv2)
    late = Total(p, mail, vb2, vr2, rv3, rv4)
    early.start()

    def prepare():
        for i in range(8):
            pl.when(p.u != i)(lambda i=i: mail.got(dor.at[i // 2, (i % 2) * 128 : (i % 2) * 128 + 128], rdo.at[i], p.nx))
        low = iota((256, 128), 1) < 64
        for t in range(4):
            d = dor[t].astype(F32)
            doa[t, 0:256] = jnp.where(low, d, 0.0).astype(B16)
            doa[t, 256:512] = jnp.where(low, pltpu.roll(d, 64, 1), 0.0).astype(B16)
            prod = d.T * ot[t]
            delta[t, :, 0:256] = jnp.sum(prod[:64], axis=0, keepdims=True)
            delta[t, :, 256:512] = jnp.sum(prod[64:], axis=0, keepdims=True)
            kt[t + 2] = ka[t + 2].astype(F32).T.astype(B16)
        dqt[...] = jnp.zeros_like(dqt)

    pl.when(p.unit)(prepare)

    def score_grads(cc, q, do, st, lse_row, delta_row):
        pr = jnp.exp(st - lse_row)
        ds = (pr * (dot_nt(va[cc], do) - delta_row)).astype(B16)
        dva[...] += dot(pr.astype(B16), do)
        dka[...] += dot(ds, q)
        return dot(kt[cc], ds)

    def clear():
        dka[...] = jnp.zeros_like(dka)
        dva[...] = jnp.zeros_like(dva)

    @pl.when(second)
    def _():
        for h in range(2):
            kt[h] = ka[h].astype(F32).T.astype(B16)

        def chunk(cc, _):
            clear()

            def step(t, _):
                q, do = qa[t, farcols], doa[t, farcols]
                dqt[t, :, farcols] += score_grads(cc, q, do, dot_nt(ka[cc], q), lse[t, :, farcols], delta[t, :, farcols])
                return 0

            lax.fori_loop(0, 4, step, 0)
            low = iota((512, 128), 1) < 64
            pack = jnp.where(low, dka[...], pltpu.roll(dva[...], 64, 1)).astype(B16)
            dfs[2 * cc] = pack[:256]
            dfs[2 * cc + 1] = pack[256:]
            return 0

        lax.fori_loop(0, 2, chunk, 0)

    mail.send(dfs, dfr, rdf.at[0], p.far, second)

    def near(t):
        clear()
        q, do = qa[t], doa[t]
        dqt[t] += score_grads(t + 2, q, do, causal(dot_nt(ka[t + 2], q)), lse[t], delta[t])
        if t < 3:

            def step(tq, _):
                q, do = qa[tq], doa[tq]
                dqt[tq] += score_grads(t + 2, q, do, dot_nt(ka[t + 2], q), lse[tq], delta[tq])
                return 0

            lax.fori_loop(t + 1, 4, step, 0)
        dtt[64:128, t * 512 : t * 512 + 512] = dka[...].T[:64].astype(B16)
        dtt[128:192, t * 512 : t * 512 + 512] = dva[...].T[:64].astype(B16)

    def add_far(t):
        rows = dfr[t].astype(F32).T
        at = pl.ds(pl.multiple_of(t * 512 + p.parity * 256, 256), 256)
        dtt[64:128, at] = (dtt[64:128, at].astype(F32) + rows[:64]).astype(B16)
        dtt[128:192, at] = (dtt[128:192, at].astype(F32) + rows[64:]).astype(B16)

    out_sum.over_x()
    ffn_over_z(2)
    pl.when(p.unit)(lambda: near(0))
    ffn_over_z(1)
    early.middle()
    pl.when(p.unit)(lambda: near(1))
    ffn_over_z(3)
    pl.when(p.unit)(lambda: near(2))
    pl.when(p.unit)(lambda: near(3))

    @pl.when(first)
    def _():
        mail.got(dfr, rdf.at[0], p.far)
        for t in range(4):
            add_far(t)

    @pl.when(p.unit)
    def _():
        for t in range(4):
            dtt[0:64, t * 512 : t * 512 + 512] = (dqt[t, 0:64] * 0.125).astype(B16)
            for k in range(3):
                e = dtt[k * 64 : k * 64 + 64, t * 512 : t * 512 + 256].astype(F32)
                o = dtt[k * 64 : k * 64 + 64, t * 512 + 256 : t * 512 + 512].astype(F32)
                packs[t, k] = jnp.concatenate([e, o], axis=0).T.astype(B16)

    for t in range(4):
        for cc in range(2):
            u = t * 2 + cc
            mail.send(packs.at[t, :, cc * 128 : cc * 128 + 128], dqr.at[p.hl], rdq.at[p.hl], (seg * 8 + u, y), both(p.unit, p.u != u))

            @pl.when(both(p.unit, p.u == u))
            def _(t=t, cc=cc):
                dqr[p.hl] = packs[t, :, cc * 128 : cc * 128 + 128]

    spread = Spread(p, mail, wag, rag, True)

    @pl.when(p.unit)
    def _():
        dw = dot(dtt[...], ns[...].reshape(2048, 768))
        bias = dot_nt(jnp.ones((16, 2048), B16), dtt[...])
        for h in range(2):
            wms[h, 0:96] = dw[h * 96 : h * 96 + 96].astype(B16)
            wms[h, 96:112, 0:192] = bias.astype(B16)
            wms[h, 96:112, 192:768] = jnp.zeros((16, 576), B16)

    mail.send(wms.at[1 - seg], wmr, rwm.at[0], p.far, p.unit)
    for k in range(1, 4):
        out_sum.over_z(k)

    for h, u in enumerate(UNITS):
        pl.when(p.u != u)(lambda h=h: mail.got(dqr.at[h], rdq.at[h], p.nx))
    for k in range(3):
        for a in range(3):
            e, o = halves(dqr[2 * a, k].astype(F32), dqr[2 * a + 1, k].astype(F32))
            col = slice(a * 128, a * 128 + 128)
            dall[k, 0:128, col] = e.astype(B16)
            dall[k, 128:256, col] = o.astype(B16)
    facc[...] = dot_nt(dall[0], wq_ref[0]) + dot_nt(dall[1], wq_ref[1]) + dot_nt(dall[2], wq_ref[2])
    for par in range(2):
        dns[par * 64 : par * 64 + 64] = facc[pl.ds(pl.multiple_of(par * 128 + (1 - y) * 64, 64), 64)].astype(B16)
    mail.send(dns, dnr, rdn.at[0], p.ny)

    @pl.when(p.unit)
    def _():
        mail.got(wmr, rwm.at[0], p.far)
        wag[p.s] = (wms[seg].astype(F32) + wmr[...].astype(F32)).astype(B16)

    spread.first()
    o_total = out_sum.result()
    woag[p.s] = o_total.astype(B16)
    spread_out = Spread(p, mail, woag, rwo, False)
    spread_out.first()
    z1, inv1 = norm_parts(xs[b].astype(F32))
    mail.got(dnr, rdn.at[0], p.ny)
    own = [facc[pl.ds(pl.multiple_of(par * 128 + y * 64, 64), 64)] for par in range(2)]
    dn1 = jnp.concatenate(own, axis=0) + dnr[...].astype(F32)
    vb2[z] = jnp.zeros((8, 768), F32)
    vb2[z, 0:1] = jnp.sum(dn1 * z1, axis=0, keepdims=True)
    vb2[z, 1:2] = jnp.sum(dn1, axis=0, keepdims=True)
    late.start()
    rest = dh_s[...] + norm_grad(z1, inv1, dn1 * row(g1_ref))
    result = jnp.zeros((128, 768), F32)
    for _k in range(3):
        piece = rest.astype(B16)
        result = result + dot(back, piece)
        rest = rest - piece.astype(F32)
    gin[...] = result
    spread.second()
    spread_out.second()
    late.middle()
    total = ffn_column(z)
    for k in range(1, 4):
        zz = (z + k) % 4
        mail.got(gzr.at[zz], rgz.at[zz], p.nx)
        total = total + gzr[zz].astype(F32)
    o_ud[...] = total
    o_tot[0] = early.finish()
    spread.third()
    spread_out.third()
    o_tot[1] = late.finish()
    spread_out.last()
    spread.last()
    mail.close()
    assert mail.used <= SENDS, mail.used


def write_out(lout, gin, wag, woag, ud, tot, o_l, o_g, o_g1, o_b1, o_wq, o_bqv, o_wo, o_bo, o_g2, o_b2, o_up, o_bup, o_dn, o_bd):
    o_l[...] = lout[...]
    o_g[...] = gin[...]
    o_up[...] = ud[:, :1536]
    o_dn[...] = ud[:, 1536:]
    for i, ref in enumerate((o_g2, o_b2, o_bo, o_bd)):
        ref[...] = tot[0, i : i + 1].reshape(768)
    for i in range(4):
        o_bup[i * 768 : i * 768 + 768] = tot[0, 4 + i : 5 + i].reshape(768)
    o_g1[...] = tot[1, 0:1].reshape(768)
    o_b1[...] = tot[1, 1:2].reshape(768)
    o_wo[...] = woag[...].reshape(768, 384).astype(F32).T
    for a in range(3):
        u0, u1 = UNITS[2 * a], UNITS[2 * a + 1]
        col = slice(a * 128, a * 128 + 128)
        w0 = jnp.concatenate([wag[u0, 0:96], wag[u0 + 8, 0:96]], axis=0).astype(F32)
        w1 = jnp.concatenate([wag[u1, 0:96], wag[u1 + 8, 0:96]], axis=0).astype(F32)
        for k in range(3):
            at = slice(k * 64, k * 64 + 64)
            o_wq[k, :, col] = jnp.concatenate([w0[at], w1[at]], axis=0).T
        r0, r1 = wag[u0, 96:112].astype(F32), wag[u1, 96:112].astype(F32)
        low = iota((16, 128), 1) < 64
        for k in range(2):
            at = slice(k * 128, k * 128 + 128)
            o_bqv[k : k + 1, col] = jnp.where(low, r0[:, at], pltpu.roll(r1[:, at], 64, 1))[0:1]


SENDS = 400


def count_table():
    kinds = np.array([[0, 0, 0, 0], [1, 0, 0, 0], [1, 1, 0, 0], [1, 0, 1, 0], [1, 1, 1, 1]], np.float64)
    shared = kinds @ kinds.T
    table = np.zeros((24, 128), np.float64)
    low = lambda v: float(np.asarray(v, dtype=ml_dtypes.bfloat16).astype(np.float64))
    for i in range(5):
        for k in range(5):
            for base, count in ((64, 1.0 + shared[i, k]), (80, shared[i, k])):
                rest = float(np.log(count)) if count > 0 else 0.0
                for e in range(3):
                    table[i, base + 3 * k + e] = low(rest)
                    rest -= low(rest)
        table[i, 96:101] = [NEGATIVE, NEGATIVE, 0.0, NEGATIVE, NEGATIVE]
        table[8 + i, 64 + 3 * i : 67 + 3 * i] = 1.0
        table[16 + i, 80 + 3 * i : 83 + 3 * i] = 1.0
        table[8 + i, 98] = table[16 + i, 98] = 1.0
    return table.astype(np.float32)


def vm(*shape):
    return pltpu.VMEM(shape, B16)


def vf(*shape):
    return pltpu.VMEM(shape, F32)


def dma(*shape):
    return pltpu.SemaphoreType.DMA(shape)


def in_vmem(count):
    return [pl.BlockSpec(memory_space=pltpu.VMEM)] * count


def fast(
    layer_input, doc_ids, cotangent, ln1_gain, ln1_bias, w_qkv, bias_qv, w_out, b_out, ln2_gain, ln2_bias, w_up, b_up, w_down, b_down
):
    out = lambda shape, dtype=F32: jax.ShapeDtypeStruct(shape, dtype)
    shapes = (
        out((128, 768), B16), out((128, 768)), out((768,)), out((768,)), out((3, 768, 384)), out((2, 384)), out((384, 768)), out((768,)),
        out((768,)), out((768,)), out((48, 1536)), out((3072,)), out((48, 1536)), out((768,)),
    )
    raw = (out((128, 768), B16), out((128, 768)), out((16, 112, 768), B16), out((16, 48, 384), B16), out((48, 3072)), out((2, 8, 768)))
    scratch = [
        vm(4, 512, 128), vm(6, 512, 128), vm(6, 512, 128), vm(4, 512, 768), vf(4, 1, 512), vf(4, 128, 256), vm(6, 128, 128),
        vm(768, 384), vf(128, 768), vm(768, 384), vf(1, 384), vf(1, 1536), vf(4, 1, 512), vf(4, 128, 512),
        vm(16, 128, 768), vf(17, 8, 128), vm(768, 3072), vm(2, 384, 768), vm(2, 128, 768), vm(12, 128, 128), vm(4, 256, 128),
        vm(4, 256, 128), vm(4, 256, 128), vm(256, 768), vm(6, 128, 512), vf(256, 768), vm(256, 768), vm(256, 768), vm(256, 1536),
        vm(256, 1536), vf(256, 768), vf(256, 768), vm(256, 768), vm(256, 768), vm(128, 768), vm(128, 768), vf(128, 768),
        vm(4, 256, 128), vm(4, 512, 128), vf(4, 1, 512), vm(6, 128, 512), vf(512, 128), vf(512, 128), vf(4, 128, 512), vm(192, 2048),
        vm(4, 256, 128), vm(4, 256, 128), vm(4, 3, 256, 128), vm(6, 3, 128, 128), vm(2, 112, 768), vm(112, 768),
        vm(768, 256), vm(768, 256), *[vm(4, 48, 3072)] * 8,
        vm(2, 4, 48, 384), vm(4, 48, 384), vm(4, 48, 384), vm(4, 48, 384), vm(4, 48, 384), vm(3, 256, 384), vm(128, 768), vm(128, 768),
        vf(4, 8, 768), vf(8, 8, 768), vf(4, 8, 768), vf(8, 8, 768),
        dma(SENDS), dma(3, 16), dma(3, 16), dma(16), dma(16), dma(12), dma(2), dma(4), dma(8), dma(2), dma(4), dma(4), dma(2, 4), dma(4),
        dma(4), dma(1), dma(6), dma(1), dma(16), dma(16), dma(1), dma(4), dma(8), dma(4), dma(8),
    ]
    args = (
        layer_input, doc_ids, cotangent, ln1_gain, ln1_bias, w_qkv.transpose(1, 0, 2), bias_qv, w_out, b_out, ln2_gain, ln2_bias, w_up,
        b_up, w_down.T, b_down, jnp.asarray(count_table()),
    )
    found = pl.pallas_call(
        kernel, out_shape=raw, in_specs=in_vmem(len(args)), out_specs=tuple(in_vmem(len(raw))), scratch_shapes=scratch,
        compiler_params=pltpu.CompilerParams(collective_id=0, has_side_effects=True, vmem_limit_bytes=LIMIT),
    )(*args)
    outs = pl.pallas_call(
        write_out, out_shape=shapes, in_specs=in_vmem(len(raw)), out_specs=tuple(in_vmem(len(shapes))),
        compiler_params=pltpu.CompilerParams(vmem_limit_bytes=LIMIT),
    )(*found)
    outs = list(outs)
    outs[4] = outs[4].transpose(1, 0, 2)
    outs[12] = outs[12].T
    return tuple(outs)


def from_behind(value, axis, by):
    length = lax.axis_size(axis)
    pairs = [(i, i + by) for i in range(length) if 0 <= i + by < length]
    return lax.ppermute(value, axis, pairs)


def layer_norm(values, gain, shift):
    mean = jnp.mean(values, axis=-1, keepdims=True)
    centred = values - mean
    spread = jnp.mean(centred * centred, axis=-1, keepdims=True)
    return centred * lax.rsqrt(spread + EPS) * gain + shift


def gelu_tanh(values):
    return jax.nn.gelu(values, approximate=True)


def pick_block(length, limit):
    chosen = 1
    for candidate in range(1, min(length, limit) + 1):
        if length % candidate == 0:
            chosen = candidate
    return chosen


def pair_counts(query_pos, key_pos, head_ids):
    total = None
    for factor, rate in LEVELS:
        width = SEG * factor
        same = query_pos[:, :, None] // width == key_pos[:, None, :] // width
        offset = (head_ids % rate)[:, None]
        pick_query = query_pos % width % rate == offset
        pick_key = key_pos % width % rate == offset
        joint = (same & pick_query[:, :, None] & pick_key[:, None, :]).astype(jnp.float32)
        total = joint if total is None else total + joint
    return total


def block_terms(
    query_blk, query_pos, query_doc, key_blk, key_pos, key_doc, head_ids, nearby, scale
):
    scores = (
        jnp.einsum("qhe,khe->hqk", query_blk, key_blk, preferred_element_type=jnp.float32) * scale
    )
    counts = pair_counts(query_pos, key_pos, head_ids)
    same_segment = query_pos[:, :, None] // SEG == key_pos[:, None, :] // SEG
    keep = same_segment if nearby else jnp.logical_not(same_segment)
    allowed = (
        keep
        & (key_pos[:, None, :] <= query_pos[:, :, None])
        & (query_doc[:, :, None] == key_doc[:, None, :])
    )
    return (scores, counts * allowed.astype(jnp.float32))


def per_device(
    layer_input,
    doc_ids,
    cotangent,
    ln1_gain,
    ln1_bias,
    w_qkv,
    bias_qv,
    w_out,
    b_out,
    ln2_gain,
    ln2_bias,
    w_up,
    b_up,
    w_down,
    b_down,
):
    seq_count = lax.axis_size("seq")
    local_heads = HEADS // lax.axis_size("head")
    local_width = local_heads * HEAD_DIM
    scale = HEAD_DIM ** (-0.5)
    f32 = jnp.float32
    b16 = jnp.bfloat16
    x_float = layer_input.astype(f32)
    norm_one = layer_norm(x_float, ln1_gain, ln1_bias)
    norm_rows, row_doc = (
        lax.all_gather(norm_one.astype(b16), "head", axis=0, tiled=True),
        lax.all_gather(doc_ids, "head", axis=0, tiled=True),
    )
    seq_tokens = norm_rows.shape[0]
    half = seq_tokens // 2
    total_tokens = seq_tokens * seq_count
    total_half = total_tokens // 2
    first_pos = lax.axis_index("seq") * seq_tokens
    last_pos = first_pos + seq_tokens - 1
    local_offsets = jnp.arange(seq_tokens, dtype=jnp.int32)
    query_pos = (first_pos + local_offsets)[None, :]
    query_doc = row_doc[None, :]
    head_ids = lax.axis_index("head") * local_heads + jnp.arange(local_heads, dtype=jnp.int32)
    parity = head_ids % 2
    pick_even = parity == 0

    def compact(rows):
        paired = rows.reshape((half, 2) + rows.shape[1:])
        mask = pick_even.reshape((1, local_heads) + (1,) * (rows.ndim - 2))
        return jnp.where(mask, paired[:, 0], paired[:, 1])

    def expand(rows):
        mask = pick_even.reshape((1, local_heads) + (1,) * (rows.ndim - 2))
        zeros = jnp.zeros_like(rows)
        paired = jnp.stack([jnp.where(mask, rows, zeros), jnp.where(mask, zeros, rows)], axis=1)
        return paired.reshape((seq_tokens,) + rows.shape[1:])

    mixed = jnp.einsum("td,dch->tch", norm_rows, w_qkv, preferred_element_type=f32)
    zero_row = jnp.zeros((1, local_width), f32)
    bias_all = jnp.concatenate([bias_qv[0:1], zero_row, bias_qv[1:2]], axis=0)
    qkv = (mixed + bias_all[None]).astype(b16)
    queries = qkv[:, 0]
    query_heads = queries.reshape(seq_tokens, local_heads, HEAD_DIM)
    key_heads = qkv[:, 1].reshape(seq_tokens, local_heads, HEAD_DIM)
    value_heads = qkv[:, 2].reshape(seq_tokens, local_heads, HEAD_DIM)
    local_keys_c = compact(key_heads)
    local_values_c = compact(value_heads)
    far_keys_all, far_values_all, doc_all = (
        lax.all_gather(local_keys_c, "seq", axis=0, tiled=True),
        lax.all_gather(local_values_c, "seq", axis=0, tiled=True),
        lax.all_gather(row_doc, "seq", axis=0, tiled=True),
    )
    segment_count = SEG // seq_tokens
    own_pair = jnp.stack([key_heads, value_heads], axis=1)
    pair_pieces = [own_pair]
    for step in range(1, segment_count):
        pair_pieces.append(from_behind(own_pair, "seq", step))
    near_pairs = jnp.concatenate(pair_pieces, axis=0)
    near_keys = near_pairs[:, 0]
    near_values = near_pairs[:, 1]
    near_flat = jnp.concatenate(
        [first_pos - step * seq_tokens + local_offsets for step in range(segment_count)]
    )
    near_doc = jnp.take(doc_all, jnp.clip(near_flat, 0, total_tokens - 1))[None, :]
    near_pos = near_flat[None, :]
    far_pos = 2 * jnp.arange(total_half, dtype=jnp.int32)[None, :] + parity[:, None]
    doc_pairs = doc_all.reshape(total_half, 2)
    far_doc = jnp.where(pick_even[:, None], doc_pairs[:, 0][None, :], doc_pairs[:, 1][None, :])
    key_block = pick_block(total_half, block_limit)
    blocks = total_half // key_block
    far_key_blocks = far_keys_all.reshape(blocks, key_block, local_heads, HEAD_DIM)
    far_value_blocks = far_values_all.reshape(blocks, key_block, local_heads, HEAD_DIM)
    far_pos_blocks = far_pos.reshape(local_heads, blocks, key_block).transpose(1, 0, 2)
    far_doc_blocks = far_doc.reshape(local_heads, blocks, key_block).transpose(1, 0, 2)
    far_begin = jnp.arange(blocks, dtype=jnp.int32) * (2 * key_block)

    def merge_stats(current, key_blk, key_pos, key_doc, nearby):
        peak, running = current
        scores, counts = block_terms(
            query_heads, query_pos, query_doc, key_blk, key_pos, key_doc, head_ids, nearby, scale
        )
        live = counts > 0
        new_peak = jnp.maximum(peak, jnp.max(jnp.where(live, scores, NEGATIVE), axis=2))
        terms = jnp.where(live, counts * jnp.exp(scores - new_peak[:, :, None]), 0.0)
        return (new_peak, running * jnp.exp(peak - new_peak) + jnp.sum(terms, axis=2))

    start_state = (
        jnp.full((local_heads, seq_tokens), NEGATIVE, f32),
        jnp.zeros((local_heads, seq_tokens), f32),
    )
    near_state = merge_stats(start_state, near_keys, near_pos, near_doc, True)

    def stats_step(state, item):
        key_blk, pos_blk, doc_blk, begin = item
        return (
            lax.cond(
                begin <= last_pos,
                lambda current: merge_stats(current, key_blk, pos_blk, doc_blk, False),
                lambda current: current,
                state,
            ),
            None,
        )

    (peak_all, running_all), _ = lax.scan(
        stats_step, near_state, (far_key_blocks, far_pos_blocks, far_doc_blocks, far_begin)
    )
    lse = peak_all + jnp.log(running_all)

    def add_output(current, key_blk, value_blk, key_pos, key_doc, nearby):
        scores, counts = block_terms(
            query_heads, query_pos, query_doc, key_blk, key_pos, key_doc, head_ids, nearby, scale
        )
        probs = jnp.where(counts > 0, counts * jnp.exp(scores - lse[:, :, None]), 0.0).astype(b16)
        return current + jnp.einsum("hqk,khe->qhe", probs, value_blk, preferred_element_type=f32)

    zero_heads = jnp.zeros((seq_tokens, local_heads, HEAD_DIM), f32)
    near_output = add_output(zero_heads, near_keys, near_values, near_pos, near_doc, True)

    def output_step(accum, item):
        key_blk, value_blk, pos_blk, doc_blk, begin = item
        return (
            lax.cond(
                begin <= last_pos,
                lambda current: add_output(current, key_blk, value_blk, pos_blk, doc_blk, False),
                lambda current: current,
                accum,
            ),
            None,
        )

    attn_exact, _ = lax.scan(
        output_step,
        near_output,
        (far_key_blocks, far_value_blocks, far_pos_blocks, far_doc_blocks, far_begin),
    )
    attn_low = attn_exact.reshape(seq_tokens, local_width).astype(b16)
    branch = lax.psum_scatter(
        jnp.dot(attn_low, w_out, preferred_element_type=f32).astype(jnp.bfloat16),
        "head",
        scatter_dimension=0,
        tiled=True,
    ).astype(jnp.float32)
    hidden_one = x_float + branch + b_out
    norm_two = layer_norm(hidden_one, ln2_gain, ln2_bias)
    norm_low = norm_two.astype(b16)
    dy_low = (cotangent.astype(f32) * (doc_ids >= 0).astype(f32)[:, None]).astype(b16)
    dy_float = dy_low.astype(f32)
    up_rows, down_rows = (
        lax.all_gather(w_up, "seq", axis=0, tiled=True),
        lax.all_gather(w_down, "seq", axis=1, tiled=True),
    )
    up_full, down_full = (
        lax.all_gather(up_rows, "head", axis=1, tiled=True),
        lax.all_gather(down_rows, "head", axis=0, tiled=True),
    )
    pre_act = jnp.dot(norm_low, up_full, preferred_element_type=f32) + b_up
    act_low = gelu_tanh(pre_act).astype(b16)
    ffn_result = jnp.dot(act_low, down_full, preferred_element_type=f32)
    d_act = jnp.einsum("td,fd->tf", dy_low, down_full, preferred_element_type=f32)
    _, gelu_back = jax.vjp(gelu_tanh, pre_act)
    d_pre = gelu_back(d_act)[0]
    d_pre_low = d_pre.astype(b16)
    bias_up_grad = jnp.sum(d_pre, axis=0)
    up_parts = jnp.einsum("td,tf->df", norm_low, d_pre_low, preferred_element_type=f32)
    down_parts = jnp.einsum("tf,td->fd", act_low, dy_low, preferred_element_type=f32)
    up_grad, down_grad = (
        lax.psum_scatter(
            up_parts.astype(jnp.bfloat16), "head", scatter_dimension=1, tiled=True
        ).astype(jnp.float32),
        lax.psum_scatter(
            down_parts.astype(jnp.bfloat16), "head", scatter_dimension=0, tiled=True
        ).astype(jnp.float32),
    )
    d_norm_two = jnp.einsum("tf,df->td", d_pre_low, up_full, preferred_element_type=f32)
    layer_output = (hidden_one + ffn_result + b_down).astype(b16)
    w_up_grad, w_down_grad = (
        lax.psum_scatter(up_grad, "seq", scatter_dimension=0, tiled=True),
        lax.psum_scatter(down_grad, "seq", scatter_dimension=1, tiled=True),
    )
    _, norm_two_back = jax.vjp(layer_norm, hidden_one, ln2_gain, ln2_bias)
    d_hidden_norm, gain_two_grad, bias_two_grad = norm_two_back(d_norm_two)
    d_hidden = dy_float + d_hidden_norm
    bias_out_grad = jnp.sum(d_hidden, axis=0)
    bias_down_grad = jnp.sum(dy_float, axis=0)
    hidden_rows = lax.all_gather(d_hidden.astype(b16), "head", axis=0, tiled=True)
    w_out_part = jnp.einsum("tc,td->cd", attn_low, hidden_rows, preferred_element_type=f32)
    d_attn = jnp.einsum("td,cd->tc", hidden_rows, w_out, preferred_element_type=f32).astype(b16)
    d_attn_heads = d_attn.reshape(seq_tokens, local_heads, HEAD_DIM)
    delta_rows = jnp.sum(d_attn_heads.astype(f32) * attn_exact, axis=2)
    delta = delta_rows.T

    def score_grads(key_blk, value_blk, key_pos, key_doc, nearby):
        scores, counts = block_terms(
            query_heads, query_pos, query_doc, key_blk, key_pos, key_doc, head_ids, nearby, scale
        )
        exact = jnp.where(counts > 0, counts * jnp.exp(scores - lse[:, :, None]), 0.0)
        d_prob = jnp.einsum("qhe,khe->hqk", d_attn_heads, value_blk, preferred_element_type=f32)
        d_score = (exact * (d_prob - delta[:, :, None])).astype(b16)
        return (exact, d_score)

    exact_near, d_score_near = score_grads(near_keys, near_values, near_pos, near_doc, True)
    d_query_near = jnp.einsum("hqk,khe->qhe", d_score_near, near_keys, preferred_element_type=f32)
    near_key_grad = jnp.einsum(
        "hqk,qhe->khe", d_score_near, query_heads, preferred_element_type=f32
    )
    near_value_grad = jnp.einsum(
        "hqk,qhe->khe", exact_near.astype(b16), d_attn_heads, preferred_element_type=f32
    )
    near_pair_grads = jnp.stack([near_key_grad, near_value_grad], axis=1)
    pair_grad = near_pair_grads[:seq_tokens]
    for step in range(1, segment_count):
        piece = near_pair_grads[step * seq_tokens : (step + 1) * seq_tokens]
        pair_grad = pair_grad + from_behind(piece.astype(jnp.bfloat16), "seq", -step).astype(
            piece.dtype
        )

    def query_grad_step(accum, item):
        key_blk, value_blk, pos_blk, doc_blk, begin = item

        def query_compute(current):
            _, d_score = score_grads(key_blk, value_blk, pos_blk, doc_blk, False)
            return current + jnp.einsum(
                "hqk,khe->qhe", d_score, key_blk, preferred_element_type=f32
            )

        return (lax.cond(begin <= last_pos, query_compute, lambda current: current, accum), None)

    d_query, _ = lax.scan(
        query_grad_step,
        d_query_near,
        (far_key_blocks, far_value_blocks, far_pos_blocks, far_doc_blocks, far_begin),
    )
    d_query = d_query * scale
    stats_rows = jnp.stack([compact(lse.T), compact(delta_rows)], axis=1)
    stats_all = lax.all_gather(stats_rows, "seq", axis=0, tiled=True)
    local_key_pos = first_pos + 2 * jnp.arange(half, dtype=jnp.int32)[None, :] + parity[:, None]
    local_key_doc = compact(jnp.broadcast_to(row_doc[:, None], (seq_tokens, local_heads))).T
    zero_compact = jnp.zeros((half, local_heads, HEAD_DIM), f32)
    query_piece = lax.all_gather(compact(query_heads), "seq", axis=0, tiled=True)
    grad_piece = lax.all_gather(compact(d_attn_heads), "seq", axis=0, tiled=True)
    length = query_piece.shape[0]
    size = pick_block(length, block_limit)
    number = length // size
    pos_piece = 2 * jnp.arange(length, dtype=jnp.int32)[None, :] + parity[:, None]
    items = (
        query_piece.reshape(number, size, local_heads, HEAD_DIM),
        grad_piece.reshape(number, size, local_heads, HEAD_DIM),
        stats_all.reshape(number, size, 2, local_heads),
        pos_piece.reshape(local_heads, number, size).transpose(1, 0, 2),
        far_doc.reshape(local_heads, number, size).transpose(1, 0, 2),
    )

    def one_step(current, item):
        query_blk, grad_blk, stats_blk, pos_blk, doc_blk = item

        def one_compute(pair):
            key_grad, value_grad = pair
            scores, counts = block_terms(
                query_blk,
                pos_blk,
                doc_blk,
                local_keys_c,
                local_key_pos,
                local_key_doc,
                head_ids,
                False,
                scale,
            )
            exact = jnp.where(
                counts > 0, counts * jnp.exp(scores - stats_blk[:, 0].T[:, :, None]), 0.0
            )
            d_prob = jnp.einsum(
                "qhe,khe->hqk", grad_blk, local_values_c, preferred_element_type=f32
            )
            d_score = (exact * (d_prob - stats_blk[:, 1].T[:, :, None])).astype(b16)
            key_grad = key_grad + jnp.einsum(
                "hqk,qhe->khe", d_score, query_blk, preferred_element_type=f32
            )
            value_grad = value_grad + jnp.einsum(
                "hqk,qhe->khe", exact.astype(b16), grad_blk, preferred_element_type=f32
            )
            return (key_grad, value_grad)

        return (
            lax.cond(jnp.max(pos_blk) >= first_pos, one_compute, lambda pair: pair, current),
            None,
        )

    result, _ = lax.scan(one_step, (zero_compact, zero_compact), items)
    far_key_grad, far_value_grad = result
    d_key = (pair_grad[:, 0] + expand(far_key_grad)) * scale
    d_value = pair_grad[:, 1] + expand(far_value_grad)
    d_qkv = jnp.stack(
        [
            d_query.reshape(seq_tokens, local_width),
            d_key.reshape(seq_tokens, local_width),
            d_value.reshape(seq_tokens, local_width),
        ],
        axis=1,
    ).astype(b16)
    d_qkv_float = d_qkv.astype(f32)
    bias_qv_part = jnp.stack(
        [jnp.sum(d_qkv_float[:, 0], axis=0), jnp.sum(d_qkv_float[:, 2], axis=0)], axis=0
    )
    w_qkv_part = jnp.einsum("td,tch->dch", norm_rows, d_qkv, preferred_element_type=f32)
    d_norm_one = lax.psum_scatter(
        jnp.einsum("tch,dch->td", d_qkv, w_qkv, preferred_element_type=f32).astype(jnp.bfloat16),
        "head",
        scatter_dimension=0,
        tiled=True,
    ).astype(jnp.float32)
    _, norm_one_back = jax.vjp(layer_norm, x_float, ln1_gain, ln1_bias)
    d_x_norm, gain_one_grad, bias_one_grad = norm_one_back(d_norm_one)
    grad_input = d_hidden + d_x_norm
    w_qkv_grad, bias_qv_grad, w_out_grad = lax.psum((w_qkv_part, bias_qv_part, w_out_part), "seq")
    summed = lax.psum(
        (
            gain_one_grad,
            bias_one_grad,
            gain_two_grad,
            bias_two_grad,
            bias_out_grad,
            bias_up_grad,
            bias_down_grad,
        ),
        ("seq", "head"),
    )
    return (
        layer_output,
        grad_input,
        summed[0],
        summed[1],
        w_qkv_grad,
        bias_qv_grad,
        w_out_grad,
        summed[4],
        summed[2],
        summed[3],
        w_up_grad,
        summed[5],
        w_down_grad,
        summed[6],
    )


def solution(mesh):
    in_specs = (
        P(("seq", "head"), None),
        P(("seq", "head")),
        P(("seq", "head"), None),
        P(),
        P(),
        P(None, None, "head"),
        P(None, "head"),
        P("head", None),
        P(),
        P(),
        P(),
        P("seq", "head"),
        P(),
        P("head", "seq"),
        P(),
    )
    out_specs = (
        P(("seq", "head"), None),
        P(("seq", "head"), None),
        P(),
        P(),
        P(None, None, "head"),
        P(None, "head"),
        P("head", None),
        P(),
        P(),
        P(),
        P("seq", "head"),
        P(),
        P("head", "seq"),
        P(),
    )
    small = mesh.shape["seq"] == 16 and mesh.shape["head"] == 2
    return jax.shard_map(
        fast if small else per_device, mesh=mesh, in_specs=in_specs, out_specs=out_specs, check_vma=False
    )
```

```python
import functools

import jax
import jax.numpy as jnp
import ml_dtypes
import numpy as np
from jax import lax
from jax.experimental import pallas as pl
from jax.experimental.pallas import tpu as pltpu
from jax.sharding import PartitionSpec as P

HEADS = 12
HEAD_DIM = 64
SEG = 2048


LEVELS = ((1, 1), (2, 2), (4, 4), (8, 6), (16, 12))
EPS = 1e-05
NEGATIVE = -1e30
block_limit = 2048


MESH = pl.DeviceIdType.MESH
VMEM = pltpu.VMEM
LIMIT = 60 << 20
F32 = jnp.float32
B16 = jnp.bfloat16


def dot(a, b):
    return jnp.dot(a, b, preferred_element_type=F32)


def dot_nt(a, b):
    return lax.dot_general(a, b, (((1,), (1,)), ((), ())), preferred_element_type=F32)


def sid(z, x, c):
    return z * 4 + x * 2 + c


class Place:
    def __init__(self):
        s = lax.axis_index("seq")
        self.s, self.y = s, lax.axis_index("head")
        self.z, self.x, self.c = s // 4, (s // 2) % 2, s % 2
        self.seg, self.zl = self.z // 2, self.z % 2
        self.u = s % 8
        self.b = self.u * 2 + self.y
        self.unit = jnp.logical_and(self.u != 3, self.u != 5)
        self.hl = self.u - self.u // 4 - self.u // 6
        self.head = self.y * 6 + self.hl
        self.parity = self.head % 2
        z, x, c, y = self.z, self.x, self.c, self.y
        self.zf = z + 1 - 2 * self.zl
        self.nx, self.ny = (sid(z, 1 - x, c), y), (s, 1 - y)
        self.nz, self.nc = (sid(self.zf, x, c), y), (sid(z, x, 1 - c), y)
        self.far = (sid((z + 2) % 4, x, c), y)
        self.fb = {"x": 4 * (1 - 2 * x), "y": 1 - 2 * y, "z": 8 * (1 - 2 * self.zl), "c": 2 * (1 - 2 * c)}

    def cube(self):
        z, x, c, y = self.z, self.x, self.c, self.y
        for k in range(1, 16):
            zz = self.zf if k & 8 else z
            xx = 1 - x if k & 4 else x
            cc = 1 - c if k & 2 else c
            yy = 1 - y if k & 1 else y
            yield (sid(zz, xx, cc), yy)

    def greet(self):
        others = list(self.cube())
        others += [(sid((self.z + 2) % 4, self.x, self.c), self.y), (sid((self.zf + 2) % 4, self.x, self.c), self.y)]
        barrier = pltpu.get_barrier_semaphore()
        for dev in others:
            pl.semaphore_signal(barrier, inc=1, device_id=dev, device_id_type=MESH)
        self.greeted = len(others)

    def meet(self):
        pl.semaphore_wait(pltpu.get_barrier_semaphore(), self.greeted)


class Mail:
    def __init__(self, sems, slots):
        self.sems, self.slots, self.used, self.sent = sems, slots, 0, {}

    def send(self, src, dst, rsem, dev, cond=None):
        k = self.used % self.slots
        self.used += 1
        self.settle(k)

        def make():
            return pltpu.make_async_remote_copy(
                src_ref=src, dst_ref=dst, send_sem=self.sems.at[k], recv_sem=rsem, device_id=dev, device_id_type=MESH
            )

        if cond is None:
            make().start()
        else:
            pl.when(cond)(lambda: make().start())
        self.sent[k] = (cond, make)

    def settle(self, k):
        if k in self.sent:
            cond, make = self.sent.pop(k)
            if cond is None:
                make().wait_send()
            else:
                pl.when(cond)(lambda: make().wait_send())

    def got(self, dst, rsem, dev):
        pltpu.make_async_remote_copy(
            src_ref=dst, dst_ref=dst, send_sem=self.sems.at[0], recv_sem=rsem, device_id=dev, device_id_type=MESH
        ).wait_recv()

    def close(self):
        for k in range(self.slots):
            self.settle(k)


def both(*terms):
    out = terms[0]
    for term in terms[1:]:
        out = jnp.logical_and(out, term)
    return out


def iota(shape, dim):
    return lax.broadcasted_iota(jnp.int32, shape, dim)


def norm_parts(v):
    mean = jnp.mean(v, axis=-1, keepdims=True)
    cen = v - mean
    inv = lax.rsqrt(jnp.mean(cen * cen, axis=-1, keepdims=True) + EPS)
    return cen * inv, inv


def norm_grad(z, inv, e):
    return (e - jnp.mean(e, axis=-1, keepdims=True) - z * jnp.mean(e * z, axis=-1, keepdims=True)) * inv


def pick_type(pos, head, rows):
    v = pos - head + 24.0
    m = v - 12.0 * jnp.floor((v + 0.5) * (1.0 / 12.0))
    out = jnp.where(m == 0.0, rows[4], rows[0])
    out = jnp.where(m == 6.0, rows[3], out)
    out = jnp.where(jnp.logical_or(m == 4.0, m == 8.0), rows[2], out)
    return jnp.where(jnp.logical_or(m == 2.0, m == 10.0), rows[1], out)


def halves(e, o):
    low = iota(e.shape, 1) < 64
    return jnp.where(low, e, pltpu.roll(o, 64, 1)), jnp.where(low, pltpu.roll(e, 64, 1), o)


UNITS = (0, 1, 2, 4, 6, 7)


class Spread:
    def __init__(self, p, mail, ref, sems, some):
        self.p, self.mail, self.ref, self.sems, self.some = p, mail, ref, sems, some

    def has(self, zz, xx, cc):
        return jnp.logical_or(cc == 0, zz % 2 == xx) if self.some else None

    def go(self, s, dev, cond):
        self.mail.send(self.ref.at[s], self.ref.at[s], self.sems.at[s], dev, cond)

    def take(self, s, cond):
        def wait():
            self.mail.got(self.ref.at[s], self.sems.at[s], self.p.nx)

        if cond is None:
            wait()
        else:
            pl.when(cond)(wait)

    def first(self):
        p = self.p
        has = self.has(p.z, p.x, p.c)
        for dev in (p.far, p.nz, p.nx, p.nc):
            self.go(p.s, dev, has)

    def onward(self, zz, devs):
        s, has = sid(zz, self.p.x, self.p.c), self.has(zz, self.p.x, self.p.c)
        self.take(s, has)
        for dev in devs:
            self.go(s, dev, has)

    def second(self):
        p = self.p
        self.onward((p.z + 2) % 4, (p.nz, p.nx, p.nc))
        self.onward(p.zf, (p.nx, p.nc))

    def third(self):
        p = self.p
        self.onward((p.zf + 2) % 4, (p.nx, p.nc))

    def fourth(self):
        p = self.p
        for zz in range(4):
            s, has = sid(zz, 1 - p.x, p.c), self.has(zz, 1 - p.x, p.c)
            self.take(s, has)
            self.go(s, p.nc, has)

    def last(self):
        p = self.p
        for zz in range(4):
            for xx in range(2):
                self.take(sid(zz, xx, 1 - p.c), self.has(zz, xx, 1 - p.c))


class Reduce:
    def __init__(self, p, mail, src, gc, gxs, gxr, gzs, gzr, rc, rx, rz):
        self.__dict__.update(locals())

    def rows(self, zz, xx, cc):
        return pl.ds(pl.multiple_of(sid(zz, xx, cc) * 48, 16), 48)

    def cores(self):
        p = self.p
        for xq in range(2):
            xx = 1 - p.x if xq == 0 else p.x
            for k in (1, 2, 3, 0):
                zz = (p.z + k) % 4
                self.mail.send(self.src.at[self.rows(zz, xx, 1 - p.c)], self.gc.at[xq, zz], self.rc.at[xq, zz], p.nc)

    def order(self):
        z, zf = self.p.z, self.p.zf
        return zf, (zf + 2) % 4, (z + 2) % 4, z

    def over_x(self):
        p = self.p
        for zz in self.order():
            self.mail.got(self.gc.at[0, zz], self.rc.at[0, zz], p.nc)
            own = self.src[self.rows(zz, 1 - p.x, p.c)].astype(F32)
            self.gxs[zz] = (own + self.gc[0, zz].astype(F32)).astype(B16)
            self.mail.send(self.gxs.at[zz], self.gxr.at[zz], self.rx.at[zz], p.nx)

    def column(self, zz):
        p = self.p
        self.mail.got(self.gc.at[1, zz], self.rc.at[1, zz], p.nc)
        self.mail.got(self.gxr.at[zz], self.rx.at[zz], p.nx)
        return self.src[self.rows(zz, p.x, p.c)].astype(F32) + self.gc[1, zz].astype(F32) + self.gxr[zz].astype(F32)

    def over_z(self):
        for i, zz in enumerate(self.order()[:2]):
            self.gzs[i] = self.column(zz).astype(B16)
            self.mail.send(self.gzs.at[i], self.gzr.at[i], self.rz.at[i], self.p.nz)

    def over_far(self):
        self.mail.got(self.gzr.at[1], self.rz.at[1], self.p.nz)
        self.gzs[2] = (self.column((self.p.z + 2) % 4) + self.gzr[1].astype(F32)).astype(B16)
        self.mail.send(self.gzs.at[2], self.gzr.at[2], self.rz.at[2], self.p.far)

    def result(self):
        total = self.column(self.p.z)
        for i in (0, 2):
            self.mail.got(self.gzr.at[i], self.rz.at[i], self.p.nz)
            total = total + self.gzr[i].astype(F32)
        return total


class Total:
    def __init__(self, p, mail, one, two, sem_one, sem_two):
        self.p, self.mail, self.one, self.two, self.sem_one, self.sem_two = p, mail, one, two, sem_one, sem_two
        self.k = (p.x * 2 + p.c) * 2 + p.y

    def start(self):
        p = self.p
        for i in range(1, 4):
            dev = (sid((p.z + i) % 4, p.x, p.c), p.y)
            self.mail.send(self.one.at[p.z], self.one.at[p.z], self.sem_one.at[p.z], dev)

    def middle(self):
        p = self.p
        for i in range(1, 4):
            zz = (p.z + i) % 4
            self.mail.got(self.one.at[zz], self.sem_one.at[zz], p.nx)
        self.two[self.k] = self.one[0] + self.one[1] + self.one[2] + self.one[3]
        for i in range(1, 8):
            xx = 1 - p.x if i & 4 else p.x
            cc = 1 - p.c if i & 2 else p.c
            yy = 1 - p.y if i & 1 else p.y
            self.mail.send(self.two.at[self.k], self.two.at[self.k], self.sem_two.at[self.k], (sid(p.z, xx, cc), yy))

    def finish(self):
        for i in range(8):
            pl.when(self.k != i)(lambda i=i: self.mail.got(self.two.at[i], self.sem_two.at[i], self.p.nx))
        out = self.two[0]
        for i in range(1, 8):
            out = out + self.two[i]
        return out


def mixed(shape, dim_to, dim_from):
    r, i = iota(shape, dim_to), iota(shape, dim_from)
    return jnp.where(i == 2 * (r & 63) + (r >> 6), 1.0, 0.0).astype(B16)


def kernel(
    x_ref, doc_ref, cot_ref, g1_ref, b1_ref, wq_ref, bqv_ref, wo_own, bo_ref, g2_ref, b2_ref, wup_ref, bup_ref, wdn_ref, bd_ref, tab_ref,
    lout, gin, wag, woag, o_ud, o_tot,
    qa, ka, va, ns, lse, ot, dpk, gwo, dh_s, wqh, bqh, buph, msc, asc,
    xs, docs, wb, wo, dyp, orecv, osend, kvs, kvf, attn, vt, hid, n2s, dys, acts, dpre, facc, dacc, ys, yr, fs, fr, fo,
    dor, doa, delta, kt, dka, dva, dqt, dtt, dfs, dfr, packs, dqr, wms, wmr, n2t, dyt, ga, gb, gd, ge, ra, rb, gxr, gzr,
    hc, hxs, hxr, hzs, hzr, dall, dns, dnr, vb1, vr1, vb2, vr2,
    ss, rsx, rsc, rsd, rsw, rso, rsf, rsy, rdo, rga, rgx, rgz, rhc, rhx, rhz, rdf, rdq, rwm, rag, rwo, rdn, rv1, rv2, rv3, rv4,
):
    p = Place()
    mail = Mail(ss, SLOTS)
    seg, x, y, z, c, b = p.seg, p.x, p.y, p.z, p.c, p.b
    first, second = both(p.unit, seg == 0), both(p.unit, seg == 1)
    row = lambda ref: ref[...].reshape(1, -1)
    p.greet()

    mix = mixed((128, 128), 0, 1)
    xs[b] = dot(mix, x_ref[...]).astype(B16)
    doc_row = doc_ref[...].astype(F32).reshape(1, 128)
    turn = jnp.where(iota((128, 128), 0) == 2 * (iota((128, 128), 1) & 63), 1.0, 0.0).astype(B16)
    turn_odd = jnp.where(iota((128, 128), 0) == 2 * (iota((128, 128), 1) & 63) + 1, 1.0, 0.0).astype(B16)
    doc8 = jnp.broadcast_to(doc_row, (8, 128)).astype(B16)
    docs[b] = jnp.where(iota((8, 128), 0) == 0, dot(doc8, turn), dot(doc8, turn_odd))
    wrow = pl.ds(pl.multiple_of(p.s * 48, 16), 48)
    wb[wrow, 0:1536] = wup_ref[...]
    wb[wrow, 1536:3072] = wdn_ref[...]
    p.meet()

    dims = ("x", "y", "z")
    nbr = {"x": p.nx, "y": p.ny, "z": p.nz}
    part = [pl.ds(k * 256, 256) for k in range(3)]
    order = [[dims[(k + j) % 3] for j in range(3)] for k in range(3)]

    bit = {"x": 1, "y": 2, "z": 4}

    def place(rel):
        return b + sum(p.fb[d] for d in dims if rel & bit[d])

    def third(rel, k):
        return xs.at[place(rel), :, part[k]]

    def pass_on(k, rel, d):
        mail.send(third(rel, k), third(rel, k), rsx.at[k, rel ^ bit[d]], nbr[d])

    def to_core(k, rel):
        mail.send(third(rel, k), third(rel, k), rsc.at[k, rel], p.nc)

    for j in range(3):
        for k in range(3):
            pass_on(k, 0, order[k][j])
    for k in range(3):
        to_core(k, 0)
    special = jnp.logical_or(b == 0, b >= 14)
    for dev in p.cube():
        mail.send(docs.at[b], docs.at[b], rsd.at[b // 14 + b // 15], dev, special)

    def rows_of(s):
        return wb.at[pl.ds(pl.multiple_of(s * 48, 16), 48), :]

    def give(s, dev, cond=None):
        mail.send(rows_of(s), rows_of(s), rsw.at[s], dev, cond)

    give(p.s, (sid((z + 1) % 4, x, c), y), z <= 2)
    give(p.s, (sid((z + 3) % 4, x, c), y), z >= 1)
    give(p.s, p.nx)
    give(p.s, p.nc)

    pair_cols = pl.ds(pl.multiple_of(p.hl // 2 * 128, 128), 128)
    for odd in range(2):

        @pl.when(p.hl % 2 == odd)
        def _(odd=odd):
            for k in range(3):
                w = wq_ref[k, :, pair_cols].astype(F32)
                w = pltpu.roll(w, 64, 1) if odd else w
                wqh[:, k * 128 : k * 128 + 128] = jnp.where(iota((768, 128), 1) < 64, w, 0.0).astype(B16)
            v = jnp.concatenate([bqv_ref[:, pair_cols], jnp.zeros((6, 128), F32)], axis=0)
            v = pltpu.roll(v, 64, 1) if odd else v
            lane = iota((1, 128), 1)
            bqh[:, 0:128] = jnp.where(lane < 64, v[0:1], 0.0)
            bqh[:, 128:256] = jnp.zeros((1, 128), F32)
            bqh[:, 256:384] = jnp.where(lane < 64, v[1:2], jnp.where(lane == 64, 1.0, 0.0))

    head = p.head.astype(F32)
    for t in range(4):
        rr = iota((512, 128), 0)
        pos = (seg * SEG + t * 512 + 2 * (rr & 255) + (rr >> 8)).astype(F32)
        qa[t] = pick_type(pos, head, [tab_ref[i : i + 1] for i in range(5)]).astype(B16)
        ka[t + 2] = pick_type(pos, head, [tab_ref[8 + i : 9 + i] for i in range(5)]).astype(B16)

    real = jnp.broadcast_to(doc_row, (128, 128)).T >= 0.0
    for k in range(6):
        cols = slice(k * 128, k * 128 + 128)
        kept = jnp.where(real, cot_ref[:, cols].astype(F32), 0.0).astype(B16)
        dyp[y, :, cols] = dot(mix, kept).astype(B16)
    for half in range(2):

        @pl.when(y == half)
        def _(half=half):
            buph[...] = bup_ref[half * 1536 : half * 1536 + 1536].reshape(1, 1536)

    wo[y] = wo_own[...]

    def qkv(i):
        rows = xs[pl.ds(2 * i, 2)].reshape(256, 768).astype(F32)
        zz, _inv = norm_parts(rows)
        n1 = (zz * row(g1_ref) + row(b1_ref)).astype(B16)
        m = (dot(n1, wqh[...]) + bqh[...]).astype(B16)
        t = i // 2
        for yy in range(2):
            for par in range(2):
                at = slice(yy * 128 + par * 64, yy * 128 + par * 64 + 64)
                to = pl.ds(pl.multiple_of(par * 256 + (i % 2) * 128 + yy * 64, 64), 64)
                qa[t, to] = m[at, :128] * B16(0.125) + qa[t, to]
                ka[t + 2, to] = m[at, 128:256] + ka[t + 2, to]
                va[t + 2, to] = m[at, 256:]
                ns[t, to] = n1[at]

    def seen(k, rel):
        mail.got(third(rel, k), rsx.at[k, rel], p.nx)
        to_core(k, rel)

    def from_core(rel):
        for k in range(3):
            mail.got(xs.at[place(rel) + p.fb["c"], :, part[k]], rsc.at[k, rel], p.nc)

    def qkv_of(rel, core=0):
        at = (place(rel) + core * p.fb["c"]) // 2
        pl.when(p.unit)(lambda: qkv(at))

    def chain(d):
        up, dn = (z - d + 4) % 4, (z + d) % 4
        has_up, has_dn = z >= d, z <= 3 - d
        su, sd = sid(up, x, c), sid(dn, x, c)
        pl.when(has_up)(lambda: mail.got(rows_of(su), rsw.at[su], p.nx))
        if d < 3:
            give(su, (sid((z + 1) % 4, x, c), y), both(has_up, z <= 2))
        give(su, p.nx, has_up)
        give(su, p.nc, has_up)
        pl.when(has_dn)(lambda: mail.got(rows_of(sd), rsw.at[sd], p.nx))
        if d < 3:
            give(sd, (sid((z + 3) % 4, x, c), y), both(has_dn, z >= 1))
        give(sd, p.nx, has_dn)
        give(sd, p.nc, has_dn)

    X, Y, Z = 1, 2, 4
    for k in range(3):
        d0, d1, d2 = order[k]
        seen(k, bit[d0])
        pass_on(k, bit[d0], d1)
        pass_on(k, bit[d0], d2)
        seen(k, bit[d1])
        pass_on(k, bit[d1], d2)
        seen(k, bit[d2])
    qkv_of(0)
    for k in range(3):
        d0, d1, d2 = order[k]
        seen(k, bit[d0] | bit[d1])
        pass_on(k, bit[d0] | bit[d1], d2)
    mail.send(dyp.at[y], dyp.at[y], rsy.at[1], p.ny)
    whalf = pl.ds(pl.multiple_of(c * 192, 64), 192)
    mail.send(wo.at[y, whalf], wo.at[y, whalf], rsy.at[0], p.ny)
    for k in range(3):
        d0, d1, d2 = order[k]
        seen(k, bit[d0] | bit[d2])
        seen(k, bit[d1] | bit[d2])
    qkv_of(X)
    qkv_of(Z)
    from_core(0)
    from_core(Y)
    qkv_of(0, 1)
    for k in range(3):
        seen(k, X | Y | Z)
    chain(1)
    qkv_of(X | Z)
    for rel in (X, Z, X | Z):
        from_core(rel)
        from_core(rel | Y)
        qkv_of(rel, 1)
    for src in (0, 14, 15):
        pl.when(b != src)(lambda src=src: mail.got(docs.at[src], rsd.at[src // 14 + src // 15], p.nx))

    lowlane = iota((256, 128), 1) < 64
    farrows = pl.ds(pl.multiple_of(p.parity * 256, 256), 256)

    @pl.when(first)
    def _():
        for t in range(4):
            kk = ka[t + 2, farrows].astype(F32)
            vv = va[t + 2, farrows].astype(F32)
            kvs[t] = jnp.where(lowlane, kk, pltpu.roll(vv, 64, 1)).astype(B16)

    mail.send(kvs, kvf, rsf.at[0], p.far, first)
    mail.send(docs.at[0], docs.at[16], rsf.at[1], p.far, first)

    def codes(src, par):
        r = docs[src, par : par + 1]
        return jnp.broadcast_to(jnp.where(r < 0.0, 4.0, r), (128, 128)).T[0:64]

    def mark(ref, at, code, query):
        lane = iota((64, 128), 1)
        hit = (lane - 96).astype(F32) == code
        if query:
            feat = jnp.where(hit, 0.0, jnp.where(lane < 101, NEGATIVE, 0.0))
        else:
            feat = jnp.where(hit, 1.0, 0.0)
        ref[at] = jnp.where(lane >= 96, feat, ref[at].astype(F32)).astype(B16)

    @pl.when(first)
    def _():
        for par in range(2):
            code = codes(0, par)
            at = slice(par * 256, par * 256 + 64)
            mark(qa.at[0], at, code, True)
            mark(ka.at[2], at, code, False)

    @pl.when(second)
    def _():
        for par in range(2):
            for yy in range(2):
                code = codes(14 + yy, par)
                at = slice(par * 256 + 128 + yy * 64, par * 256 + 192 + yy * 64)
                mark(qa.at[3], at, code, True)
                mark(ka.at[5], at, code, False)

    @pl.when(p.unit)
    def _():
        for t in range(4):
            vt[t + 2] = va[t + 2].astype(F32).T.astype(B16)

    rr, ll = iota((512, 512), 0), iota((512, 512), 1)
    causal = lambda st: jnp.where(2 * (rr & 255) + (rr >> 8) <= 2 * (ll & 255) + (ll >> 8), st, NEGATIVE)

    def near_attention(t):
        q = qa[t]

        def update(cc, carry, st):
            m, acc = carry
            m_new = jnp.maximum(m, jnp.max(st, axis=0, keepdims=True))
            pr = jnp.exp(st - m_new).astype(B16)
            return m_new, acc * jnp.exp(m - m_new) + dot(vt[cc], pr)

        state = (jnp.full((1, 512), NEGATIVE, F32), jnp.zeros((128, 512), F32))
        if t:
            state = lax.fori_loop(2, t + 2, lambda cc, s: update(cc, s, dot_nt(ka[cc], q)), state)
        msc[t], asc[t] = update(t + 2, state, causal(dot_nt(ka[t + 2], q)))

    def far_ready():
        mail.got(kvf, rsf.at[0], p.far)
        mail.got(docs.at[16], rsf.at[1], p.far)
        for t in range(4):
            rows = pl.ds((t % 2) * 256, 256)
            fpos = ((t * 256 + iota((256, 128), 0)) * 2 + p.parity).astype(F32)
            feat = pick_type(fpos, head, [tab_ref[16 + i : 17 + i] for i in range(5)])
            kv = kvf[t].astype(F32)
            ka[t // 2, rows] = jnp.where(lowlane, kv, feat).astype(B16)
            one = jnp.where(iota((256, 128), 1) == 64, 1.0, 0.0)
            va[t // 2, rows] = jnp.where(lowlane, pltpu.roll(kv, 64, 1), one).astype(B16)
        even, odd = codes(16, 0), codes(16, 1)
        mark(ka.at[0], slice(0, 64), even + p.parity.astype(F32) * (odd - even), False)
        for h in range(2):
            vt[h] = va[h].astype(F32).T.astype(B16)

    farcols = pl.ds(pl.multiple_of(p.parity * 256, 256), 256)

    def far_attention(t):
        q = qa[t, farcols]
        m = msc[t, :, farcols]
        s0, s1 = dot_nt(ka[0], q), dot_nt(ka[1], q)
        m_new = jnp.maximum(m, jnp.maximum(jnp.max(s0, axis=0, keepdims=True), jnp.max(s1, axis=0, keepdims=True)))
        acc = asc[t, :, farcols] * jnp.exp(m - m_new)
        acc = acc + dot(vt[0], jnp.exp(s0 - m_new).astype(B16))
        acc = acc + dot(vt[1], jnp.exp(s1 - m_new).astype(B16))
        msc[t, :, farcols] = m_new
        asc[t, :, farcols] = acc

    def conclude(t):
        acc = asc[t]
        total = acc[64:65]
        o = acc[:64] / total
        lse[t] = msc[t] + jnp.log(total)
        ot[t] = jnp.concatenate([o[:, :256], o[:, 256:]], axis=0)
        osend[t] = ot[t].T.astype(B16)

    def deliver(t, who):
        for cc in range(2):
            for yy in range(2):
                own = both(p.u == t * 2 + cc, y == yy)
                src = osend.at[t, cc * 128 : cc * 128 + 128]
                dev = (sid(seg * 2 + t // 2, t % 2, cc), yy)
                mail.send(src, orecv.at[p.head], rso.at[p.head], dev, both(who, jnp.logical_not(own)))

                @pl.when(both(who, own))
                def _(cc=cc):
                    orecv[p.head] = osend[t, cc * 128 : cc * 128 + 128]

    for t in range(4):
        pl.when(p.unit)(functools.partial(near_attention, t))
        pl.when(first)(functools.partial(conclude, t))
        deliver(t, first)
        if t == 1:
            chain(2)
            mail.got(wo.at[1 - y, whalf], rsy.at[0], p.ny)
            mail.send(wo.at[1 - y, whalf], wo.at[1 - y, whalf], rsy.at[4], p.nc)
    chain(3)
    pl.when(second)(far_ready)
    for t in range(4):
        pl.when(second)(functools.partial(far_attention, t))
        pl.when(second)(functools.partial(conclude, t))
        deliver(t, second)
    for zq in range(4):
        s = sid(zq, 1 - x, c)
        mail.got(rows_of(s), rsw.at[s], p.nx)
        give(s, p.nc)

    for hh in range(12):
        mine = both(p.unit, p.head == hh)
        pl.when(jnp.logical_not(mine))(lambda hh=hh: mail.got(orecv.at[hh], rso.at[hh], p.nx))
    for a in range(6):
        e, o = halves(orecv[2 * a].astype(F32), orecv[2 * a + 1].astype(F32))
        attn[0:128, a * 128 : a * 128 + 128] = e.astype(B16)
        attn[128:256, a * 128 : a * 128 + 128] = o.astype(B16)
    mail.got(wo.at[1 - y, pl.ds(pl.multiple_of((1 - c) * 192, 64), 192)], rsy.at[4], p.nc)
    mail.got(dyp.at[1 - y], rsy.at[1], p.ny)
    pair = pl.multiple_of(p.u * 2, 2)
    for par in range(2):
        for yy in range(2):
            at = pl.ds(par * 128 + yy * 64, 64)
            hid[at] = xs[pair + yy, par * 64 : par * 64 + 64].astype(F32)
            dys[at] = dyp[yy, par * 64 : par * 64 + 64]
    hid[...] = hid[...] + dot(attn[...], wo[...].reshape(768, 768)) + row(bo_ref)
    z2, _inv = norm_parts(hid[...])
    n2s[...] = (z2 * row(g2_ref) + row(b2_ref)).astype(B16)
    for i in range(8):
        s = sid(i // 2, i % 2, 1 - c)
        mail.got(rows_of(s), rsw.at[s], p.nc)

    facc[...] = jnp.zeros_like(facc)
    dacc[...] = jnp.zeros_like(dacc)
    k0 = 0.7978845608028654
    vb1[z] = jnp.zeros((8, 768), F32)

    def ffn_step(i, _):
        cols = pl.ds(pl.multiple_of(i * 256, 256), 256)
        dcols = pl.ds(pl.multiple_of(1536 + i * 256, 256), 256)
        up, dn = wb[:, cols], wb[:, dcols]
        pre = dot(n2s[...], up) + buph[:, cols]
        sq = pre * pre
        th = jnp.tanh(k0 * pre * (1.0 + 0.044715 * sq))
        half = 0.5 * (1.0 + th)
        act = (pre * half).astype(B16)
        slope = half + 0.5 * pre * (1.0 - th * th) * (k0 * (1.0 + 3.0 * 0.044715 * sq))
        dp = dot(dys[...], dn) * slope
        buph[:, cols] = jnp.sum(dp, axis=0, keepdims=True)
        dpl = dp.astype(B16)
        acts[:, cols] = act
        dpre[:, cols] = dpl
        facc[...] += dot_nt(act, dn)
        dacc[...] += dot_nt(dpl, up)
        return 0

    lax.fori_loop(0, 6, ffn_step, 0)
    ys[...] = dacc[...].astype(B16)
    mail.send(ys, yr, rsy.at[2], p.ny)
    for par in range(2):
        fo[par * 64 : par * 64 + 64] = facc[pl.ds(pl.multiple_of(par * 128 + y * 64, 64), 64)]
        fs[par * 64 : par * 64 + 64] = facc[pl.ds(pl.multiple_of(par * 128 + (1 - y) * 64, 64), 64)].astype(B16)

    n2t[...] = n2s[...].astype(F32).T.astype(B16)
    dyt[...] = dys[...].astype(F32).T.astype(B16)

    def owners(ref, xx, cc):
        at = [pl.ds(pl.multiple_of(sid(zz, xx, cc) * 48, 16), 48) for zz in range(4)]
        up = jnp.concatenate([n2t[i] for i in at], axis=0)
        dn = jnp.concatenate([dyt[i] for i in at], axis=0)

        def step(i, _):
            cols = pl.ds(pl.multiple_of(i * 256, 256), 256)
            dcols = pl.ds(pl.multiple_of(1536 + i * 256, 256), 256)
            u = dot(up, dpre[:, cols]).astype(B16)
            d = dot(dn, acts[:, cols]).astype(B16)
            for zz in range(4):
                ref[zz, :, cols] = u[zz * 48 : zz * 48 + 48]
                ref[zz, :, dcols] = d[zz * 48 : zz * 48 + 48]
            return 0

        lax.fori_loop(0, 6, step, 0)

    out_sum = Reduce(p, mail, gwo, hc, hxs, hxr, hzs, hzr, rhc, rhx, rhz)

    def ffn_over_x(i):
        zz = ring[i]
        gb[zz] = (gb[zz].astype(F32) + ra[zz].astype(F32)).astype(B16)
        mail.send(gb.at[zz], gxr.at[zz], rgx.at[zz], p.nx)

    def ffn_column(zz):
        mail.got(gxr.at[zz], rgx.at[zz], p.nx)
        return ge[zz].astype(F32) + rb[zz].astype(F32) + gxr[zz].astype(F32)

    def ffn_over_z(i):
        zz = ring[i]
        ge[zz] = ffn_column(zz).astype(B16)
        mail.send(ge.at[zz], gzr.at[i], rgz.at[i], p.nz)

    def ffn_over_far():
        zz = ring[2]
        mail.got(gzr.at[1], rgz.at[1], p.nz)
        ge[zz] = (ffn_column(zz) + gzr[1].astype(F32)).astype(B16)
        mail.send(ge.at[zz], gzr.at[2], rgz.at[2], p.far)

    ring = out_sum.order()
    owners(ga, 1 - x, 1 - c)
    mail.send(ga, ra, rga.at[0], p.nc)
    owners(gb, 1 - x, c)
    mail.got(ra, rga.at[0], p.nc)
    ffn_over_x(0)
    owners(gd, x, 1 - c)
    mail.send(gd, rb, rga.at[1], p.nc)
    owners(ge, x, c)
    mail.got(yr, rsy.at[2], p.ny)
    mail.send(fs, fr, rsy.at[3], p.ny)
    dn2 = ys[...].astype(F32) + yr[...].astype(F32)
    z2, inv2 = norm_parts(hid[...])
    dh = dys[...].astype(F32) + norm_grad(z2, inv2, dn2 * row(g2_ref))
    facc[...] = dh
    dacc[...] = dn2 * z2
    da_ = dot_nt(dh.astype(B16), wo[y])
    for a in range(3):
        e, o = halves(da_[0:128, a * 128 : a * 128 + 128], da_[128:256, a * 128 : a * 128 + 128])
        dpk[2 * a] = e.astype(B16)
        dpk[2 * a + 1] = o.astype(B16)

    mine_t = p.zl * 2 + x
    crow = pl.ds(pl.multiple_of(c * 128, 128), 128)
    for h, u in enumerate(UNITS):
        mail.send(dpk.at[h], dor.at[mine_t, crow], rdo.at[p.u], (seg * 8 + u, y), p.u != u)

        @pl.when(p.u == u)
        def _(h=h):
            dor[mine_t, crow] = dpk[h]

    for i in (1, 2, 3):
        ffn_over_x(i)
    mail.got(rb, rga.at[1], p.nc)
    ffn_over_z(0)
    gwo[...] = dot(dh.T.astype(B16), attn[:, pl.ds(pl.multiple_of(y * 384, 128), 384)]).astype(B16)
    out_sum.cores()
    mail.got(fr, rsy.at[3], p.ny)
    sums = [jnp.zeros((1, 768), F32)] * 4
    for par in range(2):
        at = pl.ds(pl.multiple_of(par * 128 + y * 64, 64), 64)
        to = slice(par * 64, par * 64 + 64)
        dh_s[to] = facc[at]
        own = (dacc[at], ys[at].astype(F32) + yr[at].astype(F32), facc[at], dys[at].astype(F32))
        sums = [total + jnp.sum(v, axis=0, keepdims=True) for total, v in zip(sums, own)]
        fo[to] = hid[at] + fo[to] + fr[to].astype(F32) + row(bd_ref)
    back = mixed((128, 128), 1, 0)
    lout[...] = dot(back, fo[...].astype(B16)).astype(B16)
    for i in range(4):
        vb1[z, i : i + 1] = sums[i]
    for half in range(2):

        @pl.when(y == half)
        def _(half=half):
            for k in range(2):
                vb1[z, 4 + 2 * half + k : 5 + 2 * half + k] = buph[:, k * 768 : k * 768 + 768]

    early = Total(p, mail, vb1, vr1, rv1, rv2)
    late = Total(p, mail, vb2, vr2, rv3, rv4)
    early.start()

    def prepare():
        for i in range(8):
            pl.when(p.u != i)(lambda i=i: mail.got(dor.at[i // 2, (i % 2) * 128 : (i % 2) * 128 + 128], rdo.at[i], p.nx))
        low = iota((256, 128), 1) < 64
        for t in range(4):
            d = dor[t].astype(F32)
            doa[t, 0:256] = jnp.where(low, d, 0.0).astype(B16)
            doa[t, 256:512] = jnp.where(low, pltpu.roll(d, 64, 1), 0.0).astype(B16)
            prod = d.T * ot[t]
            delta[t, :, 0:256] = jnp.sum(prod[:64], axis=0, keepdims=True)
            delta[t, :, 256:512] = jnp.sum(prod[64:], axis=0, keepdims=True)
            kt[t + 2] = ka[t + 2].astype(F32).T.astype(B16)
        dqt[...] = jnp.zeros_like(dqt)

    pl.when(p.unit)(prepare)

    def score_grads(cc, q, do, st, lse_row, delta_row):
        pr = jnp.exp(st - lse_row)
        ds = (pr * (dot_nt(va[cc], do) - delta_row)).astype(B16)
        dva[...] += dot(pr.astype(B16), do)
        dka[...] += dot(ds, q)
        return dot(kt[cc], ds)

    def clear():
        dka[...] = jnp.zeros_like(dka)
        dva[...] = jnp.zeros_like(dva)

    @pl.when(second)
    def _():
        for h in range(2):
            kt[h] = ka[h].astype(F32).T.astype(B16)

        def chunk(cc, _):
            clear()

            def step(t, _):
                q, do = qa[t, farcols], doa[t, farcols]
                dqt[t, :, farcols] += score_grads(cc, q, do, dot_nt(ka[cc], q), lse[t, :, farcols], delta[t, :, farcols])
                return 0

            lax.fori_loop(0, 4, step, 0)
            low = iota((512, 128), 1) < 64
            pack = jnp.where(low, dka[...], pltpu.roll(dva[...], 64, 1)).astype(B16)
            dfs[2 * cc] = pack[:256]
            dfs[2 * cc + 1] = pack[256:]
            return 0

        lax.fori_loop(0, 2, chunk, 0)

    mail.send(dfs, dfr, rdf.at[0], p.far, second)

    def near(t):
        clear()
        q, do = qa[t], doa[t]
        dqt[t] += score_grads(t + 2, q, do, causal(dot_nt(ka[t + 2], q)), lse[t], delta[t])
        if t < 3:

            def step(tq, _):
                q, do = qa[tq], doa[tq]
                dqt[tq] += score_grads(t + 2, q, do, dot_nt(ka[t + 2], q), lse[tq], delta[tq])
                return 0

            lax.fori_loop(t + 1, 4, step, 0)
        dtt[64:128, t * 512 : t * 512 + 512] = dka[...].T[:64].astype(B16)
        dtt[128:192, t * 512 : t * 512 + 512] = dva[...].T[:64].astype(B16)

    def add_far(t):
        rows = dfr[t].astype(F32).T
        at = pl.ds(pl.multiple_of(t * 512 + p.parity * 256, 256), 256)
        dtt[64:128, at] = (dtt[64:128, at].astype(F32) + rows[:64]).astype(B16)
        dtt[128:192, at] = (dtt[128:192, at].astype(F32) + rows[64:]).astype(B16)

    ffn_over_z(1)
    out_sum.over_x()
    pl.when(p.unit)(lambda: near(0))
    out_sum.over_z()
    early.middle()
    pl.when(p.unit)(lambda: near(1))
    ffn_over_far()
    out_sum.over_far()
    pl.when(p.unit)(lambda: near(2))
    pl.when(p.unit)(lambda: near(3))
    woag[p.s] = out_sum.result().astype(B16)
    spread_out = Spread(p, mail, woag, rwo, False)
    spread_out.first()

    @pl.when(first)
    def _():
        mail.got(dfr, rdf.at[0], p.far)
        for t in range(4):
            add_far(t)

    @pl.when(p.unit)
    def _():
        for t in range(4):
            dtt[0:64, t * 512 : t * 512 + 512] = (dqt[t, 0:64] * 0.125).astype(B16)
            for k in range(3):
                e = dtt[k * 64 : k * 64 + 64, t * 512 : t * 512 + 256].astype(F32)
                o = dtt[k * 64 : k * 64 + 64, t * 512 + 256 : t * 512 + 512].astype(F32)
                packs[t, k] = jnp.concatenate([e, o], axis=0).T.astype(B16)

    for t in range(4):
        for cc in range(2):
            u = t * 2 + cc
            mail.send(packs.at[t, :, cc * 128 : cc * 128 + 128], dqr.at[p.hl], rdq.at[p.hl], (seg * 8 + u, y), both(p.unit, p.u != u))

            @pl.when(both(p.unit, p.u == u))
            def _(t=t, cc=cc):
                dqr[p.hl] = packs[t, :, cc * 128 : cc * 128 + 128]

    vb2[z] = jnp.zeros((8, 768), F32)
    spread = Spread(p, mail, wag, rag, True)

    @pl.when(p.unit)
    def _():
        dw = dot(dtt[...], ns[...].reshape(2048, 768))
        for h in range(2):
            wms[h] = dw[h * 96 : h * 96 + 96].astype(B16)
        bias = dot_nt(jnp.ones((16, 2048), B16), dtt[...])[0:8]
        at = pl.ds(pl.multiple_of(p.head // 2 * 128, 128), 128)
        lane = iota((8, 128), 1) < 64
        low_q, low_v = jnp.where(lane, bias[:, 0:128], 0.0), jnp.concatenate([bias[:, 128:192], jnp.zeros((8, 64), F32)], axis=1)
        for odd in range(2):

            @pl.when(p.head % 2 == odd)
            def _(odd=odd):
                for i, v in enumerate((low_q, low_v)):
                    vb2[z, 2 + i : 3 + i, at] = (pltpu.roll(v, 64, 1) if odd else v)[0:1]

    mail.send(wms.at[1 - seg], wmr, rwm.at[0], p.far, p.unit)

    for h, u in enumerate(UNITS):
        pl.when(p.u != u)(lambda h=h: mail.got(dqr.at[h], rdq.at[h], p.nx))
    for k in range(3):
        for a in range(3):
            e, o = halves(dqr[2 * a, k].astype(F32), dqr[2 * a + 1, k].astype(F32))
            col = slice(a * 128, a * 128 + 128)
            dall[k, 0:128, col] = e.astype(B16)
            dall[k, 128:256, col] = o.astype(B16)
    facc[...] = dot_nt(dall[0], wq_ref[0]) + dot_nt(dall[1], wq_ref[1]) + dot_nt(dall[2], wq_ref[2])
    for par in range(2):
        dns[par * 64 : par * 64 + 64] = facc[pl.ds(pl.multiple_of(par * 128 + (1 - y) * 64, 64), 64)].astype(B16)
    mail.send(dns, dnr, rdn.at[0], p.ny)

    @pl.when(p.unit)
    def _():
        mail.got(wmr, rwm.at[0], p.far)
        wag[p.s] = (wms[seg].astype(F32) + wmr[...].astype(F32)).astype(B16)

    spread.first()
    spread_out.second()
    z1, inv1 = norm_parts(xs[b].astype(F32))
    mail.got(dnr, rdn.at[0], p.ny)
    own = [facc[pl.ds(pl.multiple_of(par * 128 + y * 64, 64), 64)] for par in range(2)]
    dn1 = jnp.concatenate(own, axis=0) + dnr[...].astype(F32)
    vb2[z, 0:1] = jnp.sum(dn1 * z1, axis=0, keepdims=True)
    vb2[z, 1:2] = jnp.sum(dn1, axis=0, keepdims=True)
    late.start()
    rest = dh_s[...] + norm_grad(z1, inv1, dn1 * row(g1_ref))
    result = jnp.zeros((128, 768), F32)
    for _k in range(3):
        piece = rest.astype(B16)
        result = result + dot(back, piece)
        rest = rest - piece.astype(F32)
    gin[...] = result
    spread.second()
    spread_out.third()
    late.middle()
    total = ffn_column(z)
    for i in (0, 2):
        mail.got(gzr.at[i], rgz.at[i], p.nz)
        total = total + gzr[i].astype(F32)
    o_ud[...] = total
    spread.third()
    spread_out.fourth()
    o_tot[0] = early.finish()
    spread.fourth()
    o_tot[1] = late.finish()
    spread_out.last()
    spread.last()
    mail.close()


def write_out(lout, gin, wag, woag, ud, tot, o_l, o_g, o_g1, o_b1, o_wq, o_bqv, o_wo, o_bo, o_g2, o_b2, o_up, o_bup, o_dn, o_bd):
    o_l[...] = lout[...]
    o_g[...] = gin[...]
    o_up[...] = ud[:, :1536]
    o_dn[...] = ud[:, 1536:]
    for i, ref in enumerate((o_g2, o_b2, o_bo, o_bd)):
        ref[...] = tot[0, i : i + 1].reshape(768)
    for i in range(4):
        o_bup[i * 768 : i * 768 + 768] = tot[0, 4 + i : 5 + i].reshape(768)
    o_g1[...] = tot[1, 0:1].reshape(768)
    o_b1[...] = tot[1, 1:2].reshape(768)
    o_wo[...] = woag[...].reshape(768, 384).astype(F32).T
    for a in range(3):
        u0, u1 = UNITS[2 * a], UNITS[2 * a + 1]
        col = slice(a * 128, a * 128 + 128)
        w0 = jnp.concatenate([wag[u0, 0:96], wag[u0 + 8, 0:96]], axis=0).astype(F32)
        w1 = jnp.concatenate([wag[u1, 0:96], wag[u1 + 8, 0:96]], axis=0).astype(F32)
        for k in range(3):
            at = slice(k * 64, k * 64 + 64)
            o_wq[k, :, col] = jnp.concatenate([w0[at], w1[at]], axis=0).T
    half = lax.axis_index("head")
    o_bqv[...] = tot[1, 2:4, pl.ds(pl.multiple_of(half * 384, 128), 384)]


SLOTS = 64


def count_table():
    kinds = np.array([[0, 0, 0, 0], [1, 0, 0, 0], [1, 1, 0, 0], [1, 0, 1, 0], [1, 1, 1, 1]], np.float64)
    shared = kinds @ kinds.T
    table = np.zeros((24, 128), np.float64)
    low = lambda v: float(np.asarray(v, dtype=ml_dtypes.bfloat16).astype(np.float64))
    for i in range(5):
        for k in range(5):
            for base, count in ((64, 1.0 + shared[i, k]), (80, shared[i, k])):
                rest = float(np.log(count)) if count > 0 else 0.0
                for e in range(3):
                    table[i, base + 3 * k + e] = low(rest)
                    rest -= low(rest)
        table[i, 96:101] = [NEGATIVE, NEGATIVE, 0.0, NEGATIVE, NEGATIVE]
        table[8 + i, 64 + 3 * i : 67 + 3 * i] = 1.0
        table[16 + i, 80 + 3 * i : 83 + 3 * i] = 1.0
        table[8 + i, 98] = table[16 + i, 98] = 1.0
    return table.astype(np.float32)


def vm(*shape):
    return pltpu.VMEM(shape, B16)


def vf(*shape):
    return pltpu.VMEM(shape, F32)


def dma(*shape):
    return pltpu.SemaphoreType.DMA(shape)


def in_vmem(count):
    return [pl.BlockSpec(memory_space=pltpu.VMEM)] * count


def fast(
    layer_input, doc_ids, cotangent, ln1_gain, ln1_bias, w_qkv, bias_qv, w_out, b_out, ln2_gain, ln2_bias, w_up, b_up, w_down, b_down
):
    out = lambda shape, dtype=F32: jax.ShapeDtypeStruct(shape, dtype)
    shapes = (
        out((128, 768), B16), out((128, 768)), out((768,)), out((768,)), out((3, 768, 384)), out((2, 384)), out((384, 768)), out((768,)),
        out((768,)), out((768,)), out((48, 1536)), out((3072,)), out((48, 1536)), out((768,)),
    )
    raw = (out((128, 768), B16), out((128, 768)), out((16, 96, 768), B16), out((16, 48, 384), B16), out((48, 3072)), out((2, 8, 768)))
    scratch = [
        vm(4, 512, 128), vm(6, 512, 128), vm(6, 512, 128), vm(4, 512, 768), vf(4, 1, 512), vf(4, 128, 256), vm(6, 128, 128),
        vm(768, 384), vf(128, 768), vm(768, 384), vf(1, 384), vf(1, 1536), vf(4, 1, 512), vf(4, 128, 512),
        vm(16, 128, 768), vf(17, 8, 128), vm(768, 3072), vm(2, 384, 768), vm(2, 128, 768), vm(12, 128, 128), vm(4, 256, 128),
        vm(4, 256, 128), vm(4, 256, 128), vm(256, 768), vm(6, 128, 512), vf(256, 768), vm(256, 768), vm(256, 768), vm(256, 1536),
        vm(256, 1536), vf(256, 768), vf(256, 768), vm(256, 768), vm(256, 768), vm(128, 768), vm(128, 768), vf(128, 768),
        vm(4, 256, 128), vm(4, 512, 128), vf(4, 1, 512), vm(6, 128, 512), vf(512, 128), vf(512, 128), vf(4, 128, 512), vm(192, 2048),
        vm(4, 256, 128), vm(4, 256, 128), vm(4, 3, 256, 128), vm(6, 3, 128, 128), vm(2, 96, 768), vm(96, 768),
        vm(768, 256), vm(768, 256), *[vm(4, 48, 3072)] * 8,
        vm(2, 4, 48, 384), vm(4, 48, 384), vm(4, 48, 384), vm(4, 48, 384), vm(4, 48, 384), vm(3, 256, 384), vm(128, 768), vm(128, 768),
        vf(4, 8, 768), vf(8, 8, 768), vf(4, 8, 768), vf(8, 8, 768),
        dma(SLOTS), dma(3, 8), dma(3, 8), dma(3), dma(16), dma(12), dma(2), dma(5), dma(8), dma(2), dma(4), dma(3), dma(2, 4), dma(4),
        dma(3), dma(1), dma(6), dma(1), dma(16), dma(16), dma(1), dma(4), dma(8), dma(4), dma(8),
    ]
    args = (
        layer_input, doc_ids, cotangent, ln1_gain, ln1_bias, w_qkv.transpose(1, 0, 2), bias_qv, w_out, b_out, ln2_gain, ln2_bias, w_up,
        b_up, w_down.T, b_down, jnp.asarray(count_table()),
    )
    found = pl.pallas_call(
        kernel, out_shape=raw, in_specs=in_vmem(len(args)), out_specs=tuple(in_vmem(len(raw))), scratch_shapes=scratch,
        compiler_params=pltpu.CompilerParams(collective_id=0, has_side_effects=True, vmem_limit_bytes=LIMIT),
    )(*args)
    outs = pl.pallas_call(
        write_out, out_shape=shapes, in_specs=in_vmem(len(raw)), out_specs=tuple(in_vmem(len(shapes))),
        compiler_params=pltpu.CompilerParams(vmem_limit_bytes=LIMIT),
    )(*found)
    outs = list(outs)
    outs[4] = outs[4].transpose(1, 0, 2)
    outs[12] = outs[12].T
    return tuple(outs)


def from_behind(value, axis, by):
    length = lax.axis_size(axis)
    pairs = [(i, i + by) for i in range(length) if 0 <= i + by < length]
    return lax.ppermute(value, axis, pairs)


def layer_norm(values, gain, shift):
    mean = jnp.mean(values, axis=-1, keepdims=True)
    centred = values - mean
    spread = jnp.mean(centred * centred, axis=-1, keepdims=True)
    return centred * lax.rsqrt(spread + EPS) * gain + shift


def gelu_tanh(values):
    return jax.nn.gelu(values, approximate=True)


def pick_block(length, limit):
    chosen = 1
    for candidate in range(1, min(length, limit) + 1):
        if length % candidate == 0:
            chosen = candidate
    return chosen


def pair_counts(query_pos, key_pos, head_ids):
    total = None
    for factor, rate in LEVELS:
        width = SEG * factor
        same = query_pos[:, :, None] // width == key_pos[:, None, :] // width
        offset = (head_ids % rate)[:, None]
        pick_query = query_pos % width % rate == offset
        pick_key = key_pos % width % rate == offset
        joint = (same & pick_query[:, :, None] & pick_key[:, None, :]).astype(jnp.float32)
        total = joint if total is None else total + joint
    return total


def block_terms(
    query_blk, query_pos, query_doc, key_blk, key_pos, key_doc, head_ids, nearby, scale
):
    scores = (
        jnp.einsum("qhe,khe->hqk", query_blk, key_blk, preferred_element_type=jnp.float32) * scale
    )
    counts = pair_counts(query_pos, key_pos, head_ids)
    same_segment = query_pos[:, :, None] // SEG == key_pos[:, None, :] // SEG
    keep = same_segment if nearby else jnp.logical_not(same_segment)
    allowed = (
        keep
        & (key_pos[:, None, :] <= query_pos[:, :, None])
        & (query_doc[:, :, None] == key_doc[:, None, :])
    )
    return (scores, counts * allowed.astype(jnp.float32))


def per_device(
    layer_input,
    doc_ids,
    cotangent,
    ln1_gain,
    ln1_bias,
    w_qkv,
    bias_qv,
    w_out,
    b_out,
    ln2_gain,
    ln2_bias,
    w_up,
    b_up,
    w_down,
    b_down,
):
    seq_count = lax.axis_size("seq")
    local_heads = HEADS // lax.axis_size("head")
    local_width = local_heads * HEAD_DIM
    scale = HEAD_DIM ** (-0.5)
    f32 = jnp.float32
    b16 = jnp.bfloat16
    x_float = layer_input.astype(f32)
    norm_one = layer_norm(x_float, ln1_gain, ln1_bias)
    norm_rows, row_doc = (
        lax.all_gather(norm_one.astype(b16), "head", axis=0, tiled=True),
        lax.all_gather(doc_ids, "head", axis=0, tiled=True),
    )
    seq_tokens = norm_rows.shape[0]
    half = seq_tokens // 2
    total_tokens = seq_tokens * seq_count
    total_half = total_tokens // 2
    first_pos = lax.axis_index("seq") * seq_tokens
    last_pos = first_pos + seq_tokens - 1
    local_offsets = jnp.arange(seq_tokens, dtype=jnp.int32)
    query_pos = (first_pos + local_offsets)[None, :]
    query_doc = row_doc[None, :]
    head_ids = lax.axis_index("head") * local_heads + jnp.arange(local_heads, dtype=jnp.int32)
    parity = head_ids % 2
    pick_even = parity == 0

    def compact(rows):
        paired = rows.reshape((half, 2) + rows.shape[1:])
        mask = pick_even.reshape((1, local_heads) + (1,) * (rows.ndim - 2))
        return jnp.where(mask, paired[:, 0], paired[:, 1])

    def expand(rows):
        mask = pick_even.reshape((1, local_heads) + (1,) * (rows.ndim - 2))
        zeros = jnp.zeros_like(rows)
        paired = jnp.stack([jnp.where(mask, rows, zeros), jnp.where(mask, zeros, rows)], axis=1)
        return paired.reshape((seq_tokens,) + rows.shape[1:])

    mixed = jnp.einsum("td,dch->tch", norm_rows, w_qkv, preferred_element_type=f32)
    zero_row = jnp.zeros((1, local_width), f32)
    bias_all = jnp.concatenate([bias_qv[0:1], zero_row, bias_qv[1:2]], axis=0)
    qkv = (mixed + bias_all[None]).astype(b16)
    queries = qkv[:, 0]
    query_heads = queries.reshape(seq_tokens, local_heads, HEAD_DIM)
    key_heads = qkv[:, 1].reshape(seq_tokens, local_heads, HEAD_DIM)
    value_heads = qkv[:, 2].reshape(seq_tokens, local_heads, HEAD_DIM)
    local_keys_c = compact(key_heads)
    local_values_c = compact(value_heads)
    far_keys_all, far_values_all, doc_all = (
        lax.all_gather(local_keys_c, "seq", axis=0, tiled=True),
        lax.all_gather(local_values_c, "seq", axis=0, tiled=True),
        lax.all_gather(row_doc, "seq", axis=0, tiled=True),
    )
    segment_count = SEG // seq_tokens
    own_pair = jnp.stack([key_heads, value_heads], axis=1)
    pair_pieces = [own_pair]
    for step in range(1, segment_count):
        pair_pieces.append(from_behind(own_pair, "seq", step))
    near_pairs = jnp.concatenate(pair_pieces, axis=0)
    near_keys = near_pairs[:, 0]
    near_values = near_pairs[:, 1]
    near_flat = jnp.concatenate(
        [first_pos - step * seq_tokens + local_offsets for step in range(segment_count)]
    )
    near_doc = jnp.take(doc_all, jnp.clip(near_flat, 0, total_tokens - 1))[None, :]
    near_pos = near_flat[None, :]
    far_pos = 2 * jnp.arange(total_half, dtype=jnp.int32)[None, :] + parity[:, None]
    doc_pairs = doc_all.reshape(total_half, 2)
    far_doc = jnp.where(pick_even[:, None], doc_pairs[:, 0][None, :], doc_pairs[:, 1][None, :])
    key_block = pick_block(total_half, block_limit)
    blocks = total_half // key_block
    far_key_blocks = far_keys_all.reshape(blocks, key_block, local_heads, HEAD_DIM)
    far_value_blocks = far_values_all.reshape(blocks, key_block, local_heads, HEAD_DIM)
    far_pos_blocks = far_pos.reshape(local_heads, blocks, key_block).transpose(1, 0, 2)
    far_doc_blocks = far_doc.reshape(local_heads, blocks, key_block).transpose(1, 0, 2)
    far_begin = jnp.arange(blocks, dtype=jnp.int32) * (2 * key_block)

    def merge_stats(current, key_blk, key_pos, key_doc, nearby):
        peak, running = current
        scores, counts = block_terms(
            query_heads, query_pos, query_doc, key_blk, key_pos, key_doc, head_ids, nearby, scale
        )
        live = counts > 0
        new_peak = jnp.maximum(peak, jnp.max(jnp.where(live, scores, NEGATIVE), axis=2))
        terms = jnp.where(live, counts * jnp.exp(scores - new_peak[:, :, None]), 0.0)
        return (new_peak, running * jnp.exp(peak - new_peak) + jnp.sum(terms, axis=2))

    start_state = (
        jnp.full((local_heads, seq_tokens), NEGATIVE, f32),
        jnp.zeros((local_heads, seq_tokens), f32),
    )
    near_state = merge_stats(start_state, near_keys, near_pos, near_doc, True)

    def stats_step(state, item):
        key_blk, pos_blk, doc_blk, begin = item
        return (
            lax.cond(
                begin <= last_pos,
                lambda current: merge_stats(current, key_blk, pos_blk, doc_blk, False),
                lambda current: current,
                state,
            ),
            None,
        )

    (peak_all, running_all), _ = lax.scan(
        stats_step, near_state, (far_key_blocks, far_pos_blocks, far_doc_blocks, far_begin)
    )
    lse = peak_all + jnp.log(running_all)

    def add_output(current, key_blk, value_blk, key_pos, key_doc, nearby):
        scores, counts = block_terms(
            query_heads, query_pos, query_doc, key_blk, key_pos, key_doc, head_ids, nearby, scale
        )
        probs = jnp.where(counts > 0, counts * jnp.exp(scores - lse[:, :, None]), 0.0).astype(b16)
        return current + jnp.einsum("hqk,khe->qhe", probs, value_blk, preferred_element_type=f32)

    zero_heads = jnp.zeros((seq_tokens, local_heads, HEAD_DIM), f32)
    near_output = add_output(zero_heads, near_keys, near_values, near_pos, near_doc, True)

    def output_step(accum, item):
        key_blk, value_blk, pos_blk, doc_blk, begin = item
        return (
            lax.cond(
                begin <= last_pos,
                lambda current: add_output(current, key_blk, value_blk, pos_blk, doc_blk, False),
                lambda current: current,
                accum,
            ),
            None,
        )

    attn_exact, _ = lax.scan(
        output_step,
        near_output,
        (far_key_blocks, far_value_blocks, far_pos_blocks, far_doc_blocks, far_begin),
    )
    attn_low = attn_exact.reshape(seq_tokens, local_width).astype(b16)
    branch = lax.psum_scatter(
        jnp.dot(attn_low, w_out, preferred_element_type=f32).astype(jnp.bfloat16),
        "head",
        scatter_dimension=0,
        tiled=True,
    ).astype(jnp.float32)
    hidden_one = x_float + branch + b_out
    norm_two = layer_norm(hidden_one, ln2_gain, ln2_bias)
    norm_low = norm_two.astype(b16)
    dy_low = (cotangent.astype(f32) * (doc_ids >= 0).astype(f32)[:, None]).astype(b16)
    dy_float = dy_low.astype(f32)
    up_rows, down_rows = (
        lax.all_gather(w_up, "seq", axis=0, tiled=True),
        lax.all_gather(w_down, "seq", axis=1, tiled=True),
    )
    up_full, down_full = (
        lax.all_gather(up_rows, "head", axis=1, tiled=True),
        lax.all_gather(down_rows, "head", axis=0, tiled=True),
    )
    pre_act = jnp.dot(norm_low, up_full, preferred_element_type=f32) + b_up
    act_low = gelu_tanh(pre_act).astype(b16)
    ffn_result = jnp.dot(act_low, down_full, preferred_element_type=f32)
    d_act = jnp.einsum("td,fd->tf", dy_low, down_full, preferred_element_type=f32)
    _, gelu_back = jax.vjp(gelu_tanh, pre_act)
    d_pre = gelu_back(d_act)[0]
    d_pre_low = d_pre.astype(b16)
    bias_up_grad = jnp.sum(d_pre, axis=0)
    up_parts = jnp.einsum("td,tf->df", norm_low, d_pre_low, preferred_element_type=f32)
    down_parts = jnp.einsum("tf,td->fd", act_low, dy_low, preferred_element_type=f32)
    up_grad, down_grad = (
        lax.psum_scatter(
            up_parts.astype(jnp.bfloat16), "head", scatter_dimension=1, tiled=True
        ).astype(jnp.float32),
        lax.psum_scatter(
            down_parts.astype(jnp.bfloat16), "head", scatter_dimension=0, tiled=True
        ).astype(jnp.float32),
    )
    d_norm_two = jnp.einsum("tf,df->td", d_pre_low, up_full, preferred_element_type=f32)
    layer_output = (hidden_one + ffn_result + b_down).astype(b16)
    w_up_grad, w_down_grad = (
        lax.psum_scatter(up_grad, "seq", scatter_dimension=0, tiled=True),
        lax.psum_scatter(down_grad, "seq", scatter_dimension=1, tiled=True),
    )
    _, norm_two_back = jax.vjp(layer_norm, hidden_one, ln2_gain, ln2_bias)
    d_hidden_norm, gain_two_grad, bias_two_grad = norm_two_back(d_norm_two)
    d_hidden = dy_float + d_hidden_norm
    bias_out_grad = jnp.sum(d_hidden, axis=0)
    bias_down_grad = jnp.sum(dy_float, axis=0)
    hidden_rows = lax.all_gather(d_hidden.astype(b16), "head", axis=0, tiled=True)
    w_out_part = jnp.einsum("tc,td->cd", attn_low, hidden_rows, preferred_element_type=f32)
    d_attn = jnp.einsum("td,cd->tc", hidden_rows, w_out, preferred_element_type=f32).astype(b16)
    d_attn_heads = d_attn.reshape(seq_tokens, local_heads, HEAD_DIM)
    delta_rows = jnp.sum(d_attn_heads.astype(f32) * attn_exact, axis=2)
    delta = delta_rows.T

    def score_grads(key_blk, value_blk, key_pos, key_doc, nearby):
        scores, counts = block_terms(
            query_heads, query_pos, query_doc, key_blk, key_pos, key_doc, head_ids, nearby, scale
        )
        exact = jnp.where(counts > 0, counts * jnp.exp(scores - lse[:, :, None]), 0.0)
        d_prob = jnp.einsum("qhe,khe->hqk", d_attn_heads, value_blk, preferred_element_type=f32)
        d_score = (exact * (d_prob - delta[:, :, None])).astype(b16)
        return (exact, d_score)

    exact_near, d_score_near = score_grads(near_keys, near_values, near_pos, near_doc, True)
    d_query_near = jnp.einsum("hqk,khe->qhe", d_score_near, near_keys, preferred_element_type=f32)
    near_key_grad = jnp.einsum(
        "hqk,qhe->khe", d_score_near, query_heads, preferred_element_type=f32
    )
    near_value_grad = jnp.einsum(
        "hqk,qhe->khe", exact_near.astype(b16), d_attn_heads, preferred_element_type=f32
    )
    near_pair_grads = jnp.stack([near_key_grad, near_value_grad], axis=1)
    pair_grad = near_pair_grads[:seq_tokens]
    for step in range(1, segment_count):
        piece = near_pair_grads[step * seq_tokens : (step + 1) * seq_tokens]
        pair_grad = pair_grad + from_behind(piece.astype(jnp.bfloat16), "seq", -step).astype(
            piece.dtype
        )

    def query_grad_step(accum, item):
        key_blk, value_blk, pos_blk, doc_blk, begin = item

        def query_compute(current):
            _, d_score = score_grads(key_blk, value_blk, pos_blk, doc_blk, False)
            return current + jnp.einsum(
                "hqk,khe->qhe", d_score, key_blk, preferred_element_type=f32
            )

        return (lax.cond(begin <= last_pos, query_compute, lambda current: current, accum), None)

    d_query, _ = lax.scan(
        query_grad_step,
        d_query_near,
        (far_key_blocks, far_value_blocks, far_pos_blocks, far_doc_blocks, far_begin),
    )
    d_query = d_query * scale
    stats_rows = jnp.stack([compact(lse.T), compact(delta_rows)], axis=1)
    stats_all = lax.all_gather(stats_rows, "seq", axis=0, tiled=True)
    local_key_pos = first_pos + 2 * jnp.arange(half, dtype=jnp.int32)[None, :] + parity[:, None]
    local_key_doc = compact(jnp.broadcast_to(row_doc[:, None], (seq_tokens, local_heads))).T
    zero_compact = jnp.zeros((half, local_heads, HEAD_DIM), f32)
    query_piece = lax.all_gather(compact(query_heads), "seq", axis=0, tiled=True)
    grad_piece = lax.all_gather(compact(d_attn_heads), "seq", axis=0, tiled=True)
    length = query_piece.shape[0]
    size = pick_block(length, block_limit)
    number = length // size
    pos_piece = 2 * jnp.arange(length, dtype=jnp.int32)[None, :] + parity[:, None]
    items = (
        query_piece.reshape(number, size, local_heads, HEAD_DIM),
        grad_piece.reshape(number, size, local_heads, HEAD_DIM),
        stats_all.reshape(number, size, 2, local_heads),
        pos_piece.reshape(local_heads, number, size).transpose(1, 0, 2),
        far_doc.reshape(local_heads, number, size).transpose(1, 0, 2),
    )

    def one_step(current, item):
        query_blk, grad_blk, stats_blk, pos_blk, doc_blk = item

        def one_compute(pair):
            key_grad, value_grad = pair
            scores, counts = block_terms(
                query_blk,
                pos_blk,
                doc_blk,
                local_keys_c,
                local_key_pos,
                local_key_doc,
                head_ids,
                False,
                scale,
            )
            exact = jnp.where(
                counts > 0, counts * jnp.exp(scores - stats_blk[:, 0].T[:, :, None]), 0.0
            )
            d_prob = jnp.einsum(
                "qhe,khe->hqk", grad_blk, local_values_c, preferred_element_type=f32
            )
            d_score = (exact * (d_prob - stats_blk[:, 1].T[:, :, None])).astype(b16)
            key_grad = key_grad + jnp.einsum(
                "hqk,qhe->khe", d_score, query_blk, preferred_element_type=f32
            )
            value_grad = value_grad + jnp.einsum(
                "hqk,qhe->khe", exact.astype(b16), grad_blk, preferred_element_type=f32
            )
            return (key_grad, value_grad)

        return (
            lax.cond(jnp.max(pos_blk) >= first_pos, one_compute, lambda pair: pair, current),
            None,
        )

    result, _ = lax.scan(one_step, (zero_compact, zero_compact), items)
    far_key_grad, far_value_grad = result
    d_key = (pair_grad[:, 0] + expand(far_key_grad)) * scale
    d_value = pair_grad[:, 1] + expand(far_value_grad)
    d_qkv = jnp.stack(
        [
            d_query.reshape(seq_tokens, local_width),
            d_key.reshape(seq_tokens, local_width),
            d_value.reshape(seq_tokens, local_width),
        ],
        axis=1,
    ).astype(b16)
    d_qkv_float = d_qkv.astype(f32)
    bias_qv_part = jnp.stack(
        [jnp.sum(d_qkv_float[:, 0], axis=0), jnp.sum(d_qkv_float[:, 2], axis=0)], axis=0
    )
    w_qkv_part = jnp.einsum("td,tch->dch", norm_rows, d_qkv, preferred_element_type=f32)
    d_norm_one = lax.psum_scatter(
        jnp.einsum("tch,dch->td", d_qkv, w_qkv, preferred_element_type=f32).astype(jnp.bfloat16),
        "head",
        scatter_dimension=0,
        tiled=True,
    ).astype(jnp.float32)
    _, norm_one_back = jax.vjp(layer_norm, x_float, ln1_gain, ln1_bias)
    d_x_norm, gain_one_grad, bias_one_grad = norm_one_back(d_norm_one)
    grad_input = d_hidden + d_x_norm
    w_qkv_grad, bias_qv_grad, w_out_grad = lax.psum((w_qkv_part, bias_qv_part, w_out_part), "seq")
    summed = lax.psum(
        (
            gain_one_grad,
            bias_one_grad,
            gain_two_grad,
            bias_two_grad,
            bias_out_grad,
            bias_up_grad,
            bias_down_grad,
        ),
        ("seq", "head"),
    )
    return (
        layer_output,
        grad_input,
        summed[0],
        summed[1],
        w_qkv_grad,
        bias_qv_grad,
        w_out_grad,
        summed[4],
        summed[2],
        summed[3],
        w_up_grad,
        summed[5],
        w_down_grad,
        summed[6],
    )


def solution(mesh):
    in_specs = (
        P(("seq", "head"), None),
        P(("seq", "head")),
        P(("seq", "head"), None),
        P(),
        P(),
        P(None, None, "head"),
        P(None, "head"),
        P("head", None),
        P(),
        P(),
        P(),
        P("seq", "head"),
        P(),
        P("head", "seq"),
        P(),
    )
    out_specs = (
        P(("seq", "head"), None),
        P(("seq", "head"), None),
        P(),
        P(),
        P(None, None, "head"),
        P(None, "head"),
        P("head", None),
        P(),
        P(),
        P(),
        P("seq", "head"),
        P(),
        P("head", "seq"),
        P(),
    )
    small = mesh.shape["seq"] == 16 and mesh.shape["head"] == 2
    return jax.shard_map(
        fast if small else per_device, mesh=mesh, in_specs=in_specs, out_specs=out_specs, check_vma=False
    )
```

```python
import functools

import jax
import jax.numpy as jnp
import ml_dtypes
import numpy as np
from jax import lax
from jax.experimental import pallas as pl
from jax.experimental.pallas import tpu as pltpu
from jax.sharding import PartitionSpec as P

HEADS = 12
HEAD_DIM = 64
SEG = 2048


LEVELS = ((1, 1), (2, 2), (4, 4), (8, 6), (16, 12))
EPS = 1e-05
NEGATIVE = -1e30
block_limit = 2048


MESH = pl.DeviceIdType.MESH
VMEM = pltpu.VMEM
LIMIT = 60 << 20
F32 = jnp.float32
B16 = jnp.bfloat16


def dot(a, b):
    return jnp.dot(a, b, preferred_element_type=F32)


def dot_nt(a, b):
    return lax.dot_general(a, b, (((1,), (1,)), ((), ())), preferred_element_type=F32)


def sid(z, x, c):
    return z * 4 + x * 2 + c


class Place:
    def __init__(self):
        s = lax.axis_index("seq")
        self.s, self.y = s, lax.axis_index("head")
        self.z, self.x, self.c = s // 4, (s // 2) % 2, s % 2
        self.seg, self.zl = self.z // 2, self.z % 2
        self.u = s % 8
        self.b = self.u * 2 + self.y
        self.unit = jnp.logical_and(self.u != 3, self.u != 5)
        self.hl = self.u - self.u // 4 - self.u // 6
        self.head = self.y * 6 + self.hl
        self.parity = self.head % 2
        z, x, c, y = self.z, self.x, self.c, self.y
        self.zf = z + 1 - 2 * self.zl
        self.nx, self.ny = (sid(z, 1 - x, c), y), (s, 1 - y)
        self.nz, self.nc = (sid(self.zf, x, c), y), (sid(z, x, 1 - c), y)
        self.far = (sid((z + 2) % 4, x, c), y)
        self.fb = {"x": 4 * (1 - 2 * x), "y": 1 - 2 * y, "z": 8 * (1 - 2 * self.zl), "c": 2 * (1 - 2 * c)}

    def cube(self):
        z, x, c, y = self.z, self.x, self.c, self.y
        for k in range(1, 16):
            zz = self.zf if k & 8 else z
            xx = 1 - x if k & 4 else x
            cc = 1 - c if k & 2 else c
            yy = 1 - y if k & 1 else y
            yield (sid(zz, xx, cc), yy)

    def greet(self):
        others = list(self.cube())
        others += [(sid((self.z + 2) % 4, self.x, self.c), self.y), (sid((self.zf + 2) % 4, self.x, self.c), self.y)]
        barrier = pltpu.get_barrier_semaphore()
        for dev in others:
            pl.semaphore_signal(barrier, inc=1, device_id=dev, device_id_type=MESH)
        self.greeted = len(others)

    def meet(self):
        pl.semaphore_wait(pltpu.get_barrier_semaphore(), self.greeted)


class Mail:
    def __init__(self, sems, slots):
        self.sems, self.slots, self.used, self.sent = sems, slots, 0, {}

    def send(self, src, dst, rsem, dev, cond=None):
        k = self.used % self.slots
        self.used += 1
        self.settle(k)

        def make():
            return pltpu.make_async_remote_copy(
                src_ref=src, dst_ref=dst, send_sem=self.sems.at[k], recv_sem=rsem, device_id=dev, device_id_type=MESH
            )

        if cond is None:
            make().start()
        else:
            pl.when(cond)(lambda: make().start())
        self.sent[k] = (cond, make)

    def settle(self, k):
        if k in self.sent:
            cond, make = self.sent.pop(k)
            if cond is None:
                make().wait_send()
            else:
                pl.when(cond)(lambda: make().wait_send())

    def got(self, dst, rsem, dev):
        pltpu.make_async_remote_copy(
            src_ref=dst, dst_ref=dst, send_sem=self.sems.at[0], recv_sem=rsem, device_id=dev, device_id_type=MESH
        ).wait_recv()

    def close(self):
        for k in range(self.slots):
            self.settle(k)


def both(*terms):
    out = terms[0]
    for term in terms[1:]:
        out = jnp.logical_and(out, term)
    return out


def iota(shape, dim):
    return lax.broadcasted_iota(jnp.int32, shape, dim)


def norm_parts(v):
    mean = jnp.mean(v, axis=-1, keepdims=True)
    cen = v - mean
    inv = lax.rsqrt(jnp.mean(cen * cen, axis=-1, keepdims=True) + EPS)
    return cen * inv, inv


def norm_grad(z, inv, e):
    return (e - jnp.mean(e, axis=-1, keepdims=True) - z * jnp.mean(e * z, axis=-1, keepdims=True)) * inv


def pick_type(pos, head, rows):
    v = pos - head + 24.0
    m = v - 12.0 * jnp.floor((v + 0.5) * (1.0 / 12.0))
    out = jnp.where(m == 0.0, rows[4], rows[0])
    out = jnp.where(m == 6.0, rows[3], out)
    out = jnp.where(jnp.logical_or(m == 4.0, m == 8.0), rows[2], out)
    return jnp.where(jnp.logical_or(m == 2.0, m == 10.0), rows[1], out)


def halves(e, o):
    low = iota(e.shape, 1) < 64
    return jnp.where(low, e, pltpu.roll(o, 64, 1)), jnp.where(low, pltpu.roll(e, 64, 1), o)


UNITS = (0, 1, 2, 4, 6, 7)


class Spread:
    def __init__(self, p, mail, ref, sems, some):
        self.p, self.mail, self.ref, self.sems, self.some = p, mail, ref, sems, some

    def has(self, zz, xx, cc):
        return jnp.logical_or(cc == 0, zz % 2 == xx) if self.some else None

    def go(self, s, dev, cond):
        self.mail.send(self.ref.at[s], self.ref.at[s], self.sems.at[s], dev, cond)

    def take(self, s, cond):
        def wait():
            self.mail.got(self.ref.at[s], self.sems.at[s], self.p.nx)

        if cond is None:
            wait()
        else:
            pl.when(cond)(wait)

    def first(self):
        p = self.p
        has = self.has(p.z, p.x, p.c)
        for dev in (p.far, p.nz, p.nx, p.nc):
            self.go(p.s, dev, has)

    def onward(self, zz, devs):
        s, has = sid(zz, self.p.x, self.p.c), self.has(zz, self.p.x, self.p.c)
        self.take(s, has)
        for dev in devs:
            self.go(s, dev, has)

    def second(self):
        p = self.p
        self.onward((p.z + 2) % 4, (p.nz, p.nx, p.nc))
        self.onward(p.zf, (p.nx, p.nc))

    def third(self):
        p = self.p
        self.onward((p.zf + 2) % 4, (p.nx, p.nc))

    def fourth(self):
        p = self.p
        for zz in range(4):
            s, has = sid(zz, 1 - p.x, p.c), self.has(zz, 1 - p.x, p.c)
            self.take(s, has)
            self.go(s, p.nc, has)

    def last(self):
        p = self.p
        for zz in range(4):
            for xx in range(2):
                self.take(sid(zz, xx, 1 - p.c), self.has(zz, xx, 1 - p.c))


class Reduce:
    def __init__(self, p, mail, src, gc, gxs, gxr, gzs, gzr, rc, rx, rz):
        self.__dict__.update(locals())

    def rows(self, zz, xx, cc):
        return pl.ds(pl.multiple_of(sid(zz, xx, cc) * 48, 16), 48)

    def cores(self):
        p = self.p
        for xq in range(2):
            xx = 1 - p.x if xq == 0 else p.x
            for k in (1, 2, 3, 0):
                zz = (p.z + k) % 4
                self.mail.send(self.src.at[self.rows(zz, xx, 1 - p.c)], self.gc.at[xq, zz], self.rc.at[xq, zz], p.nc)

    def order(self):
        z, zf = self.p.z, self.p.zf
        return (zf + 2) % 4, (z + 2) % 4, zf, z

    def over_x(self):
        p = self.p
        for zz in self.order():
            self.mail.got(self.gc.at[0, zz], self.rc.at[0, zz], p.nc)
            own = self.src[self.rows(zz, 1 - p.x, p.c)].astype(F32)
            self.gxs[zz] = (own + self.gc[0, zz].astype(F32)).astype(B16)
            self.mail.send(self.gxs.at[zz], self.gxr.at[zz], self.rx.at[zz], p.nx)

    def column(self, zz):
        p = self.p
        self.mail.got(self.gc.at[1, zz], self.rc.at[1, zz], p.nc)
        self.mail.got(self.gxr.at[zz], self.rx.at[zz], p.nx)
        return self.src[self.rows(zz, p.x, p.c)].astype(F32) + self.gc[1, zz].astype(F32) + self.gxr[zz].astype(F32)

    def over_z(self, i):
        self.gzs[i] = self.column(self.order()[i]).astype(B16)
        self.mail.send(self.gzs.at[i], self.gzr.at[i], self.rz.at[i], self.p.nz)

    def over_far(self):
        self.mail.got(self.gzr.at[0], self.rz.at[0], self.p.nz)
        self.gzs[1] = (self.column(self.order()[1]) + self.gzr[0].astype(F32)).astype(B16)
        self.mail.send(self.gzs.at[1], self.gzr.at[1], self.rz.at[1], self.p.far)

    def result(self):
        total = self.column(self.p.z)
        for i in (1, 2):
            self.mail.got(self.gzr.at[i], self.rz.at[i], self.p.nz)
            total = total + self.gzr[i].astype(F32)
        return total


class Total:
    def __init__(self, p, mail, one, two, sem_one, sem_two):
        self.p, self.mail, self.one, self.two, self.sem_one, self.sem_two = p, mail, one, two, sem_one, sem_two
        self.k = (p.x * 2 + p.c) * 2 + p.y

    def start(self):
        p = self.p
        for i in range(1, 4):
            dev = (sid((p.z + i) % 4, p.x, p.c), p.y)
            self.mail.send(self.one.at[p.z], self.one.at[p.z], self.sem_one.at[p.z], dev)

    def middle(self):
        p = self.p
        for i in range(1, 4):
            zz = (p.z + i) % 4
            self.mail.got(self.one.at[zz], self.sem_one.at[zz], p.nx)
        self.two[self.k] = self.one[0] + self.one[1] + self.one[2] + self.one[3]
        for i in range(1, 8):
            xx = 1 - p.x if i & 4 else p.x
            cc = 1 - p.c if i & 2 else p.c
            yy = 1 - p.y if i & 1 else p.y
            self.mail.send(self.two.at[self.k], self.two.at[self.k], self.sem_two.at[self.k], (sid(p.z, xx, cc), yy))

    def finish(self):
        for i in range(8):
            pl.when(self.k != i)(lambda i=i: self.mail.got(self.two.at[i], self.sem_two.at[i], self.p.nx))
        out = self.two[0]
        for i in range(1, 8):
            out = out + self.two[i]
        return out


def mixed(shape, dim_to, dim_from):
    r, i = iota(shape, dim_to), iota(shape, dim_from)
    return jnp.where(i == 2 * (r & 63) + (r >> 6), 1.0, 0.0).astype(B16)


def kernel(
    x_ref, doc_ref, cot_ref, g1_ref, b1_ref, wq_ref, bqv_ref, wo_own, bo_ref, g2_ref, b2_ref, wup_ref, bup_ref, wdn_ref, bd_ref, tab_ref,
    lout, gin, wag, woag, o_ud, o_tot,
    qa, ka, va, ns, lse, ot, dpk, gwo, dh_s, wqh, bqh, buph, msc, asc,
    xs, docs, wb, wo, dyp, orecv, osend, kvs, kvf, attn, vt, hid, n2s, dys, acts, dpre, facc, dacc, ys, yr, fs, fr, fo,
    dor, doa, delta, kt, dka, dva, dqt, dtt, dfs, dfr, packs, dqr, wms, wmr, n2t, dyt, ga, gb, gd, ge, ra, rb, gxr, gzr,
    hc, hxs, hxr, hzs, hzr, dall, dns, dnr, vb1, vr1, vb2, vr2,
    ss, rsx, rsc, rsd, rsw, rso, rsf, rsy, rdo, rga, rgx, rgz, rhc, rhx, rhz, rdf, rdq, rwm, rag, rwo, rdn, rv1, rv2, rv3, rv4,
):
    p = Place()
    mail = Mail(ss, SLOTS)
    seg, x, y, z, c, b = p.seg, p.x, p.y, p.z, p.c, p.b
    first, second = both(p.unit, seg == 0), both(p.unit, seg == 1)
    row = lambda ref: ref[...].reshape(1, -1)
    p.greet()

    mix = mixed((128, 128), 0, 1)
    xs[b] = dot(mix, x_ref[...]).astype(B16)
    doc_row = doc_ref[...].astype(F32).reshape(1, 128)
    turn = jnp.where(iota((128, 128), 0) == 2 * (iota((128, 128), 1) & 63), 1.0, 0.0).astype(B16)
    turn_odd = jnp.where(iota((128, 128), 0) == 2 * (iota((128, 128), 1) & 63) + 1, 1.0, 0.0).astype(B16)
    doc8 = jnp.broadcast_to(doc_row, (8, 128)).astype(B16)
    docs[b] = jnp.where(iota((8, 128), 0) == 0, dot(doc8, turn), dot(doc8, turn_odd))
    wrow = pl.ds(pl.multiple_of(p.s * 48, 16), 48)
    wb[wrow, 0:1536] = wup_ref[...]
    wb[wrow, 1536:3072] = wdn_ref[...]
    p.meet()

    dims = ("x", "y", "z")
    nbr = {"x": p.nx, "y": p.ny, "z": p.nz}
    part = [pl.ds(k * 256, 256) for k in range(3)]
    order = [[dims[(k + j) % 3] for j in range(3)] for k in range(3)]

    bit = {"x": 1, "y": 2, "z": 4}

    def place(rel):
        return b + sum(p.fb[d] for d in dims if rel & bit[d])

    def third(rel, k):
        return xs.at[place(rel), :, part[k]]

    def pass_on(k, rel, d):
        mail.send(third(rel, k), third(rel, k), rsx.at[k, rel ^ bit[d]], nbr[d])

    def to_core(k, rel):
        mail.send(third(rel, k), third(rel, k), rsc.at[k, rel], p.nc)

    for j in range(3):
        for k in range(3):
            pass_on(k, 0, order[k][j])
    for k in range(3):
        to_core(k, 0)
    special = jnp.logical_or(b == 0, b >= 14)
    for dev in p.cube():
        mail.send(docs.at[b], docs.at[b], rsd.at[b // 14 + b // 15], dev, special)

    def rows_of(s):
        return wb.at[pl.ds(pl.multiple_of(s * 48, 16), 48), :]

    def give(s, dev, cond=None):
        mail.send(rows_of(s), rows_of(s), rsw.at[s], dev, cond)


    pair_cols = pl.ds(pl.multiple_of(p.hl // 2 * 128, 128), 128)
    for odd in range(2):

        @pl.when(p.hl % 2 == odd)
        def _(odd=odd):
            for k in range(3):
                w = wq_ref[k, :, pair_cols].astype(F32)
                w = pltpu.roll(w, 64, 1) if odd else w
                wqh[:, k * 128 : k * 128 + 128] = jnp.where(iota((768, 128), 1) < 64, w, 0.0).astype(B16)
            v = jnp.concatenate([bqv_ref[:, pair_cols], jnp.zeros((6, 128), F32)], axis=0)
            v = pltpu.roll(v, 64, 1) if odd else v
            lane = iota((1, 128), 1)
            bqh[:, 0:128] = jnp.where(lane < 64, v[0:1], 0.0)
            bqh[:, 128:256] = jnp.zeros((1, 128), F32)
            bqh[:, 256:384] = jnp.where(lane < 64, v[1:2], jnp.where(lane == 64, 1.0, 0.0))

    head = p.head.astype(F32)
    for t in range(4):
        rr = iota((512, 128), 0)
        pos = (seg * SEG + t * 512 + 2 * (rr & 255) + (rr >> 8)).astype(F32)
        qa[t] = pick_type(pos, head, [tab_ref[i : i + 1] for i in range(5)]).astype(B16)
        ka[t + 2] = pick_type(pos, head, [tab_ref[8 + i : 9 + i] for i in range(5)]).astype(B16)

    real = jnp.broadcast_to(doc_row, (128, 128)).T >= 0.0
    for k in range(6):
        cols = slice(k * 128, k * 128 + 128)
        kept = jnp.where(real, cot_ref[:, cols].astype(F32), 0.0).astype(B16)
        dyp[y, :, cols] = dot(mix, kept).astype(B16)
    for half in range(2):

        @pl.when(y == half)
        def _(half=half):
            buph[...] = bup_ref[half * 1536 : half * 1536 + 1536].reshape(1, 1536)

    wo[y] = wo_own[...]

    def qkv(i):
        rows = xs[pl.ds(2 * i, 2)].reshape(256, 768).astype(F32)
        zz, _inv = norm_parts(rows)
        n1 = (zz * row(g1_ref) + row(b1_ref)).astype(B16)
        m = (dot(n1, wqh[...]) + bqh[...]).astype(B16)
        t = i // 2
        for yy in range(2):
            for par in range(2):
                at = slice(yy * 128 + par * 64, yy * 128 + par * 64 + 64)
                to = pl.ds(pl.multiple_of(par * 256 + (i % 2) * 128 + yy * 64, 64), 64)
                qa[t, to] = m[at, :128] * B16(0.125) + qa[t, to]
                ka[t + 2, to] = m[at, 128:256] + ka[t + 2, to]
                va[t + 2, to] = m[at, 256:]
                ns[t, to] = n1[at]

    def seen(k, rel):
        mail.got(third(rel, k), rsx.at[k, rel], p.nx)
        to_core(k, rel)

    def from_core(rel):
        for k in range(3):
            mail.got(xs.at[place(rel) + p.fb["c"], :, part[k]], rsc.at[k, rel], p.nc)

    def qkv_of(rel, core=0):
        at = (place(rel) + core * p.fb["c"]) // 2
        pl.when(p.unit)(lambda: qkv(at))

    def chain(d):
        up, dn = (z - d + 4) % 4, (z + d) % 4
        has_up, has_dn = z >= d, z <= 3 - d
        su, sd = sid(up, x, c), sid(dn, x, c)
        pl.when(has_up)(lambda: mail.got(rows_of(su), rsw.at[su], p.nx))
        if d < 3:
            give(su, (sid((z + 1) % 4, x, c), y), both(has_up, z <= 2))
        give(su, p.nx, has_up)
        give(su, p.nc, has_up)
        pl.when(has_dn)(lambda: mail.got(rows_of(sd), rsw.at[sd], p.nx))
        if d < 3:
            give(sd, (sid((z + 3) % 4, x, c), y), both(has_dn, z >= 1))
        give(sd, p.nx, has_dn)
        give(sd, p.nc, has_dn)

    X, Y, Z = 1, 2, 4
    for k in range(3):
        d0, d1, d2 = order[k]
        seen(k, bit[d0])
        pass_on(k, bit[d0], d1)
        pass_on(k, bit[d0], d2)
        seen(k, bit[d1])
        pass_on(k, bit[d1], d2)
        seen(k, bit[d2])
    qkv_of(0)
    for k in range(3):
        d0, d1, d2 = order[k]
        seen(k, bit[d0] | bit[d1])
        pass_on(k, bit[d0] | bit[d1], d2)
    give(p.s, (sid((z + 1) % 4, x, c), y), z <= 2)
    give(p.s, (sid((z + 3) % 4, x, c), y), z >= 1)
    give(p.s, p.nx)
    give(p.s, p.nc)
    mail.send(dyp.at[y], dyp.at[y], rsy.at[1], p.ny)
    whalf = pl.ds(pl.multiple_of(c * 192, 64), 192)
    mail.send(wo.at[y, whalf], wo.at[y, whalf], rsy.at[0], p.ny)
    for k in range(3):
        d0, d1, d2 = order[k]
        seen(k, bit[d0] | bit[d2])
        seen(k, bit[d1] | bit[d2])
    qkv_of(X)
    qkv_of(Z)
    from_core(0)
    from_core(Y)
    qkv_of(0, 1)
    for k in range(3):
        seen(k, X | Y | Z)
    qkv_of(X | Z)
    for rel in (X, Z, X | Z):
        from_core(rel)
        from_core(rel | Y)
        qkv_of(rel, 1)
        if rel == Z:
            chain(1)
    for src in (0, 14, 15):
        pl.when(b != src)(lambda src=src: mail.got(docs.at[src], rsd.at[src // 14 + src // 15], p.nx))

    lowlane = iota((256, 128), 1) < 64
    farrows = pl.ds(pl.multiple_of(p.parity * 256, 256), 256)

    @pl.when(first)
    def _():
        for t in range(4):
            kk = ka[t + 2, farrows].astype(F32)
            vv = va[t + 2, farrows].astype(F32)
            kvs[t] = jnp.where(lowlane, kk, pltpu.roll(vv, 64, 1)).astype(B16)

    mail.send(kvs, kvf, rsf.at[0], p.far, first)
    mail.send(docs.at[0], docs.at[16], rsf.at[1], p.far, first)

    def codes(src, par):
        r = docs[src, par : par + 1]
        return jnp.broadcast_to(jnp.where(r < 0.0, 4.0, r), (128, 128)).T[0:64]

    def mark(ref, at, code, query):
        lane = iota((64, 128), 1)
        hit = (lane - 96).astype(F32) == code
        if query:
            feat = jnp.where(hit, 0.0, jnp.where(lane < 101, NEGATIVE, 0.0))
        else:
            feat = jnp.where(hit, 1.0, 0.0)
        ref[at] = jnp.where(lane >= 96, feat, ref[at].astype(F32)).astype(B16)

    @pl.when(first)
    def _():
        for par in range(2):
            code = codes(0, par)
            at = slice(par * 256, par * 256 + 64)
            mark(qa.at[0], at, code, True)
            mark(ka.at[2], at, code, False)

    @pl.when(second)
    def _():
        for par in range(2):
            for yy in range(2):
                code = codes(14 + yy, par)
                at = slice(par * 256 + 128 + yy * 64, par * 256 + 192 + yy * 64)
                mark(qa.at[3], at, code, True)
                mark(ka.at[5], at, code, False)

    @pl.when(p.unit)
    def _():
        for t in range(4):
            vt[t + 2] = va[t + 2].astype(F32).T.astype(B16)

    rr, ll = iota((512, 512), 0), iota((512, 512), 1)
    causal = lambda st: jnp.where(2 * (rr & 255) + (rr >> 8) <= 2 * (ll & 255) + (ll >> 8), st, NEGATIVE)

    def near_attention(t):
        q = qa[t]

        def update(cc, carry, st):
            m, acc = carry
            m_new = jnp.maximum(m, jnp.max(st, axis=0, keepdims=True))
            pr = jnp.exp(st - m_new).astype(B16)
            return m_new, acc * jnp.exp(m - m_new) + dot(vt[cc], pr)

        state = (jnp.full((1, 512), NEGATIVE, F32), jnp.zeros((128, 512), F32))
        if t:
            state = lax.fori_loop(2, t + 2, lambda cc, s: update(cc, s, dot_nt(ka[cc], q)), state)
        msc[t], asc[t] = update(t + 2, state, causal(dot_nt(ka[t + 2], q)))

    def far_ready():
        mail.got(kvf, rsf.at[0], p.far)
        mail.got(docs.at[16], rsf.at[1], p.far)
        for t in range(4):
            rows = pl.ds((t % 2) * 256, 256)
            fpos = ((t * 256 + iota((256, 128), 0)) * 2 + p.parity).astype(F32)
            feat = pick_type(fpos, head, [tab_ref[16 + i : 17 + i] for i in range(5)])
            kv = kvf[t].astype(F32)
            ka[t // 2, rows] = jnp.where(lowlane, kv, feat).astype(B16)
            one = jnp.where(iota((256, 128), 1) == 64, 1.0, 0.0)
            va[t // 2, rows] = jnp.where(lowlane, pltpu.roll(kv, 64, 1), one).astype(B16)
        even, odd = codes(16, 0), codes(16, 1)
        mark(ka.at[0], slice(0, 64), even + p.parity.astype(F32) * (odd - even), False)
        for h in range(2):
            vt[h] = va[h].astype(F32).T.astype(B16)

    farcols = pl.ds(pl.multiple_of(p.parity * 256, 256), 256)

    def far_attention(t):
        q = qa[t, farcols]
        m = msc[t, :, farcols]
        s0, s1 = dot_nt(ka[0], q), dot_nt(ka[1], q)
        m_new = jnp.maximum(m, jnp.maximum(jnp.max(s0, axis=0, keepdims=True), jnp.max(s1, axis=0, keepdims=True)))
        acc = asc[t, :, farcols] * jnp.exp(m - m_new)
        acc = acc + dot(vt[0], jnp.exp(s0 - m_new).astype(B16))
        acc = acc + dot(vt[1], jnp.exp(s1 - m_new).astype(B16))
        msc[t, :, farcols] = m_new
        asc[t, :, farcols] = acc

    def conclude(t):
        acc = asc[t]
        total = acc[64:65]
        o = acc[:64] / total
        lse[t] = msc[t] + jnp.log(total)
        ot[t] = jnp.concatenate([o[:, :256], o[:, 256:]], axis=0)
        osend[t] = ot[t].T.astype(B16)

    def deliver(t, who):
        for cc in range(2):
            for yy in range(2):
                own = both(p.u == t * 2 + cc, y == yy)
                src = osend.at[t, cc * 128 : cc * 128 + 128]
                dev = (sid(seg * 2 + t // 2, t % 2, cc), yy)
                mail.send(src, orecv.at[p.head], rso.at[p.head], dev, both(who, jnp.logical_not(own)))

                @pl.when(both(who, own))
                def _(cc=cc):
                    orecv[p.head] = osend[t, cc * 128 : cc * 128 + 128]

    for t in range(4):
        pl.when(p.unit)(functools.partial(near_attention, t))
        pl.when(first)(functools.partial(conclude, t))
        deliver(t, first)
        if t == 2:
            chain(2)
        if t == 0:
            mail.got(wo.at[1 - y, whalf], rsy.at[0], p.ny)
            mail.send(wo.at[1 - y, whalf], wo.at[1 - y, whalf], rsy.at[4], p.nc)
    pl.when(second)(far_ready)
    for t in range(4):
        pl.when(second)(functools.partial(far_attention, t))
        pl.when(second)(functools.partial(conclude, t))
        deliver(t, second)
    chain(3)
    for zq in range(4):
        s = sid(zq, 1 - x, c)
        mail.got(rows_of(s), rsw.at[s], p.nx)
        give(s, p.nc)

    for hh in range(12):
        mine = both(p.unit, p.head == hh)
        pl.when(jnp.logical_not(mine))(lambda hh=hh: mail.got(orecv.at[hh], rso.at[hh], p.nx))
    for a in range(6):
        e, o = halves(orecv[2 * a].astype(F32), orecv[2 * a + 1].astype(F32))
        attn[0:128, a * 128 : a * 128 + 128] = e.astype(B16)
        attn[128:256, a * 128 : a * 128 + 128] = o.astype(B16)
    mail.got(wo.at[1 - y, pl.ds(pl.multiple_of((1 - c) * 192, 64), 192)], rsy.at[4], p.nc)
    mail.got(dyp.at[1 - y], rsy.at[1], p.ny)
    pair = pl.multiple_of(p.u * 2, 2)
    for par in range(2):
        for yy in range(2):
            at = pl.ds(par * 128 + yy * 64, 64)
            hid[at] = xs[pair + yy, par * 64 : par * 64 + 64].astype(F32)
            dys[at] = dyp[yy, par * 64 : par * 64 + 64]
    hid[...] = hid[...] + dot(attn[...], wo[...].reshape(768, 768)) + row(bo_ref)
    z2, _inv = norm_parts(hid[...])
    n2s[...] = (z2 * row(g2_ref) + row(b2_ref)).astype(B16)
    for i in range(8):
        s = sid(i // 2, i % 2, 1 - c)
        mail.got(rows_of(s), rsw.at[s], p.nc)

    k0 = 0.7978845608028654
    vb1[z] = jnp.zeros((8, 768), F32)

    def ffn_step(i, _):
        cols = pl.ds(pl.multiple_of(i * 256, 256), 256)
        dcols = pl.ds(pl.multiple_of(1536 + i * 256, 256), 256)
        up, dn = wb[:, cols], wb[:, dcols]
        pre = dot(n2s[...], up) + buph[:, cols]
        sq = pre * pre
        th = jnp.tanh(k0 * pre * (1.0 + 0.044715 * sq))
        half = 0.5 * (1.0 + th)
        act = (pre * half).astype(B16)
        slope = half + 0.5 * pre * (1.0 - th * th) * (k0 * (1.0 + 3.0 * 0.044715 * sq))
        dp = dot(dys[...], dn) * slope
        buph[:, cols] = jnp.sum(dp, axis=0, keepdims=True)
        dpl = dp.astype(B16)
        acts[:, cols] = act
        dpre[:, cols] = dpl
        return 0

    lax.fori_loop(0, 6, ffn_step, 0)
    for k in range(3):
        ys[k] = dot_nt(dpre[...], wb[k * 256 : k * 256 + 256, 0:1536]).astype(B16)
        mail.send(ys.at[k], yr.at[k], rsy.at[5 + k], p.ny)
    facc[...] = dot_nt(acts[:, 0:768], wb[:, 1536:2304]) + dot_nt(acts[:, 768:1536], wb[:, 2304:3072])
    for par in range(2):
        fo[par * 64 : par * 64 + 64] = facc[pl.ds(pl.multiple_of(par * 128 + y * 64, 64), 64)]
        fs[par * 64 : par * 64 + 64] = facc[pl.ds(pl.multiple_of(par * 128 + (1 - y) * 64, 64), 64)].astype(B16)

    n2t[...] = n2s[...].astype(F32).T.astype(B16)
    dyt[...] = dys[...].astype(F32).T.astype(B16)

    def owners(ref, xx, cc):
        at = [pl.ds(pl.multiple_of(sid(zz, xx, cc) * 48, 16), 48) for zz in range(4)]
        up = jnp.concatenate([n2t[i] for i in at], axis=0)
        dn = jnp.concatenate([dyt[i] for i in at], axis=0)

        def step(i, _):
            cols = pl.ds(pl.multiple_of(i * 256, 256), 256)
            dcols = pl.ds(pl.multiple_of(1536 + i * 256, 256), 256)
            u = dot(up, dpre[:, cols]).astype(B16)
            d = dot(dn, acts[:, cols]).astype(B16)
            for zz in range(4):
                ref[zz, :, cols] = u[zz * 48 : zz * 48 + 48]
                ref[zz, :, dcols] = d[zz * 48 : zz * 48 + 48]
            return 0

        lax.fori_loop(0, 6, step, 0)

    out_sum = Reduce(p, mail, gwo, hc, hxs, hxr, hzs, hzr, rhc, rhx, rhz)

    def ffn_over_x(i):
        zz = ring[i]
        gb[zz] = (gb[zz].astype(F32) + ra[zz].astype(F32)).astype(B16)
        mail.send(gb.at[zz], gxr.at[zz], rgx.at[zz], p.nx)

    def ffn_column(zz):
        mail.got(gxr.at[zz], rgx.at[zz], p.nx)
        return ge[zz].astype(F32) + rb[zz].astype(F32) + gxr[zz].astype(F32)

    def ffn_over_z(i):
        zz = ring[i]
        ge[zz] = ffn_column(zz).astype(B16)
        mail.send(ge.at[zz], gzr.at[i], rgz.at[i], p.nz)

    def ffn_over_far():
        zz = ring[1]
        mail.got(gzr.at[0], rgz.at[0], p.nz)
        ge[zz] = (ffn_column(zz) + gzr[0].astype(F32)).astype(B16)
        mail.send(ge.at[zz], gzr.at[1], rgz.at[1], p.far)

    ring = out_sum.order()
    owners(ga, 1 - x, 1 - c)
    mail.send(ga, ra, rga.at[0], p.nc)
    owners(gb, 1 - x, c)
    mail.got(ra, rga.at[0], p.nc)
    ffn_over_x(0)
    owners(gd, x, 1 - c)
    mail.send(gd, rb, rga.at[1], p.nc)
    owners(ge, x, c)
    @pl.when(p.unit)
    def _():
        for t in range(4):
            kt[t + 2] = ka[t + 2].astype(F32).T.astype(B16)
        dqt[...] = jnp.zeros_like(dqt)

    @pl.when(second)
    def _():
        for h in range(2):
            kt[h] = ka[h].astype(F32).T.astype(B16)

    for k in range(3):
        mail.got(yr.at[k], rsy.at[5 + k], p.ny)
    mail.send(fs, fr, rsy.at[3], p.ny)
    dn2 = jnp.concatenate([ys[k].astype(F32) + yr[k].astype(F32) for k in range(3)], axis=1)
    z2, inv2 = norm_parts(hid[...])
    dh = dys[...].astype(F32) + norm_grad(z2, inv2, dn2 * row(g2_ref))
    facc[...] = dh
    dacc[...] = dn2 * z2
    da_ = dot_nt(dh.astype(B16), wo[y])
    for a in range(3):
        e, o = halves(da_[0:128, a * 128 : a * 128 + 128], da_[128:256, a * 128 : a * 128 + 128])
        dpk[2 * a] = e.astype(B16)
        dpk[2 * a + 1] = o.astype(B16)

    mine_t = p.zl * 2 + x
    crow = pl.ds(pl.multiple_of(c * 128, 128), 128)
    for h, u in enumerate(UNITS):
        mail.send(dpk.at[h], dor.at[mine_t, crow], rdo.at[p.u], (seg * 8 + u, y), p.u != u)

        @pl.when(p.u == u)
        def _(h=h):
            dor[mine_t, crow] = dpk[h]

    gwo[...] = dot(dh.T.astype(B16), attn[:, pl.ds(pl.multiple_of(y * 384, 128), 384)]).astype(B16)
    out_sum.cores()
    ffn_over_x(1)
    mail.got(rb, rga.at[1], p.nc)
    ffn_over_z(0)
    out_sum.over_x()
    mail.got(fr, rsy.at[3], p.ny)
    sums = [jnp.zeros((1, 768), F32)] * 4
    for par in range(2):
        at = pl.ds(pl.multiple_of(par * 128 + y * 64, 64), 64)
        to = slice(par * 64, par * 64 + 64)
        dh_s[to] = facc[at]
        dn2_own = jnp.concatenate([ys[k, at].astype(F32) + yr[k, at].astype(F32) for k in range(3)], axis=1)
        own = (dacc[at], dn2_own, facc[at], dys[at].astype(F32))
        sums = [total + jnp.sum(v, axis=0, keepdims=True) for total, v in zip(sums, own)]
        fo[to] = hid[at] + fo[to] + fr[to].astype(F32) + row(bd_ref)
    back = mixed((128, 128), 1, 0)
    lout[...] = dot(back, fo[...].astype(B16)).astype(B16)
    for i in range(4):
        vb1[z, i : i + 1] = sums[i]
    for half in range(2):

        @pl.when(y == half)
        def _(half=half):
            for k in range(2):
                vb1[z, 4 + 2 * half + k : 5 + 2 * half + k] = buph[:, k * 768 : k * 768 + 768]

    early = Total(p, mail, vb1, vr1, rv1, rv2)
    late = Total(p, mail, vb2, vr2, rv3, rv4)
    early.start()
    ffn_over_x(2)

    def prepare():
        for i in range(8):
            pl.when(p.u != i)(lambda i=i: mail.got(dor.at[i // 2, (i % 2) * 128 : (i % 2) * 128 + 128], rdo.at[i], p.nx))
        low = iota((256, 128), 1) < 64
        for t in range(4):
            d = dor[t].astype(F32)
            doa[t, 0:256] = jnp.where(low, d, 0.0).astype(B16)
            doa[t, 256:512] = jnp.where(low, pltpu.roll(d, 64, 1), 0.0).astype(B16)
            prod = d.T * ot[t]
            delta[t, :, 0:256] = jnp.sum(prod[:64], axis=0, keepdims=True)
            delta[t, :, 256:512] = jnp.sum(prod[64:], axis=0, keepdims=True)

    pl.when(p.unit)(prepare)
    ffn_over_x(3)

    def score_grads(cc, q, do, st, lse_row, delta_row):
        pr = jnp.exp(st - lse_row)
        ds = (pr * (dot_nt(va[cc], do) - delta_row)).astype(B16)
        dva[...] += dot(pr.astype(B16), do)
        dka[...] += dot(ds, q)
        return dot(kt[cc], ds)

    def clear():
        dka[...] = jnp.zeros_like(dka)
        dva[...] = jnp.zeros_like(dva)

    def far_grads(cc):
        clear()

        def step(t, _):
            q, do = qa[t, farcols], doa[t, farcols]
            dqt[t, :, farcols] += score_grads(cc, q, do, dot_nt(ka[cc], q), lse[t, :, farcols], delta[t, :, farcols])
            return 0

        lax.fori_loop(0, 4, step, 0)
        low = iota((512, 128), 1) < 64
        pack = jnp.where(low, dka[...], pltpu.roll(dva[...], 64, 1)).astype(B16)
        dfs[2 * cc] = pack[:256]
        dfs[2 * cc + 1] = pack[256:]

    for cc in range(2):
        pl.when(second)(functools.partial(far_grads, cc))
        mail.send(dfs.at[2 * cc : 2 * cc + 2], dfr.at[2 * cc : 2 * cc + 2], rdf.at[cc], p.far, second)
    ffn_over_far()

    def near(t):
        clear()
        q, do = qa[t], doa[t]
        dqt[t] += score_grads(t + 2, q, do, causal(dot_nt(ka[t + 2], q)), lse[t], delta[t])
        for tq in range(t + 1, 4):
            q, do = qa[tq], doa[tq]
            dqt[tq] += score_grads(t + 2, q, do, dot_nt(ka[t + 2], q), lse[tq], delta[tq])
        dtt[64:128, t * 512 : t * 512 + 512] = dka[...].T[:64].astype(B16)
        dtt[128:192, t * 512 : t * 512 + 512] = dva[...].T[:64].astype(B16)

    def add_far(t):
        rows = dfr[t].astype(F32).T
        at = pl.ds(pl.multiple_of(t * 512 + p.parity * 256, 256), 256)
        dtt[64:128, at] = (dtt[64:128, at].astype(F32) + rows[:64]).astype(B16)
        dtt[128:192, at] = (dtt[128:192, at].astype(F32) + rows[64:]).astype(B16)

    out_sum.over_z(0)
    pl.when(p.unit)(lambda: near(0))
    out_sum.over_far()
    ffn_over_z(2)
    out_sum.over_z(2)
    early.middle()
    pl.when(p.unit)(lambda: near(1))
    pl.when(p.unit)(lambda: near(2))
    pl.when(p.unit)(lambda: near(3))
    woag[p.s] = out_sum.result().astype(B16)
    spread_out = Spread(p, mail, woag, rwo, False)
    spread_out.first()

    @pl.when(first)
    def _():
        for cc in range(2):
            mail.got(dfr.at[2 * cc : 2 * cc + 2], rdf.at[cc], p.far)
        for t in range(4):
            add_far(t)

    @pl.when(p.unit)
    def _():
        for t in range(4):
            dtt[0:64, t * 512 : t * 512 + 512] = (dqt[t, 0:64] * 0.125).astype(B16)
            for k in range(3):
                e = dtt[k * 64 : k * 64 + 64, t * 512 : t * 512 + 256].astype(F32)
                o = dtt[k * 64 : k * 64 + 64, t * 512 + 256 : t * 512 + 512].astype(F32)
                packs[t, k] = jnp.concatenate([e, o], axis=0).T.astype(B16)

    for t in range(4):
        for cc in range(2):
            u = t * 2 + cc
            mail.send(packs.at[t, :, cc * 128 : cc * 128 + 128], dqr.at[p.hl], rdq.at[p.hl], (seg * 8 + u, y), both(p.unit, p.u != u))

            @pl.when(both(p.unit, p.u == u))
            def _(t=t, cc=cc):
                dqr[p.hl] = packs[t, :, cc * 128 : cc * 128 + 128]

    vb2[z] = jnp.zeros((8, 768), F32)
    spread = Spread(p, mail, wag, rag, True)

    @pl.when(p.unit)
    def _():
        dw = dot(dtt[...], ns[...].reshape(2048, 768))
        for h in range(2):
            wms[h] = dw[h * 96 : h * 96 + 96].astype(B16)
        bias = dot_nt(jnp.ones((16, 2048), B16), dtt[...])[0:8]
        at = pl.ds(pl.multiple_of(p.head // 2 * 128, 128), 128)
        lane = iota((8, 128), 1) < 64
        low_q, low_v = jnp.where(lane, bias[:, 0:128], 0.0), jnp.concatenate([bias[:, 128:192], jnp.zeros((8, 64), F32)], axis=1)
        for odd in range(2):

            @pl.when(p.head % 2 == odd)
            def _(odd=odd):
                for i, v in enumerate((low_q, low_v)):
                    vb2[z, 2 + i : 3 + i, at] = (pltpu.roll(v, 64, 1) if odd else v)[0:1]

    mail.send(wms.at[1 - seg], wmr, rwm.at[0], p.far, p.unit)

    for h, u in enumerate(UNITS):
        pl.when(p.u != u)(lambda h=h: mail.got(dqr.at[h], rdq.at[h], p.nx))
    for k in range(3):
        for a in range(3):
            e, o = halves(dqr[2 * a, k].astype(F32), dqr[2 * a + 1, k].astype(F32))
            col = slice(a * 128, a * 128 + 128)
            dall[k, 0:128, col] = e.astype(B16)
            dall[k, 128:256, col] = o.astype(B16)
    facc[...] = dot_nt(dall[0], wq_ref[0]) + dot_nt(dall[1], wq_ref[1]) + dot_nt(dall[2], wq_ref[2])
    for par in range(2):
        dns[par * 64 : par * 64 + 64] = facc[pl.ds(pl.multiple_of(par * 128 + (1 - y) * 64, 64), 64)].astype(B16)
    mail.send(dns, dnr, rdn.at[0], p.ny)

    @pl.when(p.unit)
    def _():
        mail.got(wmr, rwm.at[0], p.far)
        wag[p.s] = (wms[seg].astype(F32) + wmr[...].astype(F32)).astype(B16)

    spread.first()
    spread_out.second()
    z1, inv1 = norm_parts(xs[b].astype(F32))
    mail.got(dnr, rdn.at[0], p.ny)
    own = [facc[pl.ds(pl.multiple_of(par * 128 + y * 64, 64), 64)] for par in range(2)]
    dn1 = jnp.concatenate(own, axis=0) + dnr[...].astype(F32)
    vb2[z, 0:1] = jnp.sum(dn1 * z1, axis=0, keepdims=True)
    vb2[z, 1:2] = jnp.sum(dn1, axis=0, keepdims=True)
    late.start()
    rest = dh_s[...] + norm_grad(z1, inv1, dn1 * row(g1_ref))
    result = jnp.zeros((128, 768), F32)
    for _k in range(3):
        piece = rest.astype(B16)
        result = result + dot(back, piece)
        rest = rest - piece.astype(F32)
    gin[...] = result
    spread.second()
    spread_out.third()
    late.middle()
    spread.third()
    spread_out.fourth()
    o_tot[0] = early.finish()
    spread.fourth()
    o_tot[1] = late.finish()
    total = ffn_column(z)
    for i in (1, 2):
        mail.got(gzr.at[i], rgz.at[i], p.nz)
        total = total + gzr[i].astype(F32)
    o_ud[0] = total[:, :1536]
    o_ud[1] = total[:, 1536:]
    spread_out.last()
    spread.last()
    mail.close()


def write_out(lout, gin, wag, woag, ud, tot, o_l, o_g, o_g1, o_b1, o_wq, o_bqv, o_wo, o_bo, o_g2, o_b2, o_up, o_bup, o_dn, o_bd):
    o_l[...] = lout[...]
    o_g[...] = gin[...]
    o_up[...] = ud[0]
    o_dn[...] = ud[1]
    for i, ref in enumerate((o_g2, o_b2, o_bo, o_bd)):
        ref[...] = tot[0, i : i + 1].reshape(768)
    for i in range(4):
        o_bup[i * 768 : i * 768 + 768] = tot[0, 4 + i : 5 + i].reshape(768)
    o_g1[...] = tot[1, 0:1].reshape(768)
    o_b1[...] = tot[1, 1:2].reshape(768)
    o_wo[...] = woag[...].reshape(768, 384).astype(F32).T
    for a in range(3):
        u0, u1 = UNITS[2 * a], UNITS[2 * a + 1]
        col = slice(a * 128, a * 128 + 128)
        w0 = jnp.concatenate([wag[u0, 0:96], wag[u0 + 8, 0:96]], axis=0).astype(F32)
        w1 = jnp.concatenate([wag[u1, 0:96], wag[u1 + 8, 0:96]], axis=0).astype(F32)
        for k in range(3):
            at = slice(k * 64, k * 64 + 64)
            o_wq[k, :, col] = jnp.concatenate([w0[at], w1[at]], axis=0).T
    half = lax.axis_index("head")
    o_bqv[...] = tot[1, 2:4, pl.ds(pl.multiple_of(half * 384, 128), 384)]


SLOTS = 40


def count_table():
    kinds = np.array([[0, 0, 0, 0], [1, 0, 0, 0], [1, 1, 0, 0], [1, 0, 1, 0], [1, 1, 1, 1]], np.float64)
    shared = kinds @ kinds.T
    table = np.zeros((24, 128), np.float64)
    low = lambda v: float(np.asarray(v, dtype=ml_dtypes.bfloat16).astype(np.float64))
    for i in range(5):
        for k in range(5):
            for base, count in ((64, 1.0 + shared[i, k]), (80, shared[i, k])):
                rest = float(np.log(count)) if count > 0 else 0.0
                for e in range(3):
                    table[i, base + 3 * k + e] = low(rest)
                    rest -= low(rest)
        table[i, 96:101] = [NEGATIVE, NEGATIVE, 0.0, NEGATIVE, NEGATIVE]
        table[8 + i, 64 + 3 * i : 67 + 3 * i] = 1.0
        table[16 + i, 80 + 3 * i : 83 + 3 * i] = 1.0
        table[8 + i, 98] = table[16 + i, 98] = 1.0
    return table.astype(np.float32)


def vm(*shape):
    return pltpu.VMEM(shape, B16)


def vf(*shape):
    return pltpu.VMEM(shape, F32)


def dma(*shape):
    return pltpu.SemaphoreType.DMA(shape)


def in_vmem(count):
    return [pl.BlockSpec(memory_space=pltpu.VMEM)] * count


def fast(
    layer_input, doc_ids, cotangent, ln1_gain, ln1_bias, w_qkv, bias_qv, w_out, b_out, ln2_gain, ln2_bias, w_up, b_up, w_down, b_down
):
    out = lambda shape, dtype=F32: jax.ShapeDtypeStruct(shape, dtype)
    shapes = (
        out((128, 768), B16), out((128, 768)), out((768,)), out((768,)), out((3, 768, 384)), out((2, 384)), out((384, 768)), out((768,)),
        out((768,)), out((768,)), out((48, 1536)), out((3072,)), out((48, 1536)), out((768,)),
    )
    raw = (out((128, 768), B16), out((128, 768)), out((16, 96, 768), B16), out((16, 48, 384), B16), out((2, 48, 1536)), out((2, 8, 768)))
    scratch = [
        vm(4, 512, 128), vm(6, 512, 128), vm(6, 512, 128), vm(4, 512, 768), vf(4, 1, 512), vf(4, 128, 256), vm(6, 128, 128),
        vm(768, 384), vf(128, 768), vm(768, 384), vf(1, 384), vf(1, 1536), vf(4, 1, 512), vf(4, 128, 512),
        vm(16, 128, 768), vf(17, 8, 128), vm(768, 3072), vm(2, 384, 768), vm(2, 128, 768), vm(12, 128, 128), vm(4, 256, 128),
        vm(4, 256, 128), vm(4, 256, 128), vm(256, 768), vm(6, 128, 512), vf(256, 768), vm(256, 768), vm(256, 768), vm(256, 1536),
        vm(256, 1536), vf(256, 768), vf(256, 768), vm(3, 256, 256), vm(3, 256, 256), vm(128, 768), vm(128, 768), vf(128, 768),
        vm(4, 256, 128), vm(4, 512, 128), vf(4, 1, 512), vm(6, 128, 512), vf(512, 128), vf(512, 128), vf(4, 128, 512), vm(192, 2048),
        vm(4, 256, 128), vm(4, 256, 128), vm(4, 3, 256, 128), vm(6, 3, 128, 128), vm(2, 96, 768), vm(96, 768),
        vm(768, 256), vm(768, 256), *[vm(4, 48, 3072)] * 8,
        vm(2, 4, 48, 384), vm(4, 48, 384), vm(4, 48, 384), vm(4, 48, 384), vm(4, 48, 384), vm(3, 256, 384), vm(128, 768), vm(128, 768),
        vf(4, 8, 768), vf(8, 8, 768), vf(4, 8, 768), vf(8, 8, 768),
        dma(SLOTS), dma(3, 8), dma(3, 8), dma(3), dma(16), dma(12), dma(2), dma(8), dma(8), dma(2), dma(4), dma(3), dma(2, 4), dma(4),
        dma(3), dma(2), dma(6), dma(1), dma(16), dma(16), dma(1), dma(4), dma(8), dma(4), dma(8),
    ]
    args = (
        layer_input, doc_ids, cotangent, ln1_gain, ln1_bias, w_qkv.transpose(1, 0, 2), bias_qv, w_out, b_out, ln2_gain, ln2_bias, w_up,
        b_up, w_down.T, b_down, jnp.asarray(count_table()),
    )
    found = pl.pallas_call(
        kernel, out_shape=raw, in_specs=in_vmem(len(args)), out_specs=tuple(in_vmem(len(raw))), scratch_shapes=scratch,
        compiler_params=pltpu.CompilerParams(collective_id=0, has_side_effects=True, vmem_limit_bytes=LIMIT),
    )(*args)
    outs = pl.pallas_call(
        write_out, out_shape=shapes, in_specs=in_vmem(len(raw)), out_specs=tuple(in_vmem(len(shapes))),
        compiler_params=pltpu.CompilerParams(vmem_limit_bytes=LIMIT),
    )(*found)
    outs = list(outs)
    outs[4] = outs[4].transpose(1, 0, 2)
    outs[12] = outs[12].T
    return tuple(outs)


def from_behind(value, axis, by):
    length = lax.axis_size(axis)
    pairs = [(i, i + by) for i in range(length) if 0 <= i + by < length]
    return lax.ppermute(value, axis, pairs)


def layer_norm(values, gain, shift):
    mean = jnp.mean(values, axis=-1, keepdims=True)
    centred = values - mean
    spread = jnp.mean(centred * centred, axis=-1, keepdims=True)
    return centred * lax.rsqrt(spread + EPS) * gain + shift


def gelu_tanh(values):
    return jax.nn.gelu(values, approximate=True)


def pick_block(length, limit):
    chosen = 1
    for candidate in range(1, min(length, limit) + 1):
        if length % candidate == 0:
            chosen = candidate
    return chosen


def pair_counts(query_pos, key_pos, head_ids):
    total = None
    for factor, rate in LEVELS:
        width = SEG * factor
        same = query_pos[:, :, None] // width == key_pos[:, None, :] // width
        offset = (head_ids % rate)[:, None]
        pick_query = query_pos % width % rate == offset
        pick_key = key_pos % width % rate == offset
        joint = (same & pick_query[:, :, None] & pick_key[:, None, :]).astype(jnp.float32)
        total = joint if total is None else total + joint
    return total


def block_terms(
    query_blk, query_pos, query_doc, key_blk, key_pos, key_doc, head_ids, nearby, scale
):
    scores = (
        jnp.einsum("qhe,khe->hqk", query_blk, key_blk, preferred_element_type=jnp.float32) * scale
    )
    counts = pair_counts(query_pos, key_pos, head_ids)
    same_segment = query_pos[:, :, None] // SEG == key_pos[:, None, :] // SEG
    keep = same_segment if nearby else jnp.logical_not(same_segment)
    allowed = (
        keep
        & (key_pos[:, None, :] <= query_pos[:, :, None])
        & (query_doc[:, :, None] == key_doc[:, None, :])
    )
    return (scores, counts * allowed.astype(jnp.float32))


def per_device(
    layer_input,
    doc_ids,
    cotangent,
    ln1_gain,
    ln1_bias,
    w_qkv,
    bias_qv,
    w_out,
    b_out,
    ln2_gain,
    ln2_bias,
    w_up,
    b_up,
    w_down,
    b_down,
):
    seq_count = lax.axis_size("seq")
    local_heads = HEADS // lax.axis_size("head")
    local_width = local_heads * HEAD_DIM
    scale = HEAD_DIM ** (-0.5)
    f32 = jnp.float32
    b16 = jnp.bfloat16
    x_float = layer_input.astype(f32)
    norm_one = layer_norm(x_float, ln1_gain, ln1_bias)
    norm_rows, row_doc = (
        lax.all_gather(norm_one.astype(b16), "head", axis=0, tiled=True),
        lax.all_gather(doc_ids, "head", axis=0, tiled=True),
    )
    seq_tokens = norm_rows.shape[0]
    half = seq_tokens // 2
    total_tokens = seq_tokens * seq_count
    total_half = total_tokens // 2
    first_pos = lax.axis_index("seq") * seq_tokens
    last_pos = first_pos + seq_tokens - 1
    local_offsets = jnp.arange(seq_tokens, dtype=jnp.int32)
    query_pos = (first_pos + local_offsets)[None, :]
    query_doc = row_doc[None, :]
    head_ids = lax.axis_index("head") * local_heads + jnp.arange(local_heads, dtype=jnp.int32)
    parity = head_ids % 2
    pick_even = parity == 0

    def compact(rows):
        paired = rows.reshape((half, 2) + rows.shape[1:])
        mask = pick_even.reshape((1, local_heads) + (1,) * (rows.ndim - 2))
        return jnp.where(mask, paired[:, 0], paired[:, 1])

    def expand(rows):
        mask = pick_even.reshape((1, local_heads) + (1,) * (rows.ndim - 2))
        zeros = jnp.zeros_like(rows)
        paired = jnp.stack([jnp.where(mask, rows, zeros), jnp.where(mask, zeros, rows)], axis=1)
        return paired.reshape((seq_tokens,) + rows.shape[1:])

    mixed = jnp.einsum("td,dch->tch", norm_rows, w_qkv, preferred_element_type=f32)
    zero_row = jnp.zeros((1, local_width), f32)
    bias_all = jnp.concatenate([bias_qv[0:1], zero_row, bias_qv[1:2]], axis=0)
    qkv = (mixed + bias_all[None]).astype(b16)
    queries = qkv[:, 0]
    query_heads = queries.reshape(seq_tokens, local_heads, HEAD_DIM)
    key_heads = qkv[:, 1].reshape(seq_tokens, local_heads, HEAD_DIM)
    value_heads = qkv[:, 2].reshape(seq_tokens, local_heads, HEAD_DIM)
    local_keys_c = compact(key_heads)
    local_values_c = compact(value_heads)
    far_keys_all, far_values_all, doc_all = (
        lax.all_gather(local_keys_c, "seq", axis=0, tiled=True),
        lax.all_gather(local_values_c, "seq", axis=0, tiled=True),
        lax.all_gather(row_doc, "seq", axis=0, tiled=True),
    )
    segment_count = SEG // seq_tokens
    own_pair = jnp.stack([key_heads, value_heads], axis=1)
    pair_pieces = [own_pair]
    for step in range(1, segment_count):
        pair_pieces.append(from_behind(own_pair, "seq", step))
    near_pairs = jnp.concatenate(pair_pieces, axis=0)
    near_keys = near_pairs[:, 0]
    near_values = near_pairs[:, 1]
    near_flat = jnp.concatenate(
        [first_pos - step * seq_tokens + local_offsets for step in range(segment_count)]
    )
    near_doc = jnp.take(doc_all, jnp.clip(near_flat, 0, total_tokens - 1))[None, :]
    near_pos = near_flat[None, :]
    far_pos = 2 * jnp.arange(total_half, dtype=jnp.int32)[None, :] + parity[:, None]
    doc_pairs = doc_all.reshape(total_half, 2)
    far_doc = jnp.where(pick_even[:, None], doc_pairs[:, 0][None, :], doc_pairs[:, 1][None, :])
    key_block = pick_block(total_half, block_limit)
    blocks = total_half // key_block
    far_key_blocks = far_keys_all.reshape(blocks, key_block, local_heads, HEAD_DIM)
    far_value_blocks = far_values_all.reshape(blocks, key_block, local_heads, HEAD_DIM)
    far_pos_blocks = far_pos.reshape(local_heads, blocks, key_block).transpose(1, 0, 2)
    far_doc_blocks = far_doc.reshape(local_heads, blocks, key_block).transpose(1, 0, 2)
    far_begin = jnp.arange(blocks, dtype=jnp.int32) * (2 * key_block)

    def merge_stats(current, key_blk, key_pos, key_doc, nearby):
        peak, running = current
        scores, counts = block_terms(
            query_heads, query_pos, query_doc, key_blk, key_pos, key_doc, head_ids, nearby, scale
        )
        live = counts > 0
        new_peak = jnp.maximum(peak, jnp.max(jnp.where(live, scores, NEGATIVE), axis=2))
        terms = jnp.where(live, counts * jnp.exp(scores - new_peak[:, :, None]), 0.0)
        return (new_peak, running * jnp.exp(peak - new_peak) + jnp.sum(terms, axis=2))

    start_state = (
        jnp.full((local_heads, seq_tokens), NEGATIVE, f32),
        jnp.zeros((local_heads, seq_tokens), f32),
    )
    near_state = merge_stats(start_state, near_keys, near_pos, near_doc, True)

    def stats_step(state, item):
        key_blk, pos_blk, doc_blk, begin = item
        return (
            lax.cond(
                begin <= last_pos,
                lambda current: merge_stats(current, key_blk, pos_blk, doc_blk, False),
                lambda current: current,
                state,
            ),
            None,
        )

    (peak_all, running_all), _ = lax.scan(
        stats_step, near_state, (far_key_blocks, far_pos_blocks, far_doc_blocks, far_begin)
    )
    lse = peak_all + jnp.log(running_all)

    def add_output(current, key_blk, value_blk, key_pos, key_doc, nearby):
        scores, counts = block_terms(
            query_heads, query_pos, query_doc, key_blk, key_pos, key_doc, head_ids, nearby, scale
        )
        probs = jnp.where(counts > 0, counts * jnp.exp(scores - lse[:, :, None]), 0.0).astype(b16)
        return current + jnp.einsum("hqk,khe->qhe", probs, value_blk, preferred_element_type=f32)

    zero_heads = jnp.zeros((seq_tokens, local_heads, HEAD_DIM), f32)
    near_output = add_output(zero_heads, near_keys, near_values, near_pos, near_doc, True)

    def output_step(accum, item):
        key_blk, value_blk, pos_blk, doc_blk, begin = item
        return (
            lax.cond(
                begin <= last_pos,
                lambda current: add_output(current, key_blk, value_blk, pos_blk, doc_blk, False),
                lambda current: current,
                accum,
            ),
            None,
        )

    attn_exact, _ = lax.scan(
        output_step,
        near_output,
        (far_key_blocks, far_value_blocks, far_pos_blocks, far_doc_blocks, far_begin),
    )
    attn_low = attn_exact.reshape(seq_tokens, local_width).astype(b16)
    branch = lax.psum_scatter(
        jnp.dot(attn_low, w_out, preferred_element_type=f32).astype(jnp.bfloat16),
        "head",
        scatter_dimension=0,
        tiled=True,
    ).astype(jnp.float32)
    hidden_one = x_float + branch + b_out
    norm_two = layer_norm(hidden_one, ln2_gain, ln2_bias)
    norm_low = norm_two.astype(b16)
    dy_low = (cotangent.astype(f32) * (doc_ids >= 0).astype(f32)[:, None]).astype(b16)
    dy_float = dy_low.astype(f32)
    up_rows, down_rows = (
        lax.all_gather(w_up, "seq", axis=0, tiled=True),
        lax.all_gather(w_down, "seq", axis=1, tiled=True),
    )
    up_full, down_full = (
        lax.all_gather(up_rows, "head", axis=1, tiled=True),
        lax.all_gather(down_rows, "head", axis=0, tiled=True),
    )
    pre_act = jnp.dot(norm_low, up_full, preferred_element_type=f32) + b_up
    act_low = gelu_tanh(pre_act).astype(b16)
    ffn_result = jnp.dot(act_low, down_full, preferred_element_type=f32)
    d_act = jnp.einsum("td,fd->tf", dy_low, down_full, preferred_element_type=f32)
    _, gelu_back = jax.vjp(gelu_tanh, pre_act)
    d_pre = gelu_back(d_act)[0]
    d_pre_low = d_pre.astype(b16)
    bias_up_grad = jnp.sum(d_pre, axis=0)
    up_parts = jnp.einsum("td,tf->df", norm_low, d_pre_low, preferred_element_type=f32)
    down_parts = jnp.einsum("tf,td->fd", act_low, dy_low, preferred_element_type=f32)
    up_grad, down_grad = (
        lax.psum_scatter(
            up_parts.astype(jnp.bfloat16), "head", scatter_dimension=1, tiled=True
        ).astype(jnp.float32),
        lax.psum_scatter(
            down_parts.astype(jnp.bfloat16), "head", scatter_dimension=0, tiled=True
        ).astype(jnp.float32),
    )
    d_norm_two = jnp.einsum("tf,df->td", d_pre_low, up_full, preferred_element_type=f32)
    layer_output = (hidden_one + ffn_result + b_down).astype(b16)
    w_up_grad, w_down_grad = (
        lax.psum_scatter(up_grad, "seq", scatter_dimension=0, tiled=True),
        lax.psum_scatter(down_grad, "seq", scatter_dimension=1, tiled=True),
    )
    _, norm_two_back = jax.vjp(layer_norm, hidden_one, ln2_gain, ln2_bias)
    d_hidden_norm, gain_two_grad, bias_two_grad = norm_two_back(d_norm_two)
    d_hidden = dy_float + d_hidden_norm
    bias_out_grad = jnp.sum(d_hidden, axis=0)
    bias_down_grad = jnp.sum(dy_float, axis=0)
    hidden_rows = lax.all_gather(d_hidden.astype(b16), "head", axis=0, tiled=True)
    w_out_part = jnp.einsum("tc,td->cd", attn_low, hidden_rows, preferred_element_type=f32)
    d_attn = jnp.einsum("td,cd->tc", hidden_rows, w_out, preferred_element_type=f32).astype(b16)
    d_attn_heads = d_attn.reshape(seq_tokens, local_heads, HEAD_DIM)
    delta_rows = jnp.sum(d_attn_heads.astype(f32) * attn_exact, axis=2)
    delta = delta_rows.T

    def score_grads(key_blk, value_blk, key_pos, key_doc, nearby):
        scores, counts = block_terms(
            query_heads, query_pos, query_doc, key_blk, key_pos, key_doc, head_ids, nearby, scale
        )
        exact = jnp.where(counts > 0, counts * jnp.exp(scores - lse[:, :, None]), 0.0)
        d_prob = jnp.einsum("qhe,khe->hqk", d_attn_heads, value_blk, preferred_element_type=f32)
        d_score = (exact * (d_prob - delta[:, :, None])).astype(b16)
        return (exact, d_score)

    exact_near, d_score_near = score_grads(near_keys, near_values, near_pos, near_doc, True)
    d_query_near = jnp.einsum("hqk,khe->qhe", d_score_near, near_keys, preferred_element_type=f32)
    near_key_grad = jnp.einsum(
        "hqk,qhe->khe", d_score_near, query_heads, preferred_element_type=f32
    )
    near_value_grad = jnp.einsum(
        "hqk,qhe->khe", exact_near.astype(b16), d_attn_heads, preferred_element_type=f32
    )
    near_pair_grads = jnp.stack([near_key_grad, near_value_grad], axis=1)
    pair_grad = near_pair_grads[:seq_tokens]
    for step in range(1, segment_count):
        piece = near_pair_grads[step * seq_tokens : (step + 1) * seq_tokens]
        pair_grad = pair_grad + from_behind(piece.astype(jnp.bfloat16), "seq", -step).astype(
            piece.dtype
        )

    def query_grad_step(accum, item):
        key_blk, value_blk, pos_blk, doc_blk, begin = item

        def query_compute(current):
            _, d_score = score_grads(key_blk, value_blk, pos_blk, doc_blk, False)
            return current + jnp.einsum(
                "hqk,khe->qhe", d_score, key_blk, preferred_element_type=f32
            )

        return (lax.cond(begin <= last_pos, query_compute, lambda current: current, accum), None)

    d_query, _ = lax.scan(
        query_grad_step,
        d_query_near,
        (far_key_blocks, far_value_blocks, far_pos_blocks, far_doc_blocks, far_begin),
    )
    d_query = d_query * scale
    stats_rows = jnp.stack([compact(lse.T), compact(delta_rows)], axis=1)
    stats_all = lax.all_gather(stats_rows, "seq", axis=0, tiled=True)
    local_key_pos = first_pos + 2 * jnp.arange(half, dtype=jnp.int32)[None, :] + parity[:, None]
    local_key_doc = compact(jnp.broadcast_to(row_doc[:, None], (seq_tokens, local_heads))).T
    zero_compact = jnp.zeros((half, local_heads, HEAD_DIM), f32)
    query_piece = lax.all_gather(compact(query_heads), "seq", axis=0, tiled=True)
    grad_piece = lax.all_gather(compact(d_attn_heads), "seq", axis=0, tiled=True)
    length = query_piece.shape[0]
    size = pick_block(length, block_limit)
    number = length // size
    pos_piece = 2 * jnp.arange(length, dtype=jnp.int32)[None, :] + parity[:, None]
    items = (
        query_piece.reshape(number, size, local_heads, HEAD_DIM),
        grad_piece.reshape(number, size, local_heads, HEAD_DIM),
        stats_all.reshape(number, size, 2, local_heads),
        pos_piece.reshape(local_heads, number, size).transpose(1, 0, 2),
        far_doc.reshape(local_heads, number, size).transpose(1, 0, 2),
    )

    def one_step(current, item):
        query_blk, grad_blk, stats_blk, pos_blk, doc_blk = item

        def one_compute(pair):
            key_grad, value_grad = pair
            scores, counts = block_terms(
                query_blk,
                pos_blk,
                doc_blk,
                local_keys_c,
                local_key_pos,
                local_key_doc,
                head_ids,
                False,
                scale,
            )
            exact = jnp.where(
                counts > 0, counts * jnp.exp(scores - stats_blk[:, 0].T[:, :, None]), 0.0
            )
            d_prob = jnp.einsum(
                "qhe,khe->hqk", grad_blk, local_values_c, preferred_element_type=f32
            )
            d_score = (exact * (d_prob - stats_blk[:, 1].T[:, :, None])).astype(b16)
            key_grad = key_grad + jnp.einsum(
                "hqk,qhe->khe", d_score, query_blk, preferred_element_type=f32
            )
            value_grad = value_grad + jnp.einsum(
                "hqk,qhe->khe", exact.astype(b16), grad_blk, preferred_element_type=f32
            )
            return (key_grad, value_grad)

        return (
            lax.cond(jnp.max(pos_blk) >= first_pos, one_compute, lambda pair: pair, current),
            None,
        )

    result, _ = lax.scan(one_step, (zero_compact, zero_compact), items)
    far_key_grad, far_value_grad = result
    d_key = (pair_grad[:, 0] + expand(far_key_grad)) * scale
    d_value = pair_grad[:, 1] + expand(far_value_grad)
    d_qkv = jnp.stack(
        [
            d_query.reshape(seq_tokens, local_width),
            d_key.reshape(seq_tokens, local_width),
            d_value.reshape(seq_tokens, local_width),
        ],
        axis=1,
    ).astype(b16)
    d_qkv_float = d_qkv.astype(f32)
    bias_qv_part = jnp.stack(
        [jnp.sum(d_qkv_float[:, 0], axis=0), jnp.sum(d_qkv_float[:, 2], axis=0)], axis=0
    )
    w_qkv_part = jnp.einsum("td,tch->dch", norm_rows, d_qkv, preferred_element_type=f32)
    d_norm_one = lax.psum_scatter(
        jnp.einsum("tch,dch->td", d_qkv, w_qkv, preferred_element_type=f32).astype(jnp.bfloat16),
        "head",
        scatter_dimension=0,
        tiled=True,
    ).astype(jnp.float32)
    _, norm_one_back = jax.vjp(layer_norm, x_float, ln1_gain, ln1_bias)
    d_x_norm, gain_one_grad, bias_one_grad = norm_one_back(d_norm_one)
    grad_input = d_hidden + d_x_norm
    w_qkv_grad, bias_qv_grad, w_out_grad = lax.psum((w_qkv_part, bias_qv_part, w_out_part), "seq")
    summed = lax.psum(
        (
            gain_one_grad,
            bias_one_grad,
            gain_two_grad,
            bias_two_grad,
            bias_out_grad,
            bias_up_grad,
            bias_down_grad,
        ),
        ("seq", "head"),
    )
    return (
        layer_output,
        grad_input,
        summed[0],
        summed[1],
        w_qkv_grad,
        bias_qv_grad,
        w_out_grad,
        summed[4],
        summed[2],
        summed[3],
        w_up_grad,
        summed[5],
        w_down_grad,
        summed[6],
    )


def solution(mesh):
    in_specs = (
        P(("seq", "head"), None),
        P(("seq", "head")),
        P(("seq", "head"), None),
        P(),
        P(),
        P(None, None, "head"),
        P(None, "head"),
        P("head", None),
        P(),
        P(),
        P(),
        P("seq", "head"),
        P(),
        P("head", "seq"),
        P(),
    )
    out_specs = (
        P(("seq", "head"), None),
        P(("seq", "head"), None),
        P(),
        P(),
        P(None, None, "head"),
        P(None, "head"),
        P("head", None),
        P(),
        P(),
        P(),
        P("seq", "head"),
        P(),
        P("head", "seq"),
        P(),
    )
    small = mesh.shape["seq"] == 16 and mesh.shape["head"] == 2
    return jax.shard_map(
        fast if small else per_device, mesh=mesh, in_specs=in_specs, out_specs=out_specs, check_vma=False
    )
```

```python
import functools

import jax
import jax.numpy as jnp
import ml_dtypes
import numpy as np
from jax import lax
from jax.experimental import pallas as pl
from jax.experimental.pallas import tpu as pltpu
from jax.sharding import PartitionSpec as P

HEADS = 12
HEAD_DIM = 64
SEG = 2048


LEVELS = ((1, 1), (2, 2), (4, 4), (8, 6), (16, 12))
EPS = 1e-05
NEGATIVE = -1e30
block_limit = 2048


MESH = pl.DeviceIdType.MESH
VMEM = pltpu.VMEM
LIMIT = 60 << 20
F32 = jnp.float32
B16 = jnp.bfloat16


def dot(a, b):
    return jnp.dot(a, b, preferred_element_type=F32)


def dot_nt(a, b):
    return lax.dot_general(a, b, (((1,), (1,)), ((), ())), preferred_element_type=F32)


def sid(z, x, c):
    return z * 4 + x * 2 + c


class Place:
    def __init__(self):
        s = lax.axis_index("seq")
        self.s, self.y = s, lax.axis_index("head")
        self.z, self.x, self.c = s // 4, (s // 2) % 2, s % 2
        self.seg, self.zl = self.z // 2, self.z % 2
        self.u = s % 8
        self.b = self.u * 2 + self.y
        self.unit = jnp.logical_and(self.u != 3, self.u != 5)
        self.hl = self.u - self.u // 4 - self.u // 6
        self.head = self.y * 6 + self.hl
        self.parity = self.head % 2
        z, x, c, y = self.z, self.x, self.c, self.y
        self.zf = z + 1 - 2 * self.zl
        self.nx, self.ny = (sid(z, 1 - x, c), y), (s, 1 - y)
        self.nz, self.nc = (sid(self.zf, x, c), y), (sid(z, x, 1 - c), y)
        self.far = (sid((z + 2) % 4, x, c), y)
        self.fb = {"x": 4 * (1 - 2 * x), "y": 1 - 2 * y, "z": 8 * (1 - 2 * self.zl), "c": 2 * (1 - 2 * c)}

    def cube(self):
        z, x, c, y = self.z, self.x, self.c, self.y
        for k in range(1, 16):
            zz = self.zf if k & 8 else z
            xx = 1 - x if k & 4 else x
            cc = 1 - c if k & 2 else c
            yy = 1 - y if k & 1 else y
            yield (sid(zz, xx, cc), yy)

    def greet(self):
        others = list(self.cube())
        others += [(sid((self.z + 2) % 4, self.x, self.c), self.y), (sid((self.zf + 2) % 4, self.x, self.c), self.y)]
        barrier = pltpu.get_barrier_semaphore()
        for dev in others:
            pl.semaphore_signal(barrier, inc=1, device_id=dev, device_id_type=MESH)
        self.greeted = len(others)

    def meet(self):
        pl.semaphore_wait(pltpu.get_barrier_semaphore(), self.greeted)


class Mail:
    def __init__(self, sems, slots):
        self.sems, self.slots, self.used, self.sent = sems, slots, 0, {}

    def send(self, src, dst, rsem, dev, cond=None):
        k = self.used % self.slots
        self.used += 1
        self.settle(k)

        def make():
            return pltpu.make_async_remote_copy(
                src_ref=src, dst_ref=dst, send_sem=self.sems.at[k], recv_sem=rsem, device_id=dev, device_id_type=MESH
            )

        if cond is None:
            make().start()
        else:
            pl.when(cond)(lambda: make().start())
        self.sent[k] = (cond, make)

    def settle(self, k):
        if k in self.sent:
            cond, make = self.sent.pop(k)
            if cond is None:
                make().wait_send()
            else:
                pl.when(cond)(lambda: make().wait_send())

    def got(self, dst, rsem, dev):
        pltpu.make_async_remote_copy(
            src_ref=dst, dst_ref=dst, send_sem=self.sems.at[0], recv_sem=rsem, device_id=dev, device_id_type=MESH
        ).wait_recv()

    def close(self):
        for k in range(self.slots):
            self.settle(k)


def both(*terms):
    out = terms[0]
    for term in terms[1:]:
        out = jnp.logical_and(out, term)
    return out


def iota(shape, dim):
    return lax.broadcasted_iota(jnp.int32, shape, dim)


def norm_parts(v):
    mean = jnp.mean(v, axis=-1, keepdims=True)
    cen = v - mean
    inv = lax.rsqrt(jnp.mean(cen * cen, axis=-1, keepdims=True) + EPS)
    return cen * inv, inv


def norm_grad(z, inv, e):
    return (e - jnp.mean(e, axis=-1, keepdims=True) - z * jnp.mean(e * z, axis=-1, keepdims=True)) * inv


def pick_type(pos, head, rows):
    v = pos - head + 24.0
    m = v - 12.0 * jnp.floor((v + 0.5) * (1.0 / 12.0))
    out = jnp.where(m == 0.0, rows[4], rows[0])
    out = jnp.where(m == 6.0, rows[3], out)
    out = jnp.where(jnp.logical_or(m == 4.0, m == 8.0), rows[2], out)
    return jnp.where(jnp.logical_or(m == 2.0, m == 10.0), rows[1], out)


def halves(e, o):
    low = iota(e.shape, 1) < 64
    return jnp.where(low, e, pltpu.roll(o, 64, 1)), jnp.where(low, pltpu.roll(e, 64, 1), o)


UNITS = (0, 1, 2, 4, 6, 7)


class Spread:
    def __init__(self, p, mail, ref, sems, some):
        self.p, self.mail, self.ref, self.sems, self.some = p, mail, ref, sems, some

    def has(self, zz, xx, cc):
        return jnp.logical_or(cc == 0, zz % 2 == xx) if self.some else None

    def go(self, s, dev, cond):
        self.mail.send(self.ref.at[s], self.ref.at[s], self.sems.at[s], dev, cond)

    def take(self, s, cond):
        def wait():
            self.mail.got(self.ref.at[s], self.sems.at[s], self.p.nx)

        if cond is None:
            wait()
        else:
            pl.when(cond)(wait)

    def first(self):
        p = self.p
        has = self.has(p.z, p.x, p.c)
        for dev in (p.far, p.nz, p.nx, p.nc):
            self.go(p.s, dev, has)

    def onward(self, zz, devs):
        s, has = sid(zz, self.p.x, self.p.c), self.has(zz, self.p.x, self.p.c)
        self.take(s, has)
        for dev in devs:
            self.go(s, dev, has)

    def second(self):
        p = self.p
        self.onward((p.z + 2) % 4, (p.nz, p.nx, p.nc))
        self.onward(p.zf, (p.nx, p.nc))

    def third(self):
        p = self.p
        self.onward((p.zf + 2) % 4, (p.nx, p.nc))

    def fourth(self):
        p = self.p
        for zz in range(4):
            s, has = sid(zz, 1 - p.x, p.c), self.has(zz, 1 - p.x, p.c)
            self.take(s, has)
            self.go(s, p.nc, has)

    def last(self):
        p = self.p
        for zz in range(4):
            for xx in range(2):
                self.take(sid(zz, xx, 1 - p.c), self.has(zz, xx, 1 - p.c))


class Reduce:
    def __init__(self, p, mail, src, gc, gxs, gxr, gzs, gzr, rc, rx, rz):
        self.__dict__.update(locals())

    def rows(self, zz, xx, cc):
        return pl.ds(pl.multiple_of(sid(zz, xx, cc) * 48, 16), 48)

    def cores(self):
        p = self.p
        for xq in range(2):
            xx = 1 - p.x if xq == 0 else p.x
            for k in (1, 2, 3, 0):
                zz = (p.z + k) % 4
                self.mail.send(self.src.at[self.rows(zz, xx, 1 - p.c)], self.gc.at[xq, zz], self.rc.at[xq, zz], p.nc)

    def order(self):
        z, zf = self.p.z, self.p.zf
        return (zf + 2) % 4, (z + 2) % 4, zf, z

    def over_x(self):
        p = self.p
        for zz in self.order():
            self.mail.got(self.gc.at[0, zz], self.rc.at[0, zz], p.nc)
            own = self.src[self.rows(zz, 1 - p.x, p.c)].astype(F32)
            self.gxs[zz] = (own + self.gc[0, zz].astype(F32)).astype(B16)
            self.mail.send(self.gxs.at[zz], self.gxr.at[zz], self.rx.at[zz], p.nx)

    def column(self, zz):
        p = self.p
        self.mail.got(self.gc.at[1, zz], self.rc.at[1, zz], p.nc)
        self.mail.got(self.gxr.at[zz], self.rx.at[zz], p.nx)
        return self.src[self.rows(zz, p.x, p.c)].astype(F32) + self.gc[1, zz].astype(F32) + self.gxr[zz].astype(F32)

    def over_z(self, i):
        self.gzs[i] = self.column(self.order()[i]).astype(B16)
        self.mail.send(self.gzs.at[i], self.gzr.at[i], self.rz.at[i], self.p.nz)

    def over_far(self):
        self.mail.got(self.gzr.at[0], self.rz.at[0], self.p.nz)
        self.gzs[1] = (self.column(self.order()[1]) + self.gzr[0].astype(F32)).astype(B16)
        self.mail.send(self.gzs.at[1], self.gzr.at[1], self.rz.at[1], self.p.far)

    def result(self):
        total = self.column(self.p.z)
        for i in (1, 2):
            self.mail.got(self.gzr.at[i], self.rz.at[i], self.p.nz)
            total = total + self.gzr[i].astype(F32)
        return total


class Total:
    def __init__(self, p, mail, one, two, sem_one, sem_two):
        self.p, self.mail, self.one, self.two, self.sem_one, self.sem_two = p, mail, one, two, sem_one, sem_two
        self.k = (p.x * 2 + p.c) * 2 + p.y

    def start(self):
        p = self.p
        for i in range(1, 4):
            dev = (sid((p.z + i) % 4, p.x, p.c), p.y)
            self.mail.send(self.one.at[p.z], self.one.at[p.z], self.sem_one.at[p.z], dev)

    def middle(self):
        p = self.p
        for i in range(1, 4):
            zz = (p.z + i) % 4
            self.mail.got(self.one.at[zz], self.sem_one.at[zz], p.nx)
        self.two[self.k] = self.one[0] + self.one[1] + self.one[2] + self.one[3]
        for i in range(1, 8):
            xx = 1 - p.x if i & 4 else p.x
            cc = 1 - p.c if i & 2 else p.c
            yy = 1 - p.y if i & 1 else p.y
            self.mail.send(self.two.at[self.k], self.two.at[self.k], self.sem_two.at[self.k], (sid(p.z, xx, cc), yy))

    def finish(self):
        for i in range(8):
            pl.when(self.k != i)(lambda i=i: self.mail.got(self.two.at[i], self.sem_two.at[i], self.p.nx))
        out = self.two[0]
        for i in range(1, 8):
            out = out + self.two[i]
        return out


def mixed(shape, dim_to, dim_from):
    r, i = iota(shape, dim_to), iota(shape, dim_from)
    return jnp.where(i == 2 * (r & 63) + (r >> 6), 1.0, 0.0).astype(B16)


def kernel(
    x_ref, doc_ref, cot_ref, g1_ref, b1_ref, wq_ref, bqv_ref, wo_own, bo_ref, g2_ref, b2_ref, wup_ref, bup_ref, wdn_ref, bd_ref, tab_ref,
    lout, gin, wag, woag, o_ud, o_tot,
    qa, ka, va, ns, lse, ot, dpk, gwo, dh_s, wqh, bqh, buph, msc, asc,
    xs, docs, wb, wo, dyp, orecv, osend, kvs, kvf, attn, vt, hid, n2s, dys, acts, dpre, facc, dacc, ys, yr, fs, fr, fo,
    dor, doa, delta, kt, dka, dva, dqt, dtt, dfs, dfr, packs, dqr, wms, wmr, n2t, dyt, ga, gb, gd, ge, ra, rb, gxr, gzr,
    hc, hxs, hxr, hzs, hzr, dall, dns, dnr, vb1, vr1, vb2, vr2,
    ss, rsx, rsc, rsd, rsw, rso, rsf, rsy, rdo, rga, rgx, rgz, rhc, rhx, rhz, rdf, rdq, rwm, rag, rwo, rdn, rv1, rv2, rv3, rv4,
):
    p = Place()
    mail = Mail(ss, SLOTS)
    seg, x, y, z, c, b = p.seg, p.x, p.y, p.z, p.c, p.b
    first, second = both(p.unit, seg == 0), both(p.unit, seg == 1)
    row = lambda ref: ref[...].reshape(1, -1)
    p.greet()

    mix = mixed((128, 128), 0, 1)
    xs[b] = dot(mix, x_ref[...]).astype(B16)
    doc_row = doc_ref[...].astype(F32).reshape(1, 128)
    turn = jnp.where(iota((128, 128), 0) == 2 * (iota((128, 128), 1) & 63), 1.0, 0.0).astype(B16)
    turn_odd = jnp.where(iota((128, 128), 0) == 2 * (iota((128, 128), 1) & 63) + 1, 1.0, 0.0).astype(B16)
    doc8 = jnp.broadcast_to(doc_row, (8, 128)).astype(B16)
    docs[b] = jnp.where(iota((8, 128), 0) == 0, dot(doc8, turn), dot(doc8, turn_odd))
    wrow = pl.ds(pl.multiple_of(p.s * 48, 16), 48)
    wb[wrow, 0:1536] = wup_ref[...]
    wb[wrow, 1536:3072] = wdn_ref[...]
    p.meet()

    dims = ("x", "y", "z")
    nbr = {"x": p.nx, "y": p.ny, "z": p.nz}
    part = [pl.ds(k * 256, 256) for k in range(3)]
    order = [[dims[(k + j) % 3] for j in range(3)] for k in range(3)]

    bit = {"x": 1, "y": 2, "z": 4}

    def place(rel):
        return b + sum(p.fb[d] for d in dims if rel & bit[d])

    def third(rel, k):
        return xs.at[place(rel), :, part[k]]

    def pass_on(k, rel, d):
        mail.send(third(rel, k), third(rel, k), rsx.at[k, rel ^ bit[d]], nbr[d])

    def to_core(k, rel):
        mail.send(third(rel, k), third(rel, k), rsc.at[k, rel], p.nc)

    for j in range(3):
        for k in range(3):
            pass_on(k, 0, order[k][j])
    for k in range(3):
        to_core(k, 0)
    special = jnp.logical_or(b == 0, b >= 14)
    for dev in p.cube():
        mail.send(docs.at[b], docs.at[b], rsd.at[b // 14 + b // 15], dev, special)

    def rows_of(s):
        return wb.at[pl.ds(pl.multiple_of(s * 48, 16), 48), :]

    def give(s, dev, cond=None):
        mail.send(rows_of(s), rows_of(s), rsw.at[s], dev, cond)


    pair_cols = pl.ds(pl.multiple_of(p.hl // 2 * 128, 128), 128)
    for odd in range(2):

        @pl.when(p.hl % 2 == odd)
        def _(odd=odd):
            for k in range(3):
                w = wq_ref[k, :, pair_cols].astype(F32)
                w = pltpu.roll(w, 64, 1) if odd else w
                wqh[:, k * 128 : k * 128 + 128] = jnp.where(iota((768, 128), 1) < 64, w, 0.0).astype(B16)
            v = jnp.concatenate([bqv_ref[:, pair_cols], jnp.zeros((6, 128), F32)], axis=0)
            v = pltpu.roll(v, 64, 1) if odd else v
            lane = iota((1, 128), 1)
            bqh[:, 0:128] = jnp.where(lane < 64, v[0:1], 0.0)
            bqh[:, 128:256] = jnp.zeros((1, 128), F32)
            bqh[:, 256:384] = jnp.where(lane < 64, v[1:2], jnp.where(lane == 64, 1.0, 0.0))

    head = p.head.astype(F32)
    for t in range(4):
        rr = iota((512, 128), 0)
        pos = (seg * SEG + t * 512 + 2 * (rr & 255) + (rr >> 8)).astype(F32)
        qa[t] = pick_type(pos, head, [tab_ref[i : i + 1] for i in range(5)]).astype(B16)
        ka[t + 2] = pick_type(pos, head, [tab_ref[8 + i : 9 + i] for i in range(5)]).astype(B16)

    real = jnp.broadcast_to(doc_row, (128, 128)).T >= 0.0
    for k in range(6):
        cols = slice(k * 128, k * 128 + 128)
        kept = jnp.where(real, cot_ref[:, cols].astype(F32), 0.0).astype(B16)
        dyp[y, :, cols] = dot(mix, kept).astype(B16)
    for half in range(2):

        @pl.when(y == half)
        def _(half=half):
            buph[...] = bup_ref[half * 1536 : half * 1536 + 1536].reshape(1, 1536)

    wo[y] = wo_own[...]

    def qkv(i):
        rows = xs[pl.ds(2 * i, 2)].reshape(256, 768).astype(F32)
        zz, _inv = norm_parts(rows)
        n1 = (zz * row(g1_ref) + row(b1_ref)).astype(B16)
        m = (dot(n1, wqh[...]) + bqh[...]).astype(B16)
        t = i // 2
        for yy in range(2):
            for par in range(2):
                at = slice(yy * 128 + par * 64, yy * 128 + par * 64 + 64)
                to = pl.ds(pl.multiple_of(par * 256 + (i % 2) * 128 + yy * 64, 64), 64)
                qa[t, to] = m[at, :128] * B16(0.125) + qa[t, to]
                ka[t + 2, to] = m[at, 128:256] + ka[t + 2, to]
                va[t + 2, to] = m[at, 256:]
                ns[t, to] = n1[at]

    def seen(k, rel):
        mail.got(third(rel, k), rsx.at[k, rel], p.nx)
        to_core(k, rel)

    def from_core(rel):
        for k in range(3):
            mail.got(xs.at[place(rel) + p.fb["c"], :, part[k]], rsc.at[k, rel], p.nc)

    def qkv_of(rel, core=0):
        at = (place(rel) + core * p.fb["c"]) // 2
        pl.when(p.unit)(lambda: qkv(at))

    def chain(d):
        up, dn = (z - d + 4) % 4, (z + d) % 4
        has_up, has_dn = z >= d, z <= 3 - d
        su, sd = sid(up, x, c), sid(dn, x, c)
        pl.when(has_up)(lambda: mail.got(rows_of(su), rsw.at[su], p.nx))
        if d < 3:
            give(su, (sid((z + 1) % 4, x, c), y), both(has_up, z <= 2))
        give(su, p.nx, has_up)
        give(su, p.nc, has_up)
        pl.when(has_dn)(lambda: mail.got(rows_of(sd), rsw.at[sd], p.nx))
        if d < 3:
            give(sd, (sid((z + 3) % 4, x, c), y), both(has_dn, z >= 1))
        give(sd, p.nx, has_dn)
        give(sd, p.nc, has_dn)

    X, Y, Z = 1, 2, 4
    for k in range(3):
        d0, d1, d2 = order[k]
        seen(k, bit[d0])
        pass_on(k, bit[d0], d1)
        pass_on(k, bit[d0], d2)
        seen(k, bit[d1])
        pass_on(k, bit[d1], d2)
        seen(k, bit[d2])
    qkv_of(0)
    for k in range(3):
        d0, d1, d2 = order[k]
        seen(k, bit[d0] | bit[d1])
        pass_on(k, bit[d0] | bit[d1], d2)
    give(p.s, (sid((z + 1) % 4, x, c), y), z <= 2)
    give(p.s, (sid((z + 3) % 4, x, c), y), z >= 1)
    give(p.s, p.nx)
    give(p.s, p.nc)
    mail.send(dyp.at[y], dyp.at[y], rsy.at[1], p.ny)
    whalf = pl.ds(pl.multiple_of(c * 192, 64), 192)
    mail.send(wo.at[y, whalf], wo.at[y, whalf], rsy.at[0], p.ny)
    for k in range(3):
        d0, d1, d2 = order[k]
        seen(k, bit[d0] | bit[d2])
        seen(k, bit[d1] | bit[d2])
    qkv_of(X)
    qkv_of(Z)
    from_core(0)
    from_core(Y)
    qkv_of(0, 1)
    for k in range(3):
        seen(k, X | Y | Z)
    qkv_of(X | Z)
    for rel in (X, Z, X | Z):
        from_core(rel)
        from_core(rel | Y)
        qkv_of(rel, 1)
        if rel == Z:
            chain(1)
    for src in (0, 14, 15):
        pl.when(b != src)(lambda src=src: mail.got(docs.at[src], rsd.at[src // 14 + src // 15], p.nx))

    lowlane = iota((256, 128), 1) < 64
    farrows = pl.ds(pl.multiple_of(p.parity * 256, 256), 256)

    @pl.when(first)
    def _():
        for t in range(4):
            kk = ka[t + 2, farrows].astype(F32)
            vv = va[t + 2, farrows].astype(F32)
            kvs[t] = jnp.where(lowlane, kk, pltpu.roll(vv, 64, 1)).astype(B16)

    mail.send(kvs, kvf, rsf.at[0], p.far, first)
    mail.send(docs.at[0], docs.at[16], rsf.at[1], p.far, first)

    def codes(src, par):
        r = docs[src, par : par + 1]
        return jnp.broadcast_to(jnp.where(r < 0.0, 4.0, r), (128, 128)).T[0:64]

    def mark(ref, at, code, query):
        lane = iota((64, 128), 1)
        hit = (lane - 96).astype(F32) == code
        if query:
            feat = jnp.where(hit, 0.0, jnp.where(lane < 101, NEGATIVE, 0.0))
        else:
            feat = jnp.where(hit, 1.0, 0.0)
        ref[at] = jnp.where(lane >= 96, feat, ref[at].astype(F32)).astype(B16)

    @pl.when(first)
    def _():
        for par in range(2):
            code = codes(0, par)
            at = slice(par * 256, par * 256 + 64)
            mark(qa.at[0], at, code, True)
            mark(ka.at[2], at, code, False)

    @pl.when(second)
    def _():
        for par in range(2):
            for yy in range(2):
                code = codes(14 + yy, par)
                at = slice(par * 256 + 128 + yy * 64, par * 256 + 192 + yy * 64)
                mark(qa.at[3], at, code, True)
                mark(ka.at[5], at, code, False)

    @pl.when(p.unit)
    def _():
        for t in range(4):
            vt[t + 2] = va[t + 2].astype(F32).T.astype(B16)

    rr, ll = iota((512, 512), 0), iota((512, 512), 1)
    causal = lambda st: jnp.where(2 * (rr & 255) + (rr >> 8) <= 2 * (ll & 255) + (ll >> 8), st, NEGATIVE)

    def near_attention(t):
        q = qa[t]

        def update(cc, carry, st):
            m, acc = carry
            m_new = jnp.maximum(m, jnp.max(st, axis=0, keepdims=True))
            pr = jnp.exp(st - m_new).astype(B16)
            return m_new, acc * jnp.exp(m - m_new) + dot(vt[cc], pr)

        state = (jnp.full((1, 512), NEGATIVE, F32), jnp.zeros((128, 512), F32))
        if t:
            state = lax.fori_loop(2, t + 2, lambda cc, s: update(cc, s, dot_nt(ka[cc], q)), state)
        msc[t], asc[t] = update(t + 2, state, causal(dot_nt(ka[t + 2], q)))

    def far_ready():
        mail.got(kvf, rsf.at[0], p.far)
        mail.got(docs.at[16], rsf.at[1], p.far)
        for t in range(4):
            rows = pl.ds((t % 2) * 256, 256)
            fpos = ((t * 256 + iota((256, 128), 0)) * 2 + p.parity).astype(F32)
            feat = pick_type(fpos, head, [tab_ref[16 + i : 17 + i] for i in range(5)])
            kv = kvf[t].astype(F32)
            ka[t // 2, rows] = jnp.where(lowlane, kv, feat).astype(B16)
            one = jnp.where(iota((256, 128), 1) == 64, 1.0, 0.0)
            va[t // 2, rows] = jnp.where(lowlane, pltpu.roll(kv, 64, 1), one).astype(B16)
        even, odd = codes(16, 0), codes(16, 1)
        mark(ka.at[0], slice(0, 64), even + p.parity.astype(F32) * (odd - even), False)
        for h in range(2):
            vt[h] = va[h].astype(F32).T.astype(B16)

    farcols = pl.ds(pl.multiple_of(p.parity * 256, 256), 256)

    def far_attention(t):
        q = qa[t, farcols]
        m = msc[t, :, farcols]
        s0, s1 = dot_nt(ka[0], q), dot_nt(ka[1], q)
        m_new = jnp.maximum(m, jnp.maximum(jnp.max(s0, axis=0, keepdims=True), jnp.max(s1, axis=0, keepdims=True)))
        acc = asc[t, :, farcols] * jnp.exp(m - m_new)
        acc = acc + dot(vt[0], jnp.exp(s0 - m_new).astype(B16))
        acc = acc + dot(vt[1], jnp.exp(s1 - m_new).astype(B16))
        msc[t, :, farcols] = m_new
        asc[t, :, farcols] = acc

    def conclude(t):
        acc = asc[t]
        total = acc[64:65]
        o = acc[:64] / total
        lse[t] = msc[t] + jnp.log(total)
        ot[t] = jnp.concatenate([o[:, :256], o[:, 256:]], axis=0)
        osend[t] = ot[t].T.astype(B16)

    def deliver(t, who):
        for cc in range(2):
            for yy in range(2):
                own = both(p.u == t * 2 + cc, y == yy)
                src = osend.at[t, cc * 128 : cc * 128 + 128]
                dev = (sid(seg * 2 + t // 2, t % 2, cc), yy)
                mail.send(src, orecv.at[p.head], rso.at[p.head], dev, both(who, jnp.logical_not(own)))

                @pl.when(both(who, own))
                def _(cc=cc):
                    orecv[p.head] = osend[t, cc * 128 : cc * 128 + 128]

    for t in range(4):
        pl.when(p.unit)(functools.partial(near_attention, t))
        pl.when(first)(functools.partial(conclude, t))
        deliver(t, first)
        if t == 1:
            chain(2)
        if t == 2:
            mail.got(wo.at[1 - y, whalf], rsy.at[0], p.ny)
            mail.send(wo.at[1 - y, whalf], wo.at[1 - y, whalf], rsy.at[4], p.nc)
    pl.when(second)(far_ready)
    chain(3)
    for t in range(4):
        pl.when(second)(functools.partial(far_attention, t))
        pl.when(second)(functools.partial(conclude, t))
        deliver(t, second)
    for zq in range(4):
        s = sid(zq, 1 - x, c)
        mail.got(rows_of(s), rsw.at[s], p.nx)
        give(s, p.nc)

    for hh in range(12):
        mine = both(p.unit, p.head == hh)
        pl.when(jnp.logical_not(mine))(lambda hh=hh: mail.got(orecv.at[hh], rso.at[hh], p.nx))
    for a in range(6):
        e, o = halves(orecv[2 * a].astype(F32), orecv[2 * a + 1].astype(F32))
        attn[0:128, a * 128 : a * 128 + 128] = e.astype(B16)
        attn[128:256, a * 128 : a * 128 + 128] = o.astype(B16)
    mail.got(wo.at[1 - y, pl.ds(pl.multiple_of((1 - c) * 192, 64), 192)], rsy.at[4], p.nc)
    mail.got(dyp.at[1 - y], rsy.at[1], p.ny)
    pair = pl.multiple_of(p.u * 2, 2)
    for par in range(2):
        for yy in range(2):
            at = pl.ds(par * 128 + yy * 64, 64)
            hid[at] = xs[pair + yy, par * 64 : par * 64 + 64].astype(F32)
            dys[at] = dyp[yy, par * 64 : par * 64 + 64]
    hid[...] = hid[...] + dot(attn[...], wo[...].reshape(768, 768)) + row(bo_ref)
    z2, _inv = norm_parts(hid[...])
    n2s[...] = (z2 * row(g2_ref) + row(b2_ref)).astype(B16)
    for i in range(8):
        s = sid(i // 2, i % 2, 1 - c)
        mail.got(rows_of(s), rsw.at[s], p.nc)

    k0 = 0.7978845608028654
    vb1[z] = jnp.zeros((8, 768), F32)

    def ffn_step(i, _):
        cols = pl.ds(pl.multiple_of(i * 256, 256), 256)
        dcols = pl.ds(pl.multiple_of(1536 + i * 256, 256), 256)
        up, dn = wb[:, cols], wb[:, dcols]
        pre = dot(n2s[...], up) + buph[:, cols]
        sq = pre * pre
        th = jnp.tanh(k0 * pre * (1.0 + 0.044715 * sq))
        half = 0.5 * (1.0 + th)
        act = (pre * half).astype(B16)
        slope = half + 0.5 * pre * (1.0 - th * th) * (k0 * (1.0 + 3.0 * 0.044715 * sq))
        dp = dot(dys[...], dn) * slope
        buph[:, cols] = jnp.sum(dp, axis=0, keepdims=True)
        dpl = dp.astype(B16)
        acts[:, cols] = act
        dpre[:, cols] = dpl
        return 0

    lax.fori_loop(0, 6, ffn_step, 0)
    for k in range(3):
        ys[k] = dot_nt(dpre[...], wb[k * 256 : k * 256 + 256, 0:1536]).astype(B16)
        mail.send(ys.at[k], yr.at[k], rsy.at[5 + k], p.ny)
    facc[...] = dot_nt(acts[:, 0:768], wb[:, 1536:2304]) + dot_nt(acts[:, 768:1536], wb[:, 2304:3072])
    for par in range(2):
        fo[par * 64 : par * 64 + 64] = facc[pl.ds(pl.multiple_of(par * 128 + y * 64, 64), 64)]
        fs[par * 64 : par * 64 + 64] = facc[pl.ds(pl.multiple_of(par * 128 + (1 - y) * 64, 64), 64)].astype(B16)

    n2t[...] = n2s[...].astype(F32).T.astype(B16)
    dyt[...] = dys[...].astype(F32).T.astype(B16)

    def owners(ref, xx, cc):
        at = [pl.ds(pl.multiple_of(sid(zz, xx, cc) * 48, 16), 48) for zz in range(4)]
        up = jnp.concatenate([n2t[i] for i in at], axis=0)
        dn = jnp.concatenate([dyt[i] for i in at], axis=0)

        def step(i, _):
            cols = pl.ds(pl.multiple_of(i * 256, 256), 256)
            dcols = pl.ds(pl.multiple_of(1536 + i * 256, 256), 256)
            u = dot(up, dpre[:, cols]).astype(B16)
            d = dot(dn, acts[:, cols]).astype(B16)
            for zz in range(4):
                ref[zz, :, cols] = u[zz * 48 : zz * 48 + 48]
                ref[zz, :, dcols] = d[zz * 48 : zz * 48 + 48]
            return 0

        lax.fori_loop(0, 6, step, 0)

    out_sum = Reduce(p, mail, gwo, hc, hxs, hxr, hzs, hzr, rhc, rhx, rhz)

    def ffn_over_x(i):
        zz = ring[i]
        gb[zz] = (gb[zz].astype(F32) + ra[zz].astype(F32)).astype(B16)
        mail.send(gb.at[zz], gxr.at[zz], rgx.at[zz], p.nx)

    def ffn_column(zz):
        mail.got(gxr.at[zz], rgx.at[zz], p.nx)
        return ge[zz].astype(F32) + rb[zz].astype(F32) + gxr[zz].astype(F32)

    def ffn_over_z(i):
        zz = ring[i]
        ge[zz] = ffn_column(zz).astype(B16)
        mail.send(ge.at[zz], gzr.at[i], rgz.at[i], p.nz)

    def ffn_over_far():
        zz = ring[1]
        mail.got(gzr.at[0], rgz.at[0], p.nz)
        ge[zz] = (ffn_column(zz) + gzr[0].astype(F32)).astype(B16)
        mail.send(ge.at[zz], gzr.at[1], rgz.at[1], p.far)

    ring = out_sum.order()
    owners(ga, 1 - x, 1 - c)
    mail.send(ga, ra, rga.at[0], p.nc)
    owners(gb, 1 - x, c)
    mail.got(ra, rga.at[0], p.nc)
    ffn_over_x(0)
    owners(gd, x, 1 - c)
    mail.send(gd, rb, rga.at[1], p.nc)
    owners(ge, x, c)
    @pl.when(p.unit)
    def _():
        for t in range(4):
            kt[t + 2] = ka[t + 2].astype(F32).T.astype(B16)
        dqt[...] = jnp.zeros_like(dqt)

    @pl.when(second)
    def _():
        for h in range(2):
            kt[h] = ka[h].astype(F32).T.astype(B16)

    for k in range(3):
        mail.got(yr.at[k], rsy.at[5 + k], p.ny)
    mail.send(fs, fr, rsy.at[3], p.ny)
    dn2 = jnp.concatenate([ys[k].astype(F32) + yr[k].astype(F32) for k in range(3)], axis=1)
    z2, inv2 = norm_parts(hid[...])
    dh = dys[...].astype(F32) + norm_grad(z2, inv2, dn2 * row(g2_ref))
    facc[...] = dh
    dacc[...] = dn2 * z2
    da_ = dot_nt(dh.astype(B16), wo[y])
    for a in range(3):
        e, o = halves(da_[0:128, a * 128 : a * 128 + 128], da_[128:256, a * 128 : a * 128 + 128])
        dpk[2 * a] = e.astype(B16)
        dpk[2 * a + 1] = o.astype(B16)

    mine_t = p.zl * 2 + x
    crow = pl.ds(pl.multiple_of(c * 128, 128), 128)
    for h, u in enumerate(UNITS):
        mail.send(dpk.at[h], dor.at[mine_t, crow], rdo.at[p.u], (seg * 8 + u, y), p.u != u)

        @pl.when(p.u == u)
        def _(h=h):
            dor[mine_t, crow] = dpk[h]

    gwo[...] = dot(dh.T.astype(B16), attn[:, pl.ds(pl.multiple_of(y * 384, 128), 384)]).astype(B16)
    out_sum.cores()
    ffn_over_x(1)
    mail.got(rb, rga.at[1], p.nc)
    ffn_over_z(0)
    out_sum.over_x()
    mail.got(fr, rsy.at[3], p.ny)
    sums = [jnp.zeros((1, 768), F32)] * 4
    for par in range(2):
        at = pl.ds(pl.multiple_of(par * 128 + y * 64, 64), 64)
        to = slice(par * 64, par * 64 + 64)
        dh_s[to] = facc[at]
        dn2_own = jnp.concatenate([ys[k, at].astype(F32) + yr[k, at].astype(F32) for k in range(3)], axis=1)
        own = (dacc[at], dn2_own, facc[at], dys[at].astype(F32))
        sums = [total + jnp.sum(v, axis=0, keepdims=True) for total, v in zip(sums, own)]
        fo[to] = hid[at] + fo[to] + fr[to].astype(F32) + row(bd_ref)
    back = mixed((128, 128), 1, 0)
    lout[...] = dot(back, fo[...].astype(B16)).astype(B16)
    for i in range(4):
        vb1[z, i : i + 1] = sums[i]
    for half in range(2):

        @pl.when(y == half)
        def _(half=half):
            for k in range(2):
                vb1[z, 4 + 2 * half + k : 5 + 2 * half + k] = buph[:, k * 768 : k * 768 + 768]

    early = Total(p, mail, vb1, vr1, rv1, rv2)
    late = Total(p, mail, vb2, vr2, rv3, rv4)
    early.start()
    ffn_over_x(2)

    def prepare():
        for i in range(8):
            pl.when(p.u != i)(lambda i=i: mail.got(dor.at[i // 2, (i % 2) * 128 : (i % 2) * 128 + 128], rdo.at[i], p.nx))
        low = iota((256, 128), 1) < 64
        for t in range(4):
            d = dor[t].astype(F32)
            doa[t, 0:256] = jnp.where(low, d, 0.0).astype(B16)
            doa[t, 256:512] = jnp.where(low, pltpu.roll(d, 64, 1), 0.0).astype(B16)
            prod = d.T * ot[t]
            delta[t, :, 0:256] = jnp.sum(prod[:64], axis=0, keepdims=True)
            delta[t, :, 256:512] = jnp.sum(prod[64:], axis=0, keepdims=True)

    pl.when(p.unit)(prepare)
    ffn_over_x(3)

    def score_grads(cc, q, do, st, lse_row, delta_row):
        pr = jnp.exp(st - lse_row)
        ds = (pr * (dot_nt(va[cc], do) - delta_row)).astype(B16)
        dva[...] += dot(pr.astype(B16), do)
        dka[...] += dot(ds, q)
        return dot(kt[cc], ds)

    def clear():
        dka[...] = jnp.zeros_like(dka)
        dva[...] = jnp.zeros_like(dva)

    def far_grads(cc):
        clear()

        def step(t, _):
            q, do = qa[t, farcols], doa[t, farcols]
            dqt[t, :, farcols] += score_grads(cc, q, do, dot_nt(ka[cc], q), lse[t, :, farcols], delta[t, :, farcols])
            return 0

        lax.fori_loop(0, 4, step, 0)
        low = iota((512, 128), 1) < 64
        pack = jnp.where(low, dka[...], pltpu.roll(dva[...], 64, 1)).astype(B16)
        dfs[2 * cc] = pack[:256]
        dfs[2 * cc + 1] = pack[256:]

    for cc in range(2):
        pl.when(second)(functools.partial(far_grads, cc))
        mail.send(dfs.at[2 * cc : 2 * cc + 2], dfr.at[2 * cc : 2 * cc + 2], rdf.at[cc], p.far, second)
    ffn_over_far()

    def near(t):
        clear()
        q, do = qa[t], doa[t]
        dqt[t] += score_grads(t + 2, q, do, causal(dot_nt(ka[t + 2], q)), lse[t], delta[t])
        for tq in range(t + 1, 4):
            q, do = qa[tq], doa[tq]
            dqt[tq] += score_grads(t + 2, q, do, dot_nt(ka[t + 2], q), lse[tq], delta[tq])
        dtt[64:128, t * 512 : t * 512 + 512] = dka[...].T[:64].astype(B16)
        dtt[128:192, t * 512 : t * 512 + 512] = dva[...].T[:64].astype(B16)

    def add_far(t):
        rows = dfr[t].astype(F32).T
        at = pl.ds(pl.multiple_of(t * 512 + p.parity * 256, 256), 256)
        dtt[64:128, at] = (dtt[64:128, at].astype(F32) + rows[:64]).astype(B16)
        dtt[128:192, at] = (dtt[128:192, at].astype(F32) + rows[64:]).astype(B16)

    out_sum.over_z(0)
    pl.when(p.unit)(lambda: near(0))
    out_sum.over_far()
    ffn_over_z(2)
    out_sum.over_z(2)
    early.middle()
    pl.when(p.unit)(lambda: near(1))
    pl.when(p.unit)(lambda: near(2))
    pl.when(p.unit)(lambda: near(3))
    woag[p.s] = out_sum.result().astype(B16)
    spread_out = Spread(p, mail, woag, rwo, False)
    spread_out.first()

    @pl.when(first)
    def _():
        for cc in range(2):
            mail.got(dfr.at[2 * cc : 2 * cc + 2], rdf.at[cc], p.far)
        for t in range(4):
            add_far(t)

    @pl.when(p.unit)
    def _():
        for t in range(4):
            dtt[0:64, t * 512 : t * 512 + 512] = (dqt[t, 0:64] * 0.125).astype(B16)
            for k in range(3):
                e = dtt[k * 64 : k * 64 + 64, t * 512 : t * 512 + 256].astype(F32)
                o = dtt[k * 64 : k * 64 + 64, t * 512 + 256 : t * 512 + 512].astype(F32)
                packs[t, k] = jnp.concatenate([e, o], axis=0).T.astype(B16)

    for t in range(4):
        for cc in range(2):
            u = t * 2 + cc
            mail.send(packs.at[t, :, cc * 128 : cc * 128 + 128], dqr.at[p.hl], rdq.at[p.hl], (seg * 8 + u, y), both(p.unit, p.u != u))

            @pl.when(both(p.unit, p.u == u))
            def _(t=t, cc=cc):
                dqr[p.hl] = packs[t, :, cc * 128 : cc * 128 + 128]

    vb2[z] = jnp.zeros((8, 768), F32)
    spread = Spread(p, mail, wag, rag, True)

    @pl.when(p.unit)
    def _():
        dw = dot(dtt[...], ns[...].reshape(2048, 768))
        for h in range(2):
            wms[h] = dw[h * 96 : h * 96 + 96].astype(B16)
        bias = dot_nt(jnp.ones((16, 2048), B16), dtt[...])[0:8]
        at = pl.ds(pl.multiple_of(p.head // 2 * 128, 128), 128)
        lane = iota((8, 128), 1) < 64
        low_q, low_v = jnp.where(lane, bias[:, 0:128], 0.0), jnp.concatenate([bias[:, 128:192], jnp.zeros((8, 64), F32)], axis=1)
        for odd in range(2):

            @pl.when(p.head % 2 == odd)
            def _(odd=odd):
                for i, v in enumerate((low_q, low_v)):
                    vb2[z, 2 + i : 3 + i, at] = (pltpu.roll(v, 64, 1) if odd else v)[0:1]

    mail.send(wms.at[1 - seg], wmr, rwm.at[0], p.far, p.unit)

    for h, u in enumerate(UNITS):
        pl.when(p.u != u)(lambda h=h: mail.got(dqr.at[h], rdq.at[h], p.nx))
    for k in range(3):
        for a in range(3):
            e, o = halves(dqr[2 * a, k].astype(F32), dqr[2 * a + 1, k].astype(F32))
            col = slice(a * 128, a * 128 + 128)
            dall[k, 0:128, col] = e.astype(B16)
            dall[k, 128:256, col] = o.astype(B16)
    facc[...] = dot_nt(dall[0], wq_ref[0]) + dot_nt(dall[1], wq_ref[1]) + dot_nt(dall[2], wq_ref[2])
    for par in range(2):
        dns[par * 64 : par * 64 + 64] = facc[pl.ds(pl.multiple_of(par * 128 + (1 - y) * 64, 64), 64)].astype(B16)
    mail.send(dns, dnr, rdn.at[0], p.ny)

    @pl.when(p.unit)
    def _():
        mail.got(wmr, rwm.at[0], p.far)
        wag[p.s] = (wms[seg].astype(F32) + wmr[...].astype(F32)).astype(B16)

    spread.first()
    spread_out.second()
    z1, inv1 = norm_parts(xs[b].astype(F32))
    mail.got(dnr, rdn.at[0], p.ny)
    own = [facc[pl.ds(pl.multiple_of(par * 128 + y * 64, 64), 64)] for par in range(2)]
    dn1 = jnp.concatenate(own, axis=0) + dnr[...].astype(F32)
    vb2[z, 0:1] = jnp.sum(dn1 * z1, axis=0, keepdims=True)
    vb2[z, 1:2] = jnp.sum(dn1, axis=0, keepdims=True)
    late.start()
    rest = dh_s[...] + norm_grad(z1, inv1, dn1 * row(g1_ref))
    result = jnp.zeros((128, 768), F32)
    for _k in range(3):
        piece = rest.astype(B16)
        result = result + dot(back, piece)
        rest = rest - piece.astype(F32)
    gin[...] = result
    spread.second()
    spread_out.third()
    late.middle()
    spread.third()
    spread_out.fourth()
    o_tot[0] = early.finish()
    spread.fourth()
    o_tot[1] = late.finish()
    total = ffn_column(z)
    for i in (1, 2):
        mail.got(gzr.at[i], rgz.at[i], p.nz)
        total = total + gzr[i].astype(F32)
    o_ud[0] = total[:, :1536]
    o_ud[1] = total[:, 1536:]
    spread_out.last()
    spread.last()
    mail.close()


def write_out(lout, gin, wag, woag, ud, tot, o_l, o_g, o_g1, o_b1, o_wq, o_bqv, o_wo, o_bo, o_g2, o_b2, o_up, o_bup, o_dn, o_bd):
    o_l[...] = lout[...]
    o_g[...] = gin[...]
    o_up[...] = ud[0]
    o_dn[...] = ud[1]
    for i, ref in enumerate((o_g2, o_b2, o_bo, o_bd)):
        ref[...] = tot[0, i : i + 1].reshape(768)
    for i in range(4):
        o_bup[i * 768 : i * 768 + 768] = tot[0, 4 + i : 5 + i].reshape(768)
    o_g1[...] = tot[1, 0:1].reshape(768)
    o_b1[...] = tot[1, 1:2].reshape(768)
    o_wo[...] = woag[...].reshape(768, 384).astype(F32).T
    for a in range(3):
        u0, u1 = UNITS[2 * a], UNITS[2 * a + 1]
        col = slice(a * 128, a * 128 + 128)
        w0 = jnp.concatenate([wag[u0, 0:96], wag[u0 + 8, 0:96]], axis=0).astype(F32)
        w1 = jnp.concatenate([wag[u1, 0:96], wag[u1 + 8, 0:96]], axis=0).astype(F32)
        for k in range(3):
            at = slice(k * 64, k * 64 + 64)
            o_wq[k, :, col] = jnp.concatenate([w0[at], w1[at]], axis=0).T
    half = lax.axis_index("head")
    o_bqv[...] = tot[1, 2:4, pl.ds(pl.multiple_of(half * 384, 128), 384)]


SLOTS = 40


def count_table():
    kinds = np.array([[0, 0, 0, 0], [1, 0, 0, 0], [1, 1, 0, 0], [1, 0, 1, 0], [1, 1, 1, 1]], np.float64)
    shared = kinds @ kinds.T
    table = np.zeros((24, 128), np.float64)
    low = lambda v: float(np.asarray(v, dtype=ml_dtypes.bfloat16).astype(np.float64))
    for i in range(5):
        for k in range(5):
            for base, count in ((64, 1.0 + shared[i, k]), (80, shared[i, k])):
                rest = float(np.log(count)) if count > 0 else 0.0
                for e in range(3):
                    table[i, base + 3 * k + e] = low(rest)
                    rest -= low(rest)
        table[i, 96:101] = [NEGATIVE, NEGATIVE, 0.0, NEGATIVE, NEGATIVE]
        table[8 + i, 64 + 3 * i : 67 + 3 * i] = 1.0
        table[16 + i, 80 + 3 * i : 83 + 3 * i] = 1.0
        table[8 + i, 98] = table[16 + i, 98] = 1.0
    return table.astype(np.float32)


def vm(*shape):
    return pltpu.VMEM(shape, B16)


def vf(*shape):
    return pltpu.VMEM(shape, F32)


def dma(*shape):
    return pltpu.SemaphoreType.DMA(shape)


def in_vmem(count):
    return [pl.BlockSpec(memory_space=pltpu.VMEM)] * count


def fast(
    layer_input, doc_ids, cotangent, ln1_gain, ln1_bias, w_qkv, bias_qv, w_out, b_out, ln2_gain, ln2_bias, w_up, b_up, w_down, b_down
):
    out = lambda shape, dtype=F32: jax.ShapeDtypeStruct(shape, dtype)
    shapes = (
        out((128, 768), B16), out((128, 768)), out((768,)), out((768,)), out((3, 768, 384)), out((2, 384)), out((384, 768)), out((768,)),
        out((768,)), out((768,)), out((48, 1536)), out((3072,)), out((48, 1536)), out((768,)),
    )
    raw = (out((128, 768), B16), out((128, 768)), out((16, 96, 768), B16), out((16, 48, 384), B16), out((2, 48, 1536)), out((2, 8, 768)))
    scratch = [
        vm(4, 512, 128), vm(6, 512, 128), vm(6, 512, 128), vm(4, 512, 768), vf(4, 1, 512), vf(4, 128, 256), vm(6, 128, 128),
        vm(768, 384), vf(128, 768), vm(768, 384), vf(1, 384), vf(1, 1536), vf(4, 1, 512), vf(4, 128, 512),
        vm(16, 128, 768), vf(17, 8, 128), vm(768, 3072), vm(2, 384, 768), vm(2, 128, 768), vm(12, 128, 128), vm(4, 256, 128),
        vm(4, 256, 128), vm(4, 256, 128), vm(256, 768), vm(6, 128, 512), vf(256, 768), vm(256, 768), vm(256, 768), vm(256, 1536),
        vm(256, 1536), vf(256, 768), vf(256, 768), vm(3, 256, 256), vm(3, 256, 256), vm(128, 768), vm(128, 768), vf(128, 768),
        vm(4, 256, 128), vm(4, 512, 128), vf(4, 1, 512), vm(6, 128, 512), vf(512, 128), vf(512, 128), vf(4, 128, 512), vm(192, 2048),
        vm(4, 256, 128), vm(4, 256, 128), vm(4, 3, 256, 128), vm(6, 3, 128, 128), vm(2, 96, 768), vm(96, 768),
        vm(768, 256), vm(768, 256), *[vm(4, 48, 3072)] * 8,
        vm(2, 4, 48, 384), vm(4, 48, 384), vm(4, 48, 384), vm(4, 48, 384), vm(4, 48, 384), vm(3, 256, 384), vm(128, 768), vm(128, 768),
        vf(4, 8, 768), vf(8, 8, 768), vf(4, 8, 768), vf(8, 8, 768),
        dma(SLOTS), dma(3, 8), dma(3, 8), dma(3), dma(16), dma(12), dma(2), dma(8), dma(8), dma(2), dma(4), dma(3), dma(2, 4), dma(4),
        dma(3), dma(2), dma(6), dma(1), dma(16), dma(16), dma(1), dma(4), dma(8), dma(4), dma(8),
    ]
    args = (
        layer_input, doc_ids, cotangent, ln1_gain, ln1_bias, w_qkv.transpose(1, 0, 2), bias_qv, w_out, b_out, ln2_gain, ln2_bias, w_up,
        b_up, w_down.T, b_down, jnp.asarray(count_table()),
    )
    found = pl.pallas_call(
        kernel, out_shape=raw, in_specs=in_vmem(len(args)), out_specs=tuple(in_vmem(len(raw))), scratch_shapes=scratch,
        compiler_params=pltpu.CompilerParams(collective_id=0, has_side_effects=True, vmem_limit_bytes=LIMIT),
    )(*args)
    outs = pl.pallas_call(
        write_out, out_shape=shapes, in_specs=in_vmem(len(raw)), out_specs=tuple(in_vmem(len(shapes))),
        compiler_params=pltpu.CompilerParams(vmem_limit_bytes=LIMIT),
    )(*found)
    outs = list(outs)
    outs[4] = outs[4].transpose(1, 0, 2)
    outs[12] = outs[12].T
    return tuple(outs)


def from_behind(value, axis, by):
    length = lax.axis_size(axis)
    pairs = [(i, i + by) for i in range(length) if 0 <= i + by < length]
    return lax.ppermute(value, axis, pairs)


def layer_norm(values, gain, shift):
    mean = jnp.mean(values, axis=-1, keepdims=True)
    centred = values - mean
    spread = jnp.mean(centred * centred, axis=-1, keepdims=True)
    return centred * lax.rsqrt(spread + EPS) * gain + shift


def gelu_tanh(values):
    return jax.nn.gelu(values, approximate=True)


def pick_block(length, limit):
    chosen = 1
    for candidate in range(1, min(length, limit) + 1):
        if length % candidate == 0:
            chosen = candidate
    return chosen


def pair_counts(query_pos, key_pos, head_ids):
    total = None
    for factor, rate in LEVELS:
        width = SEG * factor
        same = query_pos[:, :, None] // width == key_pos[:, None, :] // width
        offset = (head_ids % rate)[:, None]
        pick_query = query_pos % width % rate == offset
        pick_key = key_pos % width % rate == offset
        joint = (same & pick_query[:, :, None] & pick_key[:, None, :]).astype(jnp.float32)
        total = joint if total is None else total + joint
    return total


def block_terms(
    query_blk, query_pos, query_doc, key_blk, key_pos, key_doc, head_ids, nearby, scale
):
    scores = (
        jnp.einsum("qhe,khe->hqk", query_blk, key_blk, preferred_element_type=jnp.float32) * scale
    )
    counts = pair_counts(query_pos, key_pos, head_ids)
    same_segment = query_pos[:, :, None] // SEG == key_pos[:, None, :] // SEG
    keep = same_segment if nearby else jnp.logical_not(same_segment)
    allowed = (
        keep
        & (key_pos[:, None, :] <= query_pos[:, :, None])
        & (query_doc[:, :, None] == key_doc[:, None, :])
    )
    return (scores, counts * allowed.astype(jnp.float32))


def per_device(
    layer_input,
    doc_ids,
    cotangent,
    ln1_gain,
    ln1_bias,
    w_qkv,
    bias_qv,
    w_out,
    b_out,
    ln2_gain,
    ln2_bias,
    w_up,
    b_up,
    w_down,
    b_down,
):
    seq_count = lax.axis_size("seq")
    local_heads = HEADS // lax.axis_size("head")
    local_width = local_heads * HEAD_DIM
    scale = HEAD_DIM ** (-0.5)
    f32 = jnp.float32
    b16 = jnp.bfloat16
    x_float = layer_input.astype(f32)
    norm_one = layer_norm(x_float, ln1_gain, ln1_bias)
    norm_rows, row_doc = (
        lax.all_gather(norm_one.astype(b16), "head", axis=0, tiled=True),
        lax.all_gather(doc_ids, "head", axis=0, tiled=True),
    )
    seq_tokens = norm_rows.shape[0]
    half = seq_tokens // 2
    total_tokens = seq_tokens * seq_count
    total_half = total_tokens // 2
    first_pos = lax.axis_index("seq") * seq_tokens
    last_pos = first_pos + seq_tokens - 1
    local_offsets = jnp.arange(seq_tokens, dtype=jnp.int32)
    query_pos = (first_pos + local_offsets)[None, :]
    query_doc = row_doc[None, :]
    head_ids = lax.axis_index("head") * local_heads + jnp.arange(local_heads, dtype=jnp.int32)
    parity = head_ids % 2
    pick_even = parity == 0

    def compact(rows):
        paired = rows.reshape((half, 2) + rows.shape[1:])
        mask = pick_even.reshape((1, local_heads) + (1,) * (rows.ndim - 2))
        return jnp.where(mask, paired[:, 0], paired[:, 1])

    def expand(rows):
        mask = pick_even.reshape((1, local_heads) + (1,) * (rows.ndim - 2))
        zeros = jnp.zeros_like(rows)
        paired = jnp.stack([jnp.where(mask, rows, zeros), jnp.where(mask, zeros, rows)], axis=1)
        return paired.reshape((seq_tokens,) + rows.shape[1:])

    mixed = jnp.einsum("td,dch->tch", norm_rows, w_qkv, preferred_element_type=f32)
    zero_row = jnp.zeros((1, local_width), f32)
    bias_all = jnp.concatenate([bias_qv[0:1], zero_row, bias_qv[1:2]], axis=0)
    qkv = (mixed + bias_all[None]).astype(b16)
    queries = qkv[:, 0]
    query_heads = queries.reshape(seq_tokens, local_heads, HEAD_DIM)
    key_heads = qkv[:, 1].reshape(seq_tokens, local_heads, HEAD_DIM)
    value_heads = qkv[:, 2].reshape(seq_tokens, local_heads, HEAD_DIM)
    local_keys_c = compact(key_heads)
    local_values_c = compact(value_heads)
    far_keys_all, far_values_all, doc_all = (
        lax.all_gather(local_keys_c, "seq", axis=0, tiled=True),
        lax.all_gather(local_values_c, "seq", axis=0, tiled=True),
        lax.all_gather(row_doc, "seq", axis=0, tiled=True),
    )
    segment_count = SEG // seq_tokens
    own_pair = jnp.stack([key_heads, value_heads], axis=1)
    pair_pieces = [own_pair]
    for step in range(1, segment_count):
        pair_pieces.append(from_behind(own_pair, "seq", step))
    near_pairs = jnp.concatenate(pair_pieces, axis=0)
    near_keys = near_pairs[:, 0]
    near_values = near_pairs[:, 1]
    near_flat = jnp.concatenate(
        [first_pos - step * seq_tokens + local_offsets for step in range(segment_count)]
    )
    near_doc = jnp.take(doc_all, jnp.clip(near_flat, 0, total_tokens - 1))[None, :]
    near_pos = near_flat[None, :]
    far_pos = 2 * jnp.arange(total_half, dtype=jnp.int32)[None, :] + parity[:, None]
    doc_pairs = doc_all.reshape(total_half, 2)
    far_doc = jnp.where(pick_even[:, None], doc_pairs[:, 0][None, :], doc_pairs[:, 1][None, :])
    key_block = pick_block(total_half, block_limit)
    blocks = total_half // key_block
    far_key_blocks = far_keys_all.reshape(blocks, key_block, local_heads, HEAD_DIM)
    far_value_blocks = far_values_all.reshape(blocks, key_block, local_heads, HEAD_DIM)
    far_pos_blocks = far_pos.reshape(local_heads, blocks, key_block).transpose(1, 0, 2)
    far_doc_blocks = far_doc.reshape(local_heads, blocks, key_block).transpose(1, 0, 2)
    far_begin = jnp.arange(blocks, dtype=jnp.int32) * (2 * key_block)

    def merge_stats(current, key_blk, key_pos, key_doc, nearby):
        peak, running = current
        scores, counts = block_terms(
            query_heads, query_pos, query_doc, key_blk, key_pos, key_doc, head_ids, nearby, scale
        )
        live = counts > 0
        new_peak = jnp.maximum(peak, jnp.max(jnp.where(live, scores, NEGATIVE), axis=2))
        terms = jnp.where(live, counts * jnp.exp(scores - new_peak[:, :, None]), 0.0)
        return (new_peak, running * jnp.exp(peak - new_peak) + jnp.sum(terms, axis=2))

    start_state = (
        jnp.full((local_heads, seq_tokens), NEGATIVE, f32),
        jnp.zeros((local_heads, seq_tokens), f32),
    )
    near_state = merge_stats(start_state, near_keys, near_pos, near_doc, True)

    def stats_step(state, item):
        key_blk, pos_blk, doc_blk, begin = item
        return (
            lax.cond(
                begin <= last_pos,
                lambda current: merge_stats(current, key_blk, pos_blk, doc_blk, False),
                lambda current: current,
                state,
            ),
            None,
        )

    (peak_all, running_all), _ = lax.scan(
        stats_step, near_state, (far_key_blocks, far_pos_blocks, far_doc_blocks, far_begin)
    )
    lse = peak_all + jnp.log(running_all)

    def add_output(current, key_blk, value_blk, key_pos, key_doc, nearby):
        scores, counts = block_terms(
            query_heads, query_pos, query_doc, key_blk, key_pos, key_doc, head_ids, nearby, scale
        )
        probs = jnp.where(counts > 0, counts * jnp.exp(scores - lse[:, :, None]), 0.0).astype(b16)
        return current + jnp.einsum("hqk,khe->qhe", probs, value_blk, preferred_element_type=f32)

    zero_heads = jnp.zeros((seq_tokens, local_heads, HEAD_DIM), f32)
    near_output = add_output(zero_heads, near_keys, near_values, near_pos, near_doc, True)

    def output_step(accum, item):
        key_blk, value_blk, pos_blk, doc_blk, begin = item
        return (
            lax.cond(
                begin <= last_pos,
                lambda current: add_output(current, key_blk, value_blk, pos_blk, doc_blk, False),
                lambda current: current,
                accum,
            ),
            None,
        )

    attn_exact, _ = lax.scan(
        output_step,
        near_output,
        (far_key_blocks, far_value_blocks, far_pos_blocks, far_doc_blocks, far_begin),
    )
    attn_low = attn_exact.reshape(seq_tokens, local_width).astype(b16)
    branch = lax.psum_scatter(
        jnp.dot(attn_low, w_out, preferred_element_type=f32).astype(jnp.bfloat16),
        "head",
        scatter_dimension=0,
        tiled=True,
    ).astype(jnp.float32)
    hidden_one = x_float + branch + b_out
    norm_two = layer_norm(hidden_one, ln2_gain, ln2_bias)
    norm_low = norm_two.astype(b16)
    dy_low = (cotangent.astype(f32) * (doc_ids >= 0).astype(f32)[:, None]).astype(b16)
    dy_float = dy_low.astype(f32)
    up_rows, down_rows = (
        lax.all_gather(w_up, "seq", axis=0, tiled=True),
        lax.all_gather(w_down, "seq", axis=1, tiled=True),
    )
    up_full, down_full = (
        lax.all_gather(up_rows, "head", axis=1, tiled=True),
        lax.all_gather(down_rows, "head", axis=0, tiled=True),
    )
    pre_act = jnp.dot(norm_low, up_full, preferred_element_type=f32) + b_up
    act_low = gelu_tanh(pre_act).astype(b16)
    ffn_result = jnp.dot(act_low, down_full, preferred_element_type=f32)
    d_act = jnp.einsum("td,fd->tf", dy_low, down_full, preferred_element_type=f32)
    _, gelu_back = jax.vjp(gelu_tanh, pre_act)
    d_pre = gelu_back(d_act)[0]
    d_pre_low = d_pre.astype(b16)
    bias_up_grad = jnp.sum(d_pre, axis=0)
    up_parts = jnp.einsum("td,tf->df", norm_low, d_pre_low, preferred_element_type=f32)
    down_parts = jnp.einsum("tf,td->fd", act_low, dy_low, preferred_element_type=f32)
    up_grad, down_grad = (
        lax.psum_scatter(
            up_parts.astype(jnp.bfloat16), "head", scatter_dimension=1, tiled=True
        ).astype(jnp.float32),
        lax.psum_scatter(
            down_parts.astype(jnp.bfloat16), "head", scatter_dimension=0, tiled=True
        ).astype(jnp.float32),
    )
    d_norm_two = jnp.einsum("tf,df->td", d_pre_low, up_full, preferred_element_type=f32)
    layer_output = (hidden_one + ffn_result + b_down).astype(b16)
    w_up_grad, w_down_grad = (
        lax.psum_scatter(up_grad, "seq", scatter_dimension=0, tiled=True),
        lax.psum_scatter(down_grad, "seq", scatter_dimension=1, tiled=True),
    )
    _, norm_two_back = jax.vjp(layer_norm, hidden_one, ln2_gain, ln2_bias)
    d_hidden_norm, gain_two_grad, bias_two_grad = norm_two_back(d_norm_two)
    d_hidden = dy_float + d_hidden_norm
    bias_out_grad = jnp.sum(d_hidden, axis=0)
    bias_down_grad = jnp.sum(dy_float, axis=0)
    hidden_rows = lax.all_gather(d_hidden.astype(b16), "head", axis=0, tiled=True)
    w_out_part = jnp.einsum("tc,td->cd", attn_low, hidden_rows, preferred_element_type=f32)
    d_attn = jnp.einsum("td,cd->tc", hidden_rows, w_out, preferred_element_type=f32).astype(b16)
    d_attn_heads = d_attn.reshape(seq_tokens, local_heads, HEAD_DIM)
    delta_rows = jnp.sum(d_attn_heads.astype(f32) * attn_exact, axis=2)
    delta = delta_rows.T

    def score_grads(key_blk, value_blk, key_pos, key_doc, nearby):
        scores, counts = block_terms(
            query_heads, query_pos, query_doc, key_blk, key_pos, key_doc, head_ids, nearby, scale
        )
        exact = jnp.where(counts > 0, counts * jnp.exp(scores - lse[:, :, None]), 0.0)
        d_prob = jnp.einsum("qhe,khe->hqk", d_attn_heads, value_blk, preferred_element_type=f32)
        d_score = (exact * (d_prob - delta[:, :, None])).astype(b16)
        return (exact, d_score)

    exact_near, d_score_near = score_grads(near_keys, near_values, near_pos, near_doc, True)
    d_query_near = jnp.einsum("hqk,khe->qhe", d_score_near, near_keys, preferred_element_type=f32)
    near_key_grad = jnp.einsum(
        "hqk,qhe->khe", d_score_near, query_heads, preferred_element_type=f32
    )
    near_value_grad = jnp.einsum(
        "hqk,qhe->khe", exact_near.astype(b16), d_attn_heads, preferred_element_type=f32
    )
    near_pair_grads = jnp.stack([near_key_grad, near_value_grad], axis=1)
    pair_grad = near_pair_grads[:seq_tokens]
    for step in range(1, segment_count):
        piece = near_pair_grads[step * seq_tokens : (step + 1) * seq_tokens]
        pair_grad = pair_grad + from_behind(piece.astype(jnp.bfloat16), "seq", -step).astype(
            piece.dtype
        )

    def query_grad_step(accum, item):
        key_blk, value_blk, pos_blk, doc_blk, begin = item

        def query_compute(current):
            _, d_score = score_grads(key_blk, value_blk, pos_blk, doc_blk, False)
            return current + jnp.einsum(
                "hqk,khe->qhe", d_score, key_blk, preferred_element_type=f32
            )

        return (lax.cond(begin <= last_pos, query_compute, lambda current: current, accum), None)

    d_query, _ = lax.scan(
        query_grad_step,
        d_query_near,
        (far_key_blocks, far_value_blocks, far_pos_blocks, far_doc_blocks, far_begin),
    )
    d_query = d_query * scale
    stats_rows = jnp.stack([compact(lse.T), compact(delta_rows)], axis=1)
    stats_all = lax.all_gather(stats_rows, "seq", axis=0, tiled=True)
    local_key_pos = first_pos + 2 * jnp.arange(half, dtype=jnp.int32)[None, :] + parity[:, None]
    local_key_doc = compact(jnp.broadcast_to(row_doc[:, None], (seq_tokens, local_heads))).T
    zero_compact = jnp.zeros((half, local_heads, HEAD_DIM), f32)
    query_piece = lax.all_gather(compact(query_heads), "seq", axis=0, tiled=True)
    grad_piece = lax.all_gather(compact(d_attn_heads), "seq", axis=0, tiled=True)
    length = query_piece.shape[0]
    size = pick_block(length, block_limit)
    number = length // size
    pos_piece = 2 * jnp.arange(length, dtype=jnp.int32)[None, :] + parity[:, None]
    items = (
        query_piece.reshape(number, size, local_heads, HEAD_DIM),
        grad_piece.reshape(number, size, local_heads, HEAD_DIM),
        stats_all.reshape(number, size, 2, local_heads),
        pos_piece.reshape(local_heads, number, size).transpose(1, 0, 2),
        far_doc.reshape(local_heads, number, size).transpose(1, 0, 2),
    )

    def one_step(current, item):
        query_blk, grad_blk, stats_blk, pos_blk, doc_blk = item

        def one_compute(pair):
            key_grad, value_grad = pair
            scores, counts = block_terms(
                query_blk,
                pos_blk,
                doc_blk,
                local_keys_c,
                local_key_pos,
                local_key_doc,
                head_ids,
                False,
                scale,
            )
            exact = jnp.where(
                counts > 0, counts * jnp.exp(scores - stats_blk[:, 0].T[:, :, None]), 0.0
            )
            d_prob = jnp.einsum(
                "qhe,khe->hqk", grad_blk, local_values_c, preferred_element_type=f32
            )
            d_score = (exact * (d_prob - stats_blk[:, 1].T[:, :, None])).astype(b16)
            key_grad = key_grad + jnp.einsum(
                "hqk,qhe->khe", d_score, query_blk, preferred_element_type=f32
            )
            value_grad = value_grad + jnp.einsum(
                "hqk,qhe->khe", exact.astype(b16), grad_blk, preferred_element_type=f32
            )
            return (key_grad, value_grad)

        return (
            lax.cond(jnp.max(pos_blk) >= first_pos, one_compute, lambda pair: pair, current),
            None,
        )

    result, _ = lax.scan(one_step, (zero_compact, zero_compact), items)
    far_key_grad, far_value_grad = result
    d_key = (pair_grad[:, 0] + expand(far_key_grad)) * scale
    d_value = pair_grad[:, 1] + expand(far_value_grad)
    d_qkv = jnp.stack(
        [
            d_query.reshape(seq_tokens, local_width),
            d_key.reshape(seq_tokens, local_width),
            d_value.reshape(seq_tokens, local_width),
        ],
        axis=1,
    ).astype(b16)
    d_qkv_float = d_qkv.astype(f32)
    bias_qv_part = jnp.stack(
        [jnp.sum(d_qkv_float[:, 0], axis=0), jnp.sum(d_qkv_float[:, 2], axis=0)], axis=0
    )
    w_qkv_part = jnp.einsum("td,tch->dch", norm_rows, d_qkv, preferred_element_type=f32)
    d_norm_one = lax.psum_scatter(
        jnp.einsum("tch,dch->td", d_qkv, w_qkv, preferred_element_type=f32).astype(jnp.bfloat16),
        "head",
        scatter_dimension=0,
        tiled=True,
    ).astype(jnp.float32)
    _, norm_one_back = jax.vjp(layer_norm, x_float, ln1_gain, ln1_bias)
    d_x_norm, gain_one_grad, bias_one_grad = norm_one_back(d_norm_one)
    grad_input = d_hidden + d_x_norm
    w_qkv_grad, bias_qv_grad, w_out_grad = lax.psum((w_qkv_part, bias_qv_part, w_out_part), "seq")
    summed = lax.psum(
        (
            gain_one_grad,
            bias_one_grad,
            gain_two_grad,
            bias_two_grad,
            bias_out_grad,
            bias_up_grad,
            bias_down_grad,
        ),
        ("seq", "head"),
    )
    return (
        layer_output,
        grad_input,
        summed[0],
        summed[1],
        w_qkv_grad,
        bias_qv_grad,
        w_out_grad,
        summed[4],
        summed[2],
        summed[3],
        w_up_grad,
        summed[5],
        w_down_grad,
        summed[6],
    )


def solution(mesh):
    in_specs = (
        P(("seq", "head"), None),
        P(("seq", "head")),
        P(("seq", "head"), None),
        P(),
        P(),
        P(None, None, "head"),
        P(None, "head"),
        P("head", None),
        P(),
        P(),
        P(),
        P("seq", "head"),
        P(),
        P("head", "seq"),
        P(),
    )
    out_specs = (
        P(("seq", "head"), None),
        P(("seq", "head"), None),
        P(),
        P(),
        P(None, None, "head"),
        P(None, "head"),
        P("head", None),
        P(),
        P(),
        P(),
        P("seq", "head"),
        P(),
        P("head", "seq"),
        P(),
    )
    small = mesh.shape["seq"] == 16 and mesh.shape["head"] == 2
    return jax.shard_map(
        fast if small else per_device, mesh=mesh, in_specs=in_specs, out_specs=out_specs, check_vma=False
    )
```

```python
import functools

import jax
import jax.numpy as jnp
import ml_dtypes
import numpy as np
from jax import lax
from jax.experimental import pallas as pl
from jax.experimental.pallas import tpu as pltpu
from jax.sharding import PartitionSpec as P

HEADS = 12
HEAD_DIM = 64
SEG = 2048


LEVELS = ((1, 1), (2, 2), (4, 4), (8, 6), (16, 12))
EPS = 1e-05
NEGATIVE = -1e30
block_limit = 2048


MESH = pl.DeviceIdType.MESH
VMEM = pltpu.VMEM
LIMIT = 60 << 20
F32 = jnp.float32
B16 = jnp.bfloat16


def dot(a, b):
    return jnp.dot(a, b, preferred_element_type=F32)


def dot_nt(a, b):
    return lax.dot_general(a, b, (((1,), (1,)), ((), ())), preferred_element_type=F32)


def sid(z, x, c):
    return z * 4 + x * 2 + c


class Place:
    def __init__(self):
        s = lax.axis_index("seq")
        self.s, self.y = s, lax.axis_index("head")
        self.z, self.x, self.c = s // 4, (s // 2) % 2, s % 2
        self.seg, self.zl = self.z // 2, self.z % 2
        self.u = s % 8
        self.b = self.u * 2 + self.y
        self.unit = jnp.logical_and(self.u != 3, self.u != 5)
        self.hl = self.u - self.u // 4 - self.u // 6
        self.head = self.y * 6 + self.hl
        self.parity = self.head % 2
        z, x, c, y = self.z, self.x, self.c, self.y
        self.zf = z + 1 - 2 * self.zl
        self.nx, self.ny = (sid(z, 1 - x, c), y), (s, 1 - y)
        self.nz, self.nc = (sid(self.zf, x, c), y), (sid(z, x, 1 - c), y)
        self.far = (sid((z + 2) % 4, x, c), y)
        self.fb = {"x": 4 * (1 - 2 * x), "y": 1 - 2 * y, "z": 8 * (1 - 2 * self.zl), "c": 2 * (1 - 2 * c)}

    def cube(self):
        z, x, c, y = self.z, self.x, self.c, self.y
        for k in range(1, 16):
            zz = self.zf if k & 8 else z
            xx = 1 - x if k & 4 else x
            cc = 1 - c if k & 2 else c
            yy = 1 - y if k & 1 else y
            yield (sid(zz, xx, cc), yy)

    def greet(self):
        others = list(self.cube())
        others += [(sid((self.z + 2) % 4, self.x, self.c), self.y), (sid((self.zf + 2) % 4, self.x, self.c), self.y)]
        barrier = pltpu.get_barrier_semaphore()
        for dev in others:
            pl.semaphore_signal(barrier, inc=1, device_id=dev, device_id_type=MESH)
        self.greeted = len(others)

    def meet(self):
        pl.semaphore_wait(pltpu.get_barrier_semaphore(), self.greeted)


class Mail:
    def __init__(self, sems, slots):
        self.sems, self.slots, self.used, self.sent = sems, slots, 0, {}

    def send(self, src, dst, rsem, dev, cond=None):
        k = self.used % self.slots
        self.used += 1
        self.settle(k)

        def make():
            return pltpu.make_async_remote_copy(
                src_ref=src, dst_ref=dst, send_sem=self.sems.at[k], recv_sem=rsem, device_id=dev, device_id_type=MESH
            )

        if cond is None:
            make().start()
        else:
            pl.when(cond)(lambda: make().start())
        self.sent[k] = (cond, make)

    def settle(self, k):
        if k in self.sent:
            cond, make = self.sent.pop(k)
            if cond is None:
                make().wait_send()
            else:
                pl.when(cond)(lambda: make().wait_send())

    def got(self, dst, rsem, dev):
        pltpu.make_async_remote_copy(
            src_ref=dst, dst_ref=dst, send_sem=self.sems.at[0], recv_sem=rsem, device_id=dev, device_id_type=MESH
        ).wait_recv()

    def close(self):
        for k in range(self.slots):
            self.settle(k)


def both(*terms):
    out = terms[0]
    for term in terms[1:]:
        out = jnp.logical_and(out, term)
    return out


def iota(shape, dim):
    return lax.broadcasted_iota(jnp.int32, shape, dim)


def norm_parts(v):
    mean = jnp.mean(v, axis=-1, keepdims=True)
    cen = v - mean
    inv = lax.rsqrt(jnp.mean(cen * cen, axis=-1, keepdims=True) + EPS)
    return cen * inv, inv


def norm_grad(z, inv, e):
    return (e - jnp.mean(e, axis=-1, keepdims=True) - z * jnp.mean(e * z, axis=-1, keepdims=True)) * inv


def pick_type(pos, head, rows):
    v = pos - head + 24.0
    m = v - 12.0 * jnp.floor((v + 0.5) * (1.0 / 12.0))
    out = jnp.where(m == 0.0, rows[4], rows[0])
    out = jnp.where(m == 6.0, rows[3], out)
    out = jnp.where(jnp.logical_or(m == 4.0, m == 8.0), rows[2], out)
    return jnp.where(jnp.logical_or(m == 2.0, m == 10.0), rows[1], out)


def halves(e, o):
    low = iota(e.shape, 1) < 64
    return jnp.where(low, e, pltpu.roll(o, 64, 1)), jnp.where(low, pltpu.roll(e, 64, 1), o)


UNITS = (0, 1, 2, 4, 6, 7)


class Spread:
    def __init__(self, p, mail, ref, sems, some):
        self.p, self.mail, self.ref, self.sems, self.some = p, mail, ref, sems, some

    def has(self, zz, xx, cc):
        return jnp.logical_or(cc == 0, zz % 2 == xx) if self.some else None

    def go(self, s, dev, cond):
        self.mail.send(self.ref.at[s], self.ref.at[s], self.sems.at[s], dev, cond)

    def take(self, s, cond):
        def wait():
            self.mail.got(self.ref.at[s], self.sems.at[s], self.p.nx)

        if cond is None:
            wait()
        else:
            pl.when(cond)(wait)

    def first(self):
        p = self.p
        has = self.has(p.z, p.x, p.c)
        for dev in (p.far, p.nz, p.nx, p.nc):
            self.go(p.s, dev, has)

    def onward(self, zz, devs):
        s, has = sid(zz, self.p.x, self.p.c), self.has(zz, self.p.x, self.p.c)
        self.take(s, has)
        for dev in devs:
            self.go(s, dev, has)

    def second(self):
        p = self.p
        self.onward((p.z + 2) % 4, (p.nz, p.nx, p.nc))
        self.onward(p.zf, (p.nx, p.nc))

    def third(self):
        p = self.p
        self.onward((p.zf + 2) % 4, (p.nx, p.nc))

    def fourth(self):
        p = self.p
        for zz in range(4):
            s, has = sid(zz, 1 - p.x, p.c), self.has(zz, 1 - p.x, p.c)
            self.take(s, has)
            self.go(s, p.nc, has)

    def last(self):
        p = self.p
        for zz in range(4):
            for xx in range(2):
                self.take(sid(zz, xx, 1 - p.c), self.has(zz, xx, 1 - p.c))


class Reduce:
    def __init__(self, p, mail, src, gc, gxs, gxr, gzs, gzr, rc, rx, rz):
        self.__dict__.update(locals())

    def rows(self, zz, xx, cc):
        return pl.ds(pl.multiple_of(sid(zz, xx, cc) * 48, 16), 48)

    def cores(self):
        p = self.p
        for xq in range(2):
            xx = 1 - p.x if xq == 0 else p.x
            for k in (1, 2, 3, 0):
                zz = (p.z + k) % 4
                self.mail.send(self.src.at[self.rows(zz, xx, 1 - p.c)], self.gc.at[xq, zz], self.rc.at[xq, zz], p.nc)

    def order(self):
        z, zf = self.p.z, self.p.zf
        return (zf + 2) % 4, (z + 2) % 4, zf, z

    def over_x(self):
        p = self.p
        for zz in self.order():
            self.mail.got(self.gc.at[0, zz], self.rc.at[0, zz], p.nc)
            own = self.src[self.rows(zz, 1 - p.x, p.c)].astype(F32)
            self.gxs[zz] = (own + self.gc[0, zz].astype(F32)).astype(B16)
            self.mail.send(self.gxs.at[zz], self.gxr.at[zz], self.rx.at[zz], p.nx)

    def column(self, zz):
        p = self.p
        self.mail.got(self.gc.at[1, zz], self.rc.at[1, zz], p.nc)
        self.mail.got(self.gxr.at[zz], self.rx.at[zz], p.nx)
        return self.src[self.rows(zz, p.x, p.c)].astype(F32) + self.gc[1, zz].astype(F32) + self.gxr[zz].astype(F32)

    def over_z(self, i):
        self.gzs[i] = self.column(self.order()[i]).astype(B16)
        self.mail.send(self.gzs.at[i], self.gzr.at[i], self.rz.at[i], self.p.nz)

    def over_far(self):
        self.mail.got(self.gzr.at[0], self.rz.at[0], self.p.nz)
        self.gzs[1] = (self.column(self.order()[1]) + self.gzr[0].astype(F32)).astype(B16)
        self.mail.send(self.gzs.at[1], self.gzr.at[1], self.rz.at[1], self.p.far)

    def result(self):
        total = self.column(self.p.z)
        for i in (1, 2):
            self.mail.got(self.gzr.at[i], self.rz.at[i], self.p.nz)
            total = total + self.gzr[i].astype(F32)
        return total


class Total:
    def __init__(self, p, mail, one, two, sem_one, sem_two):
        self.p, self.mail, self.one, self.two, self.sem_one, self.sem_two = p, mail, one, two, sem_one, sem_two
        self.k = (p.x * 2 + p.c) * 2 + p.y

    def start(self):
        p = self.p
        for i in range(1, 4):
            dev = (sid((p.z + i) % 4, p.x, p.c), p.y)
            self.mail.send(self.one.at[p.z], self.one.at[p.z], self.sem_one.at[p.z], dev)

    def middle(self):
        p = self.p
        for i in range(1, 4):
            zz = (p.z + i) % 4
            self.mail.got(self.one.at[zz], self.sem_one.at[zz], p.nx)
        self.two[self.k] = self.one[0] + self.one[1] + self.one[2] + self.one[3]
        for i in range(1, 8):
            xx = 1 - p.x if i & 4 else p.x
            cc = 1 - p.c if i & 2 else p.c
            yy = 1 - p.y if i & 1 else p.y
            self.mail.send(self.two.at[self.k], self.two.at[self.k], self.sem_two.at[self.k], (sid(p.z, xx, cc), yy))

    def finish(self):
        for i in range(8):
            pl.when(self.k != i)(lambda i=i: self.mail.got(self.two.at[i], self.sem_two.at[i], self.p.nx))
        out = self.two[0]
        for i in range(1, 8):
            out = out + self.two[i]
        return out


def mixed(shape, dim_to, dim_from):
    r, i = iota(shape, dim_to), iota(shape, dim_from)
    return jnp.where(i == 2 * (r & 63) + (r >> 6), 1.0, 0.0).astype(B16)


def kernel(
    x_ref, doc_ref, cot_ref, g1_ref, b1_ref, wq_far, bqv_ref, wo_own, bo_ref, g2_ref, b2_ref, wup_ref, bup_ref, wdn_ref, bd_ref, tab_ref,
    lout, gin, wag, woag, o_ud, o_tot,
    qa, ka, va, ns, lse, ot, dpk, gwo, dh_s, wqh, bqh, buph, msc, asc,
    xs, docs, wb, wo, dyp, orecv, osend, kvs, kvf, attn, vt, hid, n2s, dys, acts, dpre, facc, dacc, ys, yr, fs, fr, fo,
    wq_ref, dor, doa, delta, kt, dka, dva, dqt, dtt, dfs, dfr, packs, dqr, wms, wmr, n2t, dyt, ga, gb, gd, ge, ra, rb, gxr, gzr,
    hc, hxs, hxr, hzs, hzr, dall, dns, dnr, vb1, vr1, vb2, vr2,
    ss, rsx, rsc, rsd, rsw, rso, rsf, rsy, rdo, rga, rgx, rgz, rhc, rhx, rhz, rdf, rdq, rwm, rag, rwo, rdn, rv1, rv2, rv3, rv4, lds,
):
    p = Place()
    mail = Mail(ss, SLOTS)
    seg, x, y, z, c, b = p.seg, p.x, p.y, p.z, p.c, p.b
    first, second = both(p.unit, seg == 0), both(p.unit, seg == 1)
    row = lambda ref: ref[...].reshape(1, -1)
    p.greet()
    wrow = pl.ds(pl.multiple_of(p.s * 48, 16), 48)
    loads = [
        pltpu.make_async_copy(wq_far, wq_ref, lds.at[0]),
        pltpu.make_async_copy(wup_ref, wb.at[wrow, 0:1536], lds.at[1]),
        pltpu.make_async_copy(wdn_ref, wb.at[wrow, 1536:3072], lds.at[2]),
        pltpu.make_async_copy(wo_own, wo.at[y], lds.at[3]),
    ]
    for load in loads:
        load.start()

    mix = mixed((128, 128), 0, 1)
    xs[b] = dot(mix, x_ref[...]).astype(B16)
    doc_row = doc_ref[...].astype(F32).reshape(1, 128)
    turn = jnp.where(iota((128, 128), 0) == 2 * (iota((128, 128), 1) & 63), 1.0, 0.0).astype(B16)
    turn_odd = jnp.where(iota((128, 128), 0) == 2 * (iota((128, 128), 1) & 63) + 1, 1.0, 0.0).astype(B16)
    doc8 = jnp.broadcast_to(doc_row, (8, 128)).astype(B16)
    docs[b] = jnp.where(iota((8, 128), 0) == 0, dot(doc8, turn), dot(doc8, turn_odd))
    p.meet()

    dims = ("x", "y", "z")
    nbr = {"x": p.nx, "y": p.ny, "z": p.nz}
    part = [pl.ds(k * 256, 256) for k in range(3)]
    order = [[dims[(k + j) % 3] for j in range(3)] for k in range(3)]

    bit = {"x": 1, "y": 2, "z": 4}

    def place(rel):
        return b + sum(p.fb[d] for d in dims if rel & bit[d])

    def third(rel, k):
        return xs.at[place(rel), :, part[k]]

    def pass_on(k, rel, d):
        mail.send(third(rel, k), third(rel, k), rsx.at[k, rel ^ bit[d]], nbr[d])

    def to_core(k, rel):
        mail.send(third(rel, k), third(rel, k), rsc.at[k, rel], p.nc)

    for j in range(3):
        for k in range(3):
            pass_on(k, 0, order[k][j])
    for k in range(3):
        to_core(k, 0)
    special = jnp.logical_or(b == 0, b >= 14)
    for dev in p.cube():
        mail.send(docs.at[b], docs.at[b], rsd.at[b // 14 + b // 15], dev, special)

    def rows_of(s):
        return wb.at[pl.ds(pl.multiple_of(s * 48, 16), 48), :]

    def give(s, dev, cond=None):
        mail.send(rows_of(s), rows_of(s), rsw.at[s], dev, cond)


    loads[0].wait()
    pair_cols = pl.ds(pl.multiple_of(p.hl // 2 * 128, 128), 128)
    for odd in range(2):

        @pl.when(p.hl % 2 == odd)
        def _(odd=odd):
            for k in range(3):
                w = wq_ref[k, :, pair_cols].astype(F32)
                w = pltpu.roll(w, 64, 1) if odd else w
                wqh[:, k * 128 : k * 128 + 128] = jnp.where(iota((768, 128), 1) < 64, w, 0.0).astype(B16)
            v = jnp.concatenate([bqv_ref[:, pair_cols], jnp.zeros((6, 128), F32)], axis=0)
            v = pltpu.roll(v, 64, 1) if odd else v
            lane = iota((1, 128), 1)
            bqh[:, 0:128] = jnp.where(lane < 64, v[0:1], 0.0)
            bqh[:, 128:256] = jnp.zeros((1, 128), F32)
            bqh[:, 256:384] = jnp.where(lane < 64, v[1:2], jnp.where(lane == 64, 1.0, 0.0))

    head = p.head.astype(F32)
    for t in range(4):
        rr = iota((512, 128), 0)
        pos = (seg * SEG + t * 512 + 2 * (rr & 255) + (rr >> 8)).astype(F32)
        qa[t] = pick_type(pos, head, [tab_ref[i : i + 1] for i in range(5)]).astype(B16)
        ka[t + 2] = pick_type(pos, head, [tab_ref[8 + i : 9 + i] for i in range(5)]).astype(B16)

    real = jnp.broadcast_to(doc_row, (128, 128)).T >= 0.0
    for k in range(6):
        cols = slice(k * 128, k * 128 + 128)
        kept = jnp.where(real, cot_ref[:, cols].astype(F32), 0.0).astype(B16)
        dyp[y, :, cols] = dot(mix, kept).astype(B16)
    for half in range(2):

        @pl.when(y == half)
        def _(half=half):
            buph[...] = bup_ref[half * 1536 : half * 1536 + 1536].reshape(1, 1536)

    for load in loads[1:]:
        load.wait()

    def qkv(i):
        rows = xs[pl.ds(2 * i, 2)].reshape(256, 768).astype(F32)
        zz, _inv = norm_parts(rows)
        n1 = (zz * row(g1_ref) + row(b1_ref)).astype(B16)
        m = (dot(n1, wqh[...]) + bqh[...]).astype(B16)
        t = i // 2
        for yy in range(2):
            for par in range(2):
                at = slice(yy * 128 + par * 64, yy * 128 + par * 64 + 64)
                to = pl.ds(pl.multiple_of(par * 256 + (i % 2) * 128 + yy * 64, 64), 64)
                qa[t, to] = m[at, :128] * B16(0.125) + qa[t, to]
                ka[t + 2, to] = m[at, 128:256] + ka[t + 2, to]
                va[t + 2, to] = m[at, 256:]
                ns[t, to] = n1[at]

    def seen(k, rel):
        mail.got(third(rel, k), rsx.at[k, rel], p.nx)
        to_core(k, rel)

    def from_core(rel):
        for k in range(3):
            mail.got(xs.at[place(rel) + p.fb["c"], :, part[k]], rsc.at[k, rel], p.nc)

    def qkv_of(rel, core=0):
        at = (place(rel) + core * p.fb["c"]) // 2
        pl.when(p.unit)(lambda: qkv(at))

    def chain(d):
        up, dn = (z - d + 4) % 4, (z + d) % 4
        has_up, has_dn = z >= d, z <= 3 - d
        su, sd = sid(up, x, c), sid(dn, x, c)
        pl.when(has_up)(lambda: mail.got(rows_of(su), rsw.at[su], p.nx))
        if d < 3:
            give(su, (sid((z + 1) % 4, x, c), y), both(has_up, z <= 2))
        give(su, p.nx, has_up)
        give(su, p.nc, has_up)
        pl.when(has_dn)(lambda: mail.got(rows_of(sd), rsw.at[sd], p.nx))
        if d < 3:
            give(sd, (sid((z + 3) % 4, x, c), y), both(has_dn, z >= 1))
        give(sd, p.nx, has_dn)
        give(sd, p.nc, has_dn)

    X, Y, Z = 1, 2, 4
    for k in range(3):
        d0, d1, d2 = order[k]
        seen(k, bit[d0])
        pass_on(k, bit[d0], d1)
        pass_on(k, bit[d0], d2)
        seen(k, bit[d1])
        pass_on(k, bit[d1], d2)
        seen(k, bit[d2])
    qkv_of(0)
    for k in range(3):
        d0, d1, d2 = order[k]
        seen(k, bit[d0] | bit[d1])
        pass_on(k, bit[d0] | bit[d1], d2)
    give(p.s, (sid((z + 1) % 4, x, c), y), z <= 2)
    give(p.s, (sid((z + 3) % 4, x, c), y), z >= 1)
    give(p.s, p.nx)
    give(p.s, p.nc)
    mail.send(dyp.at[y], dyp.at[y], rsy.at[1], p.ny)
    whalf = pl.ds(pl.multiple_of(c * 192, 64), 192)
    mail.send(wo.at[y, whalf], wo.at[y, whalf], rsy.at[0], p.ny)
    for k in range(3):
        d0, d1, d2 = order[k]
        seen(k, bit[d0] | bit[d2])
        seen(k, bit[d1] | bit[d2])
    qkv_of(X)
    qkv_of(Z)
    from_core(0)
    from_core(Y)
    qkv_of(0, 1)
    for k in range(3):
        seen(k, X | Y | Z)
    qkv_of(X | Z)
    for rel in (X, Z, X | Z):
        from_core(rel)
        from_core(rel | Y)
        qkv_of(rel, 1)
        if rel == Z:
            chain(1)
    for src in (0, 14, 15):
        pl.when(b != src)(lambda src=src: mail.got(docs.at[src], rsd.at[src // 14 + src // 15], p.nx))

    lowlane = iota((256, 128), 1) < 64
    farrows = pl.ds(pl.multiple_of(p.parity * 256, 256), 256)

    @pl.when(first)
    def _():
        for t in range(4):
            kk = ka[t + 2, farrows].astype(F32)
            vv = va[t + 2, farrows].astype(F32)
            kvs[t] = jnp.where(lowlane, kk, pltpu.roll(vv, 64, 1)).astype(B16)

    mail.send(kvs, kvf, rsf.at[0], p.far, first)
    mail.send(docs.at[0], docs.at[16], rsf.at[1], p.far, first)

    def codes(src, par):
        r = docs[src, par : par + 1]
        return jnp.broadcast_to(jnp.where(r < 0.0, 4.0, r), (128, 128)).T[0:64]

    def mark(ref, at, code, query):
        lane = iota((64, 128), 1)
        hit = (lane - 96).astype(F32) == code
        if query:
            feat = jnp.where(hit, 0.0, jnp.where(lane < 101, NEGATIVE, 0.0))
        else:
            feat = jnp.where(hit, 1.0, 0.0)
        ref[at] = jnp.where(lane >= 96, feat, ref[at].astype(F32)).astype(B16)

    @pl.when(first)
    def _():
        for par in range(2):
            code = codes(0, par)
            at = slice(par * 256, par * 256 + 64)
            mark(qa.at[0], at, code, True)
            mark(ka.at[2], at, code, False)

    @pl.when(second)
    def _():
        for par in range(2):
            for yy in range(2):
                code = codes(14 + yy, par)
                at = slice(par * 256 + 128 + yy * 64, par * 256 + 192 + yy * 64)
                mark(qa.at[3], at, code, True)
                mark(ka.at[5], at, code, False)

    @pl.when(p.unit)
    def _():
        for t in range(4):
            vt[t + 2] = va[t + 2].astype(F32).T.astype(B16)

    rr, ll = iota((512, 512), 0), iota((512, 512), 1)
    causal = lambda st: jnp.where(2 * (rr & 255) + (rr >> 8) <= 2 * (ll & 255) + (ll >> 8), st, NEGATIVE)

    def near_attention(t):
        q = qa[t]

        def update(cc, carry, st):
            m, acc = carry
            m_new = jnp.maximum(m, jnp.max(st, axis=0, keepdims=True))
            pr = jnp.exp(st - m_new).astype(B16)
            return m_new, acc * jnp.exp(m - m_new) + dot(vt[cc], pr)

        state = (jnp.full((1, 512), NEGATIVE, F32), jnp.zeros((128, 512), F32))
        if t:
            state = lax.fori_loop(2, t + 2, lambda cc, s: update(cc, s, dot_nt(ka[cc], q)), state)
        msc[t], asc[t] = update(t + 2, state, causal(dot_nt(ka[t + 2], q)))

    def far_ready():
        mail.got(kvf, rsf.at[0], p.far)
        mail.got(docs.at[16], rsf.at[1], p.far)
        for t in range(4):
            rows = pl.ds((t % 2) * 256, 256)
            fpos = ((t * 256 + iota((256, 128), 0)) * 2 + p.parity).astype(F32)
            feat = pick_type(fpos, head, [tab_ref[16 + i : 17 + i] for i in range(5)])
            kv = kvf[t].astype(F32)
            ka[t // 2, rows] = jnp.where(lowlane, kv, feat).astype(B16)
            one = jnp.where(iota((256, 128), 1) == 64, 1.0, 0.0)
            va[t // 2, rows] = jnp.where(lowlane, pltpu.roll(kv, 64, 1), one).astype(B16)
        even, odd = codes(16, 0), codes(16, 1)
        mark(ka.at[0], slice(0, 64), even + p.parity.astype(F32) * (odd - even), False)
        for h in range(2):
            vt[h] = va[h].astype(F32).T.astype(B16)

    farcols = pl.ds(pl.multiple_of(p.parity * 256, 256), 256)

    def far_attention(t):
        q = qa[t, farcols]
        m = msc[t, :, farcols]
        s0, s1 = dot_nt(ka[0], q), dot_nt(ka[1], q)
        m_new = jnp.maximum(m, jnp.maximum(jnp.max(s0, axis=0, keepdims=True), jnp.max(s1, axis=0, keepdims=True)))
        acc = asc[t, :, farcols] * jnp.exp(m - m_new)
        acc = acc + dot(vt[0], jnp.exp(s0 - m_new).astype(B16))
        acc = acc + dot(vt[1], jnp.exp(s1 - m_new).astype(B16))
        msc[t, :, farcols] = m_new
        asc[t, :, farcols] = acc

    def conclude(t):
        acc = asc[t]
        total = acc[64:65]
        o = acc[:64] / total
        lse[t] = msc[t] + jnp.log(total)
        ot[t] = jnp.concatenate([o[:, :256], o[:, 256:]], axis=0)
        osend[t] = ot[t].T.astype(B16)

    def deliver(t, who):
        for cc in range(2):
            for yy in range(2):
                own = both(p.u == t * 2 + cc, y == yy)
                src = osend.at[t, cc * 128 : cc * 128 + 128]
                dev = (sid(seg * 2 + t // 2, t % 2, cc), yy)
                mail.send(src, orecv.at[p.head], rso.at[p.head], dev, both(who, jnp.logical_not(own)))

                @pl.when(both(who, own))
                def _(cc=cc):
                    orecv[p.head] = osend[t, cc * 128 : cc * 128 + 128]

    for t in range(4):
        pl.when(p.unit)(functools.partial(near_attention, t))
        pl.when(first)(functools.partial(conclude, t))
        deliver(t, first)
        if t == 1:
            chain(2)
        if t == 2:
            mail.got(wo.at[1 - y, whalf], rsy.at[0], p.ny)
            mail.send(wo.at[1 - y, whalf], wo.at[1 - y, whalf], rsy.at[4], p.nc)
    pl.when(second)(far_ready)
    chain(3)
    for t in range(4):
        pl.when(second)(functools.partial(far_attention, t))
        pl.when(second)(functools.partial(conclude, t))
        deliver(t, second)
    for zq in range(4):
        s = sid(zq, 1 - x, c)
        mail.got(rows_of(s), rsw.at[s], p.nx)
        give(s, p.nc)

    for hh in range(12):
        mine = both(p.unit, p.head == hh)
        pl.when(jnp.logical_not(mine))(lambda hh=hh: mail.got(orecv.at[hh], rso.at[hh], p.nx))
    for a in range(6):
        e, o = halves(orecv[2 * a].astype(F32), orecv[2 * a + 1].astype(F32))
        attn[0:128, a * 128 : a * 128 + 128] = e.astype(B16)
        attn[128:256, a * 128 : a * 128 + 128] = o.astype(B16)
    mail.got(wo.at[1 - y, pl.ds(pl.multiple_of((1 - c) * 192, 64), 192)], rsy.at[4], p.nc)
    mail.got(dyp.at[1 - y], rsy.at[1], p.ny)
    pair = pl.multiple_of(p.u * 2, 2)
    for par in range(2):
        for yy in range(2):
            at = pl.ds(par * 128 + yy * 64, 64)
            hid[at] = xs[pair + yy, par * 64 : par * 64 + 64].astype(F32)
            dys[at] = dyp[yy, par * 64 : par * 64 + 64]
    hid[...] = hid[...] + dot(attn[...], wo[...].reshape(768, 768)) + row(bo_ref)
    z2, _inv = norm_parts(hid[...])
    n2s[...] = (z2 * row(g2_ref) + row(b2_ref)).astype(B16)
    for i in range(8):
        s = sid(i // 2, i % 2, 1 - c)
        mail.got(rows_of(s), rsw.at[s], p.nc)

    k0 = 0.7978845608028654
    vb1[z] = jnp.zeros((8, 768), F32)

    def ffn_step(i, _):
        cols = pl.ds(pl.multiple_of(i * 256, 256), 256)
        dcols = pl.ds(pl.multiple_of(1536 + i * 256, 256), 256)
        up, dn = wb[:, cols], wb[:, dcols]
        pre = dot(n2s[...], up) + buph[:, cols]
        sq = pre * pre
        th = jnp.tanh(k0 * pre * (1.0 + 0.044715 * sq))
        half = 0.5 * (1.0 + th)
        act = (pre * half).astype(B16)
        slope = half + 0.5 * pre * (1.0 - th * th) * (k0 * (1.0 + 3.0 * 0.044715 * sq))
        dp = dot(dys[...], dn) * slope
        buph[:, cols] = jnp.sum(dp, axis=0, keepdims=True)
        dpl = dp.astype(B16)
        acts[:, cols] = act
        dpre[:, cols] = dpl
        return 0

    lax.fori_loop(0, 6, ffn_step, 0)
    for k in range(3):
        ys[k] = dot_nt(dpre[...], wb[k * 256 : k * 256 + 256, 0:1536]).astype(B16)
        mail.send(ys.at[k], yr.at[k], rsy.at[5 + k], p.ny)
    facc[...] = dot_nt(acts[:, 0:768], wb[:, 1536:2304]) + dot_nt(acts[:, 768:1536], wb[:, 2304:3072])
    for par in range(2):
        fo[par * 64 : par * 64 + 64] = facc[pl.ds(pl.multiple_of(par * 128 + y * 64, 64), 64)]
        fs[par * 64 : par * 64 + 64] = facc[pl.ds(pl.multiple_of(par * 128 + (1 - y) * 64, 64), 64)].astype(B16)

    n2t[...] = n2s[...].astype(F32).T.astype(B16)
    dyt[...] = dys[...].astype(F32).T.astype(B16)

    def owners(ref, xx, cc):
        at = [pl.ds(pl.multiple_of(sid(zz, xx, cc) * 48, 16), 48) for zz in range(4)]
        up = jnp.concatenate([n2t[i] for i in at], axis=0)
        dn = jnp.concatenate([dyt[i] for i in at], axis=0)

        def step(i, _):
            cols = pl.ds(pl.multiple_of(i * 256, 256), 256)
            dcols = pl.ds(pl.multiple_of(1536 + i * 256, 256), 256)
            u = dot(up, dpre[:, cols]).astype(B16)
            d = dot(dn, acts[:, cols]).astype(B16)
            for zz in range(4):
                ref[zz, :, cols] = u[zz * 48 : zz * 48 + 48]
                ref[zz, :, dcols] = d[zz * 48 : zz * 48 + 48]
            return 0

        lax.fori_loop(0, 6, step, 0)

    out_sum = Reduce(p, mail, gwo, hc, hxs, hxr, hzs, hzr, rhc, rhx, rhz)

    def ffn_over_x(i):
        zz = ring[i]
        gb[zz] = (gb[zz].astype(F32) + ra[zz].astype(F32)).astype(B16)
        mail.send(gb.at[zz], gxr.at[zz], rgx.at[zz], p.nx)

    def ffn_column(zz):
        mail.got(gxr.at[zz], rgx.at[zz], p.nx)
        return ge[zz].astype(F32) + rb[zz].astype(F32) + gxr[zz].astype(F32)

    def ffn_over_z(i):
        zz = ring[i]
        ge[zz] = ffn_column(zz).astype(B16)
        mail.send(ge.at[zz], gzr.at[i], rgz.at[i], p.nz)

    def ffn_over_far():
        zz = ring[1]
        mail.got(gzr.at[0], rgz.at[0], p.nz)
        ge[zz] = (ffn_column(zz) + gzr[0].astype(F32)).astype(B16)
        mail.send(ge.at[zz], gzr.at[1], rgz.at[1], p.far)

    ring = out_sum.order()
    owners(ga, 1 - x, 1 - c)
    mail.send(ga, ra, rga.at[0], p.nc)
    owners(gb, 1 - x, c)
    mail.got(ra, rga.at[0], p.nc)
    ffn_over_x(0)
    owners(gd, x, 1 - c)
    mail.send(gd, rb, rga.at[1], p.nc)
    owners(ge, x, c)
    @pl.when(p.unit)
    def _():
        for t in range(4):
            kt[t + 2] = ka[t + 2].astype(F32).T.astype(B16)
        dqt[...] = jnp.zeros_like(dqt)

    @pl.when(second)
    def _():
        for h in range(2):
            kt[h] = ka[h].astype(F32).T.astype(B16)

    for k in range(3):
        mail.got(yr.at[k], rsy.at[5 + k], p.ny)
    mail.send(fs, fr, rsy.at[3], p.ny)
    dn2 = jnp.concatenate([ys[k].astype(F32) + yr[k].astype(F32) for k in range(3)], axis=1)
    z2, inv2 = norm_parts(hid[...])
    dh = dys[...].astype(F32) + norm_grad(z2, inv2, dn2 * row(g2_ref))
    facc[...] = dh
    dacc[...] = dn2 * z2
    da_ = dot_nt(dh.astype(B16), wo[y])
    for a in range(3):
        e, o = halves(da_[0:128, a * 128 : a * 128 + 128], da_[128:256, a * 128 : a * 128 + 128])
        dpk[2 * a] = e.astype(B16)
        dpk[2 * a + 1] = o.astype(B16)

    mine_t = p.zl * 2 + x
    crow = pl.ds(pl.multiple_of(c * 128, 128), 128)
    for h, u in enumerate(UNITS):
        mail.send(dpk.at[h], dor.at[mine_t, crow], rdo.at[p.u], (seg * 8 + u, y), p.u != u)

        @pl.when(p.u == u)
        def _(h=h):
            dor[mine_t, crow] = dpk[h]

    gwo[...] = dot(dh.T.astype(B16), attn[:, pl.ds(pl.multiple_of(y * 384, 128), 384)]).astype(B16)
    out_sum.cores()
    ffn_over_x(1)
    mail.got(rb, rga.at[1], p.nc)
    ffn_over_z(0)
    out_sum.over_x()
    mail.got(fr, rsy.at[3], p.ny)
    sums = [jnp.zeros((1, 768), F32)] * 4
    for par in range(2):
        at = pl.ds(pl.multiple_of(par * 128 + y * 64, 64), 64)
        to = slice(par * 64, par * 64 + 64)
        dh_s[to] = facc[at]
        dn2_own = jnp.concatenate([ys[k, at].astype(F32) + yr[k, at].astype(F32) for k in range(3)], axis=1)
        own = (dacc[at], dn2_own, facc[at], dys[at].astype(F32))
        sums = [total + jnp.sum(v, axis=0, keepdims=True) for total, v in zip(sums, own)]
        fo[to] = hid[at] + fo[to] + fr[to].astype(F32) + row(bd_ref)
    back = mixed((128, 128), 1, 0)
    lout[...] = dot(back, fo[...].astype(B16)).astype(B16)
    for i in range(4):
        vb1[z, i : i + 1] = sums[i]
    for half in range(2):

        @pl.when(y == half)
        def _(half=half):
            for k in range(2):
                vb1[z, 4 + 2 * half + k : 5 + 2 * half + k] = buph[:, k * 768 : k * 768 + 768]

    early = Total(p, mail, vb1, vr1, rv1, rv2)
    late = Total(p, mail, vb2, vr2, rv3, rv4)
    early.start()
    ffn_over_x(2)

    def prepare():
        for i in range(8):
            pl.when(p.u != i)(lambda i=i: mail.got(dor.at[i // 2, (i % 2) * 128 : (i % 2) * 128 + 128], rdo.at[i], p.nx))
        low = iota((256, 128), 1) < 64
        for t in range(4):
            d = dor[t].astype(F32)
            doa[t, 0:256] = jnp.where(low, d, 0.0).astype(B16)
            doa[t, 256:512] = jnp.where(low, pltpu.roll(d, 64, 1), 0.0).astype(B16)
            prod = d.T * ot[t]
            delta[t, :, 0:256] = jnp.sum(prod[:64], axis=0, keepdims=True)
            delta[t, :, 256:512] = jnp.sum(prod[64:], axis=0, keepdims=True)

    pl.when(p.unit)(prepare)
    ffn_over_x(3)

    def score_grads(cc, q, do, st, lse_row, delta_row):
        pr = jnp.exp(st - lse_row)
        ds = (pr * (dot_nt(va[cc], do) - delta_row)).astype(B16)
        dva[...] += dot(pr.astype(B16), do)
        dka[...] += dot(ds, q)
        return dot(kt[cc], ds)

    def clear():
        dka[...] = jnp.zeros_like(dka)
        dva[...] = jnp.zeros_like(dva)

    def far_grads(cc):
        clear()

        def step(t, _):
            q, do = qa[t, farcols], doa[t, farcols]
            dqt[t, :, farcols] += score_grads(cc, q, do, dot_nt(ka[cc], q), lse[t, :, farcols], delta[t, :, farcols])
            return 0

        lax.fori_loop(0, 4, step, 0)
        low = iota((512, 128), 1) < 64
        pack = jnp.where(low, dka[...], pltpu.roll(dva[...], 64, 1)).astype(B16)
        dfs[2 * cc] = pack[:256]
        dfs[2 * cc + 1] = pack[256:]

    for cc in range(2):
        pl.when(second)(functools.partial(far_grads, cc))
        mail.send(dfs.at[2 * cc : 2 * cc + 2], dfr.at[2 * cc : 2 * cc + 2], rdf.at[cc], p.far, second)
    ffn_over_far()

    def near(t):
        clear()
        q, do = qa[t], doa[t]
        dqt[t] += score_grads(t + 2, q, do, causal(dot_nt(ka[t + 2], q)), lse[t], delta[t])
        for tq in range(t + 1, 4):
            q, do = qa[tq], doa[tq]
            dqt[tq] += score_grads(t + 2, q, do, dot_nt(ka[t + 2], q), lse[tq], delta[tq])
        dtt[64:128, t * 512 : t * 512 + 512] = dka[...].T[:64].astype(B16)
        dtt[128:192, t * 512 : t * 512 + 512] = dva[...].T[:64].astype(B16)

    def add_far(t):
        rows = dfr[t].astype(F32).T
        at = pl.ds(pl.multiple_of(t * 512 + p.parity * 256, 256), 256)
        dtt[64:128, at] = (dtt[64:128, at].astype(F32) + rows[:64]).astype(B16)
        dtt[128:192, at] = (dtt[128:192, at].astype(F32) + rows[64:]).astype(B16)

    out_sum.over_z(0)
    pl.when(p.unit)(lambda: near(0))
    out_sum.over_far()
    ffn_over_z(2)
    out_sum.over_z(2)
    early.middle()
    pl.when(p.unit)(lambda: near(1))
    pl.when(p.unit)(lambda: near(2))
    pl.when(p.unit)(lambda: near(3))
    woag[p.s] = out_sum.result().astype(B16)
    spread_out = Spread(p, mail, woag, rwo, False)
    spread_out.first()

    @pl.when(first)
    def _():
        for cc in range(2):
            mail.got(dfr.at[2 * cc : 2 * cc + 2], rdf.at[cc], p.far)
        for t in range(4):
            add_far(t)

    @pl.when(p.unit)
    def _():
        for t in range(4):
            dtt[0:64, t * 512 : t * 512 + 512] = (dqt[t, 0:64] * 0.125).astype(B16)
            for k in range(3):
                e = dtt[k * 64 : k * 64 + 64, t * 512 : t * 512 + 256].astype(F32)
                o = dtt[k * 64 : k * 64 + 64, t * 512 + 256 : t * 512 + 512].astype(F32)
                packs[t, k] = jnp.concatenate([e, o], axis=0).T.astype(B16)

    for t in range(4):
        for cc in range(2):
            u = t * 2 + cc
            mail.send(packs.at[t, :, cc * 128 : cc * 128 + 128], dqr.at[p.hl], rdq.at[p.hl], (seg * 8 + u, y), both(p.unit, p.u != u))

            @pl.when(both(p.unit, p.u == u))
            def _(t=t, cc=cc):
                dqr[p.hl] = packs[t, :, cc * 128 : cc * 128 + 128]

    vb2[z] = jnp.zeros((8, 768), F32)
    spread = Spread(p, mail, wag, rag, True)

    @pl.when(p.unit)
    def _():
        dw = dot(dtt[...], ns[...].reshape(2048, 768))
        for h in range(2):
            wms[h] = dw[h * 96 : h * 96 + 96].astype(B16)
        bias = dot_nt(jnp.ones((16, 2048), B16), dtt[...])[0:8]
        at = pl.ds(pl.multiple_of(p.head // 2 * 128, 128), 128)
        lane = iota((8, 128), 1) < 64
        low_q, low_v = jnp.where(lane, bias[:, 0:128], 0.0), jnp.concatenate([bias[:, 128:192], jnp.zeros((8, 64), F32)], axis=1)
        for odd in range(2):

            @pl.when(p.head % 2 == odd)
            def _(odd=odd):
                for i, v in enumerate((low_q, low_v)):
                    vb2[z, 2 + i : 3 + i, at] = (pltpu.roll(v, 64, 1) if odd else v)[0:1]

    mail.send(wms.at[1 - seg], wmr, rwm.at[0], p.far, p.unit)

    for h, u in enumerate(UNITS):
        pl.when(p.u != u)(lambda h=h: mail.got(dqr.at[h], rdq.at[h], p.nx))
    for k in range(3):
        for a in range(3):
            e, o = halves(dqr[2 * a, k].astype(F32), dqr[2 * a + 1, k].astype(F32))
            col = slice(a * 128, a * 128 + 128)
            dall[k, 0:128, col] = e.astype(B16)
            dall[k, 128:256, col] = o.astype(B16)
    facc[...] = dot_nt(dall[0], wq_ref[0]) + dot_nt(dall[1], wq_ref[1]) + dot_nt(dall[2], wq_ref[2])
    for par in range(2):
        dns[par * 64 : par * 64 + 64] = facc[pl.ds(pl.multiple_of(par * 128 + (1 - y) * 64, 64), 64)].astype(B16)
    mail.send(dns, dnr, rdn.at[0], p.ny)

    @pl.when(p.unit)
    def _():
        mail.got(wmr, rwm.at[0], p.far)
        wag[p.s] = (wms[seg].astype(F32) + wmr[...].astype(F32)).astype(B16)

    spread.first()
    spread_out.second()
    z1, inv1 = norm_parts(xs[b].astype(F32))
    mail.got(dnr, rdn.at[0], p.ny)
    own = [facc[pl.ds(pl.multiple_of(par * 128 + y * 64, 64), 64)] for par in range(2)]
    dn1 = jnp.concatenate(own, axis=0) + dnr[...].astype(F32)
    vb2[z, 0:1] = jnp.sum(dn1 * z1, axis=0, keepdims=True)
    vb2[z, 1:2] = jnp.sum(dn1, axis=0, keepdims=True)
    late.start()
    rest = dh_s[...] + norm_grad(z1, inv1, dn1 * row(g1_ref))
    result = jnp.zeros((128, 768), F32)
    for _k in range(3):
        piece = rest.astype(B16)
        result = result + dot(back, piece)
        rest = rest - piece.astype(F32)
    gin[...] = result
    spread.second()
    spread_out.third()
    late.middle()
    spread.third()
    spread_out.fourth()
    o_tot[0] = early.finish()
    spread.fourth()
    o_tot[1] = late.finish()
    total = ffn_column(z)
    for i in (1, 2):
        mail.got(gzr.at[i], rgz.at[i], p.nz)
        total = total + gzr[i].astype(F32)
    o_ud[0] = total[:, :1536]
    o_ud[1] = total[:, 1536:]
    spread_out.last()
    spread.last()
    mail.close()


def write_out(lout, gin, wag, woag, ud, tot, o_l, o_g, o_g1, o_b1, o_wq, o_bqv, o_wo, o_bo, o_g2, o_b2, o_up, o_bup, o_dn, o_bd):
    o_l[...] = lout[...]
    o_g[...] = gin[...]
    o_up[...] = ud[0]
    o_dn[...] = ud[1]
    for i, ref in enumerate((o_g2, o_b2, o_bo, o_bd)):
        ref[...] = tot[0, i : i + 1].reshape(768)
    for i in range(4):
        o_bup[i * 768 : i * 768 + 768] = tot[0, 4 + i : 5 + i].reshape(768)
    o_g1[...] = tot[1, 0:1].reshape(768)
    o_b1[...] = tot[1, 1:2].reshape(768)
    o_wo[...] = woag[...].reshape(768, 384).astype(F32).T
    for a in range(3):
        u0, u1 = UNITS[2 * a], UNITS[2 * a + 1]
        col = slice(a * 128, a * 128 + 128)
        w0 = jnp.concatenate([wag[u0, 0:96], wag[u0 + 8, 0:96]], axis=0).astype(F32)
        w1 = jnp.concatenate([wag[u1, 0:96], wag[u1 + 8, 0:96]], axis=0).astype(F32)
        for k in range(3):
            at = slice(k * 64, k * 64 + 64)
            o_wq[k, :, col] = jnp.concatenate([w0[at], w1[at]], axis=0).T
    half = lax.axis_index("head")
    o_bqv[...] = tot[1, 2:4, pl.ds(pl.multiple_of(half * 384, 128), 384)]


SLOTS = 40


def count_table():
    kinds = np.array([[0, 0, 0, 0], [1, 0, 0, 0], [1, 1, 0, 0], [1, 0, 1, 0], [1, 1, 1, 1]], np.float64)
    shared = kinds @ kinds.T
    table = np.zeros((24, 128), np.float64)
    low = lambda v: float(np.asarray(v, dtype=ml_dtypes.bfloat16).astype(np.float64))
    for i in range(5):
        for k in range(5):
            for base, count in ((64, 1.0 + shared[i, k]), (80, shared[i, k])):
                rest = float(np.log(count)) if count > 0 else 0.0
                for e in range(3):
                    table[i, base + 3 * k + e] = low(rest)
                    rest -= low(rest)
        table[i, 96:101] = [NEGATIVE, NEGATIVE, 0.0, NEGATIVE, NEGATIVE]
        table[8 + i, 64 + 3 * i : 67 + 3 * i] = 1.0
        table[16 + i, 80 + 3 * i : 83 + 3 * i] = 1.0
        table[8 + i, 98] = table[16 + i, 98] = 1.0
    return table.astype(np.float32)


def vm(*shape):
    return pltpu.VMEM(shape, B16)


def vf(*shape):
    return pltpu.VMEM(shape, F32)


def dma(*shape):
    return pltpu.SemaphoreType.DMA(shape)


def in_vmem(count):
    return [pl.BlockSpec(memory_space=pltpu.VMEM)] * count


def fast(
    layer_input, doc_ids, cotangent, ln1_gain, ln1_bias, w_qkv, bias_qv, w_out, b_out, ln2_gain, ln2_bias, w_up, b_up, w_down, b_down
):
    out = lambda shape, dtype=F32: jax.ShapeDtypeStruct(shape, dtype)
    shapes = (
        out((128, 768), B16), out((128, 768)), out((768,)), out((768,)), out((3, 768, 384)), out((2, 384)), out((384, 768)), out((768,)),
        out((768,)), out((768,)), out((48, 1536)), out((3072,)), out((48, 1536)), out((768,)),
    )
    raw = (out((128, 768), B16), out((128, 768)), out((16, 96, 768), B16), out((16, 48, 384), B16), out((2, 48, 1536)), out((2, 8, 768)))
    scratch = [
        vm(4, 512, 128), vm(6, 512, 128), vm(6, 512, 128), vm(4, 512, 768), vf(4, 1, 512), vf(4, 128, 256), vm(6, 128, 128),
        vm(768, 384), vf(128, 768), vm(768, 384), vf(1, 384), vf(1, 1536), vf(4, 1, 512), vf(4, 128, 512),
        vm(16, 128, 768), vf(17, 8, 128), vm(768, 3072), vm(2, 384, 768), vm(2, 128, 768), vm(12, 128, 128), vm(4, 256, 128),
        vm(4, 256, 128), vm(4, 256, 128), vm(256, 768), vm(6, 128, 512), vf(256, 768), vm(256, 768), vm(256, 768), vm(256, 1536),
        vm(256, 1536), vf(256, 768), vf(256, 768), vm(3, 256, 256), vm(3, 256, 256), vm(128, 768), vm(128, 768), vf(128, 768),
        vm(3, 768, 384), vm(4, 256, 128), vm(4, 512, 128), vf(4, 1, 512), vm(6, 128, 512), vf(512, 128), vf(512, 128), vf(4, 128, 512), vm(192, 2048),
        vm(4, 256, 128), vm(4, 256, 128), vm(4, 3, 256, 128), vm(6, 3, 128, 128), vm(2, 96, 768), vm(96, 768),
        vm(768, 256), vm(768, 256), *[vm(4, 48, 3072)] * 8,
        vm(2, 4, 48, 384), vm(4, 48, 384), vm(4, 48, 384), vm(4, 48, 384), vm(4, 48, 384), vm(3, 256, 384), vm(128, 768), vm(128, 768),
        vf(4, 8, 768), vf(8, 8, 768), vf(4, 8, 768), vf(8, 8, 768),
        dma(SLOTS), dma(3, 8), dma(3, 8), dma(3), dma(16), dma(12), dma(2), dma(8), dma(8), dma(2), dma(4), dma(3), dma(2, 4), dma(4),
        dma(3), dma(2), dma(6), dma(1), dma(16), dma(16), dma(1), dma(4), dma(8), dma(4), dma(8), dma(4),
    ]
    args = (
        layer_input, doc_ids, cotangent, ln1_gain, ln1_bias, w_qkv.transpose(1, 0, 2), bias_qv, w_out, b_out, ln2_gain, ln2_bias, w_up,
        b_up, w_down.T, b_down, jnp.asarray(count_table()),
    )
    found = pl.pallas_call(
        kernel, out_shape=raw,
        in_specs=[pl.BlockSpec(memory_space=pl.ANY) if i in (5, 7, 11, 13) else in_vmem(1)[0] for i in range(len(args))],
        out_specs=tuple(in_vmem(len(raw))), scratch_shapes=scratch,
        compiler_params=pltpu.CompilerParams(collective_id=0, has_side_effects=True, vmem_limit_bytes=LIMIT),
    )(*args)
    outs = pl.pallas_call(
        write_out, out_shape=shapes, in_specs=in_vmem(len(raw)), out_specs=tuple(in_vmem(len(shapes))),
        compiler_params=pltpu.CompilerParams(vmem_limit_bytes=LIMIT),
    )(*found)
    outs = list(outs)
    outs[4] = outs[4].transpose(1, 0, 2)
    outs[12] = outs[12].T
    return tuple(outs)


def from_behind(value, axis, by):
    length = lax.axis_size(axis)
    pairs = [(i, i + by) for i in range(length) if 0 <= i + by < length]
    return lax.ppermute(value, axis, pairs)


def layer_norm(values, gain, shift):
    mean = jnp.mean(values, axis=-1, keepdims=True)
    centred = values - mean
    spread = jnp.mean(centred * centred, axis=-1, keepdims=True)
    return centred * lax.rsqrt(spread + EPS) * gain + shift


def gelu_tanh(values):
    return jax.nn.gelu(values, approximate=True)


def pick_block(length, limit):
    chosen = 1
    for candidate in range(1, min(length, limit) + 1):
        if length % candidate == 0:
            chosen = candidate
    return chosen


def pair_counts(query_pos, key_pos, head_ids):
    total = None
    for factor, rate in LEVELS:
        width = SEG * factor
        same = query_pos[:, :, None] // width == key_pos[:, None, :] // width
        offset = (head_ids % rate)[:, None]
        pick_query = query_pos % width % rate == offset
        pick_key = key_pos % width % rate == offset
        joint = (same & pick_query[:, :, None] & pick_key[:, None, :]).astype(jnp.float32)
        total = joint if total is None else total + joint
    return total


def block_terms(
    query_blk, query_pos, query_doc, key_blk, key_pos, key_doc, head_ids, nearby, scale
):
    scores = (
        jnp.einsum("qhe,khe->hqk", query_blk, key_blk, preferred_element_type=jnp.float32) * scale
    )
    counts = pair_counts(query_pos, key_pos, head_ids)
    same_segment = query_pos[:, :, None] // SEG == key_pos[:, None, :] // SEG
    keep = same_segment if nearby else jnp.logical_not(same_segment)
    allowed = (
        keep
        & (key_pos[:, None, :] <= query_pos[:, :, None])
        & (query_doc[:, :, None] == key_doc[:, None, :])
    )
    return (scores, counts * allowed.astype(jnp.float32))


def per_device(
    layer_input,
    doc_ids,
    cotangent,
    ln1_gain,
    ln1_bias,
    w_qkv,
    bias_qv,
    w_out,
    b_out,
    ln2_gain,
    ln2_bias,
    w_up,
    b_up,
    w_down,
    b_down,
):
    seq_count = lax.axis_size("seq")
    local_heads = HEADS // lax.axis_size("head")
    local_width = local_heads * HEAD_DIM
    scale = HEAD_DIM ** (-0.5)
    f32 = jnp.float32
    b16 = jnp.bfloat16
    x_float = layer_input.astype(f32)
    norm_one = layer_norm(x_float, ln1_gain, ln1_bias)
    norm_rows, row_doc = (
        lax.all_gather(norm_one.astype(b16), "head", axis=0, tiled=True),
        lax.all_gather(doc_ids, "head", axis=0, tiled=True),
    )
    seq_tokens = norm_rows.shape[0]
    half = seq_tokens // 2
    total_tokens = seq_tokens * seq_count
    total_half = total_tokens // 2
    first_pos = lax.axis_index("seq") * seq_tokens
    last_pos = first_pos + seq_tokens - 1
    local_offsets = jnp.arange(seq_tokens, dtype=jnp.int32)
    query_pos = (first_pos + local_offsets)[None, :]
    query_doc = row_doc[None, :]
    head_ids = lax.axis_index("head") * local_heads + jnp.arange(local_heads, dtype=jnp.int32)
    parity = head_ids % 2
    pick_even = parity == 0

    def compact(rows):
        paired = rows.reshape((half, 2) + rows.shape[1:])
        mask = pick_even.reshape((1, local_heads) + (1,) * (rows.ndim - 2))
        return jnp.where(mask, paired[:, 0], paired[:, 1])

    def expand(rows):
        mask = pick_even.reshape((1, local_heads) + (1,) * (rows.ndim - 2))
        zeros = jnp.zeros_like(rows)
        paired = jnp.stack([jnp.where(mask, rows, zeros), jnp.where(mask, zeros, rows)], axis=1)
        return paired.reshape((seq_tokens,) + rows.shape[1:])

    mixed = jnp.einsum("td,dch->tch", norm_rows, w_qkv, preferred_element_type=f32)
    zero_row = jnp.zeros((1, local_width), f32)
    bias_all = jnp.concatenate([bias_qv[0:1], zero_row, bias_qv[1:2]], axis=0)
    qkv = (mixed + bias_all[None]).astype(b16)
    queries = qkv[:, 0]
    query_heads = queries.reshape(seq_tokens, local_heads, HEAD_DIM)
    key_heads = qkv[:, 1].reshape(seq_tokens, local_heads, HEAD_DIM)
    value_heads = qkv[:, 2].reshape(seq_tokens, local_heads, HEAD_DIM)
    local_keys_c = compact(key_heads)
    local_values_c = compact(value_heads)
    far_keys_all, far_values_all, doc_all = (
        lax.all_gather(local_keys_c, "seq", axis=0, tiled=True),
        lax.all_gather(local_values_c, "seq", axis=0, tiled=True),
        lax.all_gather(row_doc, "seq", axis=0, tiled=True),
    )
    segment_count = SEG // seq_tokens
    own_pair = jnp.stack([key_heads, value_heads], axis=1)
    pair_pieces = [own_pair]
    for step in range(1, segment_count):
        pair_pieces.append(from_behind(own_pair, "seq", step))
    near_pairs = jnp.concatenate(pair_pieces, axis=0)
    near_keys = near_pairs[:, 0]
    near_values = near_pairs[:, 1]
    near_flat = jnp.concatenate(
        [first_pos - step * seq_tokens + local_offsets for step in range(segment_count)]
    )
    near_doc = jnp.take(doc_all, jnp.clip(near_flat, 0, total_tokens - 1))[None, :]
    near_pos = near_flat[None, :]
    far_pos = 2 * jnp.arange(total_half, dtype=jnp.int32)[None, :] + parity[:, None]
    doc_pairs = doc_all.reshape(total_half, 2)
    far_doc = jnp.where(pick_even[:, None], doc_pairs[:, 0][None, :], doc_pairs[:, 1][None, :])
    key_block = pick_block(total_half, block_limit)
    blocks = total_half // key_block
    far_key_blocks = far_keys_all.reshape(blocks, key_block, local_heads, HEAD_DIM)
    far_value_blocks = far_values_all.reshape(blocks, key_block, local_heads, HEAD_DIM)
    far_pos_blocks = far_pos.reshape(local_heads, blocks, key_block).transpose(1, 0, 2)
    far_doc_blocks = far_doc.reshape(local_heads, blocks, key_block).transpose(1, 0, 2)
    far_begin = jnp.arange(blocks, dtype=jnp.int32) * (2 * key_block)

    def merge_stats(current, key_blk, key_pos, key_doc, nearby):
        peak, running = current
        scores, counts = block_terms(
            query_heads, query_pos, query_doc, key_blk, key_pos, key_doc, head_ids, nearby, scale
        )
        live = counts > 0
        new_peak = jnp.maximum(peak, jnp.max(jnp.where(live, scores, NEGATIVE), axis=2))
        terms = jnp.where(live, counts * jnp.exp(scores - new_peak[:, :, None]), 0.0)
        return (new_peak, running * jnp.exp(peak - new_peak) + jnp.sum(terms, axis=2))

    start_state = (
        jnp.full((local_heads, seq_tokens), NEGATIVE, f32),
        jnp.zeros((local_heads, seq_tokens), f32),
    )
    near_state = merge_stats(start_state, near_keys, near_pos, near_doc, True)

    def stats_step(state, item):
        key_blk, pos_blk, doc_blk, begin = item
        return (
            lax.cond(
                begin <= last_pos,
                lambda current: merge_stats(current, key_blk, pos_blk, doc_blk, False),
                lambda current: current,
                state,
            ),
            None,
        )

    (peak_all, running_all), _ = lax.scan(
        stats_step, near_state, (far_key_blocks, far_pos_blocks, far_doc_blocks, far_begin)
    )
    lse = peak_all + jnp.log(running_all)

    def add_output(current, key_blk, value_blk, key_pos, key_doc, nearby):
        scores, counts = block_terms(
            query_heads, query_pos, query_doc, key_blk, key_pos, key_doc, head_ids, nearby, scale
        )
        probs = jnp.where(counts > 0, counts * jnp.exp(scores - lse[:, :, None]), 0.0).astype(b16)
        return current + jnp.einsum("hqk,khe->qhe", probs, value_blk, preferred_element_type=f32)

    zero_heads = jnp.zeros((seq_tokens, local_heads, HEAD_DIM), f32)
    near_output = add_output(zero_heads, near_keys, near_values, near_pos, near_doc, True)

    def output_step(accum, item):
        key_blk, value_blk, pos_blk, doc_blk, begin = item
        return (
            lax.cond(
                begin <= last_pos,
                lambda current: add_output(current, key_blk, value_blk, pos_blk, doc_blk, False),
                lambda current: current,
                accum,
            ),
            None,
        )

    attn_exact, _ = lax.scan(
        output_step,
        near_output,
        (far_key_blocks, far_value_blocks, far_pos_blocks, far_doc_blocks, far_begin),
    )
    attn_low = attn_exact.reshape(seq_tokens, local_width).astype(b16)
    branch = lax.psum_scatter(
        jnp.dot(attn_low, w_out, preferred_element_type=f32).astype(jnp.bfloat16),
        "head",
        scatter_dimension=0,
        tiled=True,
    ).astype(jnp.float32)
    hidden_one = x_float + branch + b_out
    norm_two = layer_norm(hidden_one, ln2_gain, ln2_bias)
    norm_low = norm_two.astype(b16)
    dy_low = (cotangent.astype(f32) * (doc_ids >= 0).astype(f32)[:, None]).astype(b16)
    dy_float = dy_low.astype(f32)
    up_rows, down_rows = (
        lax.all_gather(w_up, "seq", axis=0, tiled=True),
        lax.all_gather(w_down, "seq", axis=1, tiled=True),
    )
    up_full, down_full = (
        lax.all_gather(up_rows, "head", axis=1, tiled=True),
        lax.all_gather(down_rows, "head", axis=0, tiled=True),
    )
    pre_act = jnp.dot(norm_low, up_full, preferred_element_type=f32) + b_up
    act_low = gelu_tanh(pre_act).astype(b16)
    ffn_result = jnp.dot(act_low, down_full, preferred_element_type=f32)
    d_act = jnp.einsum("td,fd->tf", dy_low, down_full, preferred_element_type=f32)
    _, gelu_back = jax.vjp(gelu_tanh, pre_act)
    d_pre = gelu_back(d_act)[0]
    d_pre_low = d_pre.astype(b16)
    bias_up_grad = jnp.sum(d_pre, axis=0)
    up_parts = jnp.einsum("td,tf->df", norm_low, d_pre_low, preferred_element_type=f32)
    down_parts = jnp.einsum("tf,td->fd", act_low, dy_low, preferred_element_type=f32)
    up_grad, down_grad = (
        lax.psum_scatter(
            up_parts.astype(jnp.bfloat16), "head", scatter_dimension=1, tiled=True
        ).astype(jnp.float32),
        lax.psum_scatter(
            down_parts.astype(jnp.bfloat16), "head", scatter_dimension=0, tiled=True
        ).astype(jnp.float32),
    )
    d_norm_two = jnp.einsum("tf,df->td", d_pre_low, up_full, preferred_element_type=f32)
    layer_output = (hidden_one + ffn_result + b_down).astype(b16)
    w_up_grad, w_down_grad = (
        lax.psum_scatter(up_grad, "seq", scatter_dimension=0, tiled=True),
        lax.psum_scatter(down_grad, "seq", scatter_dimension=1, tiled=True),
    )
    _, norm_two_back = jax.vjp(layer_norm, hidden_one, ln2_gain, ln2_bias)
    d_hidden_norm, gain_two_grad, bias_two_grad = norm_two_back(d_norm_two)
    d_hidden = dy_float + d_hidden_norm
    bias_out_grad = jnp.sum(d_hidden, axis=0)
    bias_down_grad = jnp.sum(dy_float, axis=0)
    hidden_rows = lax.all_gather(d_hidden.astype(b16), "head", axis=0, tiled=True)
    w_out_part = jnp.einsum("tc,td->cd", attn_low, hidden_rows, preferred_element_type=f32)
    d_attn = jnp.einsum("td,cd->tc", hidden_rows, w_out, preferred_element_type=f32).astype(b16)
    d_attn_heads = d_attn.reshape(seq_tokens, local_heads, HEAD_DIM)
    delta_rows = jnp.sum(d_attn_heads.astype(f32) * attn_exact, axis=2)
    delta = delta_rows.T

    def score_grads(key_blk, value_blk, key_pos, key_doc, nearby):
        scores, counts = block_terms(
            query_heads, query_pos, query_doc, key_blk, key_pos, key_doc, head_ids, nearby, scale
        )
        exact = jnp.where(counts > 0, counts * jnp.exp(scores - lse[:, :, None]), 0.0)
        d_prob = jnp.einsum("qhe,khe->hqk", d_attn_heads, value_blk, preferred_element_type=f32)
        d_score = (exact * (d_prob - delta[:, :, None])).astype(b16)
        return (exact, d_score)

    exact_near, d_score_near = score_grads(near_keys, near_values, near_pos, near_doc, True)
    d_query_near = jnp.einsum("hqk,khe->qhe", d_score_near, near_keys, preferred_element_type=f32)
    near_key_grad = jnp.einsum(
        "hqk,qhe->khe", d_score_near, query_heads, preferred_element_type=f32
    )
    near_value_grad = jnp.einsum(
        "hqk,qhe->khe", exact_near.astype(b16), d_attn_heads, preferred_element_type=f32
    )
    near_pair_grads = jnp.stack([near_key_grad, near_value_grad], axis=1)
    pair_grad = near_pair_grads[:seq_tokens]
    for step in range(1, segment_count):
        piece = near_pair_grads[step * seq_tokens : (step + 1) * seq_tokens]
        pair_grad = pair_grad + from_behind(piece.astype(jnp.bfloat16), "seq", -step).astype(
            piece.dtype
        )

    def query_grad_step(accum, item):
        key_blk, value_blk, pos_blk, doc_blk, begin = item

        def query_compute(current):
            _, d_score = score_grads(key_blk, value_blk, pos_blk, doc_blk, False)
            return current + jnp.einsum(
                "hqk,khe->qhe", d_score, key_blk, preferred_element_type=f32
            )

        return (lax.cond(begin <= last_pos, query_compute, lambda current: current, accum), None)

    d_query, _ = lax.scan(
        query_grad_step,
        d_query_near,
        (far_key_blocks, far_value_blocks, far_pos_blocks, far_doc_blocks, far_begin),
    )
    d_query = d_query * scale
    stats_rows = jnp.stack([compact(lse.T), compact(delta_rows)], axis=1)
    stats_all = lax.all_gather(stats_rows, "seq", axis=0, tiled=True)
    local_key_pos = first_pos + 2 * jnp.arange(half, dtype=jnp.int32)[None, :] + parity[:, None]
    local_key_doc = compact(jnp.broadcast_to(row_doc[:, None], (seq_tokens, local_heads))).T
    zero_compact = jnp.zeros((half, local_heads, HEAD_DIM), f32)
    query_piece = lax.all_gather(compact(query_heads), "seq", axis=0, tiled=True)
    grad_piece = lax.all_gather(compact(d_attn_heads), "seq", axis=0, tiled=True)
    length = query_piece.shape[0]
    size = pick_block(length, block_limit)
    number = length // size
    pos_piece = 2 * jnp.arange(length, dtype=jnp.int32)[None, :] + parity[:, None]
    items = (
        query_piece.reshape(number, size, local_heads, HEAD_DIM),
        grad_piece.reshape(number, size, local_heads, HEAD_DIM),
        stats_all.reshape(number, size, 2, local_heads),
        pos_piece.reshape(local_heads, number, size).transpose(1, 0, 2),
        far_doc.reshape(local_heads, number, size).transpose(1, 0, 2),
    )

    def one_step(current, item):
        query_blk, grad_blk, stats_blk, pos_blk, doc_blk = item

        def one_compute(pair):
            key_grad, value_grad = pair
            scores, counts = block_terms(
                query_blk,
                pos_blk,
                doc_blk,
                local_keys_c,
                local_key_pos,
                local_key_doc,
                head_ids,
                False,
                scale,
            )
            exact = jnp.where(
                counts > 0, counts * jnp.exp(scores - stats_blk[:, 0].T[:, :, None]), 0.0
            )
            d_prob = jnp.einsum(
                "qhe,khe->hqk", grad_blk, local_values_c, preferred_element_type=f32
            )
            d_score = (exact * (d_prob - stats_blk[:, 1].T[:, :, None])).astype(b16)
            key_grad = key_grad + jnp.einsum(
                "hqk,qhe->khe", d_score, query_blk, preferred_element_type=f32
            )
            value_grad = value_grad + jnp.einsum(
                "hqk,qhe->khe", exact.astype(b16), grad_blk, preferred_element_type=f32
            )
            return (key_grad, value_grad)

        return (
            lax.cond(jnp.max(pos_blk) >= first_pos, one_compute, lambda pair: pair, current),
            None,
        )

    result, _ = lax.scan(one_step, (zero_compact, zero_compact), items)
    far_key_grad, far_value_grad = result
    d_key = (pair_grad[:, 0] + expand(far_key_grad)) * scale
    d_value = pair_grad[:, 1] + expand(far_value_grad)
    d_qkv = jnp.stack(
        [
            d_query.reshape(seq_tokens, local_width),
            d_key.reshape(seq_tokens, local_width),
            d_value.reshape(seq_tokens, local_width),
        ],
        axis=1,
    ).astype(b16)
    d_qkv_float = d_qkv.astype(f32)
    bias_qv_part = jnp.stack(
        [jnp.sum(d_qkv_float[:, 0], axis=0), jnp.sum(d_qkv_float[:, 2], axis=0)], axis=0
    )
    w_qkv_part = jnp.einsum("td,tch->dch", norm_rows, d_qkv, preferred_element_type=f32)
    d_norm_one = lax.psum_scatter(
        jnp.einsum("tch,dch->td", d_qkv, w_qkv, preferred_element_type=f32).astype(jnp.bfloat16),
        "head",
        scatter_dimension=0,
        tiled=True,
    ).astype(jnp.float32)
    _, norm_one_back = jax.vjp(layer_norm, x_float, ln1_gain, ln1_bias)
    d_x_norm, gain_one_grad, bias_one_grad = norm_one_back(d_norm_one)
    grad_input = d_hidden + d_x_norm
    w_qkv_grad, bias_qv_grad, w_out_grad = lax.psum((w_qkv_part, bias_qv_part, w_out_part), "seq")
    summed = lax.psum(
        (
            gain_one_grad,
            bias_one_grad,
            gain_two_grad,
            bias_two_grad,
            bias_out_grad,
            bias_up_grad,
            bias_down_grad,
        ),
        ("seq", "head"),
    )
    return (
        layer_output,
        grad_input,
        summed[0],
        summed[1],
        w_qkv_grad,
        bias_qv_grad,
        w_out_grad,
        summed[4],
        summed[2],
        summed[3],
        w_up_grad,
        summed[5],
        w_down_grad,
        summed[6],
    )


def solution(mesh):
    in_specs = (
        P(("seq", "head"), None),
        P(("seq", "head")),
        P(("seq", "head"), None),
        P(),
        P(),
        P(None, None, "head"),
        P(None, "head"),
        P("head", None),
        P(),
        P(),
        P(),
        P("seq", "head"),
        P(),
        P("head", "seq"),
        P(),
    )
    out_specs = (
        P(("seq", "head"), None),
        P(("seq", "head"), None),
        P(),
        P(),
        P(None, None, "head"),
        P(None, "head"),
        P("head", None),
        P(),
        P(),
        P(),
        P("seq", "head"),
        P(),
        P("head", "seq"),
        P(),
    )
    small = mesh.shape["seq"] == 16 and mesh.shape["head"] == 2
    return jax.shard_map(
        fast if small else per_device, mesh=mesh, in_specs=in_specs, out_specs=out_specs, check_vma=False
    )
```
